32 devices in a mesh: dp: 4 (over x, core), ctx: 8 (over z, y).
Axes of the slice: x: 2, y: 2, z: 4, core: 2. Of those that a mesh axis runs over, the one named last changes fastest.
Arguments:
- layer_in: bfloat16 [4096, 2048], P(('dp', 'ctx')), may hold values from -6 to 6
- positions: int32 [4096], P(('dp', 'ctx')), may hold values from 0 to 1023, as said below
- doc_starts: int32 [4, 3], P('dp'), may hold values from 0 to 1023, as said below
- out_grad: bfloat16 [4096, 2048], P(('dp', 'ctx')), may hold values from -6 to 6
- norm_gains: float32 [2, 2048], P(None, ('dp', 'ctx')), may hold values from 0.5 to 1.5
- norm_gains_m: float32 [2, 2048], P(None, ('dp', 'ctx')), may hold values from -160 to 160
- norm_gains_v: float32 [2, 2048], P(None, ('dp', 'ctx')), may hold values from 3440.64 to 13926.4
- w_query: float32 [2048, 2048], P(('dp', 'ctx')), may hold values from -0.25 to 0.25
- w_query_m: float32 [2048, 2048], P(('dp', 'ctx')), may hold values from -64 to 64
- w_query_v: float32 [2048, 2048], P(('dp', 'ctx')), may hold values from 655.36 to 2580.48
- key_value_weight: float32 [2048, 1024], P(('dp', 'ctx')), may hold values from -0.125 to 0.125
- key_value_first_moment: float32 [2048, 1024], P(('dp', 'ctx')), may hold values from -224 to 224
- key_value_second_moment: float32 [2048, 1024], P(('dp', 'ctx')), may hold values from 5324.8 to 21708.8
- w_out: float32 [2048, 2048], P(('dp', 'ctx')), may hold values from -0.25 to 0.25
- w_out_m: float32 [2048, 2048], P(('dp', 'ctx')), may hold values from -32 to 32
- w_out_v: float32 [2048, 2048], P(('dp', 'ctx')), may hold values from 148 to 592
- w_gate_up: float32 [2048, 16384], P(('dp', 'ctx')), may hold values from -0.125 to 0.125
- w_gate_up_m: float32 [2048, 16384], P(('dp', 'ctx')), may hold values from -32 to 32
- w_gate_up_v: float32 [2048, 16384], P(('dp', 'ctx')), may hold values from 139.264 to 552.96
- w_down: float32 [8192, 2048], P(('dp', 'ctx')), may hold values from -0.09375 to 0.09375
- w_down_m: float32 [8192, 2048], P(('dp', 'ctx')), may hold values from -24 to 24
- w_down_v: float32 [8192, 2048], P(('dp', 'ctx')), may hold values from 77.824 to 311.296
Outputs:
- layer_out: bfloat16 [4096, 2048], P(('dp', 'ctx'))
- in_grad: float32 [4096, 2048], P(('dp', 'ctx'))
- norm_gains_grad: float32 [2, 2048], P(None, ('dp', 'ctx'))
- norm_gains_m_new: float32 [2, 2048], P(None, ('dp', 'ctx'))
- norm_gains_v_new: float32 [2, 2048], P(None, ('dp', 'ctx'))
- norm_gains_new: float32 [2, 2048], P(None, ('dp', 'ctx'))
- w_query_grad: float32 [2048, 2048], P(('dp', 'ctx'))
- w_query_m_new: float32 [2048, 2048], P(('dp', 'ctx'))
- w_query_v_new: float32 [2048, 2048], P(('dp', 'ctx'))
- w_query_new: float32 [2048, 2048], P(('dp', 'ctx'))
- w_keyval_grad: float32 [2048, 1024], P(('dp', 'ctx'))
- w_keyval_m_new: float32 [2048, 1024], P(('dp', 'ctx'))
- w_keyval_v_new: float32 [2048, 1024], P(('dp', 'ctx'))
- w_keyval_new: float32 [2048, 1024], P(('dp', 'ctx'))
- w_out_grad: float32 [2048, 2048], P(('dp', 'ctx'))
- w_out_m_new: float32 [2048, 2048], P(('dp', 'ctx'))
- w_out_v_new: float32 [2048, 2048], P(('dp', 'ctx'))
- w_out_new: float32 [2048, 2048], P(('dp', 'ctx'))
- w_gate_up_grad: float32 [2048, 16384], P(('dp', 'ctx'))
- w_gate_up_m_new: float32 [2048, 16384], P(('dp', 'ctx'))
- w_gate_up_v_new: float32 [2048, 16384], P(('dp', 'ctx'))
- w_gate_up_new: float32 [2048, 16384], P(('dp', 'ctx'))
- w_down_grad: float32 [8192, 2048], P(('dp', 'ctx'))
- w_down_m_new: float32 [8192, 2048], P(('dp', 'ctx'))
- w_down_v_new: float32 [8192, 2048], P(('dp', 'ctx'))
- w_down_new: float32 [8192, 2048], P(('dp', 'ctx'))
The draws below stay inside these ranges and needn't reach their ends.
Inputs may be any that keep to these rules, and one draw needn't show every extreme that they name: Each sequence's positions are a permutation of 0 to 1023 made of 16 runs of 64 consecutive positions, each run starting at a multiple of 64, the runs in an order drawn for each sequence. `doc_starts`: in each sequence the 3 starts rise strictly over the whole sequence, the first is 0; a document runs from its start to the next start or to the sequence's end.
All inputs are finite; a program needn't handle non-finite values.
Results may differ from the reference program's by a relative error of at most 0.018.
The reference program's roundings to bfloat16 on the way count: a program that leaves them out, or rounds other values in their place, can miss the bound.
Values may be sent and summed in bfloat16 or wider, within the bound.
A program may use at most 512 MiB of HBM per device.

```python
import math
from functools import partial
import jax
import jax.numpy as jnp
from jax import lax

MODEL_WIDTH = 2048
QUERY_HEADS = 32
KEY_VALUE_HEADS = 8
HEAD_SIZE = 64
FF = 8192
STEP = 10
SEQUENCE_COUNT = 4
SEQUENCE_TOKENS = 1024
HALF = 64
NBLK = 16
TOKEN_TOTAL = 4096


def draw_positions(key, part):
    key = jax.random.fold_in(key, 11)
    seq_keys = jax.random.split(key, SEQUENCE_COUNT)
    orders = jax.vmap(lambda one_key: jax.random.permutation(one_key, NBLK))(seq_keys)
    offsets = jnp.arange(HALF, dtype=jnp.int32)
    token_placement = orders.astype(jnp.int32)[:, :, None] * HALF + offsets[None, None, :]
    return token_placement.reshape(-1).astype(jnp.int32)


def draw_doc_starts(key, part):
    key = jax.random.fold_in(key, 23)
    first_key, second_key, pick_key, early_key = jax.random.split(key, 4)
    first_start = jax.random.randint(first_key, (SEQUENCE_COUNT, 1), 1, SEQUENCE_TOKENS // 2)
    second_start = jax.random.randint(second_key, (SEQUENCE_COUNT, 1), SEQUENCE_TOKENS // 2, SEQUENCE_TOKENS)
    early_start = jax.random.randint(early_key, (SEQUENCE_COUNT, 1), 1, HALF)
    chosen = jax.random.randint(pick_key, (), 0, SEQUENCE_COUNT)
    rows = jnp.arange(SEQUENCE_COUNT, dtype=jnp.int32)[:, None]
    first_start = jnp.where(rows == chosen, early_start, first_start).astype(jnp.int32)
    second_start = jnp.where(rows == chosen, SEQUENCE_TOKENS - 1, second_start).astype(jnp.int32)
    zeros_col = jnp.zeros((SEQUENCE_COUNT, 1), jnp.int32)
    return jnp.concatenate([zeros_col, first_start, second_start], axis=1).astype(jnp.int32)


def block_levels(stream_key, extent, cuts, low, top_value):
    def one(dim, shards_of):
        steps = jax.random.uniform(jax.random.fold_in(jax.random.fold_in(stream_key, 6), dim), (shards_of,), jnp.float32, low / len(cuts), top_value / len(cuts))
        return jnp.repeat(jnp.exp(steps), extent[dim] // shards_of).reshape((-1,) + (1,) * (len(extent) - dim - 1))

    gain = one(*cuts[0])
    for cut in cuts[1:]:
        gain = gain * one(*cut)
    return gain


def gaussian(own_key, dims, spread, most, cuts=(), held_as=jnp.bfloat16):
    values = spread * jax.random.normal(own_key, dims, jnp.float32)
    if cuts:
        values = values * block_levels(own_key, dims, cuts, -0.22, 0.18)
    return jnp.clip(values, -most, most).astype(held_as)


def setup_inputs(seed: int = 0) -> dict:
    seeds = jax.random.split(jax.random.key(seed), 23)
    layer_in = gaussian(seeds[0], (TOKEN_TOTAL, MODEL_WIDTH), 1.0, 6.0, ((0, 32),))
    positions = draw_positions(jax.random.fold_in(seeds[22], 71), 0)
    doc_starts = draw_doc_starts(jax.random.fold_in(seeds[22], 71), 0)
    out_grad = gaussian(seeds[3], (TOKEN_TOTAL, MODEL_WIDTH), 1.0, 6.0, ((0, 32),))
    norm_gains = jnp.clip(1.0 + 0.1 * jax.random.normal(seeds[4], (2, MODEL_WIDTH), jnp.float32), 0.5, 1.5)
    norm_gains_m = gaussian(seeds[5], (2, MODEL_WIDTH), (0.44 * TOKEN_TOTAL ** 0.5), 160.0, ((1, 32),), jnp.float32)
    norm_gains_v = jnp.clip(jnp.exp(math.log(13926.4) - 1.3981289 * jax.random.uniform(seeds[6], (2, MODEL_WIDTH), jnp.float32) ** block_levels(seeds[6], (2, MODEL_WIDTH), ((1, 32),), -0.2, 0.2)), 3440.64, 13926.4)
    w_query = gaussian(seeds[7], (MODEL_WIDTH, QUERY_HEADS * HEAD_SIZE), (MODEL_WIDTH // 4) ** -0.5, 0.25, ((0, 32),), jnp.float32)
    w_query_m = gaussian(seeds[8], (MODEL_WIDTH, QUERY_HEADS * HEAD_SIZE), (0.19 * TOKEN_TOTAL ** 0.5), 64.0, ((0, 32),), jnp.float32)
    w_query_v = jnp.clip(jnp.exp(math.log(2580.48) - 1.370546 * jax.random.uniform(seeds[9], (MODEL_WIDTH, QUERY_HEADS * HEAD_SIZE), jnp.float32) ** block_levels(seeds[9], (MODEL_WIDTH, QUERY_HEADS * HEAD_SIZE), ((0, 32),), -0.2, 0.2)), 655.36, 2580.48)
    key_value_weight = gaussian(seeds[10], (MODEL_WIDTH, 2 * KEY_VALUE_HEADS * HEAD_SIZE), MODEL_WIDTH ** -0.5, 0.125, ((0, 32),), jnp.float32)
    key_value_first_moment = gaussian(seeds[11], (MODEL_WIDTH, 2 * KEY_VALUE_HEADS * HEAD_SIZE), (0.55 * TOKEN_TOTAL ** 0.5), 224.0, ((0, 32),), jnp.float32)
    key_value_second_moment = jnp.clip(jnp.exp(math.log(21708.8) - 1.4053426 * jax.random.uniform(seeds[12], (MODEL_WIDTH, 2 * KEY_VALUE_HEADS * HEAD_SIZE), jnp.float32) ** block_levels(seeds[12], (MODEL_WIDTH, 2 * KEY_VALUE_HEADS * HEAD_SIZE), ((0, 32),), -0.2, 0.2)), 5324.8, 21708.8)
    w_out = gaussian(seeds[13], (QUERY_HEADS * HEAD_SIZE, MODEL_WIDTH), (max(220 * MODEL_WIDTH // SEQUENCE_TOKENS, 1)) ** -0.5, 0.25, ((0, 32),), jnp.float32)
    w_out_m = gaussian(seeds[14], (QUERY_HEADS * HEAD_SIZE, MODEL_WIDTH), (2.9 * (TOKEN_TOTAL / SEQUENCE_TOKENS) ** 0.5), 32.0, ((0, 32),), jnp.float32)
    w_out_v = jnp.clip(jnp.exp(math.log(592.0) - 1.3862944 * jax.random.uniform(seeds[15], (QUERY_HEADS * HEAD_SIZE, MODEL_WIDTH), jnp.float32) ** block_levels(seeds[15], (QUERY_HEADS * HEAD_SIZE, MODEL_WIDTH), ((0, 32),), -0.2, 0.2)), 148.0, 592.0)
    w_gate_up = gaussian(seeds[16], (MODEL_WIDTH, 2 * FF), MODEL_WIDTH ** -0.5, 0.125, ((0, 32),), jnp.float32)
    w_gate_up_m = gaussian(seeds[17], (MODEL_WIDTH, 2 * FF), (0.089 * TOKEN_TOTAL ** 0.5), 32.0, ((0, 32),), jnp.float32)
    w_gate_up_v = jnp.clip(jnp.exp(math.log(552.96) - 1.3789142 * jax.random.uniform(seeds[18], (MODEL_WIDTH, 2 * FF), jnp.float32) ** block_levels(seeds[18], (MODEL_WIDTH, 2 * FF), ((0, 32),), -0.2, 0.2)), 139.264, 552.96)
    w_down = gaussian(seeds[19], (FF, MODEL_WIDTH), (FF // 2) ** -0.5, 0.09375, ((0, 32),), jnp.float32)
    w_down_m = gaussian(seeds[20], (FF, MODEL_WIDTH), (0.067 * TOKEN_TOTAL ** 0.5), 24.0, ((0, 32),), jnp.float32)
    w_down_v = jnp.clip(jnp.exp(math.log(311.296) - 1.3862944 * jax.random.uniform(seeds[21], (FF, MODEL_WIDTH), jnp.float32) ** block_levels(seeds[21], (FF, MODEL_WIDTH), ((0, 32),), -0.2, 0.2)), 77.824, 311.296)
    return {"layer_in": layer_in, "positions": positions, "doc_starts": doc_starts, "out_grad": out_grad, "norm_gains": norm_gains, "norm_gains_m": norm_gains_m, "norm_gains_v": norm_gains_v, "w_query": w_query, "w_query_m": w_query_m, "w_query_v": w_query_v, "key_value_weight": key_value_weight, "key_value_first_moment": key_value_first_moment, "key_value_second_moment": key_value_second_moment, "w_out": w_out, "w_out_m": w_out_m, "w_out_v": w_out_v, "w_gate_up": w_gate_up, "w_gate_up_m": w_gate_up_m, "w_gate_up_v": w_gate_up_v, "w_down": w_down, "w_down_m": w_down_m, "w_down_v": w_down_v}


@jax.custom_vjp
def reduced_precision(v):
    return lax.optimization_barrier(v.astype(jnp.bfloat16)).astype(jnp.float32)

@jax.custom_vjp
def low_back(v):
    return v

def low_keep(v):
    return (reduced_precision(v), None)

def low_pass(kept, grad):
    return (grad,)

def back_keep(v):
    return (v, None)

def back_low(kept, grad):
    return (reduced_precision(grad),)
reduced_precision.defvjp(low_keep, low_pass)
low_back.defvjp(back_keep, back_low)
highest = lax.Precision.HIGHEST
eps_norm = 1e-05
rope_base = 500000.0
beta_one = 0.9
beta_two = 0.95
eps_adam = 1e-08
weight_decay = 0.1
masked_score = -1e+30

def rates_for(seq_len):
    return (0.6, 0.8 / math.sqrt(MODEL_WIDTH // 4), 0.8 / math.sqrt(MODEL_WIDTH), 0.8 / math.sqrt(max(220 * MODEL_WIDTH // seq_len, 1)), 0.8 / math.sqrt(MODEL_WIDTH), 0.8 / math.sqrt(FF // 2))

def adamw(weight, grad_sum, first, second, rate, decay):
    first_new = beta_one * first + (1.0 - beta_one) * grad_sum
    second_new = beta_two * second + (1.0 - beta_two) * grad_sum * grad_sum
    first_hat = first_new / (1.0 - beta_one ** STEP)
    second_hat = second_new / (1.0 - beta_two ** STEP)
    weight_new = weight - rate * (first_hat / (jnp.sqrt(second_hat) + eps_adam) + decay * weight)
    return (first_new, second_new, weight_new)

def rms_norm(layer_rows, gain_row):
    inverse = lax.rsqrt(lax.optimization_barrier(jnp.mean(layer_rows * layer_rows, axis=-1, keepdims=True)) + eps_norm)
    return layer_rows * inverse * gain_row

def apply_rotation(value_rows, token_placement):
    half_dim = value_rows.shape[-1] // 2
    frequencies = jnp.exp(jnp.arange(half_dim, dtype=jnp.float32) * (-2.0 * math.log(rope_base) / value_rows.shape[-1]))
    angles = token_placement.astype(jnp.float32)[:, None] * frequencies[None, :]
    cosine_table = jnp.cos(angles)[:, None, :]
    sine_table = jnp.sin(angles)[:, None, :]
    first_half = value_rows[..., :half_dim]
    second_half = value_rows[..., half_dim:]
    return jnp.concatenate([first_half * cosine_table - second_half * sine_table, second_half * cosine_table + first_half * sine_table], axis=-1)

def attend_one_sequence(items):
    query_rows, key_rows, value_rows, token_placement, document_index = items
    rows_per_block = math.gcd(SEQUENCE_TOKENS, 512)
    count_of_blocks = SEQUENCE_TOKENS // rows_per_block
    query_group_size = QUERY_HEADS // KEY_VALUE_HEADS
    score_scale = 1.0 / math.sqrt(HEAD_SIZE)

    def single_block(parts):
        query_blk, place_blk, doc_blk = parts
        raw_scores = jnp.einsum('tkgd,nkd->tkgn', query_blk, key_rows, precision=highest)
        scores = low_back(raw_scores) * score_scale
        allowed = (token_placement[None, :] <= place_blk[:, None]) & (document_index[None, :] == doc_blk[:, None])
        allowed = allowed[:, None, None, :]
        masked = jnp.where(allowed, scores, masked_score)
        row_top = lax.optimization_barrier(jnp.max(masked, axis=-1, keepdims=True))
        exponent = jnp.where(allowed, jnp.exp(masked - row_top), 0.0)
        attention = exponent / lax.optimization_barrier(jnp.sum(exponent, axis=-1, keepdims=True))
        return jnp.einsum('tkgn,nkd->tkgd', reduced_precision(attention), value_rows, precision=highest)
    output_blocks = lax.map(jax.checkpoint(single_block), (query_rows.reshape(count_of_blocks, rows_per_block, KEY_VALUE_HEADS, query_group_size, HEAD_SIZE), token_placement.reshape(count_of_blocks, rows_per_block), document_index.reshape(count_of_blocks, rows_per_block)))
    return output_blocks.reshape(SEQUENCE_TOKENS, KEY_VALUE_HEADS, query_group_size, HEAD_SIZE)

def layer(layer_in, norm_gains, w_query, key_value_weight, w_out, w_gate_up, w_down, positions, document_index):
    number_of_tokens = layer_in.shape[0]
    key_value_width = KEY_VALUE_HEADS * HEAD_SIZE
    query_group_size = QUERY_HEADS // KEY_VALUE_HEADS
    gains_low = reduced_precision(norm_gains)
    input_one = reduced_precision(rms_norm(layer_in, gains_low[0]))
    query_pre = low_back(jnp.dot(input_one, reduced_precision(w_query), precision=highest))
    key_value_projected = low_back(jnp.dot(input_one, reduced_precision(key_value_weight), precision=highest))
    query_rows = reduced_precision(apply_rotation(query_pre.reshape(number_of_tokens, QUERY_HEADS, HEAD_SIZE), positions))
    key_rows = reduced_precision(apply_rotation(key_value_projected[:, :key_value_width].reshape(number_of_tokens, KEY_VALUE_HEADS, HEAD_SIZE), positions))
    value_rows = reduced_precision(key_value_projected[:, key_value_width:].reshape(number_of_tokens, KEY_VALUE_HEADS, HEAD_SIZE))
    attention_output = lax.map(attend_one_sequence, (query_rows.reshape(SEQUENCE_COUNT, SEQUENCE_TOKENS, KEY_VALUE_HEADS, query_group_size, HEAD_SIZE), key_rows.reshape(SEQUENCE_COUNT, SEQUENCE_TOKENS, KEY_VALUE_HEADS, HEAD_SIZE), value_rows.reshape(SEQUENCE_COUNT, SEQUENCE_TOKENS, KEY_VALUE_HEADS, HEAD_SIZE), positions.reshape(SEQUENCE_COUNT, SEQUENCE_TOKENS), document_index.reshape(SEQUENCE_COUNT, SEQUENCE_TOKENS)))
    mixed = reduced_precision(low_back(attention_output.reshape(number_of_tokens, QUERY_HEADS * HEAD_SIZE)))
    branch = low_back(jnp.dot(mixed, reduced_precision(w_out), precision=highest))
    middle = layer_in + branch
    input_two = reduced_precision(rms_norm(middle, gains_low[1]))
    gate_up = low_back(jnp.dot(input_two, reduced_precision(w_gate_up), precision=highest))
    hidden = reduced_precision(jax.nn.silu(gate_up[:, :FF]) * gate_up[:, FF:])
    return middle + jnp.dot(hidden, reduced_precision(w_down), precision=highest)

def reference(layer_in, positions, doc_starts, out_grad, norm_gains, norm_gains_m, norm_gains_v, w_query, w_query_m, w_query_v, key_value_weight, key_value_first_moment, key_value_second_moment, w_out, w_out_m, w_out_v, w_gate_up, w_gate_up_m, w_gate_up_v, w_down, w_down_m, w_down_v):
    starts = jnp.repeat(doc_starts, SEQUENCE_TOKENS, axis=0)
    document_index = (lax.optimization_barrier(jnp.sum((positions[:, None] >= starts).astype(jnp.int32), axis=1)) - 1).astype(jnp.int32)
    forward = partial(layer, positions=positions, document_index=document_index)
    result, pull_back = jax.vjp(forward, layer_in.astype(jnp.float32), norm_gains, w_query, key_value_weight, w_out, w_gate_up, w_down)
    grads = pull_back(result.astype(jnp.float32) * 0.0 + out_grad.astype(jnp.float32))
    rates = rates_for(SEQUENCE_TOKENS)
    gains_m_new, gains_v_new, gains_new = adamw(norm_gains, grads[1], norm_gains_m, norm_gains_v, rates[0], 0.0)
    query_m_new, query_v_new, query_new = adamw(w_query, grads[2], w_query_m, w_query_v, rates[1], weight_decay)
    keyval_m_new, keyval_v_new, keyval_new = adamw(key_value_weight, grads[3], key_value_first_moment, key_value_second_moment, rates[2], weight_decay)
    out_m_new, out_v_new, out_new = adamw(w_out, grads[4], w_out_m, w_out_v, rates[3], weight_decay)
    gate_up_m_new, gate_up_v_new, gate_up_new = adamw(w_gate_up, grads[5], w_gate_up_m, w_gate_up_v, rates[4], weight_decay)
    down_m_new, down_v_new, down_new = adamw(w_down, grads[6], w_down_m, w_down_v, rates[5], weight_decay)
    return (result.astype(jnp.bfloat16), grads[0], grads[1], gains_m_new, gains_v_new, gains_new, grads[2], query_m_new, query_v_new, query_new, grads[3], keyval_m_new, keyval_v_new, keyval_new, grads[4], out_m_new, out_v_new, out_new, grads[5], gate_up_m_new, gate_up_v_new, gate_up_new, grads[6], down_m_new, down_v_new, down_new)
```

```python
import functools
import math

import jax
import jax.numpy as jnp
from jax import lax
from jax.experimental import pallas as pl
from jax.experimental.pallas import tpu as pltpu
from jax.sharding import PartitionSpec as P

MODEL_WIDTH = 2048
QUERY_HEADS = 32
KEY_VALUE_HEADS = 8
HEAD_SIZE = 64
FF = 8192
STEP = 10


eps_norm = 1e-05
rope_base = 500000.0
beta_one = 0.9
beta_two = 0.95
eps_adam = 1e-08
weight_decay = 0.1
masked_score = -1e30


def rates_for(seq_len):
    return (
        0.6,
        0.8 / math.sqrt(MODEL_WIDTH // 4),
        0.8 / math.sqrt(MODEL_WIDTH),
        0.8 / math.sqrt(max(220 * MODEL_WIDTH // seq_len, 1)),
        0.8 / math.sqrt(MODEL_WIDTH),
        0.8 / math.sqrt(FF // 2),
    )


def adamw(weight, grad_sum, first, second, rate, decay):
    first_new = beta_one * first + (1.0 - beta_one) * grad_sum
    second_new = beta_two * second + (1.0 - beta_two) * grad_sum * grad_sum
    first_hat = first_new / (1.0 - beta_one**STEP)
    second_hat = second_new / (1.0 - beta_two**STEP)
    weight_new = weight - rate * (first_hat / (jnp.sqrt(second_hat) + eps_adam) + decay * weight)
    return (first_new, second_new, weight_new)


def norm_forward(layer_rows):
    inverse = lax.rsqrt(jnp.mean(layer_rows * layer_rows, axis=-1, keepdims=True) + eps_norm)
    return (layer_rows * inverse, inverse)


def norm_backward(grad_out, normed, inverse, gain_row):
    scaled = grad_out * gain_row
    grad_in = inverse * (scaled - normed * jnp.mean(scaled * normed, axis=-1, keepdims=True))
    return (grad_in, jnp.sum(grad_out * normed, axis=0))


def rope_tables(token_placement, head_dim):
    half_dim = head_dim // 2
    frequencies = jnp.exp(
        jnp.arange(half_dim, dtype=jnp.float32) * (-2.0 * math.log(rope_base) / head_dim)
    )
    angles = token_placement.astype(jnp.float32)[:, None] * frequencies[None, :]
    return (jnp.cos(angles)[:, None, :], jnp.sin(angles)[:, None, :])


def apply_rotation(value_rows, cosine_table, sine_table):
    half_dim = value_rows.shape[-1] // 2
    first_half = value_rows[..., :half_dim]
    second_half = value_rows[..., half_dim:]
    return jnp.concatenate(
        [
            first_half * cosine_table - second_half * sine_table,
            second_half * cosine_table + first_half * sine_table,
        ],
        axis=-1,
    )


def reverse_rotation(grad_rows, cosine_table, sine_table):
    half_dim = grad_rows.shape[-1] // 2
    first_half = grad_rows[..., :half_dim]
    second_half = grad_rows[..., half_dim:]
    return jnp.concatenate(
        [
            first_half * cosine_table + second_half * sine_table,
            second_half * cosine_table - first_half * sine_table,
        ],
        axis=-1,
    )


def doc_lookup(token_placement, starts):
    return jnp.sum((token_placement[:, None] >= starts[None, :]).astype(jnp.int32), axis=1) - 1


def times_transposed(left, right):
    return lax.dot_general(
        left, right, (((1,), (1,)), ((), ())), preferred_element_type=jnp.float32
    )


def transposed_times(left, right):
    return lax.dot_general(
        left, right, (((0,), (0,)), ((), ())), preferred_element_type=jnp.float32
    )


XS = 2
YS = 2
ZS = 4
PLANE = ZS * YS
RANKS = 2 * XS * PLANE
MESH = pl.DeviceIdType.MESH


def place():
    d = lax.axis_index("dp")
    c = lax.axis_index("ctx")
    return d, c, lax.div(d, 2), lax.rem(d, 2), lax.div(c, YS), lax.rem(c, YS)


def remote(src, dst, send_sem, recv_sem, d, c):
    return pltpu.make_async_remote_copy(
        src_ref=src,
        dst_ref=dst,
        send_sem=send_sem,
        recv_sem=recv_sem,
        device_id=(d, c),
        device_id_type=MESH,
    )


def greet(peers):
    barrier = pltpu.get_barrier_semaphore()
    for d, c in peers:
        pl.semaphore_signal(barrier, inc=1, device_id=(d, c), device_id_type=MESH)
    pl.semaphore_wait(barrier, len(peers))


def plane_peers(d, c):
    return [(d, lax.rem(c + k, PLANE)) for k in range(1, PLANE)]


def chip_peers(d, c, x, core):
    return [(x * 2 + 1 - core, c), ((1 - x) * 2 + core, c)]


class SequenceGather:
    def __init__(self, own, out, sems, chunks):
        self.own, self.out, self.chunks = own, out, chunks
        self.zs, self.zr, self.ys, self.yr, self.local_sem = sems
        self.d, self.c, _, _, self.z, self.y = place()
        self.rows = own.shape[0] // chunks
        self.sent = []

    @staticmethod
    def scratch(chunks):
        return [
            pltpu.SemaphoreType.DMA((ZS, chunks)),
            pltpu.SemaphoreType.DMA((ZS, chunks)),
            pltpu.SemaphoreType.DMA((ZS, chunks)),
            pltpu.SemaphoreType.DMA((ZS, chunks)),
            pltpu.SemaphoreType.DMA(()),
        ]

    def part(self, ref, k):
        return ref.at[pl.ds(k * self.rows, self.rows)]

    def across(self, z, k, src):
        slot = z * YS + self.y
        return remote(
            src,
            self.part(self.out.at[slot], k),
            self.ys.at[z, k],
            self.yr.at[z, k],
            self.d,
            self.z * YS + 1 - self.y,
        )

    def along(self, off, k):
        to = lax.rem(self.z + off, ZS)
        return remote(
            self.part(self.own, k),
            self.part(self.out.at[self.c], k),
            self.zs.at[off, k],
            self.zr.at[self.z, k],
            self.d,
            to * YS + self.y,
        )

    def first(self):
        self.local = pltpu.make_async_copy(self.own, self.out.at[self.c], self.local_sem)
        self.local.start()
        for k in range(self.chunks):
            for off in (2, 1, 3):
                copy = self.along(off, k)
                copy.start()
                self.sent.append(copy)
            copy = self.across(self.z, k, self.part(self.own, k))
            copy.start()
            self.sent.append(copy)

    def relay(self, k):
        for off in (1, 3, 2):
            source = lax.rem(self.z + off, ZS)
            slot = source * YS + self.y
            block = self.part(self.out.at[slot], k)
            remote(
                block, block, self.zs.at[off, k], self.zr.at[source, k], self.d, slot
            ).wait_recv()
            copy = self.across(source, k, block)
            copy.start()
            self.sent.append(copy)

    def last(self):
        for k in range(self.chunks):
            for z in range(ZS):
                block = self.part(self.out.at[z * YS + 1 - self.y], k)
                remote(
                    block,
                    block,
                    self.ys.at[z, k],
                    self.yr.at[z, k],
                    self.d,
                    self.z * YS + 1 - self.y,
                ).wait_recv()
        for copy in self.sent:
            copy.wait_send()
        self.local.wait()


class SequenceScatter:
    def __init__(self, parts, out, ybuf, stage, zbuf, sems, chunks):
        self.parts, self.out, self.chunks = parts, out, chunks
        self.ybuf, self.stage, self.zbuf = ybuf, stage, zbuf
        self.ys, self.yr, self.zs, self.zr = sems
        self.d, self.c, _, _, self.z, self.y = place()
        self.rows = parts.shape[1] // chunks
        self.sent = []

    @staticmethod
    def scratch(rows, width, chunks):
        return [
            pltpu.VMEM((ZS, rows, width), jnp.bfloat16),
            pltpu.VMEM((ZS, rows, width), jnp.bfloat16),
            pltpu.VMEM((ZS, rows, width), jnp.bfloat16),
            pltpu.SemaphoreType.DMA((ZS, chunks)),
            pltpu.SemaphoreType.DMA((ZS, chunks)),
            pltpu.SemaphoreType.DMA((ZS, chunks)),
            pltpu.SemaphoreType.DMA((ZS, chunks)),
        ]

    def span(self, k):
        return pl.ds(k * self.rows, self.rows)

    def across(self, z, k):
        return remote(
            self.parts.at[z * YS + 1 - self.y, self.span(k)],
            self.ybuf.at[z, self.span(k)],
            self.ys.at[z, k],
            self.yr.at[z, k],
            self.d,
            self.z * YS + 1 - self.y,
        )

    def along(self, off, k):
        to = lax.rem(self.z + off, ZS)
        return remote(
            self.stage.at[off, self.span(k)],
            self.zbuf.at[self.z, self.span(k)],
            self.zs.at[off, k],
            self.zr.at[self.z, k],
            self.d,
            to * YS + self.y,
        )

    def first(self):
        for k in range(self.chunks):
            for off in (2, 1, 3, 0):
                copy = self.across(lax.rem(self.z + off, ZS), k)
                copy.start()
                self.sent.append(copy)

    def relay(self, k):
        for off in (2, 1, 3):
            z = lax.rem(self.z + off, ZS)
            self.across(z, k).wait_recv()
            self.stage[off, self.span(k)] = (
                self.parts[z * YS + self.y, self.span(k)].astype(jnp.float32)
                + self.ybuf[z, self.span(k)].astype(jnp.float32)
            ).astype(jnp.bfloat16)
            copy = self.along(off, k)
            copy.start()
            self.sent.append(copy)

    def last(self, k):
        self.across(self.z, k).wait_recv()
        total = self.parts[self.c, self.span(k)].astype(jnp.float32) + self.ybuf[
            self.z, self.span(k)
        ].astype(jnp.float32)
        for off in (1, 3, 2):
            source = lax.rem(self.z + off, ZS)
            block = self.zbuf.at[source, self.span(k)]
            remote(
                block,
                block,
                self.zs.at[off, k],
                self.zr.at[source, k],
                self.d,
                source * YS + self.y,
            ).wait_recv()
            total = total + block[...].astype(jnp.float32)
        self.out[self.span(k)] = total

    def finish(self):
        for copy in self.sent:
            copy.wait_send()


class ChipGather:
    def __init__(self, out, sems, count):
        self.out, self.count = out, count
        self.cs, self.cr, self.xs, self.xr = sems
        self.d, self.c, self.x, self.core, _, _ = place()
        self.sent = []

    @staticmethod
    def scratch(count):
        return [
            pltpu.SemaphoreType.DMA((2, count)),
            pltpu.SemaphoreType.DMA((2, count)),
            pltpu.SemaphoreType.DMA((count,)),
            pltpu.SemaphoreType.DMA((count,)),
        ]

    def to_core(self, far, j, src=None):
        x = 1 - self.x if far else self.x
        block = self.out.at[(x * 2 + self.core) * self.count + j]
        return remote(
            block if src is None else src,
            block,
            self.cs.at[far, j],
            self.cr.at[far, j],
            self.x * 2 + 1 - self.core,
            self.c,
        )

    def to_x(self, j, src=None):
        block = self.out.at[self.d * self.count + j]
        return remote(
            block if src is None else src,
            block,
            self.xs.at[j],
            self.xr.at[j],
            (1 - self.x) * 2 + self.core,
            self.c,
        )

    def start(self, j, src=None):
        for copy in (self.to_x(j, src), self.to_core(0, j, src)):
            copy.start()
            self.sent.append(copy)

    def relay(self, j):
        self.to_x(j).wait_recv()
        copy = self.to_core(1, j)
        copy.start()
        self.sent.append(copy)

    def last(self):
        for far in (0, 1):
            for j in range(self.count):
                self.to_core(far, j).wait_recv()
        for copy in self.sent:
            copy.wait_send()


class WeightGather:
    def __init__(self, blocks, out, sems):
        self.blocks, self.out = blocks, out
        self.ps, self.pr, self.local_sem = sems[:3]
        self.chip = ChipGather(out, sems[3:], PLANE)
        self.d, self.c = self.chip.d, self.chip.c
        self.sent = []

    @staticmethod
    def scratch():
        return [
            pltpu.SemaphoreType.DMA((PLANE,)),
            pltpu.SemaphoreType.DMA((PLANE,)),
            pltpu.SemaphoreType.DMA(()),
        ] + ChipGather.scratch(PLANE)

    def first(self):
        self.local = pltpu.make_async_copy(
            self.blocks.at[self.c], self.out.at[self.d * PLANE + self.c], self.local_sem
        )
        self.local.start()
        for off in range(1, PLANE):
            to = lax.rem(self.c + off, PLANE)
            copy = remote(
                self.blocks.at[to],
                self.out.at[self.d * PLANE + self.c],
                self.ps.at[off],
                self.pr.at[self.c],
                self.d,
                to,
            )
            copy.start()
            self.sent.append(copy)
        self.chip.start(self.c, self.blocks.at[self.c])

    def relay(self, off):
        source = lax.rem(self.c + PLANE - off, PLANE)
        block = self.out.at[self.d * PLANE + source]
        remote(
            block, block, self.ps.at[off], self.pr.at[source], self.d, source
        ).wait_recv()
        self.chip.start(source)

    def relay_chip(self):
        for off in range(PLANE):
            self.chip.relay(lax.rem(self.c + off, PLANE))

    def last(self):
        self.chip.last()
        for copy in self.sent:
            copy.wait_send()
        self.local.wait()


def add_into(target, sources, rows, step=16):
    @pl.loop(0, rows, step=step)
    def _(r):
        at = pl.ds(pl.multiple_of(r, step), step)
        total = sources[0][at].astype(jnp.float32)
        for source in sources[1:]:
            total = total + source[at].astype(jnp.float32)
        target[at] = total.astype(target.dtype)


class ChipScatter:
    def __init__(self, parts, cbuf, stage, xbuf, sems, count):
        self.parts, self.count = parts, count
        self.cbuf, self.stage, self.xbuf = cbuf, stage, xbuf
        self.cs, self.cr, self.xs, self.xr = sems
        self.d, self.c, self.x, self.core, _, _ = place()
        self.sent = []

    @staticmethod
    def scratch(count, rows, width):
        return [
            pltpu.VMEM((2, count, rows, width), jnp.bfloat16),
            pltpu.VMEM((count, rows, width), jnp.bfloat16),
            pltpu.VMEM((count, rows, width), jnp.bfloat16),
            pltpu.SemaphoreType.DMA((2, count)),
            pltpu.SemaphoreType.DMA((2, count)),
            pltpu.SemaphoreType.DMA((count,)),
            pltpu.SemaphoreType.DMA((count,)),
        ]

    def to_core(self, far, j):
        x = 1 - self.x if far else self.x
        return remote(
            self.parts.at[(x * 2 + 1 - self.core) * self.count + j],
            self.cbuf.at[far, j],
            self.cs.at[far, j],
            self.cr.at[far, j],
            self.x * 2 + 1 - self.core,
            self.c,
        )

    def to_x(self, j):
        return remote(
            self.stage.at[j],
            self.xbuf.at[j],
            self.xs.at[j],
            self.xr.at[j],
            (1 - self.x) * 2 + self.core,
            self.c,
        )

    def start(self, j):
        for far in (1, 0):
            copy = self.to_core(far, j)
            copy.start()
            self.sent.append(copy)

    def relay(self, j):
        self.to_core(1, j).wait_recv()
        own = self.parts.at[((1 - self.x) * 2 + self.core) * self.count + j]
        add_into(self.stage.at[j], [own, self.cbuf.at[1, j]], own.shape[0])
        copy = self.to_x(j)
        copy.start()
        self.sent.append(copy)

    def total(self, j, target):
        self.to_core(0, j).wait_recv()
        self.to_x(j).wait_recv()
        own = self.parts.at[self.d * self.count + j]
        add_into(target, [own, self.cbuf.at[0, j], self.xbuf.at[j]], own.shape[0])

    def finish(self):
        for copy in self.sent:
            copy.wait_send()


class WeightScatter:
    def __init__(self, parts, out, bufs, sems):
        self.stage = bufs[0]
        self.ps, self.pr = sems[:2]
        self.chip = ChipScatter(parts, *bufs[1:], sems[2:], PLANE)
        self.out = out
        self.d, self.c = self.chip.d, self.chip.c
        self.sent = []

    @staticmethod
    def scratch(rows, width):
        chip = ChipScatter.scratch(PLANE, rows, width)
        return [
            pltpu.VMEM((PLANE, rows, width), jnp.bfloat16),
            *chip[:3],
            pltpu.SemaphoreType.DMA((PLANE,)),
            pltpu.SemaphoreType.DMA((PLANE,)),
            *chip[3:],
        ]

    def first(self):
        for off in range(1, PLANE + 1):
            self.chip.start(lax.rem(self.c + off, PLANE))

    def relay(self, off):
        self.chip.relay(lax.rem(self.c + off, PLANE))

    def send(self, off):
        to = lax.rem(self.c + off, PLANE)
        if off == PLANE:
            self.chip.total(to, self.out.at[self.c])
            return
        self.chip.total(to, self.stage.at[to])
        copy = remote(
            self.stage.at[to],
            self.out.at[self.c],
            self.ps.at[off],
            self.pr.at[self.c],
            self.d,
            to,
        )
        copy.start()
        self.sent.append(copy)

    def last(self):
        for off in range(1, PLANE):
            source = lax.rem(self.c + off, PLANE)
            block = self.out.at[source]
            remote(
                block, block, self.ps.at[off], self.pr.at[source], self.d, source
            ).wait_recv()
        for copy in self.sent:
            copy.wait_send()
        self.chip.finish()


def params(collective_id):
    return pltpu.CompilerParams(
        collective_id=collective_id, has_side_effects=True, vmem_limit_bytes=56 * 2**20
    )


ANY = pl.BlockSpec(memory_space=pl.ANY)
VMEM = pl.BlockSpec(memory_space=pltpu.VMEM)
CHUNKS = 4


def opening_kernel(rows_ref, spots_ref, blocks_ref, rows_out, spots_out, blocks_out, *scratch):
    spot_send, spot_recv, spot_local = scratch[:3]
    gather = SequenceGather(rows_ref, rows_out, scratch[3:8], CHUNKS)
    weights = WeightGather(blocks_ref, blocks_out, scratch[8:])
    d, c, x, core, z, y = place()
    greet(plane_peers(d, c) + chip_peers(d, c, x, core))
    weights.first()
    sent = []
    local = pltpu.make_async_copy(spots_ref, spots_out.at[c], spot_local)
    local.start()
    for off in range(1, PLANE):
        to = lax.rem(c + off, PLANE)
        copy = remote(
            spots_ref, spots_out.at[c], spot_send.at[off], spot_recv.at[c], d, to
        )
        copy.start()
        sent.append(copy)
    gather.first()
    for off in range(1, PLANE):
        weights.relay(off)
    for k in range(CHUNKS):
        gather.relay(k)
    weights.relay_chip()
    gather.last()
    weights.last()
    for off in range(1, PLANE):
        source = lax.rem(c + off, PLANE)
        block = spots_out.at[source]
        remote(block, block, spot_send.at[off], spot_recv.at[source], d, source).wait_recv()
    for copy in sent:
        copy.wait_send()
    local.wait()


def opening(rows, spots, blocks):
    return pl.pallas_call(
        opening_kernel,
        out_shape=(
            jax.ShapeDtypeStruct((PLANE, *rows.shape), rows.dtype),
            jax.ShapeDtypeStruct((PLANE, *spots.shape), spots.dtype),
            jax.ShapeDtypeStruct((RANKS, *blocks.shape[1:]), blocks.dtype),
        ),
        in_specs=[ANY] * 3,
        out_specs=(ANY,) * 3,
        scratch_shapes=[
            pltpu.SemaphoreType.DMA((PLANE,)),
            pltpu.SemaphoreType.DMA((PLANE,)),
            pltpu.SemaphoreType.DMA(()),
            *SequenceGather.scratch(CHUNKS),
            *WeightGather.scratch(),
        ],
        compiler_params=params(1),
        name="opening",
    )(rows, spots, blocks)


def gather_kernel(rows_ref, rows_out, *scratch):
    gather = SequenceGather(rows_ref, rows_out, scratch, CHUNKS)
    d, c, x, core, z, y = place()
    greet(
        [(d, lax.rem(z + off, ZS) * YS + y) for off in range(1, ZS)] + [(d, z * YS + 1 - y)]
    )
    gather.first()
    for k in range(CHUNKS):
        gather.relay(k)
    gather.last()


def gather_rows(rows, collective_id):
    return pl.pallas_call(
        gather_kernel,
        out_shape=jax.ShapeDtypeStruct((PLANE, *rows.shape), rows.dtype),
        in_specs=[ANY],
        out_specs=ANY,
        scratch_shapes=SequenceGather.scratch(CHUNKS),
        compiler_params=params(collective_id),
        name="gather_rows",
    )(rows)


def scatter_kernel(parts_ref, out_ref, *scratch):
    scatter = SequenceScatter(parts_ref, out_ref, *scratch[:3], scratch[3:], CHUNKS)
    d, c, x, core, z, y = place()
    greet(
        [(d, lax.rem(z + off, ZS) * YS + y) for off in range(1, ZS)] + [(d, z * YS + 1 - y)]
    )
    scatter.first()
    for k in range(CHUNKS):
        scatter.relay(k)
    for k in range(CHUNKS):
        scatter.last(k)
    scatter.finish()


def scatter_rows(parts, collective_id):
    return pl.pallas_call(
        scatter_kernel,
        out_shape=jax.ShapeDtypeStruct(parts.shape[1:], jnp.float32),
        in_specs=[VMEM],
        out_specs=VMEM,
        scratch_shapes=SequenceScatter.scratch(*parts.shape[1:], CHUNKS),
        compiler_params=params(collective_id),
        name="scatter_rows",
    )(parts)


DOWN_PARTS = 4
SCORE_SCALE = 1.0 / math.sqrt(HEAD_SIZE)
GROUP = QUERY_HEADS // KEY_VALUE_HEADS
PAIRS = GROUP // 2


def times_rows(left, right):
    return lax.dot_general(
        left, right, (((1,), (1,)), ((), ())), preferred_element_type=jnp.float32
    )


def down_kernel(rows_ref, down_ref, rows_out, down_out, *scratch):
    down_local = scratch[0]
    gather = SequenceGather(rows_ref, rows_out, scratch[1:6], CHUNKS)
    down = ChipGather(down_out, scratch[6:], DOWN_PARTS)
    d, c, x, core, z, y = place()
    greet(plane_peers(d, c) + chip_peers(d, c, x, core))
    local = pltpu.make_async_copy(
        down_ref, down_out.at[pl.ds(d * DOWN_PARTS, DOWN_PARTS)], down_local
    )
    local.start()
    gather.first()
    for j in range(DOWN_PARTS):
        down.start(j, down_ref.at[j])
    for k in range(CHUNKS):
        gather.relay(k)
    for j in range(DOWN_PARTS):
        down.relay(j)
    gather.last()
    down.last()
    local.wait()


def gather_with_down(rows, down, collective_id):
    return pl.pallas_call(
        down_kernel,
        out_shape=(
            jax.ShapeDtypeStruct((PLANE, *rows.shape), rows.dtype),
            jax.ShapeDtypeStruct((4 * DOWN_PARTS, *down.shape[1:]), down.dtype),
        ),
        in_specs=[ANY] * 2,
        out_specs=(ANY,) * 2,
        scratch_shapes=[
            pltpu.SemaphoreType.DMA(()),
            *SequenceGather.scratch(CHUNKS),
            *ChipGather.scratch(DOWN_PARTS),
        ],
        compiler_params=params(collective_id),
        name="gather_with_down",
    )(rows, down)


class PlaneExchange:
    def __init__(self, blocks, out, sems):
        self.blocks, self.out = blocks, out
        self.ps, self.pr, self.local_sem = sems
        self.d, self.c = lax.axis_index("dp"), lax.axis_index("ctx")
        self.sent = []

    @staticmethod
    def scratch():
        return [
            pltpu.SemaphoreType.DMA((PLANE,)),
            pltpu.SemaphoreType.DMA((PLANE,)),
            pltpu.SemaphoreType.DMA(()),
        ]

    def send(self, off):
        to = lax.rem(self.c + off, PLANE)
        if off % PLANE == 0:
            self.local = pltpu.make_async_copy(
                self.blocks.at[to], self.out.at[self.c], self.local_sem
            )
            self.local.start()
            return
        copy = remote(
            self.blocks.at[to],
            self.out.at[self.c],
            self.ps.at[off],
            self.pr.at[self.c],
            self.d,
            to,
        )
        copy.start()
        self.sent.append(copy)

    def arrive(self, off):
        if off % PLANE == 0:
            self.local.wait()
            return
        source = lax.rem(self.c + PLANE - off, PLANE)
        block = self.out.at[source]
        remote(
            block, block, self.ps.at[off], self.pr.at[source], self.d, source
        ).wait_recv()

    def finish(self):
        for copy in self.sent:
            copy.wait_send()


def probabilities(query, keys, spot, start, key_spots):
    scores = times_rows(query, keys) * SCORE_SCALE
    masked = jnp.where((key_spots <= spot) & (key_spots >= start), scores, masked_score)
    exponent = jnp.exp(masked - jnp.max(masked, axis=-1, keepdims=True))
    return exponent * (1.0 / jnp.sum(exponent, axis=-1, keepdims=True))


def attention_kernel(
    query_ref,
    key_ref,
    value_ref,
    spot_ref,
    start_ref,
    key_spot_ref,
    blocks_ref,
    out_rows_ref,
    mixed_out,
    blocks_out,
    out_rows_out,
    *scratch,
):
    mixed_stage = scratch[0]
    exchange = PlaneExchange(mixed_stage, mixed_out, scratch[1:4])
    weights = WeightGather(blocks_ref, blocks_out, scratch[4:11])
    d, c, x, core, z, y = place()
    gather = SequenceGather(
        out_rows_ref, out_rows_out.at[pl.ds(d * PLANE, PLANE)], scratch[11:16], 1
    )
    chip = ChipGather(out_rows_out, scratch[16:], PLANE)
    greet(plane_peers(d, c) + chip_peers(d, c, x, core))
    gather.first()
    chip.start(c, out_rows_ref)
    weights.first()
    for step in range(1, PLANE + 1):
        block = lax.rem(c + step, PLANE)

        @pl.loop(0, PAIRS)
        def _(pair):
            halves = []
            for half in range(2):
                probs = probabilities(
                    query_ref[block, pair, half],
                    key_ref[...],
                    spot_ref[block],
                    start_ref[block],
                    key_spot_ref[...],
                )
                halves.append(
                    jnp.dot(
                        probs.astype(jnp.bfloat16),
                        value_ref[...],
                        preferred_element_type=jnp.float32,
                    ).astype(jnp.bfloat16)
                )
            mixed_stage[block, pair] = jnp.concatenate(halves, axis=1)

        exchange.send(step)
        if step == 1:
            gather.relay(0)
            for off in range(1, ZS):
                chip.start(lax.rem(z + off, ZS) * YS + y)
        if step < PLANE:
            weights.relay(step)
    gather.last()
    for other in range(ZS):
        chip.start(other * YS + 1 - y)
    for off in range(PLANE):
        chip.relay(lax.rem(c + off, PLANE))
    weights.relay_chip()
    for off in range(1, PLANE + 1):
        exchange.arrive(off)
    chip.last()
    weights.last()
    exchange.finish()


def attention(query, keys, values, spots, starts, key_spots, blocks, out_rows):
    exchanged = jax.ShapeDtypeStruct(
        (PLANE, PAIRS, query.shape[3], 2 * HEAD_SIZE), jnp.bfloat16
    )
    return pl.pallas_call(
        attention_kernel,
        out_shape=(
            exchanged,
            jax.ShapeDtypeStruct((RANKS, *blocks.shape[1:]), blocks.dtype),
            jax.ShapeDtypeStruct((RANKS, *out_rows.shape), out_rows.dtype),
        ),
        in_specs=[VMEM] * 6 + [ANY] * 2,
        out_specs=(VMEM, ANY, ANY),
        scratch_shapes=[
            pltpu.VMEM(exchanged.shape, jnp.bfloat16),
            *PlaneExchange.scratch(),
            *WeightGather.scratch(),
            *SequenceGather.scratch(1),
            *ChipGather.scratch(PLANE),
        ],
        compiler_params=params(2),
        name="attention",
    )(query, keys, values, spots, starts, key_spots, blocks, out_rows)


def attention_back_kernel(
    query_ref,
    key_ref,
    value_ref,
    spot_ref,
    start_ref,
    key_spot_ref,
    mixed_ref,
    parts_ref,
    down_ref,
    query_out,
    key_out,
    value_out,
    out_ref,
    down_out,
    *scratch,
):
    mixed_all = scratch[0]
    exchange = PlaneExchange(mixed_ref, mixed_all, scratch[1:4])
    weights = WeightScatter(parts_ref, out_ref, scratch[4:8], scratch[8:14])
    down = ChipScatter(down_ref, *scratch[14:17], scratch[17:], DOWN_PARTS)
    d, c, x, core, z, y = place()
    greet(plane_peers(d, c) + chip_peers(d, c, x, core))
    for off in range(1, PLANE + 1):
        exchange.send(off)
    weights.first()
    for j in range(DOWN_PARTS):
        down.start(j)
    key_out[...] = jnp.zeros_like(key_out)
    value_out[...] = jnp.zeros_like(value_out)
    for step in range(PLANE):
        block = lax.rem(c + PLANE - step, PLANE)
        exchange.arrive(step)

        @pl.loop(0, PAIRS)
        def _(pair):
            for half in range(2):
                query = query_ref[block, pair, half]
                grad = mixed_all[block, pair][:, half * HEAD_SIZE : (half + 1) * HEAD_SIZE]
                probs = probabilities(
                    query, key_ref[...], spot_ref[block], start_ref[block], key_spot_ref[...]
                )
                grad_probs = times_rows(grad, value_ref[...])
                delta = jnp.sum(probs * grad_probs, axis=-1, keepdims=True)
                grad_scores = (probs * (grad_probs - delta) * SCORE_SCALE).astype(jnp.bfloat16)
                query_out[block, pair, half] = jnp.dot(
                    grad_scores, key_ref[...], preferred_element_type=jnp.float32
                )
                key_out[...] += transposed_times(grad_scores, query)
                value_out[...] += transposed_times(probs.astype(jnp.bfloat16), grad)

        weights.relay(step + 1)
        if step >= 2:
            weights.send(step - 1)
    for off in (PLANE - 1, PLANE):
        weights.send(off)
    for j in range(DOWN_PARTS):
        down.relay(j)
    for j in range(DOWN_PARTS):
        down.total(j, down_out.at[j])
    weights.last()
    down.finish()
    exchange.finish()


def attention_back(query, keys, values, spots, starts, key_spots, mixed, parts, down):
    return pl.pallas_call(
        attention_back_kernel,
        out_shape=(
            jax.ShapeDtypeStruct(query.shape, jnp.float32),
            jax.ShapeDtypeStruct(keys.shape, jnp.float32),
            jax.ShapeDtypeStruct(values.shape, jnp.float32),
            jax.ShapeDtypeStruct((PLANE, *parts.shape[1:]), parts.dtype),
            jax.ShapeDtypeStruct((DOWN_PARTS, *down.shape[1:]), jnp.float32),
        ),
        in_specs=[VMEM] * 9,
        out_specs=(VMEM,) * 5,
        scratch_shapes=[
            pltpu.VMEM(mixed.shape, jnp.bfloat16),
            *PlaneExchange.scratch(),
            *WeightScatter.scratch(*parts.shape[1:]),
            *ChipScatter.scratch(DOWN_PARTS, *down.shape[1:]),
        ],
        compiler_params=params(3),
        name="attention_back",
    )(query, keys, values, spots, starts, key_spots, mixed, parts, down)


def closing_kernel(rows_ref, parts_ref, outs_ref, rows_out, out_ref, outs_out, *scratch):
    scatter = SequenceScatter(rows_ref, rows_out, *scratch[:3], scratch[3:7], CHUNKS)
    weights = WeightScatter(parts_ref, out_ref, scratch[7:11], scratch[11:17])
    outs_sum = scratch[17]
    chip = ChipScatter(outs_ref, *scratch[18:21], scratch[21:25], PLANE)
    outs = SequenceScatter(outs_sum, outs_out, *scratch[25:28], scratch[28:], 1)
    d, c, x, core, z, y = place()
    greet(plane_peers(d, c) + chip_peers(d, c, x, core))
    slots = [lax.rem(z + off, ZS) * YS + 1 - y for off in (2, 1, 3, 0)]
    slots += [lax.rem(z + off, ZS) * YS + y for off in (2, 1, 3, 0)]
    for j in slots:
        chip.start(j)
    weights.first()
    scatter.first()
    for j in slots:
        chip.relay(j)
    for off in range(1, PLANE + 1):
        weights.relay(off)
    for k in range(CHUNKS):
        scatter.relay(k)
    for off in range(1, PLANE + 1):
        weights.send(off)
    for i, j in enumerate(slots):
        chip.total(j, outs_sum.at[j])
        if i < ZS:
            copy = outs.across(lax.rem(z + (2, 1, 3, 0)[i], ZS), 0)
            copy.start()
            outs.sent.append(copy)
    outs.relay(0)
    for k in range(CHUNKS):
        scatter.last(k)
    weights.last()
    outs.last(0)
    scatter.finish()
    chip.finish()
    outs.finish()


def closing(rows, parts, outs):
    return pl.pallas_call(
        closing_kernel,
        out_shape=(
            jax.ShapeDtypeStruct(rows.shape[1:], jnp.float32),
            jax.ShapeDtypeStruct((PLANE, *parts.shape[1:]), parts.dtype),
            jax.ShapeDtypeStruct(outs.shape[1:], jnp.float32),
        ),
        in_specs=[VMEM] * 3,
        out_specs=(VMEM,) * 3,
        scratch_shapes=[
            *SequenceScatter.scratch(*rows.shape[1:], CHUNKS),
            *WeightScatter.scratch(*parts.shape[1:]),
            pltpu.VMEM((PLANE, *outs.shape[1:]), jnp.bfloat16),
            *ChipScatter.scratch(PLANE, *outs.shape[1:]),
            *SequenceScatter.scratch(*outs.shape[1:], 1),
        ],
        compiler_params=params(4),
        name="closing",
    )(rows, parts, outs)


def body(
    layer_in,
    positions,
    doc_starts,
    out_grad,
    norm_gains,
    norm_gains_m,
    norm_gains_v,
    w_query,
    w_query_m,
    w_query_v,
    key_value_weight,
    key_value_first_moment,
    key_value_second_moment,
    w_out,
    w_out_m,
    w_out_v,
    w_gate_up,
    w_gate_up_m,
    w_gate_up_v,
    w_down,
    w_down_m,
    w_down_v,
):
    number_of_tokens = layer_in.shape[0]
    ctx_count = lax.axis_size("ctx")
    seq_len = number_of_tokens * ctx_count
    key_value_width = KEY_VALUE_HEADS * HEAD_SIZE
    query_group_size = QUERY_HEADS // KEY_VALUE_HEADS
    score_scale = 1.0 / math.sqrt(HEAD_SIZE)
    needed = -(-512 // number_of_tokens)
    shard_span = min(ctx_count, 1 << max(0, (needed - 1).bit_length()))
    width_of_block = shard_span * number_of_tokens
    count_of_blocks = ctx_count // shard_span
    key_places = lax.all_gather(positions, "ctx", axis=0, tiled=True)
    starts = doc_starts[0]
    own_docs = doc_lookup(positions, starts)
    key_docs = doc_lookup(key_places, starts)
    query_full, keyval_full, out_full, gains_full = (
        lax.all_gather(w_query.astype(jnp.bfloat16), ("dp", "ctx"), axis=0, tiled=True),
        lax.all_gather(key_value_weight.astype(jnp.bfloat16), ("dp", "ctx"), axis=0, tiled=True),
        lax.all_gather(w_out.astype(jnp.bfloat16), ("dp", "ctx"), axis=0, tiled=True),
        lax.all_gather(norm_gains.astype(jnp.bfloat16), ("dp", "ctx"), axis=1, tiled=True),
    )
    gain_one = gains_full[0].astype(jnp.float32)
    gain_two = gains_full[1].astype(jnp.float32)
    layer_rows = layer_in.astype(jnp.float32)
    normed_one, inverse_one = norm_forward(layer_rows)
    input_one = (normed_one * gain_one).astype(jnp.bfloat16)
    query_pre = jnp.dot(input_one, query_full, preferred_element_type=jnp.float32)
    key_value_projected = jnp.dot(input_one, keyval_full, preferred_element_type=jnp.float32)
    cosine_table, sine_table = rope_tables(positions, HEAD_SIZE)
    query_rows = (
        apply_rotation(
            query_pre.reshape(number_of_tokens, QUERY_HEADS, HEAD_SIZE), cosine_table, sine_table
        )
        .astype(jnp.bfloat16)
        .reshape(number_of_tokens, KEY_VALUE_HEADS, query_group_size, HEAD_SIZE)
    )
    keys_own = (
        apply_rotation(
            key_value_projected[:, :key_value_width].reshape(
                number_of_tokens, KEY_VALUE_HEADS, HEAD_SIZE
            ),
            cosine_table,
            sine_table,
        )
        .astype(jnp.bfloat16)
        .reshape(number_of_tokens, key_value_width)
    )
    values_own = key_value_projected[:, key_value_width:].astype(jnp.bfloat16)
    every_key, every_value = (
        lax.all_gather(keys_own, "ctx", axis=0, tiled=True),
        lax.all_gather(values_own, "ctx", axis=0, tiled=True),
    )
    blocked_keys = every_key.reshape(count_of_blocks, width_of_block, KEY_VALUE_HEADS, HEAD_SIZE)
    blocked_values = every_value.reshape(
        count_of_blocks, width_of_block, KEY_VALUE_HEADS, HEAD_SIZE
    )
    place_blocks = key_places.reshape(count_of_blocks, width_of_block)
    doc_blocks = key_docs.reshape(count_of_blocks, width_of_block)

    def visible(place_blk, doc_blk):
        allowed = (place_blk[None, :] <= positions[:, None]) & (
            doc_blk[None, :] == own_docs[:, None]
        )
        return allowed[:, None, None, :]

    def scores_of(key_blk):
        return (
            jnp.einsum("tkgd,nkd->tkgn", query_rows, key_blk, preferred_element_type=jnp.float32)
            * score_scale
        )

    def stats_step(carry, block):
        row_top, row_total = carry
        key_blk, place_blk, doc_blk = block
        allowed = visible(place_blk, doc_blk)
        masked = jnp.where(allowed, scores_of(key_blk), masked_score)
        new_top = jnp.maximum(row_top, jnp.max(masked, axis=-1, keepdims=True))
        row_total = row_total * jnp.exp(row_top - new_top) + jnp.sum(
            jnp.where(allowed, jnp.exp(masked - new_top), 0.0), axis=-1, keepdims=True
        )
        return ((new_top, row_total), None)

    statistic_shape = (number_of_tokens, KEY_VALUE_HEADS, query_group_size, 1)
    (row_top, row_total), unused = lax.scan(
        stats_step,
        (
            jnp.full(statistic_shape, masked_score, jnp.float32),
            jnp.zeros(statistic_shape, jnp.float32),
        ),
        (blocked_keys, place_blocks, doc_blocks),
    )
    log_total = row_top + jnp.log(row_total)

    def probs_of(key_blk, place_blk, doc_blk):
        allowed = visible(place_blk, doc_blk)
        masked = jnp.where(allowed, scores_of(key_blk), masked_score)
        return jnp.where(allowed, jnp.exp(masked - log_total), 0.0)

    def output_step(carry, block):
        key_blk, value_blk, place_blk, doc_blk = block
        probs_low = probs_of(key_blk, place_blk, doc_blk).astype(jnp.bfloat16)
        added = jnp.einsum(
            "tkgn,nkd->tkgd", probs_low, value_blk, preferred_element_type=jnp.float32
        )
        return (carry + added, None)

    attention_output, unused = lax.scan(
        output_step,
        jnp.zeros((number_of_tokens, KEY_VALUE_HEADS, query_group_size, HEAD_SIZE), jnp.float32),
        (blocked_keys, blocked_values, place_blocks, doc_blocks),
    )
    mixed = attention_output.reshape(number_of_tokens, QUERY_HEADS * HEAD_SIZE).astype(jnp.bfloat16)
    middle = layer_rows + jnp.dot(mixed, out_full, preferred_element_type=jnp.float32)
    normed_two, inverse_two = norm_forward(middle)
    input_two = (normed_two * gain_two).astype(jnp.bfloat16)
    gate_up_low = w_gate_up.astype(jnp.bfloat16)
    down_low = w_down.astype(jnp.bfloat16)
    columns = input_two
    gate_up = jnp.dot(
        columns,
        lax.all_gather(gate_up_low, ("dp", "ctx"), axis=0, tiled=True),
        preferred_element_type=jnp.float32,
    )
    gate_part = gate_up[:, :FF]
    up_part = gate_up[:, FF:]
    sigmoid_gate = jax.nn.sigmoid(gate_part)
    silu_gate = gate_part * sigmoid_gate
    hidden = (silu_gate * up_part).astype(jnp.bfloat16)
    columns = hidden
    down_sum = jnp.dot(
        columns,
        lax.all_gather(down_low, ("dp", "ctx"), axis=0, tiled=True),
        preferred_element_type=jnp.float32,
    )
    layer_out = (middle + down_sum).astype(jnp.bfloat16)
    grad_rows = out_grad.astype(jnp.float32)
    grad_hidden = times_transposed(
        out_grad, lax.all_gather(down_low, ("dp", "ctx"), axis=0, tiled=True)
    )
    grad_gate = grad_hidden * up_part * sigmoid_gate * (1.0 + gate_part * (1.0 - sigmoid_gate))
    grad_up = grad_hidden * silu_gate
    grad_gate_up = jnp.concatenate([grad_gate, grad_up], axis=1).astype(jnp.bfloat16)
    down_grad = lax.psum_scatter(
        transposed_times(hidden, out_grad), ("dp", "ctx"), scatter_dimension=0, tiled=True
    )
    grad_normed_two = times_transposed(
        grad_gate_up, lax.all_gather(gate_up_low, ("dp", "ctx"), axis=0, tiled=True)
    )
    gate_up_grad = lax.psum_scatter(
        transposed_times(input_two, grad_gate_up), ("dp", "ctx"), scatter_dimension=0, tiled=True
    )
    grad_norm_two, gain_two_grad = norm_backward(grad_normed_two, normed_two, inverse_two, gain_two)
    grad_middle = grad_rows + grad_norm_two
    grad_middle_low = grad_middle.astype(jnp.bfloat16)
    out_term = transposed_times(mixed, grad_middle_low)
    grad_mixed = (
        times_transposed(grad_middle_low, out_full)
        .astype(jnp.bfloat16)
        .reshape(number_of_tokens, KEY_VALUE_HEADS, query_group_size, HEAD_SIZE)
    )
    delta = jnp.sum(grad_mixed.astype(jnp.float32) * attention_output, axis=-1, keepdims=True)

    def back_step(grad_query, block):
        key_blk, value_blk, place_blk, doc_blk = block
        probs = probs_of(key_blk, place_blk, doc_blk)
        probs_low = probs.astype(jnp.bfloat16)
        grad_probs = jnp.einsum(
            "tkgd,nkd->tkgn", grad_mixed, value_blk, preferred_element_type=jnp.float32
        )
        grad_scores = (probs * (grad_probs - delta) * score_scale).astype(jnp.bfloat16)
        grad_query = grad_query + jnp.einsum(
            "tkgn,nkd->tkgd", grad_scores, key_blk, preferred_element_type=jnp.float32
        )
        key_grad = jnp.einsum(
            "tkgn,tkgd->nkd", grad_scores, query_rows, preferred_element_type=jnp.float32
        )
        value_grad = jnp.einsum(
            "tkgn,tkgd->nkd", probs_low, grad_mixed, preferred_element_type=jnp.float32
        )
        return (grad_query, (key_grad, value_grad))

    grad_query, (key_grads, value_grads) = lax.scan(
        back_step,
        jnp.zeros((number_of_tokens, KEY_VALUE_HEADS, query_group_size, HEAD_SIZE), jnp.float32),
        (blocked_keys, blocked_values, place_blocks, doc_blocks),
    )
    summed_key_gradient, value_sum = (
        lax.psum_scatter(
            key_grads.reshape(seq_len, key_value_width).astype(jnp.bfloat16),
            "ctx",
            scatter_dimension=0,
            tiled=True,
        ).astype(jnp.float32),
        lax.psum_scatter(
            value_grads.reshape(seq_len, key_value_width).astype(jnp.bfloat16),
            "ctx",
            scatter_dimension=0,
            tiled=True,
        ).astype(jnp.float32),
    )
    key_gradient_unrotated = reverse_rotation(
        summed_key_gradient.reshape(number_of_tokens, KEY_VALUE_HEADS, HEAD_SIZE),
        cosine_table,
        sine_table,
    ).reshape(number_of_tokens, key_value_width)
    grad_keyval = jnp.concatenate([key_gradient_unrotated, value_sum], axis=1).astype(jnp.bfloat16)
    grad_query_low = (
        reverse_rotation(
            grad_query.reshape(number_of_tokens, QUERY_HEADS, HEAD_SIZE), cosine_table, sine_table
        )
        .reshape(number_of_tokens, QUERY_HEADS * HEAD_SIZE)
        .astype(jnp.bfloat16)
    )
    grad_normed_one = times_transposed(grad_query_low, query_full) + times_transposed(
        grad_keyval, keyval_full
    )
    query_term = transposed_times(input_one, grad_query_low)
    keyval_term = transposed_times(input_one, grad_keyval)
    grad_norm_one, gain_one_grad = norm_backward(grad_normed_one, normed_one, inverse_one, gain_one)
    in_grad = grad_middle + grad_norm_one
    gain_term = jnp.stack([gain_one_grad, gain_two_grad])
    query_grad, keyval_grad, out_weight_grad, gains_grad = (
        lax.psum_scatter(query_term, ("dp", "ctx"), scatter_dimension=0, tiled=True),
        lax.psum_scatter(keyval_term, ("dp", "ctx"), scatter_dimension=0, tiled=True),
        lax.psum_scatter(out_term, ("dp", "ctx"), scatter_dimension=0, tiled=True),
        lax.psum_scatter(gain_term, ("dp", "ctx"), scatter_dimension=1, tiled=True),
    )
    rates = rates_for(seq_len)
    gains_m_new, gains_v_new, gains_new = adamw(
        norm_gains, gains_grad, norm_gains_m, norm_gains_v, rates[0], 0.0
    )
    query_m_new, query_v_new, query_new = adamw(
        w_query, query_grad, w_query_m, w_query_v, rates[1], weight_decay
    )
    keyval_m_new, keyval_v_new, keyval_new = adamw(
        key_value_weight,
        keyval_grad,
        key_value_first_moment,
        key_value_second_moment,
        rates[2],
        weight_decay,
    )
    out_m_new, out_v_new, out_new = adamw(
        w_out, out_weight_grad, w_out_m, w_out_v, rates[3], weight_decay
    )
    gate_up_m_new, gate_up_v_new, gate_up_new = adamw(
        w_gate_up, gate_up_grad, w_gate_up_m, w_gate_up_v, rates[4], weight_decay
    )
    down_m_new, down_v_new, down_new = adamw(
        w_down, down_grad, w_down_m, w_down_v, rates[5], weight_decay
    )
    return (
        layer_out,
        in_grad,
        gains_grad,
        gains_m_new,
        gains_v_new,
        gains_new,
        query_grad,
        query_m_new,
        query_v_new,
        query_new,
        keyval_grad,
        keyval_m_new,
        keyval_v_new,
        keyval_new,
        out_weight_grad,
        out_m_new,
        out_v_new,
        out_new,
        gate_up_grad,
        gate_up_m_new,
        gate_up_v_new,
        gate_up_new,
        down_grad,
        down_m_new,
        down_v_new,
        down_new,
    )


def tensor_parallel(
    layer_in,
    positions,
    doc_starts,
    out_grad,
    norm_gains,
    norm_gains_m,
    norm_gains_v,
    w_query,
    w_query_m,
    w_query_v,
    key_value_weight,
    key_value_first_moment,
    key_value_second_moment,
    w_out,
    w_out_m,
    w_out_v,
    w_gate_up,
    w_gate_up_m,
    w_gate_up_v,
    w_down,
    w_down_m,
    w_down_v,
):
    low = jnp.bfloat16
    own_tokens, width = layer_in.shape
    seq_len = own_tokens * PLANE
    group = GROUP
    group_width = group * HEAD_SIZE
    ff_part = FF // PLANE
    ff_own = FF // RANKS
    rows = w_query.shape[0]

    gains_low = norm_gains.astype(low)
    small = jnp.broadcast_to(
        jnp.pad(gains_low.T, ((0, 0), (0, 126)))[None], (PLANE, rows, 128)
    )
    attention_blocks = jnp.concatenate(
        [
            w_query.astype(low).reshape(rows, PLANE, group_width).transpose(1, 0, 2),
            key_value_weight.astype(low)
            .reshape(rows, 2, PLANE, HEAD_SIZE)
            .transpose(2, 0, 1, 3)
            .reshape(PLANE, rows, 2 * HEAD_SIZE),
            small,
        ],
        axis=2,
    )
    feed_blocks = (
        w_gate_up.astype(low)
        .reshape(rows, 2, 4, PLANE, ff_own)
        .transpose(3, 0, 1, 2, 4)
        .reshape(PLANE, rows, 2 * ff_part)
    )
    spots = jnp.broadcast_to(positions[None, :], (8, own_tokens))
    rows_all, spots_all, attention_all = opening(layer_in, spots, attention_blocks)
    attention_all = attention_all.reshape(width, -1)
    qkv_width = group_width + 2 * HEAD_SIZE
    qkv_weight = attention_all[:, :qkv_width]
    gain_one = attention_all[:, qkv_width].astype(jnp.float32)
    gain_two = attention_all[:, qkv_width + 1].astype(jnp.float32)
    places = spots_all[:, 0, :].reshape(seq_len)
    starts = jnp.max(
        jnp.where(doc_starts[0][None, :] <= places[:, None], doc_starts[0][None, :], 0), axis=1
    )
    normed_all, unused = norm_forward(rows_all.reshape(seq_len, width).astype(jnp.float32))
    input_one = (normed_all * gain_one).astype(low)
    projected = jnp.dot(input_one, qkv_weight, preferred_element_type=jnp.float32)
    cosine_table, sine_table = rope_tables(places, HEAD_SIZE)
    query_rows = (
        apply_rotation(
            projected[:, :group_width].reshape(seq_len, group, HEAD_SIZE),
            cosine_table,
            sine_table,
        )
        .astype(low)
        .reshape(PLANE, own_tokens, PAIRS, 2, HEAD_SIZE)
        .transpose(0, 2, 3, 1, 4)
    )
    key_rows = apply_rotation(
        projected[:, None, group_width : group_width + HEAD_SIZE], cosine_table, sine_table
    ).astype(low)[:, 0]
    value_rows = projected[:, group_width + HEAD_SIZE :].astype(low)
    token_spots = places.reshape(PLANE, own_tokens, 1)
    token_starts = starts.reshape(PLANE, own_tokens, 1)
    mixed_parts, feed_all, out_all = attention(
        query_rows,
        key_rows,
        value_rows,
        token_spots,
        token_starts,
        places[None, :],
        feed_blocks,
        w_out.astype(low),
    )
    mixed = mixed_parts.transpose(2, 0, 1, 3).reshape(own_tokens, width)
    out_weight = out_all.reshape(width, width)
    branch = jnp.dot(mixed, out_weight, preferred_element_type=jnp.float32)

    layer_rows = layer_in.astype(jnp.float32)
    middle = layer_rows + branch
    normed_two, inverse_two = norm_forward(middle)
    input_two_all, down_all = gather_with_down(
        (normed_two * gain_two).astype(low),
        w_down.astype(low).reshape(DOWN_PARTS, -1, width),
        6,
    )
    input_two = input_two_all.reshape(seq_len, width)
    grads_all = gather_rows(out_grad, 5)
    feed_weight = feed_all.reshape(width, 2 * ff_part)
    down_weight = down_all.reshape(ff_part, width)
    gate_up = jnp.dot(input_two, feed_weight, preferred_element_type=jnp.float32)
    gate_part = gate_up[:, :ff_part]
    up_part = gate_up[:, ff_part:]
    sigmoid_gate = jax.nn.sigmoid(gate_part)
    silu_gate = gate_part * sigmoid_gate
    hidden = (silu_gate * up_part).astype(low)
    down_parts = jnp.dot(hidden, down_weight, preferred_element_type=jnp.float32).astype(low)
    down_sum = scatter_rows(down_parts.reshape(PLANE, own_tokens, width), 7)
    layer_out = (middle + down_sum).astype(low)

    out_grads = grads_all.reshape(seq_len, width)
    grad_hidden = times_transposed(out_grads, down_weight)
    grad_gate = grad_hidden * up_part * sigmoid_gate * (1.0 + gate_part * (1.0 - sigmoid_gate))
    grad_up = grad_hidden * silu_gate
    grad_gate_up = jnp.concatenate([grad_gate, grad_up], axis=1).astype(low)
    normed_parts = times_transposed(grad_gate_up, feed_weight).astype(low)
    grad_normed_two = scatter_rows(normed_parts.reshape(PLANE, own_tokens, width), 8)
    down_term = transposed_times(hidden, out_grads).astype(low)
    feed_term = transposed_times(input_two, grad_gate_up).astype(low)
    grad_norm_two, unused = norm_backward(grad_normed_two, normed_two, inverse_two, gain_two)
    grad_middle = out_grad.astype(jnp.float32) + grad_norm_two
    grad_middle_low = grad_middle.astype(low)
    out_term = transposed_times(mixed, grad_middle_low).astype(low)
    grad_mixed = (
        times_transposed(grad_middle_low, out_weight)
        .astype(low)
        .reshape(own_tokens, PLANE, PAIRS, 2 * HEAD_SIZE)
        .transpose(1, 2, 0, 3)
    )
    grad_query, grad_key, grad_value, feed_grad, down_grad = attention_back(
        query_rows,
        key_rows,
        value_rows,
        token_spots,
        token_starts,
        places[None, :],
        grad_mixed,
        feed_term.reshape(RANKS, rows, 2 * ff_part),
        down_term.reshape(4 * DOWN_PARTS, -1, width),
    )
    gate_up_grad = (
        feed_grad.reshape(PLANE, rows, 2, 4, ff_own)
        .transpose(1, 2, 3, 0, 4)
        .reshape(rows, 2 * FF)
        .astype(jnp.float32)
    )
    down_grad = down_grad.reshape(w_down.shape)
    grad_query = grad_query.transpose(0, 3, 1, 2, 4).reshape(seq_len, group, HEAD_SIZE)
    grad_qkv = jnp.concatenate(
        [
            reverse_rotation(grad_query, cosine_table, sine_table).reshape(seq_len, group_width),
            reverse_rotation(grad_key[:, None], cosine_table, sine_table)[:, 0],
            grad_value,
        ],
        axis=1,
    ).astype(low)
    one_parts = times_transposed(grad_qkv, qkv_weight).astype(low)
    qkv_term = transposed_times(input_one, grad_qkv).astype(low)
    grad_normed_one, qkv_grad, out_weight_grad = closing(
        one_parts.reshape(PLANE, own_tokens, width),
        qkv_term.reshape(RANKS, rows, qkv_width),
        out_term.reshape(RANKS, rows, width),
    )
    normed_one, inverse_one = norm_forward(layer_rows)
    grad_norm_one, unused = norm_backward(grad_normed_one, normed_one, inverse_one, gain_one)
    in_grad = grad_middle + grad_norm_one
    qkv_grad = qkv_grad.astype(jnp.float32)
    query_grad = qkv_grad[:, :, :group_width].transpose(1, 0, 2).reshape(w_query.shape)
    keyval_grad = (
        qkv_grad[:, :, group_width:]
        .reshape(PLANE, rows, 2, HEAD_SIZE)
        .transpose(1, 2, 0, 3)
        .reshape(key_value_weight.shape)
    )
    def low_times(weight, grad):
        return jnp.sum(weight.astype(low).astype(jnp.float32) * grad, axis=1)

    gains_grad = jnp.stack(
        [
            low_times(w_query, query_grad) + low_times(key_value_weight, keyval_grad),
            low_times(w_gate_up, gate_up_grad),
        ]
    ) / gains_low.astype(jnp.float32)

    rates = rates_for(seq_len)
    return (
        layer_out,
        in_grad,
        gains_grad,
        *adamw(norm_gains, gains_grad, norm_gains_m, norm_gains_v, rates[0], 0.0),
        query_grad,
        *adamw(w_query, query_grad, w_query_m, w_query_v, rates[1], weight_decay),
        keyval_grad,
        *adamw(
            key_value_weight,
            keyval_grad,
            key_value_first_moment,
            key_value_second_moment,
            rates[2],
            weight_decay,
        ),
        out_weight_grad,
        *adamw(w_out, out_weight_grad, w_out_m, w_out_v, rates[3], weight_decay),
        gate_up_grad,
        *adamw(w_gate_up, gate_up_grad, w_gate_up_m, w_gate_up_v, rates[4], weight_decay),
        down_grad,
        *adamw(w_down, down_grad, w_down_m, w_down_v, rates[5], weight_decay),
    )


def solution(mesh):
    planned = tensor_parallel if dict(mesh.shape) == {"dp": 2 * XS, "ctx": ZS * YS} else body
    return jax.shard_map(
        planned,
        mesh=mesh,
        in_specs=(
            P(("dp", "ctx"), None),
            P(("dp", "ctx")),
            P("dp", None),
            P(("dp", "ctx"), None),
            P(None, ("dp", "ctx")),
            P(None, ("dp", "ctx")),
            P(None, ("dp", "ctx")),
            P(("dp", "ctx"), None),
            P(("dp", "ctx"), None),
            P(("dp", "ctx"), None),
            P(("dp", "ctx"), None),
            P(("dp", "ctx"), None),
            P(("dp", "ctx"), None),
            P(("dp", "ctx"), None),
            P(("dp", "ctx"), None),
            P(("dp", "ctx"), None),
            P(("dp", "ctx"), None),
            P(("dp", "ctx"), None),
            P(("dp", "ctx"), None),
            P(("dp", "ctx"), None),
            P(("dp", "ctx"), None),
            P(("dp", "ctx"), None),
        ),
        out_specs=(
            P(("dp", "ctx"), None),
            P(("dp", "ctx"), None),
            P(None, ("dp", "ctx")),
            P(None, ("dp", "ctx")),
            P(None, ("dp", "ctx")),
            P(None, ("dp", "ctx")),
            P(("dp", "ctx"), None),
            P(("dp", "ctx"), None),
            P(("dp", "ctx"), None),
            P(("dp", "ctx"), None),
            P(("dp", "ctx"), None),
            P(("dp", "ctx"), None),
            P(("dp", "ctx"), None),
            P(("dp", "ctx"), None),
            P(("dp", "ctx"), None),
            P(("dp", "ctx"), None),
            P(("dp", "ctx"), None),
            P(("dp", "ctx"), None),
            P(("dp", "ctx"), None),
            P(("dp", "ctx"), None),
            P(("dp", "ctx"), None),
            P(("dp", "ctx"), None),
            P(("dp", "ctx"), None),
            P(("dp", "ctx"), None),
            P(("dp", "ctx"), None),
            P(("dp", "ctx"), None),
        ),
        check_vma=False,
    )
```

```python
import functools
import math

import jax
import jax.numpy as jnp
from jax import lax
from jax.experimental import pallas as pl
from jax.experimental.pallas import tpu as pltpu
from jax.sharding import PartitionSpec as P

MODEL_WIDTH = 2048
QUERY_HEADS = 32
KEY_VALUE_HEADS = 8
HEAD_SIZE = 64
FF = 8192
STEP = 10


eps_norm = 1e-05
rope_base = 500000.0
beta_one = 0.9
beta_two = 0.95
eps_adam = 1e-08
weight_decay = 0.1
masked_score = -1e30


def rates_for(seq_len):
    return (
        0.6,
        0.8 / math.sqrt(MODEL_WIDTH // 4),
        0.8 / math.sqrt(MODEL_WIDTH),
        0.8 / math.sqrt(max(220 * MODEL_WIDTH // seq_len, 1)),
        0.8 / math.sqrt(MODEL_WIDTH),
        0.8 / math.sqrt(FF // 2),
    )


def adamw(weight, grad_sum, first, second, rate, decay):
    first_new = beta_one * first + (1.0 - beta_one) * grad_sum
    second_new = beta_two * second + (1.0 - beta_two) * grad_sum * grad_sum
    first_hat = first_new / (1.0 - beta_one**STEP)
    second_hat = second_new / (1.0 - beta_two**STEP)
    weight_new = weight - rate * (first_hat / (jnp.sqrt(second_hat) + eps_adam) + decay * weight)
    return (first_new, second_new, weight_new)


def norm_forward(layer_rows):
    inverse = lax.rsqrt(jnp.mean(layer_rows * layer_rows, axis=-1, keepdims=True) + eps_norm)
    return (layer_rows * inverse, inverse)


def norm_backward(grad_out, normed, inverse, gain_row):
    scaled = grad_out * gain_row
    grad_in = inverse * (scaled - normed * jnp.mean(scaled * normed, axis=-1, keepdims=True))
    return (grad_in, jnp.sum(grad_out * normed, axis=0))


def rope_tables(token_placement, head_dim):
    half_dim = head_dim // 2
    frequencies = jnp.exp(
        jnp.arange(half_dim, dtype=jnp.float32) * (-2.0 * math.log(rope_base) / head_dim)
    )
    angles = token_placement.astype(jnp.float32)[:, None] * frequencies[None, :]
    return (jnp.cos(angles)[:, None, :], jnp.sin(angles)[:, None, :])


def apply_rotation(value_rows, cosine_table, sine_table):
    half_dim = value_rows.shape[-1] // 2
    first_half = value_rows[..., :half_dim]
    second_half = value_rows[..., half_dim:]
    return jnp.concatenate(
        [
            first_half * cosine_table - second_half * sine_table,
            second_half * cosine_table + first_half * sine_table,
        ],
        axis=-1,
    )


def reverse_rotation(grad_rows, cosine_table, sine_table):
    half_dim = grad_rows.shape[-1] // 2
    first_half = grad_rows[..., :half_dim]
    second_half = grad_rows[..., half_dim:]
    return jnp.concatenate(
        [
            first_half * cosine_table + second_half * sine_table,
            second_half * cosine_table - first_half * sine_table,
        ],
        axis=-1,
    )


def doc_lookup(token_placement, starts):
    return jnp.sum((token_placement[:, None] >= starts[None, :]).astype(jnp.int32), axis=1) - 1


def times_transposed(left, right):
    return lax.dot_general(
        left, right, (((1,), (1,)), ((), ())), preferred_element_type=jnp.float32
    )


def transposed_times(left, right):
    return lax.dot_general(
        left, right, (((0,), (0,)), ((), ())), preferred_element_type=jnp.float32
    )


XS = 2
YS = 2
ZS = 4
PLANE = ZS * YS
RANKS = 2 * XS * PLANE
MESH = pl.DeviceIdType.MESH


def place():
    d = lax.axis_index("dp")
    c = lax.axis_index("ctx")
    return d, c, lax.div(d, 2), lax.rem(d, 2), lax.div(c, YS), lax.rem(c, YS)


def remote(src, dst, send_sem, recv_sem, d, c):
    return pltpu.make_async_remote_copy(
        src_ref=src,
        dst_ref=dst,
        send_sem=send_sem,
        recv_sem=recv_sem,
        device_id=(d, c),
        device_id_type=MESH,
    )


def greet(peers):
    barrier = pltpu.get_barrier_semaphore()
    for d, c in peers:
        pl.semaphore_signal(barrier, inc=1, device_id=(d, c), device_id_type=MESH)
    pl.semaphore_wait(barrier, len(peers))


def plane_peers(d, c):
    return [(d, lax.rem(c + k, PLANE)) for k in range(1, PLANE)]


def chip_peers(d, c, x, core):
    return [(x * 2 + 1 - core, c), ((1 - x) * 2 + core, c)]


def add_into(target, sources, rows, step=16):
    @pl.loop(0, rows, step=step)
    def _(r):
        at = pl.ds(pl.multiple_of(r, step), step)
        total = sources[0][at].astype(jnp.float32)
        for source in sources[1:]:
            total = total + source[at].astype(jnp.float32)
        target[at] = total.astype(target.dtype)


class SequenceGather:
    def __init__(self, own, out, sems, chunks):
        self.own, self.out, self.chunks = own, out, chunks
        self.zs, self.zr, self.ys, self.yr, self.local_sem = sems
        self.d, self.c, _, _, self.z, self.y = place()
        self.rows = own.shape[0] // chunks
        self.sent = []

    @staticmethod
    def scratch(chunks):
        return [
            pltpu.SemaphoreType.DMA((ZS, chunks)),
            pltpu.SemaphoreType.DMA((ZS, chunks)),
            pltpu.SemaphoreType.DMA((ZS, chunks)),
            pltpu.SemaphoreType.DMA((ZS, chunks)),
            pltpu.SemaphoreType.DMA(()),
        ]

    def part(self, ref, k):
        return ref.at[pl.ds(k * self.rows, self.rows)]

    def across(self, z, k, src):
        slot = z * YS + self.y
        return remote(
            src,
            self.part(self.out.at[slot], k),
            self.ys.at[z, k],
            self.yr.at[z, k],
            self.d,
            self.z * YS + 1 - self.y,
        )

    def along(self, off, k):
        to = lax.rem(self.z + off, ZS)
        return remote(
            self.part(self.own, k),
            self.part(self.out.at[self.c], k),
            self.zs.at[off, k],
            self.zr.at[self.z, k],
            self.d,
            to * YS + self.y,
        )

    def start(self, copy):
        copy.start()
        self.sent.append(copy)

    def first(self, by_block=False):
        self.local = pltpu.make_async_copy(self.own, self.out.at[self.c], self.local_sem)
        self.local.start()
        if by_block:
            for k in range(self.chunks):
                self.start(self.across(self.z, k, self.part(self.own, k)))
            for off in (1, 3, 2):
                for k in range(self.chunks):
                    self.start(self.along(off, k))
            return
        for k in range(self.chunks):
            for off in (2, 1, 3):
                self.start(self.along(off, k))
            self.start(self.across(self.z, k, self.part(self.own, k)))

    def relay_one(self, off, k):
        source = lax.rem(self.z + off, ZS)
        slot = source * YS + self.y
        block = self.part(self.out.at[slot], k)
        remote(
            block, block, self.zs.at[off, k], self.zr.at[source, k], self.d, slot
        ).wait_recv()
        self.start(self.across(source, k, block))

    def relay(self, k):
        for off in (1, 3, 2):
            self.relay_one(off, k)

    def arrive_across(self, z):
        for k in range(self.chunks):
            block = self.part(self.out.at[z * YS + 1 - self.y], k)
            remote(
                block,
                block,
                self.ys.at[z, k],
                self.yr.at[z, k],
                self.d,
                self.z * YS + 1 - self.y,
            ).wait_recv()

    def finish(self):
        for copy in self.sent:
            copy.wait_send()

    def last(self):
        for z in range(ZS):
            self.arrive_across(z)
        self.finish()
        self.local.wait()


class SequenceScatter:
    def __init__(self, parts, out, ybuf, stage, zbuf, sems, chunks):
        self.parts, self.out, self.chunks = parts, out, chunks
        self.ybuf, self.stage, self.zbuf = ybuf, stage, zbuf
        self.ys, self.yr, self.zs, self.zr = sems
        self.d, self.c, _, _, self.z, self.y = place()
        self.rows = parts.shape[1] // chunks
        self.sent = []

    @staticmethod
    def scratch(rows, width, chunks):
        return [
            pltpu.VMEM((ZS, rows, width), jnp.bfloat16),
            pltpu.VMEM((ZS, rows, width), jnp.bfloat16),
            pltpu.VMEM((ZS, rows, width), jnp.bfloat16),
            pltpu.SemaphoreType.DMA((ZS, chunks)),
            pltpu.SemaphoreType.DMA((ZS, chunks)),
            pltpu.SemaphoreType.DMA((ZS, chunks)),
            pltpu.SemaphoreType.DMA((ZS, chunks)),
        ]

    def span(self, k):
        return pl.ds(k * self.rows, self.rows)

    def across(self, z, k):
        return remote(
            self.parts.at[z * YS + 1 - self.y, self.span(k)],
            self.ybuf.at[z, self.span(k)],
            self.ys.at[z, k],
            self.yr.at[z, k],
            self.d,
            self.z * YS + 1 - self.y,
        )

    def along(self, off, k):
        to = lax.rem(self.z + off, ZS)
        return remote(
            self.stage.at[off, self.span(k)],
            self.zbuf.at[self.z, self.span(k)],
            self.zs.at[off, k],
            self.zr.at[self.z, k],
            self.d,
            to * YS + self.y,
        )

    def start(self, z, k):
        copy = self.across(z, k)
        copy.start()
        self.sent.append(copy)

    def first(self):
        for k in range(self.chunks):
            for off in (2, 1, 3, 0):
                self.start(lax.rem(self.z + off, ZS), k)

    def relay_one(self, off, k):
        z = lax.rem(self.z + off, ZS)
        self.across(z, k).wait_recv()
        add_into(
            self.stage.at[off, self.span(k)],
            [self.parts.at[z * YS + self.y, self.span(k)], self.ybuf.at[z, self.span(k)]],
            self.rows,
        )
        copy = self.along(off, k)
        copy.start()
        self.sent.append(copy)

    def relay(self, k):
        for off in (2, 1, 3):
            self.relay_one(off, k)

    def last(self, k):
        self.across(self.z, k).wait_recv()
        blocks = [self.parts.at[self.c, self.span(k)], self.ybuf.at[self.z, self.span(k)]]
        for off in (1, 3, 2):
            source = lax.rem(self.z + off, ZS)
            block = self.zbuf.at[source, self.span(k)]
            remote(
                block,
                block,
                self.zs.at[off, k],
                self.zr.at[source, k],
                self.d,
                source * YS + self.y,
            ).wait_recv()
            blocks.append(block)
        add_into(self.out.at[self.span(k)], blocks, self.rows)

    def finish(self):
        for copy in self.sent:
            copy.wait_send()


class ChipGather:
    def __init__(self, out, sems, count):
        self.out, self.count = out, count
        self.cs, self.cr, self.xs, self.xr = sems
        self.d, self.c, self.x, self.core, _, _ = place()
        self.sent = []

    @staticmethod
    def scratch(count):
        return [
            pltpu.SemaphoreType.DMA((2, count)),
            pltpu.SemaphoreType.DMA((2, count)),
            pltpu.SemaphoreType.DMA((count,)),
            pltpu.SemaphoreType.DMA((count,)),
        ]

    def to_core(self, far, j, src=None):
        x = 1 - self.x if far else self.x
        block = self.out.at[(x * 2 + self.core) * self.count + j]
        return remote(
            block if src is None else src,
            block,
            self.cs.at[far, j],
            self.cr.at[far, j],
            self.x * 2 + 1 - self.core,
            self.c,
        )

    def to_x(self, j, src=None):
        block = self.out.at[self.d * self.count + j]
        return remote(
            block if src is None else src,
            block,
            self.xs.at[j],
            self.xr.at[j],
            (1 - self.x) * 2 + self.core,
            self.c,
        )

    def start(self, j, src=None):
        for copy in (self.to_x(j, src), self.to_core(0, j, src)):
            copy.start()
            self.sent.append(copy)

    def relay(self, j):
        self.to_x(j).wait_recv()
        copy = self.to_core(1, j)
        copy.start()
        self.sent.append(copy)

    def last(self):
        for far in (0, 1):
            for j in range(self.count):
                self.to_core(far, j).wait_recv()
        for copy in self.sent:
            copy.wait_send()


class WeightGather:
    def __init__(self, blocks, out, sems):
        self.blocks, self.out = blocks, out
        self.ps, self.pr, self.local_sem = sems[:3]
        self.chip = ChipGather(out, sems[3:], PLANE)
        self.d, self.c = self.chip.d, self.chip.c
        self.sent = []

    @staticmethod
    def scratch():
        return [
            pltpu.SemaphoreType.DMA((PLANE,)),
            pltpu.SemaphoreType.DMA((PLANE,)),
            pltpu.SemaphoreType.DMA(()),
        ] + ChipGather.scratch(PLANE)

    def first(self):
        self.local = pltpu.make_async_copy(
            self.blocks.at[self.c], self.out.at[self.d * PLANE + self.c], self.local_sem
        )
        self.local.start()
        for off in range(1, PLANE):
            to = lax.rem(self.c + off, PLANE)
            copy = remote(
                self.blocks.at[to],
                self.out.at[self.d * PLANE + self.c],
                self.ps.at[off],
                self.pr.at[self.c],
                self.d,
                to,
            )
            copy.start()
            self.sent.append(copy)
        self.chip.start(self.c, self.blocks.at[self.c])

    def relay(self, off):
        source = lax.rem(self.c + PLANE - off, PLANE)
        block = self.out.at[self.d * PLANE + source]
        remote(
            block, block, self.ps.at[off], self.pr.at[source], self.d, source
        ).wait_recv()
        self.chip.start(source)

    def relay_chip(self):
        for off in range(PLANE):
            self.chip.relay(lax.rem(self.c + off, PLANE))

    def last(self):
        self.chip.last()
        for copy in self.sent:
            copy.wait_send()
        self.local.wait()


class ChipScatter:
    def __init__(self, parts, cbuf, stage, xbuf, sems, count):
        self.parts, self.count = parts, count
        self.cbuf, self.stage, self.xbuf = cbuf, stage, xbuf
        self.cs, self.cr, self.xs, self.xr = sems
        self.d, self.c, self.x, self.core, _, _ = place()
        self.sent = []

    @staticmethod
    def scratch(count, rows, width):
        return [
            pltpu.VMEM((2, count, rows, width), jnp.bfloat16),
            pltpu.VMEM((count, rows, width), jnp.bfloat16),
            pltpu.VMEM((count, rows, width), jnp.bfloat16),
            pltpu.SemaphoreType.DMA((2, count)),
            pltpu.SemaphoreType.DMA((2, count)),
            pltpu.SemaphoreType.DMA((count,)),
            pltpu.SemaphoreType.DMA((count,)),
        ]

    def to_core(self, far, j):
        x = 1 - self.x if far else self.x
        return remote(
            self.parts.at[(x * 2 + 1 - self.core) * self.count + j],
            self.cbuf.at[far, j],
            self.cs.at[far, j],
            self.cr.at[far, j],
            self.x * 2 + 1 - self.core,
            self.c,
        )

    def to_x(self, j):
        return remote(
            self.stage.at[j],
            self.xbuf.at[j],
            self.xs.at[j],
            self.xr.at[j],
            (1 - self.x) * 2 + self.core,
            self.c,
        )

    def start(self, j):
        for far in (1, 0):
            copy = self.to_core(far, j)
            copy.start()
            self.sent.append(copy)

    def relay(self, j):
        self.to_core(1, j).wait_recv()
        own = self.parts.at[((1 - self.x) * 2 + self.core) * self.count + j]
        add_into(self.stage.at[j], [own, self.cbuf.at[1, j]], own.shape[0])
        copy = self.to_x(j)
        copy.start()
        self.sent.append(copy)

    def total(self, j, target):
        self.to_core(0, j).wait_recv()
        self.to_x(j).wait_recv()
        own = self.parts.at[self.d * self.count + j]
        add_into(target, [own, self.cbuf.at[0, j], self.xbuf.at[j]], own.shape[0])

    def finish(self):
        for copy in self.sent:
            copy.wait_send()


class WeightScatter:
    def __init__(self, parts, out, bufs, sems):
        self.stage = bufs[0]
        self.ps, self.pr = sems[:2]
        self.chip = ChipScatter(parts, *bufs[1:], sems[2:], PLANE)
        self.out = out
        self.d, self.c = self.chip.d, self.chip.c
        self.sent = []

    @staticmethod
    def scratch(rows, width):
        chip = ChipScatter.scratch(PLANE, rows, width)
        return [
            pltpu.VMEM((PLANE, rows, width), jnp.bfloat16),
            *chip[:3],
            pltpu.SemaphoreType.DMA((PLANE,)),
            pltpu.SemaphoreType.DMA((PLANE,)),
            *chip[3:],
        ]

    def first(self):
        for off in range(1, PLANE + 1):
            self.chip.start(lax.rem(self.c + off, PLANE))

    def relay(self, off):
        self.chip.relay(lax.rem(self.c + off, PLANE))

    def send(self, off):
        to = lax.rem(self.c + off, PLANE)
        if off == PLANE:
            self.chip.total(to, self.out.at[self.c])
            return
        self.chip.total(to, self.stage.at[to])
        copy = remote(
            self.stage.at[to],
            self.out.at[self.c],
            self.ps.at[off],
            self.pr.at[self.c],
            self.d,
            to,
        )
        copy.start()
        self.sent.append(copy)

    def last(self):
        for off in range(1, PLANE):
            source = lax.rem(self.c + off, PLANE)
            block = self.out.at[source]
            remote(
                block, block, self.ps.at[off], self.pr.at[source], self.d, source
            ).wait_recv()
        for copy in self.sent:
            copy.wait_send()
        self.chip.finish()


def params(collective_id):
    return pltpu.CompilerParams(
        collective_id=collective_id, has_side_effects=True, vmem_limit_bytes=56 * 2**20
    )


ANY = pl.BlockSpec(memory_space=pl.ANY)
VMEM = pl.BlockSpec(memory_space=pltpu.VMEM)
CHUNKS = 4


def opening_kernel(rows_ref, spots_ref, blocks_ref, rows_out, spots_out, blocks_out, *scratch):
    spot_send, spot_recv, spot_local = scratch[:3]
    gather = SequenceGather(rows_ref, rows_out, scratch[3:8], CHUNKS)
    weights = WeightGather(blocks_ref, blocks_out, scratch[8:])
    d, c, x, core, z, y = place()
    greet(plane_peers(d, c) + chip_peers(d, c, x, core))
    weights.first()
    sent = []
    local = pltpu.make_async_copy(spots_ref, spots_out.at[c], spot_local)
    local.start()
    for off in range(1, PLANE):
        to = lax.rem(c + off, PLANE)
        copy = remote(
            spots_ref, spots_out.at[c], spot_send.at[off], spot_recv.at[c], d, to
        )
        copy.start()
        sent.append(copy)
    gather.first()
    for off in range(1, PLANE):
        weights.relay(off)
    for k in range(CHUNKS):
        gather.relay(k)
    weights.relay_chip()
    gather.last()
    weights.last()
    for off in range(1, PLANE):
        source = lax.rem(c + off, PLANE)
        block = spots_out.at[source]
        remote(block, block, spot_send.at[off], spot_recv.at[source], d, source).wait_recv()
    for copy in sent:
        copy.wait_send()
    local.wait()


def opening(rows, spots, blocks):
    return pl.pallas_call(
        opening_kernel,
        out_shape=(
            jax.ShapeDtypeStruct((PLANE, *rows.shape), rows.dtype),
            jax.ShapeDtypeStruct((PLANE, *spots.shape), spots.dtype),
            jax.ShapeDtypeStruct((RANKS, *blocks.shape[1:]), blocks.dtype),
        ),
        in_specs=[ANY] * 3,
        out_specs=(ANY,) * 3,
        scratch_shapes=[
            pltpu.SemaphoreType.DMA((PLANE,)),
            pltpu.SemaphoreType.DMA((PLANE,)),
            pltpu.SemaphoreType.DMA(()),
            *SequenceGather.scratch(CHUNKS),
            *WeightGather.scratch(),
        ],
        compiler_params=params(1),
        name="opening",
    )(rows, spots, blocks)


DOWN_PARTS = 4
SCORE_SCALE = 1.0 / math.sqrt(HEAD_SIZE)
GROUP = QUERY_HEADS // KEY_VALUE_HEADS
PAIRS = GROUP // 2


def times_rows(left, right):
    return lax.dot_general(
        left, right, (((1,), (1,)), ((), ())), preferred_element_type=jnp.float32
    )


class PlaneExchange:
    def __init__(self, blocks, out, sems):
        self.blocks, self.out = blocks, out
        self.ps, self.pr, self.local_sem = sems
        self.d, self.c = lax.axis_index("dp"), lax.axis_index("ctx")
        self.sent = []

    @staticmethod
    def scratch():
        return [
            pltpu.SemaphoreType.DMA((PLANE,)),
            pltpu.SemaphoreType.DMA((PLANE,)),
            pltpu.SemaphoreType.DMA(()),
        ]

    def send(self, off):
        to = lax.rem(self.c + off, PLANE)
        if off % PLANE == 0:
            self.local = pltpu.make_async_copy(
                self.blocks.at[to], self.out.at[self.c], self.local_sem
            )
            self.local.start()
            return
        copy = remote(
            self.blocks.at[to],
            self.out.at[self.c],
            self.ps.at[off],
            self.pr.at[self.c],
            self.d,
            to,
        )
        copy.start()
        self.sent.append(copy)

    def arrive(self, off):
        if off % PLANE == 0:
            self.local.wait()
            return
        source = lax.rem(self.c + PLANE - off, PLANE)
        block = self.out.at[source]
        remote(
            block, block, self.ps.at[off], self.pr.at[source], self.d, source
        ).wait_recv()

    def finish(self):
        for copy in self.sent:
            copy.wait_send()


def probabilities(query, keys, spot, start, key_spots):
    scores = times_rows(query, keys) * SCORE_SCALE
    masked = jnp.where((key_spots <= spot) & (key_spots >= start), scores, masked_score)
    exponent = jnp.exp(masked - jnp.max(masked, axis=-1, keepdims=True))
    return exponent * (1.0 / jnp.sum(exponent, axis=-1, keepdims=True))


def attention_kernel(
    query_ref,
    key_ref,
    value_ref,
    spot_ref,
    start_ref,
    key_spot_ref,
    blocks_ref,
    out_rows_ref,
    down_ref,
    rows_ref,
    mixed_out,
    blocks_out,
    out_rows_out,
    down_out,
    rows_out,
    *scratch,
):
    mixed_stage = scratch[0]
    exchange = PlaneExchange(mixed_stage, mixed_out, scratch[1:4])
    weights = WeightGather(blocks_ref, blocks_out, scratch[4:11])
    d, c, x, core, z, y = place()
    gather = SequenceGather(
        out_rows_ref, out_rows_out.at[pl.ds(d * PLANE, PLANE)], scratch[11:16], 1
    )
    chip = ChipGather(out_rows_out, scratch[16:20], PLANE)
    rows = SequenceGather(rows_ref, rows_out, scratch[20:25], CHUNKS)
    down = ChipGather(down_out, scratch[25:29], DOWN_PARTS)
    greet(plane_peers(d, c) + chip_peers(d, c, x, core))
    gather.first()
    chip.start(c, out_rows_ref)
    weights.first()
    local = pltpu.make_async_copy(
        down_ref, down_out.at[pl.ds(d * DOWN_PARTS, DOWN_PARTS)], scratch[29]
    )
    local.start()
    for j in range(DOWN_PARTS):
        down.start(j, down_ref.at[j])
    rows.first()
    for step in range(1, PLANE + 1):
        block = lax.rem(c + step, PLANE)

        @pl.loop(0, PAIRS)
        def _(pair):
            halves = []
            for half in range(2):
                probs = probabilities(
                    query_ref[block, pair, half],
                    key_ref[...],
                    spot_ref[block],
                    start_ref[block],
                    key_spot_ref[...],
                )
                halves.append(
                    jnp.dot(
                        probs.astype(jnp.bfloat16),
                        value_ref[...],
                        preferred_element_type=jnp.float32,
                    ).astype(jnp.bfloat16)
                )
            mixed_stage[block, pair] = jnp.concatenate(halves, axis=1)

        exchange.send(step)
        if step == 1:
            gather.relay(0)
            for off in range(1, ZS):
                chip.start(lax.rem(z + off, ZS) * YS + y)
        if step < PLANE:
            weights.relay(step)
    gather.last()
    for other in range(ZS):
        chip.start(other * YS + 1 - y)
    for k in range(CHUNKS):
        rows.relay(k)
    for j in range(DOWN_PARTS):
        down.relay(j)
    for off in range(PLANE):
        chip.relay(lax.rem(c + off, PLANE))
    weights.relay_chip()
    for off in range(1, PLANE + 1):
        exchange.arrive(off)
    rows.last()
    down.last()
    chip.last()
    weights.last()
    exchange.finish()
    local.wait()


def attention(query, keys, values, spots, starts, key_spots, blocks, out_rows, down, rows):
    exchanged = jax.ShapeDtypeStruct(
        (PLANE, PAIRS, query.shape[3], 2 * HEAD_SIZE), jnp.bfloat16
    )
    return pl.pallas_call(
        attention_kernel,
        out_shape=(
            exchanged,
            jax.ShapeDtypeStruct((RANKS, *blocks.shape[1:]), blocks.dtype),
            jax.ShapeDtypeStruct((RANKS, *out_rows.shape), out_rows.dtype),
            jax.ShapeDtypeStruct((4 * DOWN_PARTS, *down.shape[1:]), down.dtype),
            jax.ShapeDtypeStruct((PLANE, *rows.shape), rows.dtype),
        ),
        in_specs=[VMEM] * 6 + [ANY] * 4,
        out_specs=(VMEM, ANY, ANY, ANY, ANY),
        scratch_shapes=[
            pltpu.VMEM(exchanged.shape, jnp.bfloat16),
            *PlaneExchange.scratch(),
            *WeightGather.scratch(),
            *SequenceGather.scratch(1),
            *ChipGather.scratch(PLANE),
            *SequenceGather.scratch(CHUNKS),
            *ChipGather.scratch(DOWN_PARTS),
            pltpu.SemaphoreType.DMA(()),
        ],
        compiler_params=params(2),
        name="attention",
    )(query, keys, values, spots, starts, key_spots, blocks, out_rows, down, rows)


def feed_kernel(
    rows_ref,
    grads_ref,
    weight_ref,
    down_ref,
    rows_all,
    hidden_out,
    grad_out,
    normed_out,
    total_out,
    *scratch,
):
    normed_parts, down_parts = scratch[:2]
    gather = SequenceGather(rows_ref, rows_all, scratch[2:7], 2)
    normed = SequenceScatter(normed_parts, normed_out, *scratch[7:10], scratch[10:14], 1)
    total = SequenceScatter(down_parts, total_out, *scratch[14:17], scratch[17:21], 1)
    d, c, x, core, z, y = place()
    greet(
        [(d, lax.rem(z + off, ZS) * YS + y) for off in range(1, ZS)] + [(d, z * YS + 1 - y)]
    )
    tokens, width = rows_ref.shape
    part = hidden_out.shape[2]
    tile = 256

    def work(pair):
        both = pl.ds(pair * YS, YS)

        @pl.loop(0, part, step=tile)
        def _(n):
            at = pl.ds(pl.multiple_of(n, tile), tile)
            after = pl.ds(pl.multiple_of(n + part, tile), tile)
            rows = rows_all[both].reshape(YS * tokens, width)
            gate = jnp.dot(rows, weight_ref[:, at], preferred_element_type=jnp.float32)
            up = jnp.dot(rows, weight_ref[:, after], preferred_element_type=jnp.float32)
            grad = times_rows(grads_ref[both].reshape(YS * tokens, width), down_ref[at, :])
            sigmoid = jax.nn.sigmoid(gate)
            silu = gate * sigmoid
            gate_grad = grad * up * sigmoid * (1.0 + gate * (1.0 - sigmoid))

            def held(value):
                return value.astype(jnp.bfloat16).reshape(YS, tokens, tile)

            hidden_out[both, :, at] = held(silu * up)
            grad_out[both, :, at] = held(gate_grad)
            grad_out[both, :, after] = held(grad * silu)

        @pl.loop(0, width, step=2 * tile)
        def _(n):
            at = pl.ds(pl.multiple_of(n, 2 * tile), 2 * tile)
            grads = grad_out[both].reshape(YS * tokens, 2 * part)
            hidden = hidden_out[both].reshape(YS * tokens, part)
            normed_parts[both, :, at] = (
                times_rows(grads, weight_ref[at, :])
                .astype(jnp.bfloat16)
                .reshape(YS, tokens, 2 * tile)
            )
            down_parts[both, :, at] = (
                jnp.dot(hidden, down_ref[:, at], preferred_element_type=jnp.float32)
                .astype(jnp.bfloat16)
                .reshape(YS, tokens, 2 * tile)
            )

    def pair_of(off):
        return lax.rem(z + off, ZS)

    gather.first(by_block=True)
    gather.local.wait()
    gather.arrive_across(z)
    work(z)
    order = (1, 3, 2)
    for k in range(2):
        gather.relay_one(1, k)
    for k in range(2):
        gather.relay_one(3, k)
    for step, off in enumerate(order):
        gather.arrive_across(pair_of(off))
        work(pair_of(off))
        normed.start(pair_of(off), 0)
        if step == 0:
            for k in range(2):
                gather.relay_one(2, k)
        else:
            normed.relay_one(order[step - 1], 0)
            total.start(pair_of(order[step - 1]), 0)
    normed.relay_one(2, 0)
    normed.start(z, 0)
    total.start(pair_of(2), 0)
    total.start(z, 0)
    for off in order:
        total.relay_one(off, 0)
    normed.last(0)
    total.last(0)
    gather.finish()
    normed.finish()
    total.finish()


def feed(rows, grads, weight, down):
    part = down.shape[0]
    summed = jax.ShapeDtypeStruct(rows.shape, jnp.float32)
    return pl.pallas_call(
        feed_kernel,
        out_shape=(
            jax.ShapeDtypeStruct((PLANE, *rows.shape), rows.dtype),
            jax.ShapeDtypeStruct((PLANE, rows.shape[0], part), rows.dtype),
            jax.ShapeDtypeStruct((PLANE, rows.shape[0], 2 * part), rows.dtype),
            summed,
            summed,
        ),
        in_specs=[ANY] + [VMEM] * 3,
        out_specs=(VMEM,) * 5,
        scratch_shapes=[
            pltpu.VMEM((PLANE, *rows.shape), rows.dtype),
            pltpu.VMEM((PLANE, *rows.shape), rows.dtype),
            *SequenceGather.scratch(2),
            *SequenceScatter.scratch(*rows.shape, 1),
            *SequenceScatter.scratch(*rows.shape, 1),
        ],
        compiler_params=params(5),
        name="feed",
    )(rows, grads, weight, down)


def attention_back_kernel(
    query_ref,
    key_ref,
    value_ref,
    spot_ref,
    start_ref,
    key_spot_ref,
    mixed_ref,
    parts_ref,
    down_ref,
    query_out,
    key_out,
    value_out,
    out_ref,
    down_out,
    *scratch,
):
    mixed_all = scratch[0]
    exchange = PlaneExchange(mixed_ref, mixed_all, scratch[1:4])
    weights = WeightScatter(parts_ref, out_ref, scratch[4:8], scratch[8:14])
    down = ChipScatter(down_ref, *scratch[14:17], scratch[17:], DOWN_PARTS)
    d, c, x, core, z, y = place()
    greet(plane_peers(d, c) + chip_peers(d, c, x, core))
    for off in range(1, PLANE + 1):
        exchange.send(off)
    weights.first()
    for j in range(DOWN_PARTS):
        down.start(j)
    key_out[...] = jnp.zeros_like(key_out)
    value_out[...] = jnp.zeros_like(value_out)
    for step in range(PLANE):
        block = lax.rem(c + PLANE - step, PLANE)
        exchange.arrive(step)

        @pl.loop(0, PAIRS)
        def _(pair):
            for half in range(2):
                query = query_ref[block, pair, half]
                grad = mixed_all[block, pair][:, half * HEAD_SIZE : (half + 1) * HEAD_SIZE]
                probs = probabilities(
                    query, key_ref[...], spot_ref[block], start_ref[block], key_spot_ref[...]
                )
                grad_probs = times_rows(grad, value_ref[...])
                delta = jnp.sum(probs * grad_probs, axis=-1, keepdims=True)
                grad_scores = (probs * (grad_probs - delta) * SCORE_SCALE).astype(jnp.bfloat16)
                query_out[block, pair, half] = jnp.dot(
                    grad_scores, key_ref[...], preferred_element_type=jnp.float32
                )
                key_out[...] += transposed_times(grad_scores, query)
                value_out[...] += transposed_times(probs.astype(jnp.bfloat16), grad)

        weights.relay(step + 1)
        if step >= 2:
            weights.send(step - 1)
    for off in (PLANE - 1, PLANE):
        weights.send(off)
    for j in range(DOWN_PARTS):
        down.relay(j)
    for j in range(DOWN_PARTS):
        down.total(j, down_out.at[j])
    weights.last()
    down.finish()
    exchange.finish()


def attention_back(query, keys, values, spots, starts, key_spots, mixed, parts, down):
    return pl.pallas_call(
        attention_back_kernel,
        out_shape=(
            jax.ShapeDtypeStruct(query.shape, jnp.float32),
            jax.ShapeDtypeStruct(keys.shape, jnp.float32),
            jax.ShapeDtypeStruct(values.shape, jnp.float32),
            jax.ShapeDtypeStruct((PLANE, *parts.shape[1:]), parts.dtype),
            jax.ShapeDtypeStruct((DOWN_PARTS, *down.shape[1:]), jnp.float32),
        ),
        in_specs=[VMEM] * 9,
        out_specs=(VMEM,) * 5,
        scratch_shapes=[
            pltpu.VMEM(mixed.shape, jnp.bfloat16),
            *PlaneExchange.scratch(),
            *WeightScatter.scratch(*parts.shape[1:]),
            *ChipScatter.scratch(DOWN_PARTS, *down.shape[1:]),
        ],
        compiler_params=params(3),
        name="attention_back",
    )(query, keys, values, spots, starts, key_spots, mixed, parts, down)


def closing_kernel(rows_ref, parts_ref, outs_ref, rows_out, out_ref, outs_out, *scratch):
    scatter = SequenceScatter(rows_ref, rows_out, *scratch[:3], scratch[3:7], CHUNKS)
    weights = WeightScatter(parts_ref, out_ref, scratch[7:11], scratch[11:17])
    outs_sum = scratch[17]
    chip = ChipScatter(outs_ref, *scratch[18:21], scratch[21:25], PLANE)
    outs = SequenceScatter(outs_sum, outs_out, *scratch[25:28], scratch[28:], 1)
    d, c, x, core, z, y = place()
    greet(plane_peers(d, c) + chip_peers(d, c, x, core))
    slots = [lax.rem(z + off, ZS) * YS + 1 - y for off in (2, 1, 3, 0)]
    slots += [lax.rem(z + off, ZS) * YS + y for off in (2, 1, 3, 0)]
    for j in slots:
        chip.start(j)
    weights.first()
    scatter.first()
    for j in slots:
        chip.relay(j)
    for off in range(1, PLANE + 1):
        weights.relay(off)
    for k in range(CHUNKS):
        scatter.relay(k)
    for off in range(1, PLANE + 1):
        weights.send(off)
    for i, j in enumerate(slots):
        chip.total(j, outs_sum.at[j])
        if i < ZS:
            copy = outs.across(lax.rem(z + (2, 1, 3, 0)[i], ZS), 0)
            copy.start()
            outs.sent.append(copy)
    outs.relay(0)
    for k in range(CHUNKS):
        scatter.last(k)
    weights.last()
    outs.last(0)
    scatter.finish()
    chip.finish()
    outs.finish()


def closing(rows, parts, outs):
    return pl.pallas_call(
        closing_kernel,
        out_shape=(
            jax.ShapeDtypeStruct(rows.shape[1:], jnp.float32),
            jax.ShapeDtypeStruct((PLANE, *parts.shape[1:]), parts.dtype),
            jax.ShapeDtypeStruct(outs.shape[1:], jnp.float32),
        ),
        in_specs=[VMEM] * 3,
        out_specs=(VMEM,) * 3,
        scratch_shapes=[
            *SequenceScatter.scratch(*rows.shape[1:], CHUNKS),
            *WeightScatter.scratch(*parts.shape[1:]),
            pltpu.VMEM((PLANE, *outs.shape[1:]), jnp.bfloat16),
            *ChipScatter.scratch(PLANE, *outs.shape[1:]),
            *SequenceScatter.scratch(*outs.shape[1:], 1),
        ],
        compiler_params=params(4),
        name="closing",
    )(rows, parts, outs)


def body(
    layer_in,
    positions,
    doc_starts,
    out_grad,
    norm_gains,
    norm_gains_m,
    norm_gains_v,
    w_query,
    w_query_m,
    w_query_v,
    key_value_weight,
    key_value_first_moment,
    key_value_second_moment,
    w_out,
    w_out_m,
    w_out_v,
    w_gate_up,
    w_gate_up_m,
    w_gate_up_v,
    w_down,
    w_down_m,
    w_down_v,
):
    number_of_tokens = layer_in.shape[0]
    ctx_count = lax.axis_size("ctx")
    seq_len = number_of_tokens * ctx_count
    key_value_width = KEY_VALUE_HEADS * HEAD_SIZE
    query_group_size = QUERY_HEADS // KEY_VALUE_HEADS
    score_scale = 1.0 / math.sqrt(HEAD_SIZE)
    needed = -(-512 // number_of_tokens)
    shard_span = min(ctx_count, 1 << max(0, (needed - 1).bit_length()))
    width_of_block = shard_span * number_of_tokens
    count_of_blocks = ctx_count // shard_span
    key_places = lax.all_gather(positions, "ctx", axis=0, tiled=True)
    starts = doc_starts[0]
    own_docs = doc_lookup(positions, starts)
    key_docs = doc_lookup(key_places, starts)
    query_full, keyval_full, out_full, gains_full = (
        lax.all_gather(w_query.astype(jnp.bfloat16), ("dp", "ctx"), axis=0, tiled=True),
        lax.all_gather(key_value_weight.astype(jnp.bfloat16), ("dp", "ctx"), axis=0, tiled=True),
        lax.all_gather(w_out.astype(jnp.bfloat16), ("dp", "ctx"), axis=0, tiled=True),
        lax.all_gather(norm_gains.astype(jnp.bfloat16), ("dp", "ctx"), axis=1, tiled=True),
    )
    gain_one = gains_full[0].astype(jnp.float32)
    gain_two = gains_full[1].astype(jnp.float32)
    layer_rows = layer_in.astype(jnp.float32)
    normed_one, inverse_one = norm_forward(layer_rows)
    input_one = (normed_one * gain_one).astype(jnp.bfloat16)
    query_pre = jnp.dot(input_one, query_full, preferred_element_type=jnp.float32)
    key_value_projected = jnp.dot(input_one, keyval_full, preferred_element_type=jnp.float32)
    cosine_table, sine_table = rope_tables(positions, HEAD_SIZE)
    query_rows = (
        apply_rotation(
            query_pre.reshape(number_of_tokens, QUERY_HEADS, HEAD_SIZE), cosine_table, sine_table
        )
        .astype(jnp.bfloat16)
        .reshape(number_of_tokens, KEY_VALUE_HEADS, query_group_size, HEAD_SIZE)
    )
    keys_own = (
        apply_rotation(
            key_value_projected[:, :key_value_width].reshape(
                number_of_tokens, KEY_VALUE_HEADS, HEAD_SIZE
            ),
            cosine_table,
            sine_table,
        )
        .astype(jnp.bfloat16)
        .reshape(number_of_tokens, key_value_width)
    )
    values_own = key_value_projected[:, key_value_width:].astype(jnp.bfloat16)
    every_key, every_value = (
        lax.all_gather(keys_own, "ctx", axis=0, tiled=True),
        lax.all_gather(values_own, "ctx", axis=0, tiled=True),
    )
    blocked_keys = every_key.reshape(count_of_blocks, width_of_block, KEY_VALUE_HEADS, HEAD_SIZE)
    blocked_values = every_value.reshape(
        count_of_blocks, width_of_block, KEY_VALUE_HEADS, HEAD_SIZE
    )
    place_blocks = key_places.reshape(count_of_blocks, width_of_block)
    doc_blocks = key_docs.reshape(count_of_blocks, width_of_block)

    def visible(place_blk, doc_blk):
        allowed = (place_blk[None, :] <= positions[:, None]) & (
            doc_blk[None, :] == own_docs[:, None]
        )
        return allowed[:, None, None, :]

    def scores_of(key_blk):
        return (
            jnp.einsum("tkgd,nkd->tkgn", query_rows, key_blk, preferred_element_type=jnp.float32)
            * score_scale
        )

    def stats_step(carry, block):
        row_top, row_total = carry
        key_blk, place_blk, doc_blk = block
        allowed = visible(place_blk, doc_blk)
        masked = jnp.where(allowed, scores_of(key_blk), masked_score)
        new_top = jnp.maximum(row_top, jnp.max(masked, axis=-1, keepdims=True))
        row_total = row_total * jnp.exp(row_top - new_top) + jnp.sum(
            jnp.where(allowed, jnp.exp(masked - new_top), 0.0), axis=-1, keepdims=True
        )
        return ((new_top, row_total), None)

    statistic_shape = (number_of_tokens, KEY_VALUE_HEADS, query_group_size, 1)
    (row_top, row_total), unused = lax.scan(
        stats_step,
        (
            jnp.full(statistic_shape, masked_score, jnp.float32),
            jnp.zeros(statistic_shape, jnp.float32),
        ),
        (blocked_keys, place_blocks, doc_blocks),
    )
    log_total = row_top + jnp.log(row_total)

    def probs_of(key_blk, place_blk, doc_blk):
        allowed = visible(place_blk, doc_blk)
        masked = jnp.where(allowed, scores_of(key_blk), masked_score)
        return jnp.where(allowed, jnp.exp(masked - log_total), 0.0)

    def output_step(carry, block):
        key_blk, value_blk, place_blk, doc_blk = block
        probs_low = probs_of(key_blk, place_blk, doc_blk).astype(jnp.bfloat16)
        added = jnp.einsum(
            "tkgn,nkd->tkgd", probs_low, value_blk, preferred_element_type=jnp.float32
        )
        return (carry + added, None)

    attention_output, unused = lax.scan(
        output_step,
        jnp.zeros((number_of_tokens, KEY_VALUE_HEADS, query_group_size, HEAD_SIZE), jnp.float32),
        (blocked_keys, blocked_values, place_blocks, doc_blocks),
    )
    mixed = attention_output.reshape(number_of_tokens, QUERY_HEADS * HEAD_SIZE).astype(jnp.bfloat16)
    middle = layer_rows + jnp.dot(mixed, out_full, preferred_element_type=jnp.float32)
    normed_two, inverse_two = norm_forward(middle)
    input_two = (normed_two * gain_two).astype(jnp.bfloat16)
    gate_up_low = w_gate_up.astype(jnp.bfloat16)
    down_low = w_down.astype(jnp.bfloat16)
    columns = input_two
    gate_up = jnp.dot(
        columns,
        lax.all_gather(gate_up_low, ("dp", "ctx"), axis=0, tiled=True),
        preferred_element_type=jnp.float32,
    )
    gate_part = gate_up[:, :FF]
    up_part = gate_up[:, FF:]
    sigmoid_gate = jax.nn.sigmoid(gate_part)
    silu_gate = gate_part * sigmoid_gate
    hidden = (silu_gate * up_part).astype(jnp.bfloat16)
    columns = hidden
    down_sum = jnp.dot(
        columns,
        lax.all_gather(down_low, ("dp", "ctx"), axis=0, tiled=True),
        preferred_element_type=jnp.float32,
    )
    layer_out = (middle + down_sum).astype(jnp.bfloat16)
    grad_rows = out_grad.astype(jnp.float32)
    grad_hidden = times_transposed(
        out_grad, lax.all_gather(down_low, ("dp", "ctx"), axis=0, tiled=True)
    )
    grad_gate = grad_hidden * up_part * sigmoid_gate * (1.0 + gate_part * (1.0 - sigmoid_gate))
    grad_up = grad_hidden * silu_gate
    grad_gate_up = jnp.concatenate([grad_gate, grad_up], axis=1).astype(jnp.bfloat16)
    down_grad = lax.psum_scatter(
        transposed_times(hidden, out_grad), ("dp", "ctx"), scatter_dimension=0, tiled=True
    )
    grad_normed_two = times_transposed(
        grad_gate_up, lax.all_gather(gate_up_low, ("dp", "ctx"), axis=0, tiled=True)
    )
    gate_up_grad = lax.psum_scatter(
        transposed_times(input_two, grad_gate_up), ("dp", "ctx"), scatter_dimension=0, tiled=True
    )
    grad_norm_two, gain_two_grad = norm_backward(grad_normed_two, normed_two, inverse_two, gain_two)
    grad_middle = grad_rows + grad_norm_two
    grad_middle_low = grad_middle.astype(jnp.bfloat16)
    out_term = transposed_times(mixed, grad_middle_low)
    grad_mixed = (
        times_transposed(grad_middle_low, out_full)
        .astype(jnp.bfloat16)
        .reshape(number_of_tokens, KEY_VALUE_HEADS, query_group_size, HEAD_SIZE)
    )
    delta = jnp.sum(grad_mixed.astype(jnp.float32) * attention_output, axis=-1, keepdims=True)

    def back_step(grad_query, block):
        key_blk, value_blk, place_blk, doc_blk = block
        probs = probs_of(key_blk, place_blk, doc_blk)
        probs_low = probs.astype(jnp.bfloat16)
        grad_probs = jnp.einsum(
            "tkgd,nkd->tkgn", grad_mixed, value_blk, preferred_element_type=jnp.float32
        )
        grad_scores = (probs * (grad_probs - delta) * score_scale).astype(jnp.bfloat16)
        grad_query = grad_query + jnp.einsum(
            "tkgn,nkd->tkgd", grad_scores, key_blk, preferred_element_type=jnp.float32
        )
        key_grad = jnp.einsum(
            "tkgn,tkgd->nkd", grad_scores, query_rows, preferred_element_type=jnp.float32
        )
        value_grad = jnp.einsum(
            "tkgn,tkgd->nkd", probs_low, grad_mixed, preferred_element_type=jnp.float32
        )
        return (grad_query, (key_grad, value_grad))

    grad_query, (key_grads, value_grads) = lax.scan(
        back_step,
        jnp.zeros((number_of_tokens, KEY_VALUE_HEADS, query_group_size, HEAD_SIZE), jnp.float32),
        (blocked_keys, blocked_values, place_blocks, doc_blocks),
    )
    summed_key_gradient, value_sum = (
        lax.psum_scatter(
            key_grads.reshape(seq_len, key_value_width).astype(jnp.bfloat16),
            "ctx",
            scatter_dimension=0,
            tiled=True,
        ).astype(jnp.float32),
        lax.psum_scatter(
            value_grads.reshape(seq_len, key_value_width).astype(jnp.bfloat16),
            "ctx",
            scatter_dimension=0,
            tiled=True,
        ).astype(jnp.float32),
    )
    key_gradient_unrotated = reverse_rotation(
        summed_key_gradient.reshape(number_of_tokens, KEY_VALUE_HEADS, HEAD_SIZE),
        cosine_table,
        sine_table,
    ).reshape(number_of_tokens, key_value_width)
    grad_keyval = jnp.concatenate([key_gradient_unrotated, value_sum], axis=1).astype(jnp.bfloat16)
    grad_query_low = (
        reverse_rotation(
            grad_query.reshape(number_of_tokens, QUERY_HEADS, HEAD_SIZE), cosine_table, sine_table
        )
        .reshape(number_of_tokens, QUERY_HEADS * HEAD_SIZE)
        .astype(jnp.bfloat16)
    )
    grad_normed_one = times_transposed(grad_query_low, query_full) + times_transposed(
        grad_keyval, keyval_full
    )
    query_term = transposed_times(input_one, grad_query_low)
    keyval_term = transposed_times(input_one, grad_keyval)
    grad_norm_one, gain_one_grad = norm_backward(grad_normed_one, normed_one, inverse_one, gain_one)
    in_grad = grad_middle + grad_norm_one
    gain_term = jnp.stack([gain_one_grad, gain_two_grad])
    query_grad, keyval_grad, out_weight_grad, gains_grad = (
        lax.psum_scatter(query_term, ("dp", "ctx"), scatter_dimension=0, tiled=True),
        lax.psum_scatter(keyval_term, ("dp", "ctx"), scatter_dimension=0, tiled=True),
        lax.psum_scatter(out_term, ("dp", "ctx"), scatter_dimension=0, tiled=True),
        lax.psum_scatter(gain_term, ("dp", "ctx"), scatter_dimension=1, tiled=True),
    )
    rates = rates_for(seq_len)
    gains_m_new, gains_v_new, gains_new = adamw(
        norm_gains, gains_grad, norm_gains_m, norm_gains_v, rates[0], 0.0
    )
    query_m_new, query_v_new, query_new = adamw(
        w_query, query_grad, w_query_m, w_query_v, rates[1], weight_decay
    )
    keyval_m_new, keyval_v_new, keyval_new = adamw(
        key_value_weight,
        keyval_grad,
        key_value_first_moment,
        key_value_second_moment,
        rates[2],
        weight_decay,
    )
    out_m_new, out_v_new, out_new = adamw(
        w_out, out_weight_grad, w_out_m, w_out_v, rates[3], weight_decay
    )
    gate_up_m_new, gate_up_v_new, gate_up_new = adamw(
        w_gate_up, gate_up_grad, w_gate_up_m, w_gate_up_v, rates[4], weight_decay
    )
    down_m_new, down_v_new, down_new = adamw(
        w_down, down_grad, w_down_m, w_down_v, rates[5], weight_decay
    )
    return (
        layer_out,
        in_grad,
        gains_grad,
        gains_m_new,
        gains_v_new,
        gains_new,
        query_grad,
        query_m_new,
        query_v_new,
        query_new,
        keyval_grad,
        keyval_m_new,
        keyval_v_new,
        keyval_new,
        out_weight_grad,
        out_m_new,
        out_v_new,
        out_new,
        gate_up_grad,
        gate_up_m_new,
        gate_up_v_new,
        gate_up_new,
        down_grad,
        down_m_new,
        down_v_new,
        down_new,
    )


def tensor_parallel(
    layer_in,
    positions,
    doc_starts,
    out_grad,
    norm_gains,
    norm_gains_m,
    norm_gains_v,
    w_query,
    w_query_m,
    w_query_v,
    key_value_weight,
    key_value_first_moment,
    key_value_second_moment,
    w_out,
    w_out_m,
    w_out_v,
    w_gate_up,
    w_gate_up_m,
    w_gate_up_v,
    w_down,
    w_down_m,
    w_down_v,
):
    low = jnp.bfloat16
    own_tokens, width = layer_in.shape
    seq_len = own_tokens * PLANE
    group = GROUP
    group_width = group * HEAD_SIZE
    ff_part = FF // PLANE
    ff_own = FF // RANKS
    rows = w_query.shape[0]

    gains_low = norm_gains.astype(low)
    small = jnp.broadcast_to(
        jnp.pad(gains_low.T, ((0, 0), (0, 126)))[None], (PLANE, rows, 128)
    )
    attention_blocks = jnp.concatenate(
        [
            w_query.astype(low).reshape(rows, PLANE, group_width).transpose(1, 0, 2),
            key_value_weight.astype(low)
            .reshape(rows, 2, PLANE, HEAD_SIZE)
            .transpose(2, 0, 1, 3)
            .reshape(PLANE, rows, 2 * HEAD_SIZE),
            small,
        ],
        axis=2,
    )
    feed_blocks = (
        w_gate_up.astype(low)
        .reshape(rows, 2, 4, PLANE, ff_own)
        .transpose(3, 0, 1, 2, 4)
        .reshape(PLANE, rows, 2 * ff_part)
    )
    spots = jnp.broadcast_to(positions[None, :], (8, own_tokens))
    rows_all, spots_all, attention_all = opening(layer_in, spots, attention_blocks)
    attention_all = attention_all.reshape(width, -1)
    qkv_width = group_width + 2 * HEAD_SIZE
    qkv_weight = attention_all[:, :qkv_width]
    gain_one = attention_all[:, qkv_width].astype(jnp.float32)
    gain_two = attention_all[:, qkv_width + 1].astype(jnp.float32)
    places = spots_all[:, 0, :].reshape(seq_len)
    starts = jnp.max(
        jnp.where(doc_starts[0][None, :] <= places[:, None], doc_starts[0][None, :], 0), axis=1
    )
    normed_all, unused = norm_forward(rows_all.reshape(seq_len, width).astype(jnp.float32))
    input_one = (normed_all * gain_one).astype(low)
    projected = jnp.dot(input_one, qkv_weight, preferred_element_type=jnp.float32)
    cosine_table, sine_table = rope_tables(places, HEAD_SIZE)
    query_rows = (
        apply_rotation(
            projected[:, :group_width].reshape(seq_len, group, HEAD_SIZE),
            cosine_table,
            sine_table,
        )
        .astype(low)
        .reshape(PLANE, own_tokens, PAIRS, 2, HEAD_SIZE)
        .transpose(0, 2, 3, 1, 4)
    )
    key_rows = apply_rotation(
        projected[:, None, group_width : group_width + HEAD_SIZE], cosine_table, sine_table
    ).astype(low)[:, 0]
    value_rows = projected[:, group_width + HEAD_SIZE :].astype(low)
    token_spots = places.reshape(PLANE, own_tokens, 1)
    token_starts = starts.reshape(PLANE, own_tokens, 1)
    mixed_parts, feed_all, out_all, down_all, grads_all = attention(
        query_rows,
        key_rows,
        value_rows,
        token_spots,
        token_starts,
        places[None, :],
        feed_blocks,
        w_out.astype(low),
        w_down.astype(low).reshape(DOWN_PARTS, -1, width),
        out_grad,
    )
    mixed = mixed_parts.transpose(2, 0, 1, 3).reshape(own_tokens, width)
    out_weight = out_all.reshape(width, width)
    branch = jnp.dot(mixed, out_weight, preferred_element_type=jnp.float32)

    layer_rows = layer_in.astype(jnp.float32)
    middle = layer_rows + branch
    normed_two, inverse_two = norm_forward(middle)
    input_two_all, hidden_all, grad_gate_up_all, grad_normed_two, down_sum = feed(
        (normed_two * gain_two).astype(low),
        grads_all,
        feed_all.reshape(width, 2 * ff_part),
        down_all.reshape(ff_part, width),
    )
    input_two = input_two_all.reshape(seq_len, width)
    hidden = hidden_all.reshape(seq_len, ff_part)
    grad_gate_up = grad_gate_up_all.reshape(seq_len, 2 * ff_part)
    layer_out = (middle + down_sum).astype(low)

    out_grads = grads_all.reshape(seq_len, width)
    down_term = transposed_times(hidden, out_grads).astype(low)
    feed_term = transposed_times(input_two, grad_gate_up).astype(low)
    grad_norm_two, unused = norm_backward(grad_normed_two, normed_two, inverse_two, gain_two)
    grad_middle = out_grad.astype(jnp.float32) + grad_norm_two
    grad_middle_low = grad_middle.astype(low)
    out_term = transposed_times(mixed, grad_middle_low).astype(low)
    grad_mixed = (
        times_transposed(grad_middle_low, out_weight)
        .astype(low)
        .reshape(own_tokens, PLANE, PAIRS, 2 * HEAD_SIZE)
        .transpose(1, 2, 0, 3)
    )
    grad_query, grad_key, grad_value, feed_grad, down_grad = attention_back(
        query_rows,
        key_rows,
        value_rows,
        token_spots,
        token_starts,
        places[None, :],
        grad_mixed,
        feed_term.reshape(RANKS, rows, 2 * ff_part),
        down_term.reshape(4 * DOWN_PARTS, -1, width),
    )
    gate_up_grad = (
        feed_grad.reshape(PLANE, rows, 2, 4, ff_own)
        .transpose(1, 2, 3, 0, 4)
        .reshape(rows, 2 * FF)
        .astype(jnp.float32)
    )
    down_grad = down_grad.reshape(w_down.shape)
    grad_query = grad_query.transpose(0, 3, 1, 2, 4).reshape(seq_len, group, HEAD_SIZE)
    grad_qkv = jnp.concatenate(
        [
            reverse_rotation(grad_query, cosine_table, sine_table).reshape(seq_len, group_width),
            reverse_rotation(grad_key[:, None], cosine_table, sine_table)[:, 0],
            grad_value,
        ],
        axis=1,
    ).astype(low)
    one_parts = times_transposed(grad_qkv, qkv_weight).astype(low)
    qkv_term = transposed_times(input_one, grad_qkv).astype(low)
    grad_normed_one, qkv_grad, out_weight_grad = closing(
        one_parts.reshape(PLANE, own_tokens, width),
        qkv_term.reshape(RANKS, rows, qkv_width),
        out_term.reshape(RANKS, rows, width),
    )
    normed_one, inverse_one = norm_forward(layer_rows)
    grad_norm_one, unused = norm_backward(grad_normed_one, normed_one, inverse_one, gain_one)
    in_grad = grad_middle + grad_norm_one
    qkv_grad = qkv_grad.astype(jnp.float32)
    query_grad = qkv_grad[:, :, :group_width].transpose(1, 0, 2).reshape(w_query.shape)
    keyval_grad = (
        qkv_grad[:, :, group_width:]
        .reshape(PLANE, rows, 2, HEAD_SIZE)
        .transpose(1, 2, 0, 3)
        .reshape(key_value_weight.shape)
    )
    def low_times(weight, grad):
        return jnp.sum(weight.astype(low).astype(jnp.float32) * grad, axis=1)

    gains_grad = jnp.stack(
        [
            low_times(w_query, query_grad) + low_times(key_value_weight, keyval_grad),
            low_times(w_gate_up, gate_up_grad),
        ]
    ) / gains_low.astype(jnp.float32)

    rates = rates_for(seq_len)
    return (
        layer_out,
        in_grad,
        gains_grad,
        *adamw(norm_gains, gains_grad, norm_gains_m, norm_gains_v, rates[0], 0.0),
        query_grad,
        *adamw(w_query, query_grad, w_query_m, w_query_v, rates[1], weight_decay),
        keyval_grad,
        *adamw(
            key_value_weight,
            keyval_grad,
            key_value_first_moment,
            key_value_second_moment,
            rates[2],
            weight_decay,
        ),
        out_weight_grad,
        *adamw(w_out, out_weight_grad, w_out_m, w_out_v, rates[3], weight_decay),
        gate_up_grad,
        *adamw(w_gate_up, gate_up_grad, w_gate_up_m, w_gate_up_v, rates[4], weight_decay),
        down_grad,
        *adamw(w_down, down_grad, w_down_m, w_down_v, rates[5], weight_decay),
    )


def solution(mesh):
    planned = tensor_parallel if dict(mesh.shape) == {"dp": 2 * XS, "ctx": ZS * YS} else body
    return jax.shard_map(
        planned,
        mesh=mesh,
        in_specs=(
            P(("dp", "ctx"), None),
            P(("dp", "ctx")),
            P("dp", None),
            P(("dp", "ctx"), None),
            P(None, ("dp", "ctx")),
            P(None, ("dp", "ctx")),
            P(None, ("dp", "ctx")),
            P(("dp", "ctx"), None),
            P(("dp", "ctx"), None),
            P(("dp", "ctx"), None),
            P(("dp", "ctx"), None),
            P(("dp", "ctx"), None),
            P(("dp", "ctx"), None),
            P(("dp", "ctx"), None),
            P(("dp", "ctx"), None),
            P(("dp", "ctx"), None),
            P(("dp", "ctx"), None),
            P(("dp", "ctx"), None),
            P(("dp", "ctx"), None),
            P(("dp", "ctx"), None),
            P(("dp", "ctx"), None),
            P(("dp", "ctx"), None),
        ),
        out_specs=(
            P(("dp", "ctx"), None),
            P(("dp", "ctx"), None),
            P(None, ("dp", "ctx")),
            P(None, ("dp", "ctx")),
            P(None, ("dp", "ctx")),
            P(None, ("dp", "ctx")),
            P(("dp", "ctx"), None),
            P(("dp", "ctx"), None),
            P(("dp", "ctx"), None),
            P(("dp", "ctx"), None),
            P(("dp", "ctx"), None),
            P(("dp", "ctx"), None),
            P(("dp", "ctx"), None),
            P(("dp", "ctx"), None),
            P(("dp", "ctx"), None),
            P(("dp", "ctx"), None),
            P(("dp", "ctx"), None),
            P(("dp", "ctx"), None),
            P(("dp", "ctx"), None),
            P(("dp", "ctx"), None),
            P(("dp", "ctx"), None),
            P(("dp", "ctx"), None),
            P(("dp", "ctx"), None),
            P(("dp", "ctx"), None),
            P(("dp", "ctx"), None),
            P(("dp", "ctx"), None),
        ),
        check_vma=False,
    )
```

```python
import functools
import math

import jax
import jax.numpy as jnp
from jax import lax
from jax.experimental import pallas as pl
from jax.experimental.pallas import tpu as pltpu
from jax.sharding import PartitionSpec as P

MODEL_WIDTH = 2048
QUERY_HEADS = 32
KEY_VALUE_HEADS = 8
HEAD_SIZE = 64
FF = 8192
STEP = 10


eps_norm = 1e-05
rope_base = 500000.0
beta_one = 0.9
beta_two = 0.95
eps_adam = 1e-08
weight_decay = 0.1
masked_score = -1e30


def rates_for(seq_len):
    return (
        0.6,
        0.8 / math.sqrt(MODEL_WIDTH // 4),
        0.8 / math.sqrt(MODEL_WIDTH),
        0.8 / math.sqrt(max(220 * MODEL_WIDTH // seq_len, 1)),
        0.8 / math.sqrt(MODEL_WIDTH),
        0.8 / math.sqrt(FF // 2),
    )


def adamw(weight, grad_sum, first, second, rate, decay):
    first_new = beta_one * first + (1.0 - beta_one) * grad_sum
    second_new = beta_two * second + (1.0 - beta_two) * grad_sum * grad_sum
    first_hat = first_new / (1.0 - beta_one**STEP)
    second_hat = second_new / (1.0 - beta_two**STEP)
    weight_new = weight - rate * (first_hat / (jnp.sqrt(second_hat) + eps_adam) + decay * weight)
    return (first_new, second_new, weight_new)


def norm_forward(layer_rows):
    inverse = lax.rsqrt(jnp.mean(layer_rows * layer_rows, axis=-1, keepdims=True) + eps_norm)
    return (layer_rows * inverse, inverse)


def norm_backward(grad_out, normed, inverse, gain_row):
    scaled = grad_out * gain_row
    grad_in = inverse * (scaled - normed * jnp.mean(scaled * normed, axis=-1, keepdims=True))
    return (grad_in, jnp.sum(grad_out * normed, axis=0))


def rope_tables(token_placement, head_dim):
    half_dim = head_dim // 2
    frequencies = jnp.exp(
        jnp.arange(half_dim, dtype=jnp.float32) * (-2.0 * math.log(rope_base) / head_dim)
    )
    angles = token_placement.astype(jnp.float32)[:, None] * frequencies[None, :]
    return (jnp.cos(angles)[:, None, :], jnp.sin(angles)[:, None, :])


def apply_rotation(value_rows, cosine_table, sine_table):
    half_dim = value_rows.shape[-1] // 2
    first_half = value_rows[..., :half_dim]
    second_half = value_rows[..., half_dim:]
    return jnp.concatenate(
        [
            first_half * cosine_table - second_half * sine_table,
            second_half * cosine_table + first_half * sine_table,
        ],
        axis=-1,
    )


def reverse_rotation(grad_rows, cosine_table, sine_table):
    half_dim = grad_rows.shape[-1] // 2
    first_half = grad_rows[..., :half_dim]
    second_half = grad_rows[..., half_dim:]
    return jnp.concatenate(
        [
            first_half * cosine_table + second_half * sine_table,
            second_half * cosine_table - first_half * sine_table,
        ],
        axis=-1,
    )


def doc_lookup(token_placement, starts):
    return jnp.sum((token_placement[:, None] >= starts[None, :]).astype(jnp.int32), axis=1) - 1


def times_transposed(left, right):
    return lax.dot_general(
        left, right, (((1,), (1,)), ((), ())), preferred_element_type=jnp.float32
    )


def transposed_times(left, right):
    return lax.dot_general(
        left, right, (((0,), (0,)), ((), ())), preferred_element_type=jnp.float32
    )


XS = 2
YS = 2
ZS = 4
PLANE = ZS * YS
RANKS = 2 * XS * PLANE
MESH = pl.DeviceIdType.MESH


def place():
    d = lax.axis_index("dp")
    c = lax.axis_index("ctx")
    return d, c, lax.div(d, 2), lax.rem(d, 2), lax.div(c, YS), lax.rem(c, YS)


def remote(src, dst, send_sem, recv_sem, d, c):
    return pltpu.make_async_remote_copy(
        src_ref=src,
        dst_ref=dst,
        send_sem=send_sem,
        recv_sem=recv_sem,
        device_id=(d, c),
        device_id_type=MESH,
    )


def greet(peers):
    barrier = pltpu.get_barrier_semaphore()
    for d, c in peers:
        pl.semaphore_signal(barrier, inc=1, device_id=(d, c), device_id_type=MESH)
    pl.semaphore_wait(barrier, len(peers))


def plane_peers(d, c):
    return [(d, lax.rem(c + k, PLANE)) for k in range(1, PLANE)]


def chip_peers(d, c, x, core):
    return [(x * 2 + 1 - core, c), ((1 - x) * 2 + core, c)]


def add_into(target, sources, rows, step=16):
    @pl.loop(0, rows, step=step)
    def _(r):
        at = pl.ds(pl.multiple_of(r, step), step)
        total = sources[0][at].astype(jnp.float32)
        for source in sources[1:]:
            total = total + source[at].astype(jnp.float32)
        target[at] = total.astype(target.dtype)


def near_first(z):
    half = lax.div(z, 2)
    return [half * 4 + 1 - z, 2 - half, 3 - 3 * half]


class SequenceGather:
    def __init__(self, own, out, sems, chunks):
        self.own, self.out, self.chunks = own, out, chunks
        self.zs, self.zr, self.ys, self.yr, self.local_sem = sems
        self.d, self.c, _, _, self.z, self.y = place()
        self.rows = own.shape[0] // chunks
        self.sent = []

    @staticmethod
    def scratch(chunks):
        return [
            pltpu.SemaphoreType.DMA((ZS, chunks)),
            pltpu.SemaphoreType.DMA((ZS, chunks)),
            pltpu.SemaphoreType.DMA((ZS, chunks)),
            pltpu.SemaphoreType.DMA((ZS, chunks)),
            pltpu.SemaphoreType.DMA(()),
        ]

    def part(self, ref, k):
        return ref.at[pl.ds(k * self.rows, self.rows)]

    def across(self, z, k, src):
        slot = z * YS + self.y
        return remote(
            src,
            self.part(self.out.at[slot], k),
            self.ys.at[z, k],
            self.yr.at[z, k],
            self.d,
            self.z * YS + 1 - self.y,
        )

    def along(self, to, k):
        return remote(
            self.part(self.own, k),
            self.part(self.out.at[self.c], k),
            self.zs.at[to, k],
            self.zr.at[self.z, k],
            self.d,
            to * YS + self.y,
        )

    def start(self, copy):
        copy.start()
        self.sent.append(copy)

    def first(self, by_block=False):
        self.local = pltpu.make_async_copy(self.own, self.out.at[self.c], self.local_sem)
        self.local.start()
        near = near_first(self.z)
        if by_block:
            for k in range(self.chunks):
                self.start(self.across(self.z, k, self.part(self.own, k)))
            for to in near:
                for k in range(self.chunks):
                    self.start(self.along(to, k))
            return
        for k in range(self.chunks):
            for to in near[::-1]:
                self.start(self.along(to, k))
            self.start(self.across(self.z, k, self.part(self.own, k)))

    def relay_one(self, source, k):
        slot = source * YS + self.y
        block = self.part(self.out.at[slot], k)
        remote(
            block, block, self.zs.at[source, k], self.zr.at[source, k], self.d, slot
        ).wait_recv()
        self.start(self.across(source, k, block))

    def relay(self, k):
        for source in near_first(self.z):
            self.relay_one(source, k)

    def relay_block(self, source):
        for k in range(self.chunks):
            self.relay_one(source, k)

    def arrive_across(self, z):
        for k in range(self.chunks):
            block = self.part(self.out.at[z * YS + 1 - self.y], k)
            remote(
                block,
                block,
                self.ys.at[z, k],
                self.yr.at[z, k],
                self.d,
                self.z * YS + 1 - self.y,
            ).wait_recv()

    def finish(self):
        for copy in self.sent:
            copy.wait_send()

    def last(self):
        for z in range(ZS):
            self.arrive_across(z)
        self.finish()
        self.local.wait()


class SequenceScatter:
    def __init__(self, parts, out, ybuf, zbuf, sems, chunks):
        self.parts, self.out, self.chunks = parts, out, chunks
        self.ybuf, self.zbuf = ybuf, zbuf
        self.ys, self.yr, self.zs, self.zr = sems
        self.d, self.c, _, _, self.z, self.y = place()
        self.rows = parts.shape[1] // chunks
        self.sent = []

    @staticmethod
    def scratch(rows, width, chunks):
        return [
            pltpu.VMEM((ZS, rows, width), jnp.bfloat16),
            pltpu.VMEM((ZS, rows, width), jnp.bfloat16),
            pltpu.SemaphoreType.DMA((ZS, chunks)),
            pltpu.SemaphoreType.DMA((ZS, chunks)),
            pltpu.SemaphoreType.DMA((ZS, chunks)),
            pltpu.SemaphoreType.DMA((ZS, chunks)),
        ]

    def span(self, k):
        return pl.ds(k * self.rows, self.rows)

    def across(self, z, k):
        return remote(
            self.parts.at[z * YS + 1 - self.y, self.span(k)],
            self.ybuf.at[z, self.span(k)],
            self.ys.at[z, k],
            self.yr.at[z, k],
            self.d,
            self.z * YS + 1 - self.y,
        )

    def along(self, to, k):
        return remote(
            self.ybuf.at[to, self.span(k)],
            self.zbuf.at[self.z, self.span(k)],
            self.zs.at[to, k],
            self.zr.at[self.z, k],
            self.d,
            to * YS + self.y,
        )

    def start(self, z, k):
        copy = self.across(z, k)
        copy.start()
        self.sent.append(copy)

    def first(self):
        for k in range(self.chunks):
            for z in (*near_first(self.z)[::-1], self.z):
                self.start(z, k)

    def relay_one(self, z, k):
        self.across(z, k).wait_recv()
        block = self.ybuf.at[z, self.span(k)]
        add_into(block, [self.parts.at[z * YS + self.y, self.span(k)], block], self.rows)
        copy = self.along(z, k)
        copy.start()
        self.sent.append(copy)

    def relay(self, k):
        for z in near_first(self.z)[::-1]:
            self.relay_one(z, k)

    def last(self, k):
        self.across(self.z, k).wait_recv()
        blocks = [self.parts.at[self.c, self.span(k)], self.ybuf.at[self.z, self.span(k)]]
        for source in near_first(self.z):
            block = self.zbuf.at[source, self.span(k)]
            remote(
                block,
                block,
                self.zs.at[source, k],
                self.zr.at[source, k],
                self.d,
                source * YS + self.y,
            ).wait_recv()
            blocks.append(block)
        add_into(self.out.at[self.span(k)], blocks, self.rows)

    def finish(self):
        for copy in self.sent:
            copy.wait_send()


class ChipGather:
    def __init__(self, out, sems, count):
        self.out, self.count = out, count
        self.cs, self.cr, self.xs, self.xr = sems
        self.d, self.c, self.x, self.core, _, _ = place()
        self.sent = []

    @staticmethod
    def scratch(count):
        return [
            pltpu.SemaphoreType.DMA((2, count)),
            pltpu.SemaphoreType.DMA((2, count)),
            pltpu.SemaphoreType.DMA((count,)),
            pltpu.SemaphoreType.DMA((count,)),
        ]

    def to_core(self, far, j, src=None):
        x = 1 - self.x if far else self.x
        block = self.out.at[(x * 2 + self.core) * self.count + j]
        return remote(
            block if src is None else src,
            block,
            self.cs.at[far, j],
            self.cr.at[far, j],
            self.x * 2 + 1 - self.core,
            self.c,
        )

    def to_x(self, j, src=None):
        block = self.out.at[self.d * self.count + j]
        return remote(
            block if src is None else src,
            block,
            self.xs.at[j],
            self.xr.at[j],
            (1 - self.x) * 2 + self.core,
            self.c,
        )

    def start(self, j, src=None):
        for copy in (self.to_x(j, src), self.to_core(0, j, src)):
            copy.start()
            self.sent.append(copy)

    def relay(self, j):
        self.to_x(j).wait_recv()
        copy = self.to_core(1, j)
        copy.start()
        self.sent.append(copy)

    def last(self):
        for far in (0, 1):
            for j in range(self.count):
                self.to_core(far, j).wait_recv()
        for copy in self.sent:
            copy.wait_send()


class WeightGather:
    def __init__(self, blocks, out, sems):
        self.blocks, self.out = blocks, out
        self.ps, self.pr, self.local_sem = sems[:3]
        self.chip = ChipGather(out, sems[3:], PLANE)
        self.d, self.c = self.chip.d, self.chip.c
        self.sent = []

    @staticmethod
    def scratch():
        return [
            pltpu.SemaphoreType.DMA((PLANE,)),
            pltpu.SemaphoreType.DMA((PLANE,)),
            pltpu.SemaphoreType.DMA(()),
        ] + ChipGather.scratch(PLANE)

    def first(self):
        self.local = pltpu.make_async_copy(
            self.blocks.at[self.c], self.out.at[self.d * PLANE + self.c], self.local_sem
        )
        self.local.start()
        for off in range(1, PLANE):
            to = lax.rem(self.c + off, PLANE)
            copy = remote(
                self.blocks.at[to],
                self.out.at[self.d * PLANE + self.c],
                self.ps.at[off],
                self.pr.at[self.c],
                self.d,
                to,
            )
            copy.start()
            self.sent.append(copy)
        self.chip.start(self.c, self.blocks.at[self.c])

    def relay(self, off):
        source = lax.rem(self.c + PLANE - off, PLANE)
        block = self.out.at[self.d * PLANE + source]
        remote(
            block, block, self.ps.at[off], self.pr.at[source], self.d, source
        ).wait_recv()
        self.chip.start(source)

    def relay_chip(self):
        for off in range(PLANE):
            self.chip.relay(lax.rem(self.c + off, PLANE))

    def last(self):
        self.chip.last()
        for copy in self.sent:
            copy.wait_send()
        self.local.wait()


class ChipScatter:
    def __init__(self, parts, cbuf, stage, xbuf, sems, count):
        self.parts, self.count = parts, count
        self.cbuf, self.stage, self.xbuf = cbuf, stage, xbuf
        self.cs, self.cr, self.xs, self.xr = sems
        self.d, self.c, self.x, self.core, _, _ = place()
        self.sent = []

    @staticmethod
    def scratch(count, rows, width):
        return [
            pltpu.VMEM((2, count, rows, width), jnp.bfloat16),
            pltpu.VMEM((count, rows, width), jnp.bfloat16),
            pltpu.VMEM((count, rows, width), jnp.bfloat16),
            pltpu.SemaphoreType.DMA((2, count)),
            pltpu.SemaphoreType.DMA((2, count)),
            pltpu.SemaphoreType.DMA((count,)),
            pltpu.SemaphoreType.DMA((count,)),
        ]

    def to_core(self, far, j):
        x = 1 - self.x if far else self.x
        return remote(
            self.parts.at[(x * 2 + 1 - self.core) * self.count + j],
            self.cbuf.at[far, j],
            self.cs.at[far, j],
            self.cr.at[far, j],
            self.x * 2 + 1 - self.core,
            self.c,
        )

    def to_x(self, j):
        return remote(
            self.stage.at[j],
            self.xbuf.at[j],
            self.xs.at[j],
            self.xr.at[j],
            (1 - self.x) * 2 + self.core,
            self.c,
        )

    def start(self, j):
        for far in (1, 0):
            copy = self.to_core(far, j)
            copy.start()
            self.sent.append(copy)

    def relay(self, j):
        self.to_core(1, j).wait_recv()
        own = self.parts.at[((1 - self.x) * 2 + self.core) * self.count + j]
        add_into(self.stage.at[j], [own, self.cbuf.at[1, j]], own.shape[0])
        copy = self.to_x(j)
        copy.start()
        self.sent.append(copy)

    def total(self, j, target):
        self.to_core(0, j).wait_recv()
        self.to_x(j).wait_recv()
        own = self.parts.at[self.d * self.count + j]
        add_into(target, [own, self.cbuf.at[0, j], self.xbuf.at[j]], own.shape[0])

    def finish(self):
        for copy in self.sent:
            copy.wait_send()


class WeightScatter:
    def __init__(self, parts, out, bufs, sems):
        self.stage = bufs[0]
        self.ps, self.pr = sems[:2]
        self.chip = ChipScatter(parts, *bufs[1:], sems[2:], PLANE)
        self.out = out
        self.d, self.c = self.chip.d, self.chip.c
        self.sent = []

    @staticmethod
    def scratch(rows, width):
        chip = ChipScatter.scratch(PLANE, rows, width)
        return [
            pltpu.VMEM((PLANE, rows, width), jnp.bfloat16),
            *chip[:3],
            pltpu.SemaphoreType.DMA((PLANE,)),
            pltpu.SemaphoreType.DMA((PLANE,)),
            *chip[3:],
        ]

    def first(self):
        for off in range(1, PLANE + 1):
            self.chip.start(lax.rem(self.c + off, PLANE))

    def relay(self, off):
        self.chip.relay(lax.rem(self.c + off, PLANE))

    def send(self, off):
        to = lax.rem(self.c + off, PLANE)
        if off == PLANE:
            self.chip.total(to, self.out.at[self.c])
            return
        self.chip.total(to, self.stage.at[to])
        copy = remote(
            self.stage.at[to],
            self.out.at[self.c],
            self.ps.at[off],
            self.pr.at[self.c],
            self.d,
            to,
        )
        copy.start()
        self.sent.append(copy)

    def last(self):
        for off in range(1, PLANE):
            source = lax.rem(self.c + off, PLANE)
            block = self.out.at[source]
            remote(
                block, block, self.ps.at[off], self.pr.at[source], self.d, source
            ).wait_recv()
        for copy in self.sent:
            copy.wait_send()
        self.chip.finish()


def params(collective_id):
    return pltpu.CompilerParams(
        collective_id=collective_id, has_side_effects=True, vmem_limit_bytes=56 * 2**20
    )


ANY = pl.BlockSpec(memory_space=pl.ANY)
VMEM = pl.BlockSpec(memory_space=pltpu.VMEM)
CHUNKS = 4


DOWN_PARTS = 4
SCORE_SCALE = 1.0 / math.sqrt(HEAD_SIZE)
GROUP = QUERY_HEADS // KEY_VALUE_HEADS
PAIRS = GROUP // 2


def times_rows(left, right):
    return lax.dot_general(
        left, right, (((1,), (1,)), ((), ())), preferred_element_type=jnp.float32
    )


class PlaneExchange:
    def __init__(self, blocks, out, sems):
        self.blocks, self.out = blocks, out
        self.ps, self.pr, self.local_sem = sems
        self.d, self.c = lax.axis_index("dp"), lax.axis_index("ctx")
        self.sent = []

    @staticmethod
    def scratch():
        return [
            pltpu.SemaphoreType.DMA((PLANE,)),
            pltpu.SemaphoreType.DMA((PLANE,)),
            pltpu.SemaphoreType.DMA(()),
        ]

    def send(self, off):
        to = lax.rem(self.c + off, PLANE)
        if off % PLANE == 0:
            self.local = pltpu.make_async_copy(
                self.blocks.at[to], self.out.at[self.c], self.local_sem
            )
            self.local.start()
            return
        copy = remote(
            self.blocks.at[to],
            self.out.at[self.c],
            self.ps.at[off],
            self.pr.at[self.c],
            self.d,
            to,
        )
        copy.start()
        self.sent.append(copy)

    def arrive(self, off):
        if off % PLANE == 0:
            self.local.wait()
            return
        source = lax.rem(self.c + PLANE - off, PLANE)
        block = self.out.at[source]
        remote(
            block, block, self.ps.at[off], self.pr.at[source], self.d, source
        ).wait_recv()

    def finish(self):
        for copy in self.sent:
            copy.wait_send()


def probabilities(query, keys, spot, start, key_spots):
    scores = times_rows(query, keys) * SCORE_SCALE
    masked = jnp.where((key_spots <= spot) & (key_spots >= start), scores, masked_score)
    exponent = jnp.exp(masked - jnp.max(masked, axis=-1, keepdims=True))
    return exponent * (1.0 / jnp.sum(exponent, axis=-1, keepdims=True))


def rotate(value, table, back=False):
    lane = lax.broadcasted_iota(jnp.int32, value.shape, 1)
    turned = pltpu.roll(table, HEAD_SIZE, 1)
    cosine = jnp.where(lane < HEAD_SIZE, table, turned)
    sine = jnp.where(lane < HEAD_SIZE, turned, table)
    half = HEAD_SIZE // 2
    other = jnp.where(
        lax.rem(lane, HEAD_SIZE) < half,
        pltpu.roll(value, 2 * HEAD_SIZE - half, 1),
        pltpu.roll(value, half, 1),
    )
    if back:
        return value * cosine - other * sine
    return value * cosine + other * sine


QKV_WIDTH = (GROUP + 2) * HEAD_SIZE


def attention_kernel(
    starts_ref,
    rows_ref,
    table_ref,
    spots_ref,
    qkv_ref,
    blocks_ref,
    out_rows_ref,
    down_ref,
    grads_ref,
    input_out,
    table_out,
    qkv_out,
    gains_out,
    query_out,
    key_out,
    value_out,
    spot_out,
    start_out,
    key_spot_out,
    mixed_out,
    blocks_out,
    out_rows_out,
    down_out,
    grads_out,
    *scratch,
):
    mixed_stage, spots_all, rows_all = scratch[:3]
    scratch = list(scratch[3:])

    def take(count):
        taken, scratch[:count] = scratch[:count], []
        return taken

    d, c, x, core, z, y = place()
    exchange = PlaneExchange(mixed_stage, mixed_out, take(3))
    qkv = WeightGather(qkv_ref, qkv_out, take(7))
    weights = WeightGather(blocks_ref, blocks_out, take(7))
    outs = SequenceGather(out_rows_ref, out_rows_out.at[pl.ds(d * PLANE, PLANE)], take(5), 1)
    outs_chip = ChipGather(out_rows_out, take(4), PLANE)
    rows = SequenceGather(rows_ref, rows_all, take(5), 2)
    table = SequenceGather(table_ref, table_out, take(5), 1)
    grads = SequenceGather(grads_ref, grads_out, take(5), CHUNKS)
    down = ChipGather(down_out, take(4), DOWN_PARTS)
    spot_send, spot_recv, spot_local, down_local = take(4)
    greet(plane_peers(d, c) + chip_peers(d, c, x, core))
    order = near_first(z)

    qkv.first()
    spots_own = pltpu.make_async_copy(spots_ref, spots_all.at[c], spot_local)
    spots_own.start()
    spots_sent = []
    for off in range(1, PLANE):
        to = lax.rem(c + off, PLANE)
        copy = remote(
            spots_ref, spots_all.at[c], spot_send.at[off], spot_recv.at[c], d, to
        )
        copy.start()
        spots_sent.append(copy)
    table.first()
    rows.first(by_block=True)
    down_own = pltpu.make_async_copy(
        down_ref, down_out.at[pl.ds(d * DOWN_PARTS, DOWN_PARTS)], down_local
    )
    down_own.start()
    for j in range(DOWN_PARTS):
        down.start(j, down_ref.at[j])
    outs.first()
    outs_chip.start(c, out_rows_ref)
    for off in range(1, PLANE):
        qkv.relay(off)
    table.relay(0)
    rows.relay_block(order[0])
    qkv.relay_chip()
    rows.relay_block(order[1])
    rows.relay_block(order[2])
    weights.first()
    for off in range(1, PLANE):
        source = lax.rem(c + off, PLANE)
        block = spots_all.at[source]
        remote(block, block, spot_send.at[off], spot_recv.at[source], d, source).wait_recv()
    spots_own.wait()
    table.last()
    for slot in range(PLANE):
        key_spot_out[:, slot * 128 : (slot + 1) * 128] = spots_all[slot]
        spot = jnp.broadcast_to(spots_all[slot][:1], (128, 128)).T[:, :1]
        start = jnp.zeros_like(spot)
        for doc in range(starts_ref.shape[1]):
            first = starts_ref[0, doc].astype(jnp.float32)
            start = jnp.maximum(start, jnp.where(spot >= first, first, 0.0))
        spot_out[slot] = spot
        start_out[slot] = start
    qkv.last()
    for pair in range(RANKS // 2):
        columns = qkv_out[2 * pair : 2 * pair + 2, :, QKV_WIDTH:]
        turned = columns.reshape(128, 128).astype(jnp.float32).T
        gains_out[:, pair * 128 : (pair + 1) * 128] = turned[:8]

    tokens, width = rows_ref.shape
    wide = 2 * HEAD_SIZE

    def project(pair):
        for slot in range(YS):

            @pl.loop(0, tokens, step=32)
            def _(r):
                at = pl.ds(pl.multiple_of(r, 32), 32)
                value = rows_all[pair * YS + slot, at].astype(jnp.float32)
                inverse = lax.rsqrt(
                    jnp.mean(value * value, axis=-1, keepdims=True) + eps_norm
                )
                input_out[pair * YS + slot, at] = (value * inverse * gains_out[:1]).astype(
                    jnp.bfloat16
                )

        both = pl.ds(pair * YS, YS)
        weight = qkv_out[:, :, :QKV_WIDTH].reshape(width, QKV_WIDTH)
        projected = jnp.dot(
            input_out[both].reshape(YS * tokens, width),
            weight,
            preferred_element_type=jnp.float32,
        )
        turns = table_out[both].reshape(YS * tokens, wide)
        for slot in range(YS):
            span = slice(slot * tokens, (slot + 1) * tokens)
            block = pair * YS + slot
            for heads in range(PAIRS):
                query = rotate(
                    projected[span, heads * wide : (heads + 1) * wide], turns[span]
                ).astype(jnp.bfloat16)
                query_out[block, heads, 0] = query[:, :HEAD_SIZE]
                query_out[block, heads, 1] = query[:, HEAD_SIZE:]
            key = rotate(projected[span, PAIRS * wide :], turns[span])
            key_out[block] = key[:, :HEAD_SIZE].astype(jnp.bfloat16)
            value_out[block] = projected[span, PAIRS * wide + HEAD_SIZE :].astype(
                jnp.bfloat16
            )

    rows.local.wait()
    rows.arrive_across(z)
    project(z)
    outs.relay(0)
    for source in order:
        outs_chip.start(source * YS + y)
    for pair in order:
        rows.arrive_across(pair)
        project(pair)
    rows.finish()
    for other in range(ZS):
        outs.arrive_across(other)
        outs_chip.start(other * YS + 1 - y)
    grads.first()

    for step in range(1, PLANE + 1):
        block = lax.rem(c + step, PLANE)

        @pl.loop(0, PAIRS)
        def _(pair):
            halves = []
            keys = key_out[...].reshape(PLANE * tokens, HEAD_SIZE)
            values = value_out[...].reshape(PLANE * tokens, HEAD_SIZE)
            for half in range(2):
                probs = probabilities(
                    query_out[block, pair, half],
                    keys,
                    spot_out[block],
                    start_out[block],
                    key_spot_out[:1],
                )
                halves.append(
                    jnp.dot(
                        probs.astype(jnp.bfloat16), values, preferred_element_type=jnp.float32
                    ).astype(jnp.bfloat16)
                )
            mixed_stage[block, pair] = jnp.concatenate(halves, axis=1)

        exchange.send(step)
        if step < PLANE:
            weights.relay(step)
    for k in range(CHUNKS):
        grads.relay(k)
    for j in range(DOWN_PARTS):
        down.relay(j)
    for off in range(PLANE):
        outs_chip.relay(lax.rem(c + off, PLANE))
    weights.relay_chip()
    for off in range(1, PLANE + 1):
        exchange.arrive(off)
    grads.last()
    down.last()
    outs_chip.last()
    weights.last()
    outs.finish()
    outs.local.wait()
    exchange.finish()
    for copy in spots_sent:
        copy.wait_send()
    down_own.wait()


def attention(starts, rows, table, spots, qkv, blocks, out_rows, down, grads):
    low, full = jnp.bfloat16, jnp.float32
    tokens, width = rows.shape
    mixed = jax.ShapeDtypeStruct((PLANE, PAIRS, tokens, 2 * HEAD_SIZE), low)
    seq_len = PLANE * tokens
    return pl.pallas_call(
        attention_kernel,
        out_shape=(
            jax.ShapeDtypeStruct((PLANE, tokens, width), low),
            jax.ShapeDtypeStruct((PLANE, *table.shape), full),
            jax.ShapeDtypeStruct((RANKS, *qkv.shape[1:]), low),
            jax.ShapeDtypeStruct((8, width), full),
            jax.ShapeDtypeStruct((PLANE, PAIRS, 2, tokens, HEAD_SIZE), low),
            jax.ShapeDtypeStruct((PLANE, tokens, HEAD_SIZE), low),
            jax.ShapeDtypeStruct((PLANE, tokens, HEAD_SIZE), low),
            jax.ShapeDtypeStruct((PLANE, tokens, 1), full),
            jax.ShapeDtypeStruct((PLANE, tokens, 1), full),
            jax.ShapeDtypeStruct((8, seq_len), full),
            mixed,
            jax.ShapeDtypeStruct((RANKS, *blocks.shape[1:]), low),
            jax.ShapeDtypeStruct((RANKS, *out_rows.shape), low),
            jax.ShapeDtypeStruct((4 * DOWN_PARTS, *down.shape[1:]), low),
            jax.ShapeDtypeStruct((PLANE, *grads.shape), low),
        ),
        in_specs=[pl.BlockSpec(memory_space=pltpu.SMEM)] + [ANY] * 8,
        out_specs=(VMEM,) * 11 + (ANY,) * 4,
        scratch_shapes=[
            pltpu.VMEM(mixed.shape, low),
            pltpu.VMEM((PLANE, *spots.shape), full),
            pltpu.VMEM((PLANE, tokens, width), low),
            *PlaneExchange.scratch(),
            *WeightGather.scratch(),
            *WeightGather.scratch(),
            *SequenceGather.scratch(1),
            *ChipGather.scratch(PLANE),
            *SequenceGather.scratch(2),
            *SequenceGather.scratch(1),
            *SequenceGather.scratch(CHUNKS),
            *ChipGather.scratch(DOWN_PARTS),
            pltpu.SemaphoreType.DMA((PLANE,)),
            pltpu.SemaphoreType.DMA((PLANE,)),
            pltpu.SemaphoreType.DMA(()),
            pltpu.SemaphoreType.DMA(()),
        ],
        compiler_params=params(2),
        name="attention",
    )(starts, rows, table, spots, qkv, blocks, out_rows, down, grads)


def feed_kernel(
    rows_ref,
    grads_ref,
    weight_ref,
    down_ref,
    rows_all,
    hidden_out,
    grad_out,
    normed_out,
    total_out,
    *scratch,
):
    normed_parts, down_parts = scratch[:2]
    gather = SequenceGather(rows_ref, rows_all, scratch[2:7], 2)
    normed = SequenceScatter(normed_parts, normed_out, *scratch[7:9], scratch[9:13], 1)
    total = SequenceScatter(down_parts, total_out, *scratch[13:15], scratch[15:19], 1)
    d, c, x, core, z, y = place()
    greet(
        [(d, lax.rem(z + off, ZS) * YS + y) for off in range(1, ZS)] + [(d, z * YS + 1 - y)]
    )
    tokens, width = rows_ref.shape
    part = hidden_out.shape[2]
    tile = 256

    def work(pair):
        both = pl.ds(pair * YS, YS)

        @pl.loop(0, part, step=tile)
        def _(n):
            at = pl.ds(pl.multiple_of(n, tile), tile)
            after = pl.ds(pl.multiple_of(n + part, tile), tile)
            rows = rows_all[both].reshape(YS * tokens, width)
            gate = jnp.dot(rows, weight_ref[:, at], preferred_element_type=jnp.float32)
            up = jnp.dot(rows, weight_ref[:, after], preferred_element_type=jnp.float32)
            grad = times_rows(grads_ref[both].reshape(YS * tokens, width), down_ref[at, :])
            sigmoid = jax.nn.sigmoid(gate)
            silu = gate * sigmoid
            gate_grad = grad * up * sigmoid * (1.0 + gate * (1.0 - sigmoid))

            def held(value):
                return value.astype(jnp.bfloat16).reshape(YS, tokens, tile)

            hidden_out[both, :, at] = held(silu * up)
            grad_out[both, :, at] = held(gate_grad)
            grad_out[both, :, after] = held(grad * silu)

        @pl.loop(0, width, step=2 * tile)
        def _(n):
            at = pl.ds(pl.multiple_of(n, 2 * tile), 2 * tile)
            grads = grad_out[both].reshape(YS * tokens, 2 * part)
            hidden = hidden_out[both].reshape(YS * tokens, part)
            normed_parts[both, :, at] = (
                times_rows(grads, weight_ref[at, :])
                .astype(jnp.bfloat16)
                .reshape(YS, tokens, 2 * tile)
            )
            down_parts[both, :, at] = (
                jnp.dot(hidden, down_ref[:, at], preferred_element_type=jnp.float32)
                .astype(jnp.bfloat16)
                .reshape(YS, tokens, 2 * tile)
            )

    order = near_first(z)
    gather.first(by_block=True)
    gather.local.wait()
    gather.arrive_across(z)
    work(z)
    gather.relay_block(order[0])
    gather.relay_block(order[1])
    for step, pair in enumerate(order):
        gather.arrive_across(pair)
        work(pair)
        normed.start(pair, 0)
        if step == 0:
            gather.relay_block(order[2])
        else:
            normed.relay_one(order[step - 1], 0)
            total.start(order[step - 1], 0)
    normed.relay_one(order[2], 0)
    normed.start(z, 0)
    total.start(order[2], 0)
    total.start(z, 0)
    for pair in order:
        total.relay_one(pair, 0)
    normed.last(0)
    total.last(0)
    gather.finish()
    normed.finish()
    total.finish()


def feed(rows, grads, weight, down):
    part = down.shape[0]
    summed = jax.ShapeDtypeStruct(rows.shape, jnp.float32)
    return pl.pallas_call(
        feed_kernel,
        out_shape=(
            jax.ShapeDtypeStruct((PLANE, *rows.shape), rows.dtype),
            jax.ShapeDtypeStruct((PLANE, rows.shape[0], part), rows.dtype),
            jax.ShapeDtypeStruct((PLANE, rows.shape[0], 2 * part), rows.dtype),
            summed,
            summed,
        ),
        in_specs=[ANY] + [VMEM] * 3,
        out_specs=(VMEM,) * 5,
        scratch_shapes=[
            pltpu.VMEM((PLANE, *rows.shape), rows.dtype),
            pltpu.VMEM((PLANE, *rows.shape), rows.dtype),
            *SequenceGather.scratch(2),
            *SequenceScatter.scratch(*rows.shape, 1),
            *SequenceScatter.scratch(*rows.shape, 1),
        ],
        compiler_params=params(5),
        name="feed",
    )(rows, grads, weight, down)


def attention_back_kernel(
    query_ref,
    key_ref,
    value_ref,
    spot_ref,
    start_ref,
    key_spot_ref,
    mixed_ref,
    parts_ref,
    down_ref,
    query_out,
    key_out,
    value_out,
    out_ref,
    down_out,
    *scratch,
):
    mixed_all = scratch[0]
    exchange = PlaneExchange(mixed_ref, mixed_all, scratch[1:4])
    weights = WeightScatter(parts_ref, out_ref, scratch[4:8], scratch[8:14])
    down = ChipScatter(down_ref, *scratch[14:17], scratch[17:], DOWN_PARTS)
    d, c, x, core, z, y = place()
    greet(plane_peers(d, c) + chip_peers(d, c, x, core))
    for off in range(1, PLANE + 1):
        exchange.send(off)
    weights.first()
    for j in range(DOWN_PARTS):
        down.start(j)
    key_out[...] = jnp.zeros_like(key_out)
    value_out[...] = jnp.zeros_like(value_out)
    for step in range(PLANE):
        block = lax.rem(c + PLANE - step, PLANE)
        exchange.arrive(step)

        @pl.loop(0, PAIRS)
        def _(pair):
            keys = key_ref[...].reshape(key_out.shape)
            values = value_ref[...].reshape(value_out.shape)
            for half in range(2):
                query = query_ref[block, pair, half]
                grad = mixed_all[block, pair][:, half * HEAD_SIZE : (half + 1) * HEAD_SIZE]
                probs = probabilities(
                    query, keys, spot_ref[block], start_ref[block], key_spot_ref[:1]
                )
                grad_probs = times_rows(grad, values)
                delta = jnp.sum(probs * grad_probs, axis=-1, keepdims=True)
                grad_scores = (probs * (grad_probs - delta) * SCORE_SCALE).astype(jnp.bfloat16)
                query_out[block, pair, half] = jnp.dot(
                    grad_scores, keys, preferred_element_type=jnp.float32
                )
                key_out[...] += transposed_times(grad_scores, query)
                value_out[...] += transposed_times(probs.astype(jnp.bfloat16), grad)

        weights.relay(step + 1)
        if step >= 2:
            weights.send(step - 1)
    for off in (PLANE - 1, PLANE):
        weights.send(off)
    for j in range(DOWN_PARTS):
        down.relay(j)
    for j in range(DOWN_PARTS):
        down.total(j, down_out.at[j])
    weights.last()
    down.finish()
    exchange.finish()


def attention_back(query, keys, values, spots, starts, key_spots, mixed, parts, down):
    return pl.pallas_call(
        attention_back_kernel,
        out_shape=(
            jax.ShapeDtypeStruct(query.shape, jnp.float32),
            jax.ShapeDtypeStruct((PLANE * keys.shape[1], HEAD_SIZE), jnp.float32),
            jax.ShapeDtypeStruct((PLANE * values.shape[1], HEAD_SIZE), jnp.float32),
            jax.ShapeDtypeStruct((PLANE, *parts.shape[1:]), parts.dtype),
            jax.ShapeDtypeStruct((DOWN_PARTS, *down.shape[1:]), jnp.float32),
        ),
        in_specs=[VMEM] * 9,
        out_specs=(VMEM,) * 5,
        scratch_shapes=[
            pltpu.VMEM(mixed.shape, jnp.bfloat16),
            *PlaneExchange.scratch(),
            *WeightScatter.scratch(*parts.shape[1:]),
            *ChipScatter.scratch(DOWN_PARTS, *down.shape[1:]),
        ],
        compiler_params=params(3),
        name="attention_back",
    )(query, keys, values, spots, starts, key_spots, mixed, parts, down)


def closing_kernel(rows_ref, parts_ref, outs_ref, rows_out, out_ref, outs_out, *scratch):
    scatter = SequenceScatter(rows_ref, rows_out, *scratch[:2], scratch[2:6], CHUNKS)
    weights = WeightScatter(parts_ref, out_ref, scratch[6:10], scratch[10:16])
    outs_sum = scratch[16]
    chip = ChipScatter(outs_ref, *scratch[17:20], scratch[20:24], PLANE)
    outs = SequenceScatter(outs_sum, outs_out, *scratch[24:26], scratch[26:], 1)
    d, c, x, core, z, y = place()
    greet(plane_peers(d, c) + chip_peers(d, c, x, core))
    places = (*near_first(z)[::-1], z)
    slots = [place * YS + 1 - y for place in places] + [place * YS + y for place in places]
    for j in slots:
        chip.start(j)
    weights.first()
    scatter.first()
    for j in slots:
        chip.relay(j)
    for off in range(1, PLANE + 1):
        weights.relay(off)
    for k in range(CHUNKS):
        scatter.relay(k)
    for off in range(1, PLANE + 1):
        weights.send(off)
    for i, j in enumerate(slots):
        chip.total(j, outs_sum.at[j])
        if i < ZS:
            outs.start(places[i], 0)
    outs.relay(0)
    for k in range(CHUNKS):
        scatter.last(k)
    weights.last()
    outs.last(0)
    scatter.finish()
    chip.finish()
    outs.finish()


def closing(rows, parts, outs):
    return pl.pallas_call(
        closing_kernel,
        out_shape=(
            jax.ShapeDtypeStruct(rows.shape[1:], jnp.float32),
            jax.ShapeDtypeStruct((PLANE, *parts.shape[1:]), parts.dtype),
            jax.ShapeDtypeStruct(outs.shape[1:], jnp.float32),
        ),
        in_specs=[VMEM] * 3,
        out_specs=(VMEM,) * 3,
        scratch_shapes=[
            *SequenceScatter.scratch(*rows.shape[1:], CHUNKS),
            *WeightScatter.scratch(*parts.shape[1:]),
            pltpu.VMEM((PLANE, *outs.shape[1:]), jnp.bfloat16),
            *ChipScatter.scratch(PLANE, *outs.shape[1:]),
            *SequenceScatter.scratch(*outs.shape[1:], 1),
        ],
        compiler_params=params(4),
        name="closing",
    )(rows, parts, outs)


def body(
    layer_in,
    positions,
    doc_starts,
    out_grad,
    norm_gains,
    norm_gains_m,
    norm_gains_v,
    w_query,
    w_query_m,
    w_query_v,
    key_value_weight,
    key_value_first_moment,
    key_value_second_moment,
    w_out,
    w_out_m,
    w_out_v,
    w_gate_up,
    w_gate_up_m,
    w_gate_up_v,
    w_down,
    w_down_m,
    w_down_v,
):
    number_of_tokens = layer_in.shape[0]
    ctx_count = lax.axis_size("ctx")
    seq_len = number_of_tokens * ctx_count
    key_value_width = KEY_VALUE_HEADS * HEAD_SIZE
    query_group_size = QUERY_HEADS // KEY_VALUE_HEADS
    score_scale = 1.0 / math.sqrt(HEAD_SIZE)
    needed = -(-512 // number_of_tokens)
    shard_span = min(ctx_count, 1 << max(0, (needed - 1).bit_length()))
    width_of_block = shard_span * number_of_tokens
    count_of_blocks = ctx_count // shard_span
    key_places = lax.all_gather(positions, "ctx", axis=0, tiled=True)
    starts = doc_starts[0]
    own_docs = doc_lookup(positions, starts)
    key_docs = doc_lookup(key_places, starts)
    query_full, keyval_full, out_full, gains_full = (
        lax.all_gather(w_query.astype(jnp.bfloat16), ("dp", "ctx"), axis=0, tiled=True),
        lax.all_gather(key_value_weight.astype(jnp.bfloat16), ("dp", "ctx"), axis=0, tiled=True),
        lax.all_gather(w_out.astype(jnp.bfloat16), ("dp", "ctx"), axis=0, tiled=True),
        lax.all_gather(norm_gains.astype(jnp.bfloat16), ("dp", "ctx"), axis=1, tiled=True),
    )
    gain_one = gains_full[0].astype(jnp.float32)
    gain_two = gains_full[1].astype(jnp.float32)
    layer_rows = layer_in.astype(jnp.float32)
    normed_one, inverse_one = norm_forward(layer_rows)
    input_one = (normed_one * gain_one).astype(jnp.bfloat16)
    query_pre = jnp.dot(input_one, query_full, preferred_element_type=jnp.float32)
    key_value_projected = jnp.dot(input_one, keyval_full, preferred_element_type=jnp.float32)
    cosine_table, sine_table = rope_tables(positions, HEAD_SIZE)
    query_rows = (
        apply_rotation(
            query_pre.reshape(number_of_tokens, QUERY_HEADS, HEAD_SIZE), cosine_table, sine_table
        )
        .astype(jnp.bfloat16)
        .reshape(number_of_tokens, KEY_VALUE_HEADS, query_group_size, HEAD_SIZE)
    )
    keys_own = (
        apply_rotation(
            key_value_projected[:, :key_value_width].reshape(
                number_of_tokens, KEY_VALUE_HEADS, HEAD_SIZE
            ),
            cosine_table,
            sine_table,
        )
        .astype(jnp.bfloat16)
        .reshape(number_of_tokens, key_value_width)
    )
    values_own = key_value_projected[:, key_value_width:].astype(jnp.bfloat16)
    every_key, every_value = (
        lax.all_gather(keys_own, "ctx", axis=0, tiled=True),
        lax.all_gather(values_own, "ctx", axis=0, tiled=True),
    )
    blocked_keys = every_key.reshape(count_of_blocks, width_of_block, KEY_VALUE_HEADS, HEAD_SIZE)
    blocked_values = every_value.reshape(
        count_of_blocks, width_of_block, KEY_VALUE_HEADS, HEAD_SIZE
    )
    place_blocks = key_places.reshape(count_of_blocks, width_of_block)
    doc_blocks = key_docs.reshape(count_of_blocks, width_of_block)

    def visible(place_blk, doc_blk):
        allowed = (place_blk[None, :] <= positions[:, None]) & (
            doc_blk[None, :] == own_docs[:, None]
        )
        return allowed[:, None, None, :]

    def scores_of(key_blk):
        return (
            jnp.einsum("tkgd,nkd->tkgn", query_rows, key_blk, preferred_element_type=jnp.float32)
            * score_scale
        )

    def stats_step(carry, block):
        row_top, row_total = carry
        key_blk, place_blk, doc_blk = block
        allowed = visible(place_blk, doc_blk)
        masked = jnp.where(allowed, scores_of(key_blk), masked_score)
        new_top = jnp.maximum(row_top, jnp.max(masked, axis=-1, keepdims=True))
        row_total = row_total * jnp.exp(row_top - new_top) + jnp.sum(
            jnp.where(allowed, jnp.exp(masked - new_top), 0.0), axis=-1, keepdims=True
        )
        return ((new_top, row_total), None)

    statistic_shape = (number_of_tokens, KEY_VALUE_HEADS, query_group_size, 1)
    (row_top, row_total), unused = lax.scan(
        stats_step,
        (
            jnp.full(statistic_shape, masked_score, jnp.float32),
            jnp.zeros(statistic_shape, jnp.float32),
        ),
        (blocked_keys, place_blocks, doc_blocks),
    )
    log_total = row_top + jnp.log(row_total)

    def probs_of(key_blk, place_blk, doc_blk):
        allowed = visible(place_blk, doc_blk)
        masked = jnp.where(allowed, scores_of(key_blk), masked_score)
        return jnp.where(allowed, jnp.exp(masked - log_total), 0.0)

    def output_step(carry, block):
        key_blk, value_blk, place_blk, doc_blk = block
        probs_low = probs_of(key_blk, place_blk, doc_blk).astype(jnp.bfloat16)
        added = jnp.einsum(
            "tkgn,nkd->tkgd", probs_low, value_blk, preferred_element_type=jnp.float32
        )
        return (carry + added, None)

    attention_output, unused = lax.scan(
        output_step,
        jnp.zeros((number_of_tokens, KEY_VALUE_HEADS, query_group_size, HEAD_SIZE), jnp.float32),
        (blocked_keys, blocked_values, place_blocks, doc_blocks),
    )
    mixed = attention_output.reshape(number_of_tokens, QUERY_HEADS * HEAD_SIZE).astype(jnp.bfloat16)
    middle = layer_rows + jnp.dot(mixed, out_full, preferred_element_type=jnp.float32)
    normed_two, inverse_two = norm_forward(middle)
    input_two = (normed_two * gain_two).astype(jnp.bfloat16)
    gate_up_low = w_gate_up.astype(jnp.bfloat16)
    down_low = w_down.astype(jnp.bfloat16)
    columns = input_two
    gate_up = jnp.dot(
        columns,
        lax.all_gather(gate_up_low, ("dp", "ctx"), axis=0, tiled=True),
        preferred_element_type=jnp.float32,
    )
    gate_part = gate_up[:, :FF]
    up_part = gate_up[:, FF:]
    sigmoid_gate = jax.nn.sigmoid(gate_part)
    silu_gate = gate_part * sigmoid_gate
    hidden = (silu_gate * up_part).astype(jnp.bfloat16)
    columns = hidden
    down_sum = jnp.dot(
        columns,
        lax.all_gather(down_low, ("dp", "ctx"), axis=0, tiled=True),
        preferred_element_type=jnp.float32,
    )
    layer_out = (middle + down_sum).astype(jnp.bfloat16)
    grad_rows = out_grad.astype(jnp.float32)
    grad_hidden = times_transposed(
        out_grad, lax.all_gather(down_low, ("dp", "ctx"), axis=0, tiled=True)
    )
    grad_gate = grad_hidden * up_part * sigmoid_gate * (1.0 + gate_part * (1.0 - sigmoid_gate))
    grad_up = grad_hidden * silu_gate
    grad_gate_up = jnp.concatenate([grad_gate, grad_up], axis=1).astype(jnp.bfloat16)
    down_grad = lax.psum_scatter(
        transposed_times(hidden, out_grad), ("dp", "ctx"), scatter_dimension=0, tiled=True
    )
    grad_normed_two = times_transposed(
        grad_gate_up, lax.all_gather(gate_up_low, ("dp", "ctx"), axis=0, tiled=True)
    )
    gate_up_grad = lax.psum_scatter(
        transposed_times(input_two, grad_gate_up), ("dp", "ctx"), scatter_dimension=0, tiled=True
    )
    grad_norm_two, gain_two_grad = norm_backward(grad_normed_two, normed_two, inverse_two, gain_two)
    grad_middle = grad_rows + grad_norm_two
    grad_middle_low = grad_middle.astype(jnp.bfloat16)
    out_term = transposed_times(mixed, grad_middle_low)
    grad_mixed = (
        times_transposed(grad_middle_low, out_full)
        .astype(jnp.bfloat16)
        .reshape(number_of_tokens, KEY_VALUE_HEADS, query_group_size, HEAD_SIZE)
    )
    delta = jnp.sum(grad_mixed.astype(jnp.float32) * attention_output, axis=-1, keepdims=True)

    def back_step(grad_query, block):
        key_blk, value_blk, place_blk, doc_blk = block
        probs = probs_of(key_blk, place_blk, doc_blk)
        probs_low = probs.astype(jnp.bfloat16)
        grad_probs = jnp.einsum(
            "tkgd,nkd->tkgn", grad_mixed, value_blk, preferred_element_type=jnp.float32
        )
        grad_scores = (probs * (grad_probs - delta) * score_scale).astype(jnp.bfloat16)
        grad_query = grad_query + jnp.einsum(
            "tkgn,nkd->tkgd", grad_scores, key_blk, preferred_element_type=jnp.float32
        )
        key_grad = jnp.einsum(
            "tkgn,tkgd->nkd", grad_scores, query_rows, preferred_element_type=jnp.float32
        )
        value_grad = jnp.einsum(
            "tkgn,tkgd->nkd", probs_low, grad_mixed, preferred_element_type=jnp.float32
        )
        return (grad_query, (key_grad, value_grad))

    grad_query, (key_grads, value_grads) = lax.scan(
        back_step,
        jnp.zeros((number_of_tokens, KEY_VALUE_HEADS, query_group_size, HEAD_SIZE), jnp.float32),
        (blocked_keys, blocked_values, place_blocks, doc_blocks),
    )
    summed_key_gradient, value_sum = (
        lax.psum_scatter(
            key_grads.reshape(seq_len, key_value_width).astype(jnp.bfloat16),
            "ctx",
            scatter_dimension=0,
            tiled=True,
        ).astype(jnp.float32),
        lax.psum_scatter(
            value_grads.reshape(seq_len, key_value_width).astype(jnp.bfloat16),
            "ctx",
            scatter_dimension=0,
            tiled=True,
        ).astype(jnp.float32),
    )
    key_gradient_unrotated = reverse_rotation(
        summed_key_gradient.reshape(number_of_tokens, KEY_VALUE_HEADS, HEAD_SIZE),
        cosine_table,
        sine_table,
    ).reshape(number_of_tokens, key_value_width)
    grad_keyval = jnp.concatenate([key_gradient_unrotated, value_sum], axis=1).astype(jnp.bfloat16)
    grad_query_low = (
        reverse_rotation(
            grad_query.reshape(number_of_tokens, QUERY_HEADS, HEAD_SIZE), cosine_table, sine_table
        )
        .reshape(number_of_tokens, QUERY_HEADS * HEAD_SIZE)
        .astype(jnp.bfloat16)
    )
    grad_normed_one = times_transposed(grad_query_low, query_full) + times_transposed(
        grad_keyval, keyval_full
    )
    query_term = transposed_times(input_one, grad_query_low)
    keyval_term = transposed_times(input_one, grad_keyval)
    grad_norm_one, gain_one_grad = norm_backward(grad_normed_one, normed_one, inverse_one, gain_one)
    in_grad = grad_middle + grad_norm_one
    gain_term = jnp.stack([gain_one_grad, gain_two_grad])
    query_grad, keyval_grad, out_weight_grad, gains_grad = (
        lax.psum_scatter(query_term, ("dp", "ctx"), scatter_dimension=0, tiled=True),
        lax.psum_scatter(keyval_term, ("dp", "ctx"), scatter_dimension=0, tiled=True),
        lax.psum_scatter(out_term, ("dp", "ctx"), scatter_dimension=0, tiled=True),
        lax.psum_scatter(gain_term, ("dp", "ctx"), scatter_dimension=1, tiled=True),
    )
    rates = rates_for(seq_len)
    gains_m_new, gains_v_new, gains_new = adamw(
        norm_gains, gains_grad, norm_gains_m, norm_gains_v, rates[0], 0.0
    )
    query_m_new, query_v_new, query_new = adamw(
        w_query, query_grad, w_query_m, w_query_v, rates[1], weight_decay
    )
    keyval_m_new, keyval_v_new, keyval_new = adamw(
        key_value_weight,
        keyval_grad,
        key_value_first_moment,
        key_value_second_moment,
        rates[2],
        weight_decay,
    )
    out_m_new, out_v_new, out_new = adamw(
        w_out, out_weight_grad, w_out_m, w_out_v, rates[3], weight_decay
    )
    gate_up_m_new, gate_up_v_new, gate_up_new = adamw(
        w_gate_up, gate_up_grad, w_gate_up_m, w_gate_up_v, rates[4], weight_decay
    )
    down_m_new, down_v_new, down_new = adamw(
        w_down, down_grad, w_down_m, w_down_v, rates[5], weight_decay
    )
    return (
        layer_out,
        in_grad,
        gains_grad,
        gains_m_new,
        gains_v_new,
        gains_new,
        query_grad,
        query_m_new,
        query_v_new,
        query_new,
        keyval_grad,
        keyval_m_new,
        keyval_v_new,
        keyval_new,
        out_weight_grad,
        out_m_new,
        out_v_new,
        out_new,
        gate_up_grad,
        gate_up_m_new,
        gate_up_v_new,
        gate_up_new,
        down_grad,
        down_m_new,
        down_v_new,
        down_new,
    )


def tensor_parallel(
    layer_in,
    positions,
    doc_starts,
    out_grad,
    norm_gains,
    norm_gains_m,
    norm_gains_v,
    w_query,
    w_query_m,
    w_query_v,
    key_value_weight,
    key_value_first_moment,
    key_value_second_moment,
    w_out,
    w_out_m,
    w_out_v,
    w_gate_up,
    w_gate_up_m,
    w_gate_up_v,
    w_down,
    w_down_m,
    w_down_v,
):
    low = jnp.bfloat16
    own_tokens, width = layer_in.shape
    seq_len = own_tokens * PLANE
    group = GROUP
    group_width = group * HEAD_SIZE
    ff_part = FF // PLANE
    ff_own = FF // RANKS
    rows = w_query.shape[0]

    gains_low = norm_gains.astype(low)
    small = jnp.broadcast_to(
        jnp.pad(gains_low.T, ((0, 0), (0, 126)))[None], (PLANE, rows, 128)
    )
    attention_blocks = jnp.concatenate(
        [
            w_query.astype(low).reshape(rows, PLANE, group_width).transpose(1, 0, 2),
            key_value_weight.astype(low)
            .reshape(rows, 2, PLANE, HEAD_SIZE)
            .transpose(2, 0, 1, 3)
            .reshape(PLANE, rows, 2 * HEAD_SIZE),
            small,
        ],
        axis=2,
    )
    feed_blocks = (
        w_gate_up.astype(low)
        .reshape(rows, 2, 4, PLANE, ff_own)
        .transpose(3, 0, 1, 2, 4)
        .reshape(PLANE, rows, 2 * ff_part)
    )
    spots = jnp.broadcast_to(positions[None, :].astype(jnp.float32), (8, own_tokens))
    cosine_own, sine_own = rope_tables(positions, HEAD_SIZE)
    cosine_own, sine_own = cosine_own[:, 0], sine_own[:, 0]
    table = jnp.concatenate([cosine_own, cosine_own, -sine_own, sine_own], axis=1)
    qkv_width = QKV_WIDTH
    (
        input_one_all,
        table_all,
        attention_all,
        gain_rows,
        query_rows,
        key_rows,
        value_rows,
        token_spots,
        token_starts,
        key_spots,
        mixed_parts,
        feed_all,
        out_all,
        down_all,
        grads_all,
    ) = attention(
        doc_starts,
        layer_in,
        table,
        spots,
        attention_blocks,
        feed_blocks,
        w_out.astype(low),
        w_down.astype(low).reshape(DOWN_PARTS, -1, width),
        out_grad,
    )
    gain_one, gain_two = gain_rows[0], gain_rows[1]
    input_one = input_one_all.reshape(seq_len, width)
    qkv_weight = attention_all.reshape(width, -1)[:, :qkv_width]
    cosine_table = table_all[:, :, : HEAD_SIZE // 2].reshape(seq_len, 1, -1)
    sine_table = table_all[:, :, 3 * HEAD_SIZE // 2 :].reshape(seq_len, 1, -1)
    mixed = mixed_parts.transpose(2, 0, 1, 3).reshape(own_tokens, width)
    out_weight = out_all.reshape(width, width)
    branch = jnp.dot(mixed, out_weight, preferred_element_type=jnp.float32)

    layer_rows = layer_in.astype(jnp.float32)
    middle = layer_rows + branch
    normed_two, inverse_two = norm_forward(middle)
    input_two_all, hidden_all, grad_gate_up_all, grad_normed_two, down_sum = feed(
        (normed_two * gain_two).astype(low),
        grads_all,
        feed_all.reshape(width, 2 * ff_part),
        down_all.reshape(ff_part, width),
    )
    input_two = input_two_all.reshape(seq_len, width)
    hidden = hidden_all.reshape(seq_len, ff_part)
    grad_gate_up = grad_gate_up_all.reshape(seq_len, 2 * ff_part)
    layer_out = (middle + down_sum).astype(low)

    out_grads = grads_all.reshape(seq_len, width)
    down_term = transposed_times(hidden, out_grads).astype(low)
    feed_term = transposed_times(input_two, grad_gate_up).astype(low)
    grad_norm_two, unused = norm_backward(grad_normed_two, normed_two, inverse_two, gain_two)
    grad_middle = out_grad.astype(jnp.float32) + grad_norm_two
    grad_middle_low = grad_middle.astype(low)
    out_term = transposed_times(mixed, grad_middle_low).astype(low)
    grad_mixed = (
        times_transposed(grad_middle_low, out_weight)
        .astype(low)
        .reshape(own_tokens, PLANE, PAIRS, 2 * HEAD_SIZE)
        .transpose(1, 2, 0, 3)
    )
    grad_query, grad_key, grad_value, feed_grad, down_grad = attention_back(
        query_rows,
        key_rows,
        value_rows,
        token_spots,
        token_starts,
        key_spots,
        grad_mixed,
        feed_term.reshape(RANKS, rows, 2 * ff_part),
        down_term.reshape(4 * DOWN_PARTS, -1, width),
    )
    gate_up_grad = (
        feed_grad.reshape(PLANE, rows, 2, 4, ff_own)
        .transpose(1, 2, 3, 0, 4)
        .reshape(rows, 2 * FF)
        .astype(jnp.float32)
    )
    down_grad = down_grad.reshape(w_down.shape)
    grad_query = grad_query.transpose(0, 3, 1, 2, 4).reshape(seq_len, group, HEAD_SIZE)
    grad_qkv = jnp.concatenate(
        [
            reverse_rotation(grad_query, cosine_table, sine_table).reshape(seq_len, group_width),
            reverse_rotation(grad_key[:, None], cosine_table, sine_table)[:, 0],
            grad_value,
        ],
        axis=1,
    ).astype(low)
    one_parts = times_transposed(grad_qkv, qkv_weight).astype(low)
    qkv_term = transposed_times(input_one, grad_qkv).astype(low)
    grad_normed_one, qkv_grad, out_weight_grad = closing(
        one_parts.reshape(PLANE, own_tokens, width),
        qkv_term.reshape(RANKS, rows, qkv_width),
        out_term.reshape(RANKS, rows, width),
    )
    normed_one, inverse_one = norm_forward(layer_rows)
    grad_norm_one, unused = norm_backward(grad_normed_one, normed_one, inverse_one, gain_one)
    in_grad = grad_middle + grad_norm_one
    qkv_grad = qkv_grad.astype(jnp.float32)
    query_grad = qkv_grad[:, :, :group_width].transpose(1, 0, 2).reshape(w_query.shape)
    keyval_grad = (
        qkv_grad[:, :, group_width:]
        .reshape(PLANE, rows, 2, HEAD_SIZE)
        .transpose(1, 2, 0, 3)
        .reshape(key_value_weight.shape)
    )
    def low_times(weight, grad):
        return jnp.sum(weight.astype(low).astype(jnp.float32) * grad, axis=1)

    gains_grad = jnp.stack(
        [
            low_times(w_query, query_grad) + low_times(key_value_weight, keyval_grad),
            low_times(w_gate_up, gate_up_grad),
        ]
    ) / gains_low.astype(jnp.float32)

    rates = rates_for(seq_len)
    return (
        layer_out,
        in_grad,
        gains_grad,
        *adamw(norm_gains, gains_grad, norm_gains_m, norm_gains_v, rates[0], 0.0),
        query_grad,
        *adamw(w_query, query_grad, w_query_m, w_query_v, rates[1], weight_decay),
        keyval_grad,
        *adamw(
            key_value_weight,
            keyval_grad,
            key_value_first_moment,
            key_value_second_moment,
            rates[2],
            weight_decay,
        ),
        out_weight_grad,
        *adamw(w_out, out_weight_grad, w_out_m, w_out_v, rates[3], weight_decay),
        gate_up_grad,
        *adamw(w_gate_up, gate_up_grad, w_gate_up_m, w_gate_up_v, rates[4], weight_decay),
        down_grad,
        *adamw(w_down, down_grad, w_down_m, w_down_v, rates[5], weight_decay),
    )


def solution(mesh):
    planned = tensor_parallel if dict(mesh.shape) == {"dp": 2 * XS, "ctx": ZS * YS} else body
    return jax.shard_map(
        planned,
        mesh=mesh,
        in_specs=(
            P(("dp", "ctx"), None),
            P(("dp", "ctx")),
            P("dp", None),
            P(("dp", "ctx"), None),
            P(None, ("dp", "ctx")),
            P(None, ("dp", "ctx")),
            P(None, ("dp", "ctx")),
            P(("dp", "ctx"), None),
            P(("dp", "ctx"), None),
            P(("dp", "ctx"), None),
            P(("dp", "ctx"), None),
            P(("dp", "ctx"), None),
            P(("dp", "ctx"), None),
            P(("dp", "ctx"), None),
            P(("dp", "ctx"), None),
            P(("dp", "ctx"), None),
            P(("dp", "ctx"), None),
            P(("dp", "ctx"), None),
            P(("dp", "ctx"), None),
            P(("dp", "ctx"), None),
            P(("dp", "ctx"), None),
            P(("dp", "ctx"), None),
        ),
        out_specs=(
            P(("dp", "ctx"), None),
            P(("dp", "ctx"), None),
            P(None, ("dp", "ctx")),
            P(None, ("dp", "ctx")),
            P(None, ("dp", "ctx")),
            P(None, ("dp", "ctx")),
            P(("dp", "ctx"), None),
            P(("dp", "ctx"), None),
            P(("dp", "ctx"), None),
            P(("dp", "ctx"), None),
            P(("dp", "ctx"), None),
            P(("dp", "ctx"), None),
            P(("dp", "ctx"), None),
            P(("dp", "ctx"), None),
            P(("dp", "ctx"), None),
            P(("dp", "ctx"), None),
            P(("dp", "ctx"), None),
            P(("dp", "ctx"), None),
            P(("dp", "ctx"), None),
            P(("dp", "ctx"), None),
            P(("dp", "ctx"), None),
            P(("dp", "ctx"), None),
            P(("dp", "ctx"), None),
            P(("dp", "ctx"), None),
            P(("dp", "ctx"), None),
            P(("dp", "ctx"), None),
        ),
        check_vma=False,
    )
```

```python
import functools
import math

import jax
import jax.numpy as jnp
from jax import lax
from jax.experimental import pallas as pl
from jax.experimental.pallas import tpu as pltpu
from jax.sharding import PartitionSpec as P

MODEL_WIDTH = 2048
QUERY_HEADS = 32
KEY_VALUE_HEADS = 8
HEAD_SIZE = 64
FF = 8192
STEP = 10


eps_norm = 1e-05
rope_base = 500000.0
beta_one = 0.9
beta_two = 0.95
eps_adam = 1e-08
weight_decay = 0.1
masked_score = -1e30


def rates_for(seq_len):
    return (
        0.6,
        0.8 / math.sqrt(MODEL_WIDTH // 4),
        0.8 / math.sqrt(MODEL_WIDTH),
        0.8 / math.sqrt(max(220 * MODEL_WIDTH // seq_len, 1)),
        0.8 / math.sqrt(MODEL_WIDTH),
        0.8 / math.sqrt(FF // 2),
    )


def adamw(weight, grad_sum, first, second, rate, decay):
    first_new = beta_one * first + (1.0 - beta_one) * grad_sum
    second_new = beta_two * second + (1.0 - beta_two) * grad_sum * grad_sum
    first_hat = first_new / (1.0 - beta_one**STEP)
    second_hat = second_new / (1.0 - beta_two**STEP)
    weight_new = weight - rate * (first_hat / (jnp.sqrt(second_hat) + eps_adam) + decay * weight)
    return (first_new, second_new, weight_new)


def norm_forward(layer_rows):
    inverse = lax.rsqrt(jnp.mean(layer_rows * layer_rows, axis=-1, keepdims=True) + eps_norm)
    return (layer_rows * inverse, inverse)


def norm_backward(grad_out, normed, inverse, gain_row):
    scaled = grad_out * gain_row
    grad_in = inverse * (scaled - normed * jnp.mean(scaled * normed, axis=-1, keepdims=True))
    return (grad_in, jnp.sum(grad_out * normed, axis=0))


def rope_tables(token_placement, head_dim):
    half_dim = head_dim // 2
    frequencies = jnp.exp(
        jnp.arange(half_dim, dtype=jnp.float32) * (-2.0 * math.log(rope_base) / head_dim)
    )
    angles = token_placement.astype(jnp.float32)[:, None] * frequencies[None, :]
    return (jnp.cos(angles)[:, None, :], jnp.sin(angles)[:, None, :])


def apply_rotation(value_rows, cosine_table, sine_table):
    half_dim = value_rows.shape[-1] // 2
    first_half = value_rows[..., :half_dim]
    second_half = value_rows[..., half_dim:]
    return jnp.concatenate(
        [
            first_half * cosine_table - second_half * sine_table,
            second_half * cosine_table + first_half * sine_table,
        ],
        axis=-1,
    )


def reverse_rotation(grad_rows, cosine_table, sine_table):
    half_dim = grad_rows.shape[-1] // 2
    first_half = grad_rows[..., :half_dim]
    second_half = grad_rows[..., half_dim:]
    return jnp.concatenate(
        [
            first_half * cosine_table + second_half * sine_table,
            second_half * cosine_table - first_half * sine_table,
        ],
        axis=-1,
    )


def doc_lookup(token_placement, starts):
    return jnp.sum((token_placement[:, None] >= starts[None, :]).astype(jnp.int32), axis=1) - 1


def times_transposed(left, right):
    return lax.dot_general(
        left, right, (((1,), (1,)), ((), ())), preferred_element_type=jnp.float32
    )


def transposed_times(left, right):
    return lax.dot_general(
        left, right, (((0,), (0,)), ((), ())), preferred_element_type=jnp.float32
    )


XS = 2
YS = 2
ZS = 4
PLANE = ZS * YS
RANKS = 2 * XS * PLANE
MESH = pl.DeviceIdType.MESH


def place():
    d = lax.axis_index("dp")
    c = lax.axis_index("ctx")
    return d, c, lax.div(d, 2), lax.rem(d, 2), lax.div(c, YS), lax.rem(c, YS)


def remote(src, dst, send_sem, recv_sem, d, c):
    return pltpu.make_async_remote_copy(
        src_ref=src,
        dst_ref=dst,
        send_sem=send_sem,
        recv_sem=recv_sem,
        device_id=(d, c),
        device_id_type=MESH,
    )


def greet(peers):
    barrier = pltpu.get_barrier_semaphore()
    for d, c in peers:
        pl.semaphore_signal(barrier, inc=1, device_id=(d, c), device_id_type=MESH)
    pl.semaphore_wait(barrier, len(peers))


def plane_peers(d, c):
    return [(d, lax.rem(c + k, PLANE)) for k in range(1, PLANE)]


def chip_peers(d, c, x, core):
    return [(x * 2 + 1 - core, c), ((1 - x) * 2 + core, c)]


def add_into(target, sources, rows, step=16):
    @pl.loop(0, rows, step=step)
    def _(r):
        at = pl.ds(pl.multiple_of(r, step), step)
        total = sources[0][at].astype(jnp.float32)
        for source in sources[1:]:
            total = total + source[at].astype(jnp.float32)
        target[at] = total.astype(target.dtype)


def near_first(z):
    half = lax.div(z, 2)
    return [half * 4 + 1 - z, 2 - half, 3 - 3 * half]


class SequenceGather:
    def __init__(self, own, out, sems, chunks):
        self.own, self.out, self.chunks = own, out, chunks
        self.zs, self.zr, self.ys, self.yr, self.local_sem = sems
        self.d, self.c, _, _, self.z, self.y = place()
        self.rows = own.shape[0] // chunks
        self.sent = []

    @staticmethod
    def scratch(chunks):
        return [
            pltpu.SemaphoreType.DMA((ZS, chunks)),
            pltpu.SemaphoreType.DMA((ZS, chunks)),
            pltpu.SemaphoreType.DMA((ZS, chunks)),
            pltpu.SemaphoreType.DMA((ZS, chunks)),
            pltpu.SemaphoreType.DMA(()),
        ]

    def part(self, ref, k):
        return ref.at[pl.ds(k * self.rows, self.rows)]

    def across(self, z, k, src):
        slot = z * YS + self.y
        return remote(
            src,
            self.part(self.out.at[slot], k),
            self.ys.at[z, k],
            self.yr.at[z, k],
            self.d,
            self.z * YS + 1 - self.y,
        )

    def along(self, to, k):
        return remote(
            self.part(self.own, k),
            self.part(self.out.at[self.c], k),
            self.zs.at[to, k],
            self.zr.at[self.z, k],
            self.d,
            to * YS + self.y,
        )

    def start(self, copy):
        copy.start()
        self.sent.append(copy)

    def first(self, by_block=False):
        self.local = pltpu.make_async_copy(self.own, self.out.at[self.c], self.local_sem)
        self.local.start()
        near = near_first(self.z)
        if by_block:
            for k in range(self.chunks):
                self.start(self.across(self.z, k, self.part(self.own, k)))
            for to in near:
                for k in range(self.chunks):
                    self.start(self.along(to, k))
            return
        for k in range(self.chunks):
            for to in near[::-1]:
                self.start(self.along(to, k))
            self.start(self.across(self.z, k, self.part(self.own, k)))

    def relay_one(self, source, k):
        slot = source * YS + self.y
        block = self.part(self.out.at[slot], k)
        remote(
            block, block, self.zs.at[source, k], self.zr.at[source, k], self.d, slot
        ).wait_recv()
        self.start(self.across(source, k, block))

    def relay(self, k):
        for source in near_first(self.z):
            self.relay_one(source, k)

    def relay_block(self, source):
        for k in range(self.chunks):
            self.relay_one(source, k)

    def arrive_across(self, z):
        for k in range(self.chunks):
            block = self.part(self.out.at[z * YS + 1 - self.y], k)
            remote(
                block,
                block,
                self.ys.at[z, k],
                self.yr.at[z, k],
                self.d,
                self.z * YS + 1 - self.y,
            ).wait_recv()

    def finish(self):
        for copy in self.sent:
            copy.wait_send()

    def last(self):
        for z in range(ZS):
            self.arrive_across(z)
        self.finish()
        self.local.wait()


class SequenceScatter:
    def __init__(self, parts, out, ybuf, zbuf, sems, chunks):
        self.parts, self.out, self.chunks = parts, out, chunks
        self.ybuf, self.zbuf = ybuf, zbuf
        self.ys, self.yr, self.zs, self.zr = sems
        self.d, self.c, _, _, self.z, self.y = place()
        self.rows = parts.shape[1] // chunks
        self.sent = []

    @staticmethod
    def scratch(rows, width, chunks):
        return [
            pltpu.VMEM((ZS, rows, width), jnp.bfloat16),
            pltpu.VMEM((ZS, rows, width), jnp.bfloat16),
            pltpu.SemaphoreType.DMA((ZS, chunks)),
            pltpu.SemaphoreType.DMA((ZS, chunks)),
            pltpu.SemaphoreType.DMA((ZS, chunks)),
            pltpu.SemaphoreType.DMA((ZS, chunks)),
        ]

    def span(self, k):
        return pl.ds(k * self.rows, self.rows)

    def across(self, z, k):
        return remote(
            self.parts.at[z * YS + 1 - self.y, self.span(k)],
            self.ybuf.at[z, self.span(k)],
            self.ys.at[z, k],
            self.yr.at[z, k],
            self.d,
            self.z * YS + 1 - self.y,
        )

    def along(self, to, k):
        return remote(
            self.ybuf.at[to, self.span(k)],
            self.zbuf.at[self.z, self.span(k)],
            self.zs.at[to, k],
            self.zr.at[self.z, k],
            self.d,
            to * YS + self.y,
        )

    def start(self, z, k):
        copy = self.across(z, k)
        copy.start()
        self.sent.append(copy)

    def first(self):
        for k in range(self.chunks):
            for z in (*near_first(self.z)[::-1], self.z):
                self.start(z, k)

    def relay_one(self, z, k):
        self.across(z, k).wait_recv()
        block = self.ybuf.at[z, self.span(k)]
        add_into(block, [self.parts.at[z * YS + self.y, self.span(k)], block], self.rows)
        copy = self.along(z, k)
        copy.start()
        self.sent.append(copy)

    def relay(self, k):
        for z in near_first(self.z)[::-1]:
            self.relay_one(z, k)

    def last(self, k):
        self.across(self.z, k).wait_recv()
        blocks = [self.parts.at[self.c, self.span(k)], self.ybuf.at[self.z, self.span(k)]]
        for source in near_first(self.z):
            block = self.zbuf.at[source, self.span(k)]
            remote(
                block,
                block,
                self.zs.at[source, k],
                self.zr.at[source, k],
                self.d,
                source * YS + self.y,
            ).wait_recv()
            blocks.append(block)
        add_into(self.out.at[self.span(k)], blocks, self.rows)

    def finish(self):
        for copy in self.sent:
            copy.wait_send()


class ChipGather:
    def __init__(self, out, sems, count):
        self.out, self.count = out, count
        self.cs, self.cr, self.xs, self.xr = sems
        self.d, self.c, self.x, self.core, _, _ = place()
        self.sent = []

    @staticmethod
    def scratch(count):
        return [
            pltpu.SemaphoreType.DMA((2, count)),
            pltpu.SemaphoreType.DMA((2, count)),
            pltpu.SemaphoreType.DMA((count,)),
            pltpu.SemaphoreType.DMA((count,)),
        ]

    def to_core(self, far, j, src=None):
        x = 1 - self.x if far else self.x
        block = self.out.at[(x * 2 + self.core) * self.count + j]
        return remote(
            block if src is None else src,
            block,
            self.cs.at[far, j],
            self.cr.at[far, j],
            self.x * 2 + 1 - self.core,
            self.c,
        )

    def to_x(self, j, src=None):
        block = self.out.at[self.d * self.count + j]
        return remote(
            block if src is None else src,
            block,
            self.xs.at[j],
            self.xr.at[j],
            (1 - self.x) * 2 + self.core,
            self.c,
        )

    def start(self, j, src=None):
        for copy in (self.to_x(j, src), self.to_core(0, j, src)):
            copy.start()
            self.sent.append(copy)

    def relay(self, j):
        self.to_x(j).wait_recv()
        copy = self.to_core(1, j)
        copy.start()
        self.sent.append(copy)

    def last(self):
        for far in (0, 1):
            for j in range(self.count):
                self.to_core(far, j).wait_recv()
        for copy in self.sent:
            copy.wait_send()


class WeightGather:
    def __init__(self, blocks, out, sems):
        self.blocks, self.out = blocks, out
        self.ps, self.pr, self.local_sem = sems[:3]
        self.chip = ChipGather(out, sems[3:], PLANE)
        self.d, self.c = self.chip.d, self.chip.c
        self.sent = []

    @staticmethod
    def scratch():
        return [
            pltpu.SemaphoreType.DMA((PLANE,)),
            pltpu.SemaphoreType.DMA((PLANE,)),
            pltpu.SemaphoreType.DMA(()),
        ] + ChipGather.scratch(PLANE)

    def first(self):
        self.local = pltpu.make_async_copy(
            self.blocks.at[self.c], self.out.at[self.d * PLANE + self.c], self.local_sem
        )
        self.local.start()
        for off in range(1, PLANE):
            to = lax.rem(self.c + off, PLANE)
            copy = remote(
                self.blocks.at[to],
                self.out.at[self.d * PLANE + self.c],
                self.ps.at[off],
                self.pr.at[self.c],
                self.d,
                to,
            )
            copy.start()
            self.sent.append(copy)
        self.chip.start(self.c, self.blocks.at[self.c])

    def relay(self, off):
        source = lax.rem(self.c + PLANE - off, PLANE)
        block = self.out.at[self.d * PLANE + source]
        remote(
            block, block, self.ps.at[off], self.pr.at[source], self.d, source
        ).wait_recv()
        self.chip.start(source)

    def relay_chip(self):
        for off in range(PLANE):
            self.chip.relay(lax.rem(self.c + off, PLANE))

    def last(self):
        self.chip.last()
        for copy in self.sent:
            copy.wait_send()
        self.local.wait()


class ChipScatter:
    def __init__(self, parts, cbuf, stage, xbuf, sems, count):
        self.parts, self.count = parts, count
        self.cbuf, self.stage, self.xbuf = cbuf, stage, xbuf
        self.cs, self.cr, self.xs, self.xr = sems
        self.d, self.c, self.x, self.core, _, _ = place()
        self.sent = []

    @staticmethod
    def scratch(count, rows, width):
        return [
            pltpu.VMEM((2, count, rows, width), jnp.bfloat16),
            pltpu.VMEM((count, rows, width), jnp.bfloat16),
            pltpu.VMEM((count, rows, width), jnp.bfloat16),
            pltpu.SemaphoreType.DMA((2, count)),
            pltpu.SemaphoreType.DMA((2, count)),
            pltpu.SemaphoreType.DMA((count,)),
            pltpu.SemaphoreType.DMA((count,)),
        ]

    def to_core(self, far, j):
        x = 1 - self.x if far else self.x
        return remote(
            self.parts.at[(x * 2 + 1 - self.core) * self.count + j],
            self.cbuf.at[far, j],
            self.cs.at[far, j],
            self.cr.at[far, j],
            self.x * 2 + 1 - self.core,
            self.c,
        )

    def to_x(self, j):
        return remote(
            self.stage.at[j],
            self.xbuf.at[j],
            self.xs.at[j],
            self.xr.at[j],
            (1 - self.x) * 2 + self.core,
            self.c,
        )

    def start(self, j):
        for far in (1, 0):
            copy = self.to_core(far, j)
            copy.start()
            self.sent.append(copy)

    def relay(self, j):
        self.to_core(1, j).wait_recv()
        own = self.parts.at[((1 - self.x) * 2 + self.core) * self.count + j]
        add_into(self.stage.at[j], [own, self.cbuf.at[1, j]], own.shape[0])
        copy = self.to_x(j)
        copy.start()
        self.sent.append(copy)

    def total(self, j, target):
        self.to_core(0, j).wait_recv()
        self.to_x(j).wait_recv()
        own = self.parts.at[self.d * self.count + j]
        add_into(target, [own, self.cbuf.at[0, j], self.xbuf.at[j]], own.shape[0])

    def finish(self):
        for copy in self.sent:
            copy.wait_send()


class WeightScatter:
    def __init__(self, parts, out, bufs, sems):
        self.stage = bufs[0]
        self.ps, self.pr = sems[:2]
        self.chip = ChipScatter(parts, *bufs[1:], sems[2:], PLANE)
        self.out = out
        self.d, self.c = self.chip.d, self.chip.c
        self.sent = []

    @staticmethod
    def scratch(rows, width):
        chip = ChipScatter.scratch(PLANE, rows, width)
        return [
            pltpu.VMEM((PLANE, rows, width), jnp.bfloat16),
            *chip[:3],
            pltpu.SemaphoreType.DMA((PLANE,)),
            pltpu.SemaphoreType.DMA((PLANE,)),
            *chip[3:],
        ]

    def first(self):
        for off in range(1, PLANE + 1):
            self.chip.start(lax.rem(self.c + off, PLANE))

    def relay(self, off):
        self.chip.relay(lax.rem(self.c + off, PLANE))

    def send(self, off):
        to = lax.rem(self.c + off, PLANE)
        if off == PLANE:
            self.chip.total(to, self.out.at[self.c])
            return
        self.chip.total(to, self.stage.at[to])
        copy = remote(
            self.stage.at[to],
            self.out.at[self.c],
            self.ps.at[off],
            self.pr.at[self.c],
            self.d,
            to,
        )
        copy.start()
        self.sent.append(copy)

    def last(self):
        for off in range(1, PLANE):
            source = lax.rem(self.c + off, PLANE)
            block = self.out.at[source]
            remote(
                block, block, self.ps.at[off], self.pr.at[source], self.d, source
            ).wait_recv()
        for copy in self.sent:
            copy.wait_send()
        self.chip.finish()


def params(collective_id, mebibytes=56):
    return pltpu.CompilerParams(
        collective_id=collective_id, has_side_effects=True, vmem_limit_bytes=mebibytes * 2**20
    )


ANY = pl.BlockSpec(memory_space=pl.ANY)
VMEM = pl.BlockSpec(memory_space=pltpu.VMEM)
CHUNKS = 4


DOWN_PARTS = 4
SCORE_SCALE = 1.0 / math.sqrt(HEAD_SIZE)
GROUP = QUERY_HEADS // KEY_VALUE_HEADS
PAIRS = GROUP // 2


def times_rows(left, right):
    return lax.dot_general(
        left, right, (((1,), (1,)), ((), ())), preferred_element_type=jnp.float32
    )


class PlaneExchange:
    def __init__(self, blocks, out, sems):
        self.blocks, self.out = blocks, out
        self.ps, self.pr, self.local_sem = sems
        self.d, self.c = lax.axis_index("dp"), lax.axis_index("ctx")
        self.sent = []

    @staticmethod
    def scratch():
        return [
            pltpu.SemaphoreType.DMA((PLANE,)),
            pltpu.SemaphoreType.DMA((PLANE,)),
            pltpu.SemaphoreType.DMA(()),
        ]

    def send(self, off):
        to = lax.rem(self.c + off, PLANE)
        if off % PLANE == 0:
            self.local = pltpu.make_async_copy(
                self.blocks.at[to], self.out.at[self.c], self.local_sem
            )
            self.local.start()
            return
        copy = remote(
            self.blocks.at[to],
            self.out.at[self.c],
            self.ps.at[off],
            self.pr.at[self.c],
            self.d,
            to,
        )
        copy.start()
        self.sent.append(copy)

    def arrive(self, off):
        if off % PLANE == 0:
            self.local.wait()
            return
        source = lax.rem(self.c + PLANE - off, PLANE)
        block = self.out.at[source]
        remote(
            block, block, self.ps.at[off], self.pr.at[source], self.d, source
        ).wait_recv()

    def finish(self):
        for copy in self.sent:
            copy.wait_send()


def probabilities(query, keys, spot, start, key_spots):
    scores = times_rows(query, keys) * SCORE_SCALE
    masked = jnp.where((key_spots <= spot) & (key_spots >= start), scores, masked_score)
    exponent = jnp.exp(masked - jnp.max(masked, axis=-1, keepdims=True))
    return exponent * (1.0 / jnp.sum(exponent, axis=-1, keepdims=True))


def rotate(value, table, back=False):
    lane = lax.broadcasted_iota(jnp.int32, value.shape, 1)
    turned = pltpu.roll(table, HEAD_SIZE, 1)
    cosine = jnp.where(lane < HEAD_SIZE, table, turned)
    sine = jnp.where(lane < HEAD_SIZE, turned, table)
    half = HEAD_SIZE // 2
    other = jnp.where(
        lax.rem(lane, HEAD_SIZE) < half,
        pltpu.roll(value, 2 * HEAD_SIZE - half, 1),
        pltpu.roll(value, half, 1),
    )
    if back:
        return value * cosine - other * sine
    return value * cosine + other * sine


QKV_WIDTH = (GROUP + 2) * HEAD_SIZE


def attention_kernel(
    starts_ref,
    rows_ref,
    table_ref,
    spots_ref,
    qkv_ref,
    blocks_ref,
    out_rows_ref,
    down_ref,
    input_out,
    table_out,
    qkv_out,
    gains_out,
    query_out,
    key_out,
    value_out,
    spot_out,
    start_out,
    key_spot_out,
    mixed_out,
    blocks_out,
    out_rows_out,
    down_out,
    *scratch,
):
    mixed_stage, spots_all, rows_all = scratch[:3]
    scratch = list(scratch[3:])

    def take(count):
        taken, scratch[:count] = scratch[:count], []
        return taken

    d, c, x, core, z, y = place()
    exchange = PlaneExchange(mixed_stage, mixed_out, take(3))
    qkv = WeightGather(qkv_ref, qkv_out, take(7))
    weights = WeightGather(blocks_ref, blocks_out, take(7))
    outs = SequenceGather(out_rows_ref, out_rows_out.at[pl.ds(d * PLANE, PLANE)], take(5), 1)
    outs_chip = ChipGather(out_rows_out, take(4), PLANE)
    rows = SequenceGather(rows_ref, rows_all, take(5), 2)
    table = SequenceGather(table_ref, table_out, take(5), 1)
    down = ChipGather(down_out, take(4), DOWN_PARTS)
    spot_send, spot_recv, spot_local, down_local = take(4)
    greet(plane_peers(d, c) + chip_peers(d, c, x, core))
    order = near_first(z)

    qkv.first()
    spots_own = pltpu.make_async_copy(spots_ref, spots_all.at[c], spot_local)
    spots_own.start()
    spots_sent = []
    for off in range(1, PLANE):
        to = lax.rem(c + off, PLANE)
        copy = remote(
            spots_ref, spots_all.at[c], spot_send.at[off], spot_recv.at[c], d, to
        )
        copy.start()
        spots_sent.append(copy)
    table.first()
    rows.first(by_block=True)
    down_own = pltpu.make_async_copy(
        down_ref, down_out.at[pl.ds(d * DOWN_PARTS, DOWN_PARTS)], down_local
    )
    down_own.start()
    for j in range(DOWN_PARTS):
        down.start(j, down_ref.at[j])
    outs.first()
    outs_chip.start(c, out_rows_ref)
    for off in range(1, PLANE):
        qkv.relay(off)
    table.relay(0)
    rows.relay_block(order[0])
    qkv.relay_chip()
    rows.relay_block(order[1])
    rows.relay_block(order[2])
    weights.first()
    for off in range(1, PLANE):
        source = lax.rem(c + off, PLANE)
        block = spots_all.at[source]
        remote(block, block, spot_send.at[off], spot_recv.at[source], d, source).wait_recv()
    spots_own.wait()
    table.last()
    for slot in range(PLANE):
        key_spot_out[:, slot * 128 : (slot + 1) * 128] = spots_all[slot]
        spot = jnp.broadcast_to(spots_all[slot][:1], (128, 128)).T[:, :1]
        start = jnp.zeros_like(spot)
        for doc in range(starts_ref.shape[1]):
            first = starts_ref[0, doc].astype(jnp.float32)
            start = jnp.maximum(start, jnp.where(spot >= first, first, 0.0))
        spot_out[slot] = spot
        start_out[slot] = start
    qkv.last()
    for pair in range(RANKS // 2):
        columns = qkv_out[2 * pair : 2 * pair + 2, :, QKV_WIDTH:]
        turned = columns.reshape(128, 128).astype(jnp.float32).T
        gains_out[:, pair * 128 : (pair + 1) * 128] = turned[:8]

    tokens, width = rows_ref.shape
    wide = 2 * HEAD_SIZE

    def project(pair):
        for slot in range(YS):

            @pl.loop(0, tokens, step=32)
            def _(r):
                at = pl.ds(pl.multiple_of(r, 32), 32)
                value = rows_all[pair * YS + slot, at].astype(jnp.float32)
                inverse = lax.rsqrt(
                    jnp.mean(value * value, axis=-1, keepdims=True) + eps_norm
                )
                input_out[pair * YS + slot, at] = (value * inverse * gains_out[:1]).astype(
                    jnp.bfloat16
                )

        both = pl.ds(pair * YS, YS)
        weight = qkv_out[:, :, :QKV_WIDTH].reshape(width, QKV_WIDTH)
        projected = jnp.dot(
            input_out[both].reshape(YS * tokens, width),
            weight,
            preferred_element_type=jnp.float32,
        )
        turns = table_out[both].reshape(YS * tokens, wide)
        for slot in range(YS):
            span = slice(slot * tokens, (slot + 1) * tokens)
            block = pair * YS + slot
            for heads in range(PAIRS):
                query = rotate(
                    projected[span, heads * wide : (heads + 1) * wide], turns[span]
                ).astype(jnp.bfloat16)
                query_out[block, heads, 0] = query[:, :HEAD_SIZE]
                query_out[block, heads, 1] = query[:, HEAD_SIZE:]
            key = rotate(projected[span, PAIRS * wide :], turns[span])
            key_out[block] = key[:, :HEAD_SIZE].astype(jnp.bfloat16)
            value_out[block] = projected[span, PAIRS * wide + HEAD_SIZE :].astype(
                jnp.bfloat16
            )

    rows.local.wait()
    rows.arrive_across(z)
    project(z)
    outs.relay(0)
    for source in order:
        outs_chip.start(source * YS + y)
    for pair in order:
        rows.arrive_across(pair)
        project(pair)
    rows.finish()
    for other in range(ZS):
        outs.arrive_across(other)
        outs_chip.start(other * YS + 1 - y)

    for step in range(1, PLANE + 1):
        block = lax.rem(c + step, PLANE)

        @pl.loop(0, PAIRS)
        def _(pair):
            halves = []
            keys = key_out[...].reshape(PLANE * tokens, HEAD_SIZE)
            values = value_out[...].reshape(PLANE * tokens, HEAD_SIZE)
            for half in range(2):
                probs = probabilities(
                    query_out[block, pair, half],
                    keys,
                    spot_out[block],
                    start_out[block],
                    key_spot_out[:1],
                )
                halves.append(
                    jnp.dot(
                        probs.astype(jnp.bfloat16), values, preferred_element_type=jnp.float32
                    ).astype(jnp.bfloat16)
                )
            mixed_stage[block, pair] = jnp.concatenate(halves, axis=1)

        exchange.send(step)
        if step < PLANE:
            weights.relay(step)
    for j in range(DOWN_PARTS):
        down.relay(j)
    for off in range(PLANE):
        outs_chip.relay(lax.rem(c + off, PLANE))
    weights.relay_chip()
    for off in range(1, PLANE + 1):
        exchange.arrive(off)
    down.last()
    outs_chip.last()
    weights.last()
    outs.finish()
    outs.local.wait()
    exchange.finish()
    for copy in spots_sent:
        copy.wait_send()
    down_own.wait()


def attention(starts, rows, table, spots, qkv, blocks, out_rows, down):
    low, full = jnp.bfloat16, jnp.float32
    tokens, width = rows.shape
    mixed = jax.ShapeDtypeStruct((PLANE, PAIRS, tokens, 2 * HEAD_SIZE), low)
    seq_len = PLANE * tokens
    return pl.pallas_call(
        attention_kernel,
        out_shape=(
            jax.ShapeDtypeStruct((PLANE, tokens, width), low),
            jax.ShapeDtypeStruct((PLANE, *table.shape), full),
            jax.ShapeDtypeStruct((RANKS, *qkv.shape[1:]), low),
            jax.ShapeDtypeStruct((8, width), full),
            jax.ShapeDtypeStruct((PLANE, PAIRS, 2, tokens, HEAD_SIZE), low),
            jax.ShapeDtypeStruct((PLANE, tokens, HEAD_SIZE), low),
            jax.ShapeDtypeStruct((PLANE, tokens, HEAD_SIZE), low),
            jax.ShapeDtypeStruct((PLANE, tokens, 1), full),
            jax.ShapeDtypeStruct((PLANE, tokens, 1), full),
            jax.ShapeDtypeStruct((8, seq_len), full),
            mixed,
            jax.ShapeDtypeStruct((RANKS, *blocks.shape[1:]), low),
            jax.ShapeDtypeStruct((RANKS, *out_rows.shape), low),
            jax.ShapeDtypeStruct((4 * DOWN_PARTS, *down.shape[1:]), low),
        ),
        in_specs=[pl.BlockSpec(memory_space=pltpu.SMEM)] + [ANY] * 7,
        out_specs=(VMEM,) * 11 + (ANY,) * 3,
        scratch_shapes=[
            pltpu.VMEM(mixed.shape, low),
            pltpu.VMEM((PLANE, *spots.shape), full),
            pltpu.VMEM((PLANE, tokens, width), low),
            *PlaneExchange.scratch(),
            *WeightGather.scratch(),
            *WeightGather.scratch(),
            *SequenceGather.scratch(1),
            *ChipGather.scratch(PLANE),
            *SequenceGather.scratch(2),
            *SequenceGather.scratch(1),
            *ChipGather.scratch(DOWN_PARTS),
            pltpu.SemaphoreType.DMA((PLANE,)),
            pltpu.SemaphoreType.DMA((PLANE,)),
            pltpu.SemaphoreType.DMA(()),
            pltpu.SemaphoreType.DMA(()),
        ],
        compiler_params=params(2),
        name="attention",
    )(starts, rows, table, spots, qkv, blocks, out_rows, down)


def feed_kernel(
    rows_ref,
    grads_ref,
    weight_ref,
    down_ref,
    normed_out,
    total_out,
    weight_grad_out,
    down_grad_out,
    *scratch,
):
    rows_all, grads_all, slope_gate, slope_up, hidden_all, gate_grads = scratch[:6]
    normed_parts, down_parts, turned, stage, stage_sem = scratch[6:11]
    scratch = list(scratch[11:])

    def take(count):
        taken, scratch[:count] = scratch[:count], []
        return taken

    rows = SequenceGather(rows_ref, rows_all, take(5), 2)
    grads = SequenceGather(grads_ref, grads_all, take(5), 2)
    normed = SequenceScatter(normed_parts, normed_out, *take(2), take(4), 1)
    total = SequenceScatter(down_parts, total_out, *take(2), take(4), 1)
    d, c, x, core, z, y = place()
    greet(
        [(d, lax.rem(z + off, ZS) * YS + y) for off in range(1, ZS)] + [(d, z * YS + 1 - y)]
    )
    tokens, width = rows_ref.shape
    part = down_ref.shape[0]
    tile = 256
    blocks = PLANE // 2
    half = lax.div(z, 2)
    near, mid, far = near_first(z)

    def slots(side):
        return pl.ds(side * blocks, blocks)

    def columns(n, start=0, size=tile):
        return pl.ds(pl.multiple_of(n + start, size), size)

    def flat(ref, side):
        value = ref[slots(side)]
        return value.reshape(blocks * tokens, value.shape[2])

    def held(value, dtype=jnp.bfloat16):
        return value.astype(dtype).reshape(blocks, tokens, value.shape[1])

    def forward(side):
        @pl.loop(0, part, step=tile)
        def _(n):
            at, after = columns(n), columns(n, part)
            value = flat(rows_all, side)
            gate = jnp.dot(value, weight_ref[:, at], preferred_element_type=jnp.float32)
            up = jnp.dot(value, weight_ref[:, after], preferred_element_type=jnp.float32)
            sigmoid = jax.nn.sigmoid(gate)
            silu = gate * sigmoid
            hidden_all[slots(side), :, at] = held(silu * up)
            slope_up[slots(side), :, at] = held(silu, jnp.float32)
            slope_gate[slots(side), :, at] = held(
                up * sigmoid * (1.0 + gate * (1.0 - sigmoid)), jnp.float32
            )

    def downward(side):
        @pl.loop(0, width, step=2 * tile)
        def _(n):
            at = columns(n, 0, 2 * tile)
            down_parts[slots(side), :, at] = held(
                jnp.dot(
                    flat(hidden_all, side), down_ref[:, at], preferred_element_type=jnp.float32
                )
            )

    def backward(side):
        @pl.loop(0, part, step=tile)
        def _(n):
            at, after = columns(n), columns(n, part)
            grad = held(times_rows(flat(grads_all, side), down_ref[at, :]), jnp.float32)
            gate_grads[slots(side), :, at] = (grad * slope_gate[slots(side), :, at]).astype(
                jnp.bfloat16
            )
            gate_grads[slots(side), :, after] = (grad * slope_up[slots(side), :, at]).astype(
                jnp.bfloat16
            )

    def inward(side):
        @pl.loop(0, width, step=2 * tile)
        def _(n):
            at = columns(n, 0, 2 * tile)
            normed_parts[slots(side), :, at] = held(
                times_rows(flat(gate_grads, side), weight_ref[at, :])
            )

    tiles = [(hidden_all, grads_all, down_grad_out, n) for n in range(part // tile)]
    tiles += [(rows_all, gate_grads, weight_grad_out, n) for n in range(width // tile)]
    copies = []

    def weight_grad(i):
        left, right, out, n = tiles[i]
        if i >= 2:
            copies[i - 2].wait()
        value = left[:, :, n * tile : (n + 1) * tile].reshape(PLANE * tokens, tile)
        turned[...] = value.T

        @pl.loop(0, width, step=2 * tile)
        def _(m):
            at = columns(m, 0, 2 * tile)
            stage[i % 2, :, at] = jnp.dot(
                turned[...],
                right[:, :, at].reshape(PLANE * tokens, 2 * tile),
                preferred_element_type=jnp.float32,
            ).astype(jnp.bfloat16)

        copy = pltpu.make_async_copy(
            stage.at[i % 2], out.at[pl.ds(n * tile, tile)], stage_sem.at[i % 2]
        )
        copy.start()
        copies.append(copy)

    rows.first(by_block=True)
    rows.local.wait()
    rows.relay_block(near)
    rows.arrive_across(z)
    rows.arrive_across(near)
    forward(half)
    rows.relay_block(mid)
    rows.relay_block(far)
    grads.first(by_block=True)
    downward(half)
    total.start(near, 0)
    total.start(z, 0)
    rows.arrive_across(mid)
    rows.arrive_across(far)
    forward(1 - half)
    grads.local.wait()
    grads.relay_block(near)
    downward(1 - half)
    total.start(mid, 0)
    total.start(far, 0)
    total.relay_one(near, 0)
    grads.arrive_across(z)
    grads.arrive_across(near)
    backward(half)
    total.relay_one(mid, 0)
    total.relay_one(far, 0)
    grads.relay_block(mid)
    grads.relay_block(far)
    inward(half)
    normed.start(near, 0)
    normed.start(z, 0)
    grads.arrive_across(mid)
    grads.arrive_across(far)
    backward(1 - half)
    inward(1 - half)
    normed.start(far, 0)
    normed.start(mid, 0)
    normed.relay_one(near, 0)
    for i in range(2):
        weight_grad(i)
    normed.relay_one(far, 0)
    weight_grad(2)
    normed.relay_one(mid, 0)
    for i in range(3, len(tiles)):
        weight_grad(i)
    total.last(0)
    normed.last(0)
    for copy in copies[-2:]:
        copy.wait()
    rows.finish()
    grads.finish()
    normed.finish()
    total.finish()


def feed(rows, grads, weight, down):
    part, width = down.shape
    low = rows.dtype
    tokens = rows.shape[0]
    summed = jax.ShapeDtypeStruct(rows.shape, jnp.float32)
    return pl.pallas_call(
        feed_kernel,
        out_shape=(
            summed,
            summed,
            jax.ShapeDtypeStruct(weight.shape, low),
            jax.ShapeDtypeStruct(down.shape, low),
        ),
        in_specs=[ANY] * 2 + [VMEM] * 2,
        out_specs=(VMEM,) * 2 + (ANY,) * 2,
        scratch_shapes=[
            pltpu.VMEM((PLANE, tokens, width), low),
            pltpu.VMEM((PLANE, tokens, width), low),
            pltpu.VMEM((PLANE, tokens, part), jnp.float32),
            pltpu.VMEM((PLANE, tokens, part), jnp.float32),
            pltpu.VMEM((PLANE, tokens, part), low),
            pltpu.VMEM((PLANE, tokens, 2 * part), low),
            pltpu.VMEM((PLANE, tokens, width), low),
            pltpu.VMEM((PLANE, tokens, width), low),
            pltpu.VMEM((256, PLANE * tokens), low),
            pltpu.VMEM((2, 256, width), low),
            pltpu.SemaphoreType.DMA((2,)),
            *SequenceGather.scratch(2),
            *SequenceGather.scratch(2),
            *SequenceScatter.scratch(tokens, width, 1),
            *SequenceScatter.scratch(tokens, width, 1),
        ],
        compiler_params=params(5, 60),
        name="feed",
    )(rows, grads, weight, down)


def attention_back_kernel(
    query_ref,
    key_ref,
    value_ref,
    spot_ref,
    start_ref,
    key_spot_ref,
    mixed_ref,
    parts_ref,
    down_ref,
    query_out,
    key_out,
    value_out,
    out_ref,
    down_out,
    *scratch,
):
    mixed_all = scratch[0]
    exchange = PlaneExchange(mixed_ref, mixed_all, scratch[1:4])
    weights = WeightScatter(parts_ref, out_ref, scratch[4:8], scratch[8:14])
    down = ChipScatter(down_ref, *scratch[14:17], scratch[17:], DOWN_PARTS)
    d, c, x, core, z, y = place()
    greet(plane_peers(d, c) + chip_peers(d, c, x, core))
    for off in range(1, PLANE + 1):
        exchange.send(off)
    weights.first()
    for j in range(DOWN_PARTS):
        down.start(j)
    key_out[...] = jnp.zeros_like(key_out)
    value_out[...] = jnp.zeros_like(value_out)
    for step in range(PLANE):
        block = lax.rem(c + PLANE - step, PLANE)
        exchange.arrive(step)

        @pl.loop(0, PAIRS)
        def _(pair):
            keys = key_ref[...].reshape(key_out.shape)
            values = value_ref[...].reshape(value_out.shape)
            for half in range(2):
                query = query_ref[block, pair, half]
                grad = mixed_all[block, pair][:, half * HEAD_SIZE : (half + 1) * HEAD_SIZE]
                probs = probabilities(
                    query, keys, spot_ref[block], start_ref[block], key_spot_ref[:1]
                )
                grad_probs = times_rows(grad, values)
                delta = jnp.sum(probs * grad_probs, axis=-1, keepdims=True)
                grad_scores = (probs * (grad_probs - delta) * SCORE_SCALE).astype(jnp.bfloat16)
                query_out[block, pair, half] = jnp.dot(
                    grad_scores, keys, preferred_element_type=jnp.float32
                )
                key_out[...] += transposed_times(grad_scores, query)
                value_out[...] += transposed_times(probs.astype(jnp.bfloat16), grad)

        weights.relay(step + 1)
        if step >= 2:
            weights.send(step - 1)
    for off in (PLANE - 1, PLANE):
        weights.send(off)
    for j in range(DOWN_PARTS):
        down.relay(j)
    for j in range(DOWN_PARTS):
        down.total(j, down_out.at[j])
    weights.last()
    down.finish()
    exchange.finish()


def attention_back(query, keys, values, spots, starts, key_spots, mixed, parts, down):
    return pl.pallas_call(
        attention_back_kernel,
        out_shape=(
            jax.ShapeDtypeStruct(query.shape, jnp.float32),
            jax.ShapeDtypeStruct((PLANE * keys.shape[1], HEAD_SIZE), jnp.float32),
            jax.ShapeDtypeStruct((PLANE * values.shape[1], HEAD_SIZE), jnp.float32),
            jax.ShapeDtypeStruct((PLANE, *parts.shape[1:]), parts.dtype),
            jax.ShapeDtypeStruct((DOWN_PARTS, *down.shape[1:]), jnp.float32),
        ),
        in_specs=[VMEM] * 9,
        out_specs=(VMEM,) * 5,
        scratch_shapes=[
            pltpu.VMEM(mixed.shape, jnp.bfloat16),
            *PlaneExchange.scratch(),
            *WeightScatter.scratch(*parts.shape[1:]),
            *ChipScatter.scratch(DOWN_PARTS, *down.shape[1:]),
        ],
        compiler_params=params(3),
        name="attention_back",
    )(query, keys, values, spots, starts, key_spots, mixed, parts, down)


def closing_kernel(rows_ref, parts_ref, outs_ref, rows_out, out_ref, outs_out, *scratch):
    scatter = SequenceScatter(rows_ref, rows_out, *scratch[:2], scratch[2:6], CHUNKS)
    weights = WeightScatter(parts_ref, out_ref, scratch[6:10], scratch[10:16])
    outs_sum = scratch[16]
    chip = ChipScatter(outs_ref, *scratch[17:20], scratch[20:24], PLANE)
    outs = SequenceScatter(outs_sum, outs_out, *scratch[24:26], scratch[26:], 1)
    d, c, x, core, z, y = place()
    greet(plane_peers(d, c) + chip_peers(d, c, x, core))
    places = (*near_first(z)[::-1], z)
    slots = [place * YS + 1 - y for place in places] + [place * YS + y for place in places]
    for j in slots:
        chip.start(j)
    weights.first()
    scatter.first()
    for j in slots:
        chip.relay(j)
    for off in range(1, PLANE + 1):
        weights.relay(off)
    for k in range(CHUNKS):
        scatter.relay(k)
    for off in range(1, PLANE + 1):
        weights.send(off)
    for i, j in enumerate(slots):
        chip.total(j, outs_sum.at[j])
        if i < ZS:
            outs.start(places[i], 0)
    outs.relay(0)
    for k in range(CHUNKS):
        scatter.last(k)
    weights.last()
    outs.last(0)
    scatter.finish()
    chip.finish()
    outs.finish()


def closing(rows, parts, outs):
    return pl.pallas_call(
        closing_kernel,
        out_shape=(
            jax.ShapeDtypeStruct(rows.shape[1:], jnp.float32),
            jax.ShapeDtypeStruct((PLANE, *parts.shape[1:]), parts.dtype),
            jax.ShapeDtypeStruct(outs.shape[1:], jnp.float32),
        ),
        in_specs=[VMEM] * 3,
        out_specs=(VMEM,) * 3,
        scratch_shapes=[
            *SequenceScatter.scratch(*rows.shape[1:], CHUNKS),
            *WeightScatter.scratch(*parts.shape[1:]),
            pltpu.VMEM((PLANE, *outs.shape[1:]), jnp.bfloat16),
            *ChipScatter.scratch(PLANE, *outs.shape[1:]),
            *SequenceScatter.scratch(*outs.shape[1:], 1),
        ],
        compiler_params=params(4),
        name="closing",
    )(rows, parts, outs)


def body(
    layer_in,
    positions,
    doc_starts,
    out_grad,
    norm_gains,
    norm_gains_m,
    norm_gains_v,
    w_query,
    w_query_m,
    w_query_v,
    key_value_weight,
    key_value_first_moment,
    key_value_second_moment,
    w_out,
    w_out_m,
    w_out_v,
    w_gate_up,
    w_gate_up_m,
    w_gate_up_v,
    w_down,
    w_down_m,
    w_down_v,
):
    number_of_tokens = layer_in.shape[0]
    ctx_count = lax.axis_size("ctx")
    seq_len = number_of_tokens * ctx_count
    key_value_width = KEY_VALUE_HEADS * HEAD_SIZE
    query_group_size = QUERY_HEADS // KEY_VALUE_HEADS
    score_scale = 1.0 / math.sqrt(HEAD_SIZE)
    needed = -(-512 // number_of_tokens)
    shard_span = min(ctx_count, 1 << max(0, (needed - 1).bit_length()))
    width_of_block = shard_span * number_of_tokens
    count_of_blocks = ctx_count // shard_span
    key_places = lax.all_gather(positions, "ctx", axis=0, tiled=True)
    starts = doc_starts[0]
    own_docs = doc_lookup(positions, starts)
    key_docs = doc_lookup(key_places, starts)
    query_full, keyval_full, out_full, gains_full = (
        lax.all_gather(w_query.astype(jnp.bfloat16), ("dp", "ctx"), axis=0, tiled=True),
        lax.all_gather(key_value_weight.astype(jnp.bfloat16), ("dp", "ctx"), axis=0, tiled=True),
        lax.all_gather(w_out.astype(jnp.bfloat16), ("dp", "ctx"), axis=0, tiled=True),
        lax.all_gather(norm_gains.astype(jnp.bfloat16), ("dp", "ctx"), axis=1, tiled=True),
    )
    gain_one = gains_full[0].astype(jnp.float32)
    gain_two = gains_full[1].astype(jnp.float32)
    layer_rows = layer_in.astype(jnp.float32)
    normed_one, inverse_one = norm_forward(layer_rows)
    input_one = (normed_one * gain_one).astype(jnp.bfloat16)
    query_pre = jnp.dot(input_one, query_full, preferred_element_type=jnp.float32)
    key_value_projected = jnp.dot(input_one, keyval_full, preferred_element_type=jnp.float32)
    cosine_table, sine_table = rope_tables(positions, HEAD_SIZE)
    query_rows = (
        apply_rotation(
            query_pre.reshape(number_of_tokens, QUERY_HEADS, HEAD_SIZE), cosine_table, sine_table
        )
        .astype(jnp.bfloat16)
        .reshape(number_of_tokens, KEY_VALUE_HEADS, query_group_size, HEAD_SIZE)
    )
    keys_own = (
        apply_rotation(
            key_value_projected[:, :key_value_width].reshape(
                number_of_tokens, KEY_VALUE_HEADS, HEAD_SIZE
            ),
            cosine_table,
            sine_table,
        )
        .astype(jnp.bfloat16)
        .reshape(number_of_tokens, key_value_width)
    )
    values_own = key_value_projected[:, key_value_width:].astype(jnp.bfloat16)
    every_key, every_value = (
        lax.all_gather(keys_own, "ctx", axis=0, tiled=True),
        lax.all_gather(values_own, "ctx", axis=0, tiled=True),
    )
    blocked_keys = every_key.reshape(count_of_blocks, width_of_block, KEY_VALUE_HEADS, HEAD_SIZE)
    blocked_values = every_value.reshape(
        count_of_blocks, width_of_block, KEY_VALUE_HEADS, HEAD_SIZE
    )
    place_blocks = key_places.reshape(count_of_blocks, width_of_block)
    doc_blocks = key_docs.reshape(count_of_blocks, width_of_block)

    def visible(place_blk, doc_blk):
        allowed = (place_blk[None, :] <= positions[:, None]) & (
            doc_blk[None, :] == own_docs[:, None]
        )
        return allowed[:, None, None, :]

    def scores_of(key_blk):
        return (
            jnp.einsum("tkgd,nkd->tkgn", query_rows, key_blk, preferred_element_type=jnp.float32)
            * score_scale
        )

    def stats_step(carry, block):
        row_top, row_total = carry
        key_blk, place_blk, doc_blk = block
        allowed = visible(place_blk, doc_blk)
        masked = jnp.where(allowed, scores_of(key_blk), masked_score)
        new_top = jnp.maximum(row_top, jnp.max(masked, axis=-1, keepdims=True))
        row_total = row_total * jnp.exp(row_top - new_top) + jnp.sum(
            jnp.where(allowed, jnp.exp(masked - new_top), 0.0), axis=-1, keepdims=True
        )
        return ((new_top, row_total), None)

    statistic_shape = (number_of_tokens, KEY_VALUE_HEADS, query_group_size, 1)
    (row_top, row_total), unused = lax.scan(
        stats_step,
        (
            jnp.full(statistic_shape, masked_score, jnp.float32),
            jnp.zeros(statistic_shape, jnp.float32),
        ),
        (blocked_keys, place_blocks, doc_blocks),
    )
    log_total = row_top + jnp.log(row_total)

    def probs_of(key_blk, place_blk, doc_blk):
        allowed = visible(place_blk, doc_blk)
        masked = jnp.where(allowed, scores_of(key_blk), masked_score)
        return jnp.where(allowed, jnp.exp(masked - log_total), 0.0)

    def output_step(carry, block):
        key_blk, value_blk, place_blk, doc_blk = block
        probs_low = probs_of(key_blk, place_blk, doc_blk).astype(jnp.bfloat16)
        added = jnp.einsum(
            "tkgn,nkd->tkgd", probs_low, value_blk, preferred_element_type=jnp.float32
        )
        return (carry + added, None)

    attention_output, unused = lax.scan(
        output_step,
        jnp.zeros((number_of_tokens, KEY_VALUE_HEADS, query_group_size, HEAD_SIZE), jnp.float32),
        (blocked_keys, blocked_values, place_blocks, doc_blocks),
    )
    mixed = attention_output.reshape(number_of_tokens, QUERY_HEADS * HEAD_SIZE).astype(jnp.bfloat16)
    middle = layer_rows + jnp.dot(mixed, out_full, preferred_element_type=jnp.float32)
    normed_two, inverse_two = norm_forward(middle)
    input_two = (normed_two * gain_two).astype(jnp.bfloat16)
    gate_up_low = w_gate_up.astype(jnp.bfloat16)
    down_low = w_down.astype(jnp.bfloat16)
    columns = input_two
    gate_up = jnp.dot(
        columns,
        lax.all_gather(gate_up_low, ("dp", "ctx"), axis=0, tiled=True),
        preferred_element_type=jnp.float32,
    )
    gate_part = gate_up[:, :FF]
    up_part = gate_up[:, FF:]
    sigmoid_gate = jax.nn.sigmoid(gate_part)
    silu_gate = gate_part * sigmoid_gate
    hidden = (silu_gate * up_part).astype(jnp.bfloat16)
    columns = hidden
    down_sum = jnp.dot(
        columns,
        lax.all_gather(down_low, ("dp", "ctx"), axis=0, tiled=True),
        preferred_element_type=jnp.float32,
    )
    layer_out = (middle + down_sum).astype(jnp.bfloat16)
    grad_rows = out_grad.astype(jnp.float32)
    grad_hidden = times_transposed(
        out_grad, lax.all_gather(down_low, ("dp", "ctx"), axis=0, tiled=True)
    )
    grad_gate = grad_hidden * up_part * sigmoid_gate * (1.0 + gate_part * (1.0 - sigmoid_gate))
    grad_up = grad_hidden * silu_gate
    grad_gate_up = jnp.concatenate([grad_gate, grad_up], axis=1).astype(jnp.bfloat16)
    down_grad = lax.psum_scatter(
        transposed_times(hidden, out_grad), ("dp", "ctx"), scatter_dimension=0, tiled=True
    )
    grad_normed_two = times_transposed(
        grad_gate_up, lax.all_gather(gate_up_low, ("dp", "ctx"), axis=0, tiled=True)
    )
    gate_up_grad = lax.psum_scatter(
        transposed_times(input_two, grad_gate_up), ("dp", "ctx"), scatter_dimension=0, tiled=True
    )
    grad_norm_two, gain_two_grad = norm_backward(grad_normed_two, normed_two, inverse_two, gain_two)
    grad_middle = grad_rows + grad_norm_two
    grad_middle_low = grad_middle.astype(jnp.bfloat16)
    out_term = transposed_times(mixed, grad_middle_low)
    grad_mixed = (
        times_transposed(grad_middle_low, out_full)
        .astype(jnp.bfloat16)
        .reshape(number_of_tokens, KEY_VALUE_HEADS, query_group_size, HEAD_SIZE)
    )
    delta = jnp.sum(grad_mixed.astype(jnp.float32) * attention_output, axis=-1, keepdims=True)

    def back_step(grad_query, block):
        key_blk, value_blk, place_blk, doc_blk = block
        probs = probs_of(key_blk, place_blk, doc_blk)
        probs_low = probs.astype(jnp.bfloat16)
        grad_probs = jnp.einsum(
            "tkgd,nkd->tkgn", grad_mixed, value_blk, preferred_element_type=jnp.float32
        )
        grad_scores = (probs * (grad_probs - delta) * score_scale).astype(jnp.bfloat16)
        grad_query = grad_query + jnp.einsum(
            "tkgn,nkd->tkgd", grad_scores, key_blk, preferred_element_type=jnp.float32
        )
        key_grad = jnp.einsum(
            "tkgn,tkgd->nkd", grad_scores, query_rows, preferred_element_type=jnp.float32
        )
        value_grad = jnp.einsum(
            "tkgn,tkgd->nkd", probs_low, grad_mixed, preferred_element_type=jnp.float32
        )
        return (grad_query, (key_grad, value_grad))

    grad_query, (key_grads, value_grads) = lax.scan(
        back_step,
        jnp.zeros((number_of_tokens, KEY_VALUE_HEADS, query_group_size, HEAD_SIZE), jnp.float32),
        (blocked_keys, blocked_values, place_blocks, doc_blocks),
    )
    summed_key_gradient, value_sum = (
        lax.psum_scatter(
            key_grads.reshape(seq_len, key_value_width).astype(jnp.bfloat16),
            "ctx",
            scatter_dimension=0,
            tiled=True,
        ).astype(jnp.float32),
        lax.psum_scatter(
            value_grads.reshape(seq_len, key_value_width).astype(jnp.bfloat16),
            "ctx",
            scatter_dimension=0,
            tiled=True,
        ).astype(jnp.float32),
    )
    key_gradient_unrotated = reverse_rotation(
        summed_key_gradient.reshape(number_of_tokens, KEY_VALUE_HEADS, HEAD_SIZE),
        cosine_table,
        sine_table,
    ).reshape(number_of_tokens, key_value_width)
    grad_keyval = jnp.concatenate([key_gradient_unrotated, value_sum], axis=1).astype(jnp.bfloat16)
    grad_query_low = (
        reverse_rotation(
            grad_query.reshape(number_of_tokens, QUERY_HEADS, HEAD_SIZE), cosine_table, sine_table
        )
        .reshape(number_of_tokens, QUERY_HEADS * HEAD_SIZE)
        .astype(jnp.bfloat16)
    )
    grad_normed_one = times_transposed(grad_query_low, query_full) + times_transposed(
        grad_keyval, keyval_full
    )
    query_term = transposed_times(input_one, grad_query_low)
    keyval_term = transposed_times(input_one, grad_keyval)
    grad_norm_one, gain_one_grad = norm_backward(grad_normed_one, normed_one, inverse_one, gain_one)
    in_grad = grad_middle + grad_norm_one
    gain_term = jnp.stack([gain_one_grad, gain_two_grad])
    query_grad, keyval_grad, out_weight_grad, gains_grad = (
        lax.psum_scatter(query_term, ("dp", "ctx"), scatter_dimension=0, tiled=True),
        lax.psum_scatter(keyval_term, ("dp", "ctx"), scatter_dimension=0, tiled=True),
        lax.psum_scatter(out_term, ("dp", "ctx"), scatter_dimension=0, tiled=True),
        lax.psum_scatter(gain_term, ("dp", "ctx"), scatter_dimension=1, tiled=True),
    )
    rates = rates_for(seq_len)
    gains_m_new, gains_v_new, gains_new = adamw(
        norm_gains, gains_grad, norm_gains_m, norm_gains_v, rates[0], 0.0
    )
    query_m_new, query_v_new, query_new = adamw(
        w_query, query_grad, w_query_m, w_query_v, rates[1], weight_decay
    )
    keyval_m_new, keyval_v_new, keyval_new = adamw(
        key_value_weight,
        keyval_grad,
        key_value_first_moment,
        key_value_second_moment,
        rates[2],
        weight_decay,
    )
    out_m_new, out_v_new, out_new = adamw(
        w_out, out_weight_grad, w_out_m, w_out_v, rates[3], weight_decay
    )
    gate_up_m_new, gate_up_v_new, gate_up_new = adamw(
        w_gate_up, gate_up_grad, w_gate_up_m, w_gate_up_v, rates[4], weight_decay
    )
    down_m_new, down_v_new, down_new = adamw(
        w_down, down_grad, w_down_m, w_down_v, rates[5], weight_decay
    )
    return (
        layer_out,
        in_grad,
        gains_grad,
        gains_m_new,
        gains_v_new,
        gains_new,
        query_grad,
        query_m_new,
        query_v_new,
        query_new,
        keyval_grad,
        keyval_m_new,
        keyval_v_new,
        keyval_new,
        out_weight_grad,
        out_m_new,
        out_v_new,
        out_new,
        gate_up_grad,
        gate_up_m_new,
        gate_up_v_new,
        gate_up_new,
        down_grad,
        down_m_new,
        down_v_new,
        down_new,
    )


def tensor_parallel(
    layer_in,
    positions,
    doc_starts,
    out_grad,
    norm_gains,
    norm_gains_m,
    norm_gains_v,
    w_query,
    w_query_m,
    w_query_v,
    key_value_weight,
    key_value_first_moment,
    key_value_second_moment,
    w_out,
    w_out_m,
    w_out_v,
    w_gate_up,
    w_gate_up_m,
    w_gate_up_v,
    w_down,
    w_down_m,
    w_down_v,
):
    low = jnp.bfloat16
    own_tokens, width = layer_in.shape
    seq_len = own_tokens * PLANE
    group = GROUP
    group_width = group * HEAD_SIZE
    ff_part = FF // PLANE
    ff_own = FF // RANKS
    rows = w_query.shape[0]

    gains_low = norm_gains.astype(low)
    small = jnp.broadcast_to(
        jnp.pad(gains_low.T, ((0, 0), (0, 126)))[None], (PLANE, rows, 128)
    )
    attention_blocks = jnp.concatenate(
        [
            w_query.astype(low).reshape(rows, PLANE, group_width).transpose(1, 0, 2),
            key_value_weight.astype(low)
            .reshape(rows, 2, PLANE, HEAD_SIZE)
            .transpose(2, 0, 1, 3)
            .reshape(PLANE, rows, 2 * HEAD_SIZE),
            small,
        ],
        axis=2,
    )
    feed_blocks = (
        w_gate_up.astype(low)
        .reshape(rows, 2, 4, PLANE, ff_own)
        .transpose(3, 0, 1, 2, 4)
        .reshape(PLANE, rows, 2 * ff_part)
    )
    spots = jnp.broadcast_to(positions[None, :].astype(jnp.float32), (8, own_tokens))
    cosine_own, sine_own = rope_tables(positions, HEAD_SIZE)
    cosine_own, sine_own = cosine_own[:, 0], sine_own[:, 0]
    table = jnp.concatenate([cosine_own, cosine_own, -sine_own, sine_own], axis=1)
    qkv_width = QKV_WIDTH
    (
        input_one_all,
        table_all,
        attention_all,
        gain_rows,
        query_rows,
        key_rows,
        value_rows,
        token_spots,
        token_starts,
        key_spots,
        mixed_parts,
        feed_all,
        out_all,
        down_all,
    ) = attention(
        doc_starts,
        layer_in,
        table,
        spots,
        attention_blocks,
        feed_blocks,
        w_out.astype(low),
        w_down.astype(low).reshape(DOWN_PARTS, -1, width),
    )
    gain_one, gain_two = gain_rows[0], gain_rows[1]
    input_one = input_one_all.reshape(seq_len, width)
    qkv_weight = attention_all.reshape(width, -1)[:, :qkv_width]
    cosine_table = table_all[:, :, : HEAD_SIZE // 2].reshape(seq_len, 1, -1)
    sine_table = table_all[:, :, 3 * HEAD_SIZE // 2 :].reshape(seq_len, 1, -1)
    mixed = mixed_parts.transpose(2, 0, 1, 3).reshape(own_tokens, width)
    out_weight = out_all.reshape(width, width)
    branch = jnp.dot(mixed, out_weight, preferred_element_type=jnp.float32)

    layer_rows = layer_in.astype(jnp.float32)
    middle = layer_rows + branch
    normed_two, inverse_two = norm_forward(middle)
    grad_normed_two, down_sum, feed_term, down_term = feed(
        (normed_two * gain_two).astype(low),
        out_grad,
        feed_all.reshape(width, 2 * ff_part),
        down_all.reshape(ff_part, width),
    )
    layer_out = (middle + down_sum).astype(low)

    grad_norm_two, unused = norm_backward(grad_normed_two, normed_two, inverse_two, gain_two)
    grad_middle = out_grad.astype(jnp.float32) + grad_norm_two
    grad_middle_low = grad_middle.astype(low)
    out_term = transposed_times(mixed, grad_middle_low).astype(low)
    grad_mixed = (
        times_transposed(grad_middle_low, out_weight)
        .astype(low)
        .reshape(own_tokens, PLANE, PAIRS, 2 * HEAD_SIZE)
        .transpose(1, 2, 0, 3)
    )
    grad_query, grad_key, grad_value, feed_grad, down_grad = attention_back(
        query_rows,
        key_rows,
        value_rows,
        token_spots,
        token_starts,
        key_spots,
        grad_mixed,
        feed_term.reshape(RANKS, rows, 2 * ff_part),
        down_term.reshape(4 * DOWN_PARTS, -1, width),
    )
    gate_up_grad = (
        feed_grad.reshape(PLANE, rows, 2, 4, ff_own)
        .transpose(1, 2, 3, 0, 4)
        .reshape(rows, 2 * FF)
        .astype(jnp.float32)
    )
    down_grad = down_grad.reshape(w_down.shape)
    grad_query = grad_query.transpose(0, 3, 1, 2, 4).reshape(seq_len, group, HEAD_SIZE)
    grad_qkv = jnp.concatenate(
        [
            reverse_rotation(grad_query, cosine_table, sine_table).reshape(seq_len, group_width),
            reverse_rotation(grad_key[:, None], cosine_table, sine_table)[:, 0],
            grad_value,
        ],
        axis=1,
    ).astype(low)
    one_parts = times_transposed(grad_qkv, qkv_weight).astype(low)
    qkv_term = transposed_times(input_one, grad_qkv).astype(low)
    grad_normed_one, qkv_grad, out_weight_grad = closing(
        one_parts.reshape(PLANE, own_tokens, width),
        qkv_term.reshape(RANKS, rows, qkv_width),
        out_term.reshape(RANKS, rows, width),
    )
    normed_one, inverse_one = norm_forward(layer_rows)
    grad_norm_one, unused = norm_backward(grad_normed_one, normed_one, inverse_one, gain_one)
    in_grad = grad_middle + grad_norm_one
    qkv_grad = qkv_grad.astype(jnp.float32)
    query_grad = qkv_grad[:, :, :group_width].transpose(1, 0, 2).reshape(w_query.shape)
    keyval_grad = (
        qkv_grad[:, :, group_width:]
        .reshape(PLANE, rows, 2, HEAD_SIZE)
        .transpose(1, 2, 0, 3)
        .reshape(key_value_weight.shape)
    )
    def low_times(weight, grad):
        return jnp.sum(weight.astype(low).astype(jnp.float32) * grad, axis=1)

    gains_grad = jnp.stack(
        [
            low_times(w_query, query_grad) + low_times(key_value_weight, keyval_grad),
            low_times(w_gate_up, gate_up_grad),
        ]
    ) / gains_low.astype(jnp.float32)

    rates = rates_for(seq_len)
    return (
        layer_out,
        in_grad,
        gains_grad,
        *adamw(norm_gains, gains_grad, norm_gains_m, norm_gains_v, rates[0], 0.0),
        query_grad,
        *adamw(w_query, query_grad, w_query_m, w_query_v, rates[1], weight_decay),
        keyval_grad,
        *adamw(
            key_value_weight,
            keyval_grad,
            key_value_first_moment,
            key_value_second_moment,
            rates[2],
            weight_decay,
        ),
        out_weight_grad,
        *adamw(w_out, out_weight_grad, w_out_m, w_out_v, rates[3], weight_decay),
        gate_up_grad,
        *adamw(w_gate_up, gate_up_grad, w_gate_up_m, w_gate_up_v, rates[4], weight_decay),
        down_grad,
        *adamw(w_down, down_grad, w_down_m, w_down_v, rates[5], weight_decay),
    )


def solution(mesh):
    planned = tensor_parallel if dict(mesh.shape) == {"dp": 2 * XS, "ctx": ZS * YS} else body
    return jax.shard_map(
        planned,
        mesh=mesh,
        in_specs=(
            P(("dp", "ctx"), None),
            P(("dp", "ctx")),
            P("dp", None),
            P(("dp", "ctx"), None),
            P(None, ("dp", "ctx")),
            P(None, ("dp", "ctx")),
            P(None, ("dp", "ctx")),
            P(("dp", "ctx"), None),
            P(("dp", "ctx"), None),
            P(("dp", "ctx"), None),
            P(("dp", "ctx"), None),
            P(("dp", "ctx"), None),
            P(("dp", "ctx"), None),
            P(("dp", "ctx"), None),
            P(("dp", "ctx"), None),
            P(("dp", "ctx"), None),
            P(("dp", "ctx"), None),
            P(("dp", "ctx"), None),
            P(("dp", "ctx"), None),
            P(("dp", "ctx"), None),
            P(("dp", "ctx"), None),
            P(("dp", "ctx"), None),
        ),
        out_specs=(
            P(("dp", "ctx"), None),
            P(("dp", "ctx"), None),
            P(None, ("dp", "ctx")),
            P(None, ("dp", "ctx")),
            P(None, ("dp", "ctx")),
            P(None, ("dp", "ctx")),
            P(("dp", "ctx"), None),
            P(("dp", "ctx"), None),
            P(("dp", "ctx"), None),
            P(("dp", "ctx"), None),
            P(("dp", "ctx"), None),
            P(("dp", "ctx"), None),
            P(("dp", "ctx"), None),
            P(("dp", "ctx"), None),
            P(("dp", "ctx"), None),
            P(("dp", "ctx"), None),
            P(("dp", "ctx"), None),
            P(("dp", "ctx"), None),
            P(("dp", "ctx"), None),
            P(("dp", "ctx"), None),
            P(("dp", "ctx"), None),
            P(("dp", "ctx"), None),
            P(("dp", "ctx"), None),
            P(("dp", "ctx"), None),
            P(("dp", "ctx"), None),
            P(("dp", "ctx"), None),
        ),
        check_vma=False,
    )
```

```python
import functools
import math

import jax
import jax.numpy as jnp
from jax import lax
from jax.experimental import pallas as pl
from jax.experimental.pallas import tpu as pltpu
from jax.sharding import PartitionSpec as P

MODEL_WIDTH = 2048
QUERY_HEADS = 32
KEY_VALUE_HEADS = 8
HEAD_SIZE = 64
FF = 8192
STEP = 10


eps_norm = 1e-05
rope_base = 500000.0
beta_one = 0.9
beta_two = 0.95
eps_adam = 1e-08
weight_decay = 0.1
masked_score = -1e30


def rates_for(seq_len):
    return (
        0.6,
        0.8 / math.sqrt(MODEL_WIDTH // 4),
        0.8 / math.sqrt(MODEL_WIDTH),
        0.8 / math.sqrt(max(220 * MODEL_WIDTH // seq_len, 1)),
        0.8 / math.sqrt(MODEL_WIDTH),
        0.8 / math.sqrt(FF // 2),
    )


def adamw(weight, grad_sum, first, second, rate, decay):
    first_new = beta_one * first + (1.0 - beta_one) * grad_sum
    second_new = beta_two * second + (1.0 - beta_two) * grad_sum * grad_sum
    first_hat = first_new / (1.0 - beta_one**STEP)
    second_hat = second_new / (1.0 - beta_two**STEP)
    weight_new = weight - rate * (first_hat / (jnp.sqrt(second_hat) + eps_adam) + decay * weight)
    return (first_new, second_new, weight_new)


def norm_forward(layer_rows):
    inverse = lax.rsqrt(jnp.mean(layer_rows * layer_rows, axis=-1, keepdims=True) + eps_norm)
    return (layer_rows * inverse, inverse)


def norm_backward(grad_out, normed, inverse, gain_row):
    scaled = grad_out * gain_row
    grad_in = inverse * (scaled - normed * jnp.mean(scaled * normed, axis=-1, keepdims=True))
    return (grad_in, jnp.sum(grad_out * normed, axis=0))


def rope_tables(token_placement, head_dim):
    half_dim = head_dim // 2
    frequencies = jnp.exp(
        jnp.arange(half_dim, dtype=jnp.float32) * (-2.0 * math.log(rope_base) / head_dim)
    )
    angles = token_placement.astype(jnp.float32)[:, None] * frequencies[None, :]
    return (jnp.cos(angles)[:, None, :], jnp.sin(angles)[:, None, :])


def apply_rotation(value_rows, cosine_table, sine_table):
    half_dim = value_rows.shape[-1] // 2
    first_half = value_rows[..., :half_dim]
    second_half = value_rows[..., half_dim:]
    return jnp.concatenate(
        [
            first_half * cosine_table - second_half * sine_table,
            second_half * cosine_table + first_half * sine_table,
        ],
        axis=-1,
    )


def reverse_rotation(grad_rows, cosine_table, sine_table):
    half_dim = grad_rows.shape[-1] // 2
    first_half = grad_rows[..., :half_dim]
    second_half = grad_rows[..., half_dim:]
    return jnp.concatenate(
        [
            first_half * cosine_table + second_half * sine_table,
            second_half * cosine_table - first_half * sine_table,
        ],
        axis=-1,
    )


def doc_lookup(token_placement, starts):
    return jnp.sum((token_placement[:, None] >= starts[None, :]).astype(jnp.int32), axis=1) - 1


def times_transposed(left, right):
    return lax.dot_general(
        left, right, (((1,), (1,)), ((), ())), preferred_element_type=jnp.float32
    )


def transposed_times(left, right):
    return lax.dot_general(
        left, right, (((0,), (0,)), ((), ())), preferred_element_type=jnp.float32
    )


XS = 2
YS = 2
ZS = 4
PLANE = ZS * YS
RANKS = 2 * XS * PLANE
MESH = pl.DeviceIdType.MESH


def place():
    d = lax.axis_index("dp")
    c = lax.axis_index("ctx")
    return d, c, lax.div(d, 2), lax.rem(d, 2), lax.div(c, YS), lax.rem(c, YS)


def remote(src, dst, send_sem, recv_sem, d, c):
    return pltpu.make_async_remote_copy(
        src_ref=src,
        dst_ref=dst,
        send_sem=send_sem,
        recv_sem=recv_sem,
        device_id=(d, c),
        device_id_type=MESH,
    )


def greet(peers):
    barrier = pltpu.get_barrier_semaphore()
    for d, c in peers:
        pl.semaphore_signal(barrier, inc=1, device_id=(d, c), device_id_type=MESH)
    pl.semaphore_wait(barrier, len(peers))


def plane_peers(d, c):
    return [(d, lax.rem(c + k, PLANE)) for k in range(1, PLANE)]


def chip_peers(d, c, x, core):
    return [(x * 2 + 1 - core, c), ((1 - x) * 2 + core, c)]


def add_into(target, sources, rows, step=16):
    @pl.loop(0, rows, step=step)
    def _(r):
        at = pl.ds(pl.multiple_of(r, step), step)
        total = sources[0][at].astype(jnp.float32)
        for source in sources[1:]:
            total = total + source[at].astype(jnp.float32)
        target[at] = total.astype(target.dtype)


def near_first(z):
    half = lax.div(z, 2)
    return [half * 4 + 1 - z, 2 - half, 3 - 3 * half]


class SequenceGather:
    def __init__(self, own, out, sems, chunks):
        self.own, self.out, self.chunks = own, out, chunks
        self.zs, self.zr, self.ys, self.yr, self.local_sem = sems
        self.d, self.c, _, _, self.z, self.y = place()
        self.rows = own.shape[0] // chunks
        self.sent = []

    @staticmethod
    def scratch(chunks):
        return [
            pltpu.SemaphoreType.DMA((ZS, chunks)),
            pltpu.SemaphoreType.DMA((ZS, chunks)),
            pltpu.SemaphoreType.DMA((ZS, chunks)),
            pltpu.SemaphoreType.DMA((ZS, chunks)),
            pltpu.SemaphoreType.DMA(()),
        ]

    def part(self, ref, k):
        return ref.at[pl.ds(k * self.rows, self.rows)]

    def across(self, z, k, src):
        slot = z * YS + self.y
        return remote(
            src,
            self.part(self.out.at[slot], k),
            self.ys.at[z, k],
            self.yr.at[z, k],
            self.d,
            self.z * YS + 1 - self.y,
        )

    def along(self, to, k):
        return remote(
            self.part(self.own, k),
            self.part(self.out.at[self.c], k),
            self.zs.at[to, k],
            self.zr.at[self.z, k],
            self.d,
            to * YS + self.y,
        )

    def start(self, copy):
        copy.start()
        self.sent.append(copy)

    def first(self, by_block=False):
        self.local = pltpu.make_async_copy(self.own, self.out.at[self.c], self.local_sem)
        self.local.start()
        near = near_first(self.z)
        if by_block:
            for k in range(self.chunks):
                self.start(self.across(self.z, k, self.part(self.own, k)))
            for to in near:
                for k in range(self.chunks):
                    self.start(self.along(to, k))
            return
        for k in range(self.chunks):
            for to in near[::-1]:
                self.start(self.along(to, k))
            self.start(self.across(self.z, k, self.part(self.own, k)))

    def relay_one(self, source, k):
        slot = source * YS + self.y
        block = self.part(self.out.at[slot], k)
        remote(
            block, block, self.zs.at[source, k], self.zr.at[source, k], self.d, slot
        ).wait_recv()
        self.start(self.across(source, k, block))

    def relay(self, k):
        for source in near_first(self.z):
            self.relay_one(source, k)

    def relay_block(self, source):
        for k in range(self.chunks):
            self.relay_one(source, k)

    def arrive_across(self, z):
        for k in range(self.chunks):
            block = self.part(self.out.at[z * YS + 1 - self.y], k)
            remote(
                block,
                block,
                self.ys.at[z, k],
                self.yr.at[z, k],
                self.d,
                self.z * YS + 1 - self.y,
            ).wait_recv()

    def finish(self):
        for copy in self.sent:
            copy.wait_send()

    def last(self):
        for z in range(ZS):
            self.arrive_across(z)
        self.finish()
        self.local.wait()


class SequenceScatter:
    def __init__(self, parts, out, ybuf, zbuf, sems, chunks):
        self.parts, self.out, self.chunks = parts, out, chunks
        self.ybuf, self.zbuf = ybuf, zbuf
        self.ys, self.yr, self.zs, self.zr = sems
        self.d, self.c, _, _, self.z, self.y = place()
        self.rows = parts.shape[1] // chunks
        self.sent = []

    @staticmethod
    def scratch(rows, width, chunks):
        return [
            pltpu.VMEM((ZS, rows, width), jnp.bfloat16),
            pltpu.VMEM((ZS, rows, width), jnp.bfloat16),
            pltpu.SemaphoreType.DMA((ZS, chunks)),
            pltpu.SemaphoreType.DMA((ZS, chunks)),
            pltpu.SemaphoreType.DMA((ZS, chunks)),
            pltpu.SemaphoreType.DMA((ZS, chunks)),
        ]

    def span(self, k):
        return pl.ds(k * self.rows, self.rows)

    def across(self, z, k):
        return remote(
            self.parts.at[z * YS + 1 - self.y, self.span(k)],
            self.ybuf.at[z, self.span(k)],
            self.ys.at[z, k],
            self.yr.at[z, k],
            self.d,
            self.z * YS + 1 - self.y,
        )

    def along(self, to, k):
        return remote(
            self.ybuf.at[to, self.span(k)],
            self.zbuf.at[self.z, self.span(k)],
            self.zs.at[to, k],
            self.zr.at[self.z, k],
            self.d,
            to * YS + self.y,
        )

    def start(self, z, k):
        copy = self.across(z, k)
        copy.start()
        self.sent.append(copy)

    def first(self):
        for k in range(self.chunks):
            for z in (*near_first(self.z)[::-1], self.z):
                self.start(z, k)

    def relay_one(self, z, k):
        self.across(z, k).wait_recv()
        block = self.ybuf.at[z, self.span(k)]
        add_into(block, [self.parts.at[z * YS + self.y, self.span(k)], block], self.rows)
        copy = self.along(z, k)
        copy.start()
        self.sent.append(copy)

    def relay(self, k):
        for z in near_first(self.z)[::-1]:
            self.relay_one(z, k)

    def last(self, k):
        self.across(self.z, k).wait_recv()
        blocks = [self.parts.at[self.c, self.span(k)], self.ybuf.at[self.z, self.span(k)]]
        for source in near_first(self.z):
            block = self.zbuf.at[source, self.span(k)]
            remote(
                block,
                block,
                self.zs.at[source, k],
                self.zr.at[source, k],
                self.d,
                source * YS + self.y,
            ).wait_recv()
            blocks.append(block)
        add_into(self.out.at[self.span(k)], blocks, self.rows)

    def finish(self):
        for copy in self.sent:
            copy.wait_send()


class ChipGather:
    def __init__(self, out, sems, count):
        self.out, self.count = out, count
        self.cs, self.cr, self.xs, self.xr = sems
        self.d, self.c, self.x, self.core, _, _ = place()
        self.sent = []

    @staticmethod
    def scratch(count):
        return [
            pltpu.SemaphoreType.DMA((2, count)),
            pltpu.SemaphoreType.DMA((2, count)),
            pltpu.SemaphoreType.DMA((count,)),
            pltpu.SemaphoreType.DMA((count,)),
        ]

    def to_core(self, far, j, src=None):
        x = 1 - self.x if far else self.x
        block = self.out.at[(x * 2 + self.core) * self.count + j]
        return remote(
            block if src is None else src,
            block,
            self.cs.at[far, j],
            self.cr.at[far, j],
            self.x * 2 + 1 - self.core,
            self.c,
        )

    def to_x(self, j, src=None):
        block = self.out.at[self.d * self.count + j]
        return remote(
            block if src is None else src,
            block,
            self.xs.at[j],
            self.xr.at[j],
            (1 - self.x) * 2 + self.core,
            self.c,
        )

    def start(self, j, src=None):
        for copy in (self.to_x(j, src), self.to_core(0, j, src)):
            copy.start()
            self.sent.append(copy)

    def relay(self, j):
        self.to_x(j).wait_recv()
        copy = self.to_core(1, j)
        copy.start()
        self.sent.append(copy)

    def last(self):
        for far in (0, 1):
            for j in range(self.count):
                self.to_core(far, j).wait_recv()
        for copy in self.sent:
            copy.wait_send()


class WeightGather:
    def __init__(self, blocks, out, sems):
        self.blocks, self.out = blocks, out
        self.ps, self.pr, self.local_sem = sems[:3]
        self.chip = ChipGather(out, sems[3:], PLANE)
        self.d, self.c = self.chip.d, self.chip.c
        self.sent = []

    @staticmethod
    def scratch():
        return [
            pltpu.SemaphoreType.DMA((PLANE,)),
            pltpu.SemaphoreType.DMA((PLANE,)),
            pltpu.SemaphoreType.DMA(()),
        ] + ChipGather.scratch(PLANE)

    def send(self, off):
        to = lax.rem(self.c + off, PLANE)
        copy = remote(
            self.blocks.at[to],
            self.out.at[self.d * PLANE + self.c],
            self.ps.at[off],
            self.pr.at[self.c],
            self.d,
            to,
        )
        copy.start()
        self.sent.append(copy)

    def first(self, ahead=PLANE - 1):
        self.ahead = ahead
        self.local = pltpu.make_async_copy(
            self.blocks.at[self.c], self.out.at[self.d * PLANE + self.c], self.local_sem
        )
        self.local.start()
        for off in range(1, 1 + ahead):
            self.send(off)
        self.chip.start(self.c, self.blocks.at[self.c])

    def relay(self, off):
        if off + self.ahead < PLANE:
            self.send(off + self.ahead)
        source = lax.rem(self.c + PLANE - off, PLANE)
        block = self.out.at[self.d * PLANE + source]
        remote(
            block, block, self.ps.at[off], self.pr.at[source], self.d, source
        ).wait_recv()
        self.chip.start(source)

    def relay_chip(self):
        for off in range(PLANE):
            self.chip.relay(lax.rem(self.c + off, PLANE))

    def last(self):
        self.chip.last()
        for copy in self.sent:
            copy.wait_send()
        self.local.wait()


class ChipScatter:
    def __init__(self, parts, cbuf, stage, xbuf, sems, count):
        self.parts, self.count = parts, count
        self.cbuf, self.stage, self.xbuf = cbuf, stage, xbuf
        self.cs, self.cr, self.xs, self.xr = sems
        self.d, self.c, self.x, self.core, _, _ = place()
        self.sent = []

    @staticmethod
    def scratch(count, rows, width):
        return [
            pltpu.VMEM((2, count, rows, width), jnp.bfloat16),
            pltpu.VMEM((count, rows, width), jnp.bfloat16),
            pltpu.VMEM((count, rows, width), jnp.bfloat16),
            pltpu.SemaphoreType.DMA((2, count)),
            pltpu.SemaphoreType.DMA((2, count)),
            pltpu.SemaphoreType.DMA((count,)),
            pltpu.SemaphoreType.DMA((count,)),
        ]

    def to_core(self, far, j):
        x = 1 - self.x if far else self.x
        return remote(
            self.parts.at[(x * 2 + 1 - self.core) * self.count + j],
            self.cbuf.at[far, j],
            self.cs.at[far, j],
            self.cr.at[far, j],
            self.x * 2 + 1 - self.core,
            self.c,
        )

    def to_x(self, j):
        return remote(
            self.stage.at[j],
            self.xbuf.at[j],
            self.xs.at[j],
            self.xr.at[j],
            (1 - self.x) * 2 + self.core,
            self.c,
        )

    def start(self, j):
        for far in (1, 0):
            copy = self.to_core(far, j)
            copy.start()
            self.sent.append(copy)

    def relay(self, j):
        self.to_core(1, j).wait_recv()
        own = self.parts.at[((1 - self.x) * 2 + self.core) * self.count + j]
        add_into(self.stage.at[j], [own, self.cbuf.at[1, j]], own.shape[0])
        copy = self.to_x(j)
        copy.start()
        self.sent.append(copy)

    def total(self, j, target):
        self.to_core(0, j).wait_recv()
        self.to_x(j).wait_recv()
        own = self.parts.at[self.d * self.count + j]
        add_into(target, [own, self.cbuf.at[0, j], self.xbuf.at[j]], own.shape[0])

    def finish(self):
        for copy in self.sent:
            copy.wait_send()


class WeightScatter:
    def __init__(self, parts, out, bufs, sems):
        self.stage = bufs[0]
        self.ps, self.pr = sems[:2]
        self.chip = ChipScatter(parts, *bufs[1:], sems[2:], PLANE)
        self.out = out
        self.d, self.c = self.chip.d, self.chip.c
        self.sent = []

    @staticmethod
    def scratch(rows, width):
        chip = ChipScatter.scratch(PLANE, rows, width)
        return [
            pltpu.VMEM((PLANE, rows, width), jnp.bfloat16),
            *chip[:3],
            pltpu.SemaphoreType.DMA((PLANE,)),
            pltpu.SemaphoreType.DMA((PLANE,)),
            *chip[3:],
        ]

    def first(self):
        for off in range(1, PLANE + 1):
            self.chip.start(lax.rem(self.c + off, PLANE))

    def relay(self, off):
        self.chip.relay(lax.rem(self.c + off, PLANE))

    def send(self, off):
        to = lax.rem(self.c + off, PLANE)
        if off == PLANE:
            self.chip.total(to, self.out.at[self.c])
            return
        self.chip.total(to, self.stage.at[to])
        copy = remote(
            self.stage.at[to],
            self.out.at[self.c],
            self.ps.at[off],
            self.pr.at[self.c],
            self.d,
            to,
        )
        copy.start()
        self.sent.append(copy)

    def last(self):
        for off in range(1, PLANE):
            source = lax.rem(self.c + off, PLANE)
            block = self.out.at[source]
            remote(
                block, block, self.ps.at[off], self.pr.at[source], self.d, source
            ).wait_recv()
        for copy in self.sent:
            copy.wait_send()
        self.chip.finish()


def params(collective_id, mebibytes=56):
    return pltpu.CompilerParams(
        collective_id=collective_id, has_side_effects=True, vmem_limit_bytes=mebibytes * 2**20
    )


ANY = pl.BlockSpec(memory_space=pl.ANY)
VMEM = pl.BlockSpec(memory_space=pltpu.VMEM)
CHUNKS = 4


DOWN_PARTS = 4
SCORE_SCALE = 1.0 / math.sqrt(HEAD_SIZE)
GROUP = QUERY_HEADS // KEY_VALUE_HEADS
PAIRS = GROUP // 2


def times_rows(left, right):
    return lax.dot_general(
        left, right, (((1,), (1,)), ((), ())), preferred_element_type=jnp.float32
    )


class PlaneExchange:
    def __init__(self, blocks, out, sems):
        self.blocks, self.out = blocks, out
        self.ps, self.pr, self.local_sem = sems
        self.d, self.c = lax.axis_index("dp"), lax.axis_index("ctx")
        self.sent = []

    @staticmethod
    def scratch():
        return [
            pltpu.SemaphoreType.DMA((PLANE,)),
            pltpu.SemaphoreType.DMA((PLANE,)),
            pltpu.SemaphoreType.DMA(()),
        ]

    def send(self, off):
        to = lax.rem(self.c + off, PLANE)
        if off % PLANE == 0:
            self.local = pltpu.make_async_copy(
                self.blocks.at[to], self.out.at[self.c], self.local_sem
            )
            self.local.start()
            return
        copy = remote(
            self.blocks.at[to],
            self.out.at[self.c],
            self.ps.at[off],
            self.pr.at[self.c],
            self.d,
            to,
        )
        copy.start()
        self.sent.append(copy)

    def arrive(self, off):
        if off % PLANE == 0:
            self.local.wait()
            return
        source = lax.rem(self.c + PLANE - off, PLANE)
        block = self.out.at[source]
        remote(
            block, block, self.ps.at[off], self.pr.at[source], self.d, source
        ).wait_recv()

    def finish(self):
        for copy in self.sent:
            copy.wait_send()


def probabilities(query, keys, spot, start, key_spots):
    scores = times_rows(query, keys) * SCORE_SCALE
    masked = jnp.where((key_spots <= spot) & (key_spots >= start), scores, masked_score)
    exponent = jnp.exp(masked - jnp.max(masked, axis=-1, keepdims=True))
    return exponent * (1.0 / jnp.sum(exponent, axis=-1, keepdims=True))


def rotate(value, table, back=False):
    lane = lax.broadcasted_iota(jnp.int32, value.shape, 1)
    turned = pltpu.roll(table, HEAD_SIZE, 1)
    cosine = jnp.where(lane < HEAD_SIZE, table, turned)
    sine = jnp.where(lane < HEAD_SIZE, turned, table)
    half = HEAD_SIZE // 2
    other = jnp.where(
        lax.rem(lane, HEAD_SIZE) < half,
        pltpu.roll(value, 2 * HEAD_SIZE - half, 1),
        pltpu.roll(value, half, 1),
    )
    if back:
        return value * cosine - other * sine
    return value * cosine + other * sine


QKV_WIDTH = (GROUP + 2) * HEAD_SIZE


def attention_kernel(
    starts_ref,
    rows_ref,
    table_ref,
    spots_ref,
    qkv_ref,
    blocks_ref,
    out_rows_ref,
    down_ref,
    grads_ref,
    input_out,
    table_out,
    qkv_out,
    gains_out,
    query_out,
    key_out,
    value_out,
    spot_out,
    start_out,
    key_spot_out,
    mixed_out,
    blocks_out,
    out_rows_out,
    down_out,
    grads_out,
    *scratch,
):
    mixed_stage, spots_all, rows_all = scratch[:3]
    scratch = list(scratch[3:])

    def take(count):
        taken, scratch[:count] = scratch[:count], []
        return taken

    d, c, x, core, z, y = place()
    exchange = PlaneExchange(mixed_stage, mixed_out, take(3))
    qkv = WeightGather(qkv_ref, qkv_out, take(7))
    weights = WeightGather(blocks_ref, blocks_out, take(7))
    outs = SequenceGather(out_rows_ref, out_rows_out.at[pl.ds(d * PLANE, PLANE)], take(5), 1)
    outs_chip = ChipGather(out_rows_out, take(4), PLANE)
    rows = SequenceGather(rows_ref, rows_all, take(5), 2)
    table = SequenceGather(table_ref, table_out, take(5), 1)
    grads = SequenceGather(grads_ref, grads_out, take(5), CHUNKS)
    down = ChipGather(down_out, take(4), DOWN_PARTS)
    spot_send, spot_recv, spot_local, down_local = take(4)
    greet(plane_peers(d, c) + chip_peers(d, c, x, core))
    order = near_first(z)

    qkv.first()
    spots_own = pltpu.make_async_copy(spots_ref, spots_all.at[c], spot_local)
    spots_own.start()
    spots_sent = []
    for off in range(1, PLANE):
        to = lax.rem(c + off, PLANE)
        copy = remote(
            spots_ref, spots_all.at[c], spot_send.at[off], spot_recv.at[c], d, to
        )
        copy.start()
        spots_sent.append(copy)
    table.first()
    rows.first(by_block=True)
    down_own = pltpu.make_async_copy(
        down_ref, down_out.at[pl.ds(d * DOWN_PARTS, DOWN_PARTS)], down_local
    )
    down_own.start()
    for j in range(DOWN_PARTS):
        down.start(j, down_ref.at[j])
    outs.first()
    outs_chip.start(c, out_rows_ref)
    for off in range(1, PLANE):
        qkv.relay(off)
    table.relay(0)
    rows.relay_block(order[0])
    weights.first(2)
    qkv.relay_chip()
    rows.relay_block(order[1])
    rows.relay_block(order[2])
    for off in range(1, PLANE):
        source = lax.rem(c + off, PLANE)
        block = spots_all.at[source]
        remote(block, block, spot_send.at[off], spot_recv.at[source], d, source).wait_recv()
    spots_own.wait()
    table.last()
    for slot in range(PLANE):
        key_spot_out[:, slot * 128 : (slot + 1) * 128] = spots_all[slot]
        spot = jnp.broadcast_to(spots_all[slot][:1], (128, 128)).T[:, :1]
        start = jnp.zeros_like(spot)
        for doc in range(starts_ref.shape[1]):
            first = starts_ref[0, doc].astype(jnp.float32)
            start = jnp.maximum(start, jnp.where(spot >= first, first, 0.0))
        spot_out[slot] = spot
        start_out[slot] = start
    qkv.last()
    for pair in range(RANKS // 2):
        columns = qkv_out[2 * pair : 2 * pair + 2, :, QKV_WIDTH:]
        turned = columns.reshape(128, 128).astype(jnp.float32).T
        gains_out[:, pair * 128 : (pair + 1) * 128] = turned[:8]

    tokens, width = rows_ref.shape
    wide = 2 * HEAD_SIZE

    def project(pair):
        for slot in range(YS):

            @pl.loop(0, tokens, step=32)
            def _(r):
                at = pl.ds(pl.multiple_of(r, 32), 32)
                value = rows_all[pair * YS + slot, at].astype(jnp.float32)
                inverse = lax.rsqrt(
                    jnp.mean(value * value, axis=-1, keepdims=True) + eps_norm
                )
                input_out[pair * YS + slot, at] = (value * inverse * gains_out[:1]).astype(
                    jnp.bfloat16
                )

        both = pl.ds(pair * YS, YS)
        weight = qkv_out[:, :, :QKV_WIDTH].reshape(width, QKV_WIDTH)
        projected = jnp.dot(
            input_out[both].reshape(YS * tokens, width),
            weight,
            preferred_element_type=jnp.float32,
        )
        turns = table_out[both].reshape(YS * tokens, wide)
        for slot in range(YS):
            span = slice(slot * tokens, (slot + 1) * tokens)
            block = pair * YS + slot
            for heads in range(PAIRS):
                query = rotate(
                    projected[span, heads * wide : (heads + 1) * wide], turns[span]
                ).astype(jnp.bfloat16)
                query_out[block, heads, 0] = query[:, :HEAD_SIZE]
                query_out[block, heads, 1] = query[:, HEAD_SIZE:]
            key = rotate(projected[span, PAIRS * wide :], turns[span])
            key_out[block] = key[:, :HEAD_SIZE].astype(jnp.bfloat16)
            value_out[block] = projected[span, PAIRS * wide + HEAD_SIZE :].astype(
                jnp.bfloat16
            )

    rows.local.wait()
    rows.arrive_across(z)
    project(z)
    outs.relay(0)
    for source in order:
        outs_chip.start(source * YS + y)
    weights.relay(1)
    grads.first()
    for step, pair in enumerate(order):
        rows.arrive_across(pair)
        project(pair)
        weights.relay(step + 2)
    rows.finish()
    for other in range(ZS):
        outs.arrive_across(other)
        outs_chip.start(other * YS + 1 - y)

    for step in range(1, PLANE + 1):
        block = lax.rem(c + step, PLANE)

        @pl.loop(0, PAIRS)
        def _(pair):
            halves = []
            keys = key_out[...].reshape(PLANE * tokens, HEAD_SIZE)
            values = value_out[...].reshape(PLANE * tokens, HEAD_SIZE)
            for half in range(2):
                probs = probabilities(
                    query_out[block, pair, half],
                    keys,
                    spot_out[block],
                    start_out[block],
                    key_spot_out[:1],
                )
                halves.append(
                    jnp.dot(
                        probs.astype(jnp.bfloat16), values, preferred_element_type=jnp.float32
                    ).astype(jnp.bfloat16)
                )
            mixed_stage[block, pair] = jnp.concatenate(halves, axis=1)

        exchange.send(step)
        if step < 4:
            weights.relay(step + 4)
        if step == 4:
            for j in range(DOWN_PARTS):
                down.relay(j)
        if step == 5:
            for off in range(PLANE):
                outs_chip.relay(lax.rem(c + off, PLANE))
        if step > 5:
            grads.relay(step - 6)
    for off in range(4):
        weights.chip.relay(lax.rem(c + PLANE - off, PLANE))
    for k in (3,):
        grads.relay(k)
    for off in range(4, PLANE):
        weights.chip.relay(lax.rem(c + PLANE - off, PLANE))
    for off in range(1, PLANE + 1):
        exchange.arrive(off)
    grads.last()
    down.last()
    outs_chip.last()
    weights.last()
    outs.finish()
    outs.local.wait()
    exchange.finish()
    for copy in spots_sent:
        copy.wait_send()
    down_own.wait()


def attention(starts, rows, table, spots, qkv, blocks, out_rows, down, grads):
    low, full = jnp.bfloat16, jnp.float32
    tokens, width = rows.shape
    mixed = jax.ShapeDtypeStruct((PLANE, PAIRS, tokens, 2 * HEAD_SIZE), low)
    seq_len = PLANE * tokens
    return pl.pallas_call(
        attention_kernel,
        out_shape=(
            jax.ShapeDtypeStruct((PLANE, tokens, width), low),
            jax.ShapeDtypeStruct((PLANE, *table.shape), full),
            jax.ShapeDtypeStruct((RANKS, *qkv.shape[1:]), low),
            jax.ShapeDtypeStruct((8, width), full),
            jax.ShapeDtypeStruct((PLANE, PAIRS, 2, tokens, HEAD_SIZE), low),
            jax.ShapeDtypeStruct((PLANE, tokens, HEAD_SIZE), low),
            jax.ShapeDtypeStruct((PLANE, tokens, HEAD_SIZE), low),
            jax.ShapeDtypeStruct((PLANE, tokens, 1), full),
            jax.ShapeDtypeStruct((PLANE, tokens, 1), full),
            jax.ShapeDtypeStruct((8, seq_len), full),
            mixed,
            jax.ShapeDtypeStruct((RANKS, *blocks.shape[1:]), low),
            jax.ShapeDtypeStruct((RANKS, *out_rows.shape), low),
            jax.ShapeDtypeStruct((4 * DOWN_PARTS, *down.shape[1:]), low),
            jax.ShapeDtypeStruct((PLANE, *grads.shape), low),
        ),
        in_specs=[pl.BlockSpec(memory_space=pltpu.SMEM)] + [ANY] * 8,
        out_specs=(VMEM,) * 11 + (ANY,) * 4,
        scratch_shapes=[
            pltpu.VMEM(mixed.shape, low),
            pltpu.VMEM((PLANE, *spots.shape), full),
            pltpu.VMEM((PLANE, tokens, width), low),
            *PlaneExchange.scratch(),
            *WeightGather.scratch(),
            *WeightGather.scratch(),
            *SequenceGather.scratch(1),
            *ChipGather.scratch(PLANE),
            *SequenceGather.scratch(2),
            *SequenceGather.scratch(1),
            *SequenceGather.scratch(CHUNKS),
            *ChipGather.scratch(DOWN_PARTS),
            pltpu.SemaphoreType.DMA((PLANE,)),
            pltpu.SemaphoreType.DMA((PLANE,)),
            pltpu.SemaphoreType.DMA(()),
            pltpu.SemaphoreType.DMA(()),
        ],
        compiler_params=params(2),
        name="attention",
    )(starts, rows, table, spots, qkv, blocks, out_rows, down, grads)


def feed_kernel(
    rows_ref,
    grads_all,
    weight_ref,
    down_ref,
    normed_out,
    total_out,
    weight_grad_out,
    down_grad_out,
    *scratch,
):
    rows_all, slope_gate, slope_up, hidden_all, gate_grads = scratch[:5]
    normed_parts, down_parts, turned, stage, stage_sem = scratch[5:10]
    scratch = list(scratch[10:])

    def take(count):
        taken, scratch[:count] = scratch[:count], []
        return taken

    rows = SequenceGather(rows_ref, rows_all, take(5), 2)
    normed = SequenceScatter(normed_parts, normed_out, *take(2), take(4), 1)
    total = SequenceScatter(down_parts, total_out, *take(2), take(4), 1)
    d, c, x, core, z, y = place()
    greet(
        [(d, lax.rem(z + off, ZS) * YS + y) for off in range(1, ZS)] + [(d, z * YS + 1 - y)]
    )
    tokens, width = rows_ref.shape
    part = down_ref.shape[0]
    tile = 256
    blocks = PLANE // 2
    half = lax.div(z, 2)
    near, mid, far = near_first(z)

    def slots(side):
        return pl.ds(side * blocks, blocks)

    def columns(n, start=0, size=tile):
        return pl.ds(pl.multiple_of(n + start, size), size)

    def flat(ref, side):
        value = ref[slots(side)]
        return value.reshape(blocks * tokens, value.shape[2])

    def held(value, dtype=jnp.bfloat16):
        return value.astype(dtype).reshape(blocks, tokens, value.shape[1])

    def forward(side):
        @pl.loop(0, part, step=tile)
        def _(n):
            at, after = columns(n), columns(n, part)
            value = flat(rows_all, side)
            gate = jnp.dot(value, weight_ref[:, at], preferred_element_type=jnp.float32)
            up = jnp.dot(value, weight_ref[:, after], preferred_element_type=jnp.float32)
            sigmoid = jax.nn.sigmoid(gate)
            silu = gate * sigmoid
            hidden_all[slots(side), :, at] = held(silu * up)
            slope_up[slots(side), :, at] = held(silu, jnp.float32)
            slope_gate[slots(side), :, at] = held(
                up * sigmoid * (1.0 + gate * (1.0 - sigmoid)), jnp.float32
            )

    def downward(side):
        @pl.loop(0, width, step=2 * tile)
        def _(n):
            at = columns(n, 0, 2 * tile)
            down_parts[slots(side), :, at] = held(
                jnp.dot(
                    flat(hidden_all, side), down_ref[:, at], preferred_element_type=jnp.float32
                )
            )

    def backward(side):
        @pl.loop(0, part, step=tile)
        def _(n):
            at, after = columns(n), columns(n, part)
            grad = held(times_rows(flat(grads_all, side), down_ref[at, :]), jnp.float32)
            gate_grads[slots(side), :, at] = (grad * slope_gate[slots(side), :, at]).astype(
                jnp.bfloat16
            )
            gate_grads[slots(side), :, after] = (grad * slope_up[slots(side), :, at]).astype(
                jnp.bfloat16
            )

    def inward(side):
        @pl.loop(0, width, step=2 * tile)
        def _(n):
            at = columns(n, 0, 2 * tile)
            normed_parts[slots(side), :, at] = held(
                times_rows(flat(gate_grads, side), weight_ref[at, :])
            )

    tiles = [(hidden_all, grads_all, down_grad_out, n) for n in range(part // tile)]
    tiles += [(rows_all, gate_grads, weight_grad_out, n) for n in range(width // tile)]
    copies = []

    def weight_grad(i):
        left, right, out, n = tiles[i]
        if i >= 2:
            copies[i - 2].wait()
        value = left[:, :, n * tile : (n + 1) * tile].reshape(PLANE * tokens, tile)
        turned[...] = value.T

        @pl.loop(0, width, step=2 * tile)
        def _(m):
            at = columns(m, 0, 2 * tile)
            stage[i % 2, :, at] = jnp.dot(
                turned[...],
                right[:, :, at].reshape(PLANE * tokens, 2 * tile),
                preferred_element_type=jnp.float32,
            ).astype(jnp.bfloat16)

        copy = pltpu.make_async_copy(
            stage.at[i % 2], out.at[pl.ds(n * tile, tile)], stage_sem.at[i % 2]
        )
        copy.start()
        copies.append(copy)

    rows.first(by_block=True)
    rows.local.wait()
    rows.relay_block(near)
    rows.arrive_across(z)
    rows.arrive_across(near)
    forward(half)
    rows.relay_block(mid)
    rows.relay_block(far)
    backward(half)
    inward(half)
    normed.start(near, 0)
    normed.start(z, 0)
    rows.arrive_across(mid)
    rows.arrive_across(far)
    forward(1 - half)
    backward(1 - half)
    inward(1 - half)
    normed.start(far, 0)
    normed.start(mid, 0)
    normed.relay_one(near, 0)
    downward(1 - half)
    total.start(far, 0)
    total.start(mid, 0)
    normed.relay_one(far, 0)
    downward(half)
    total.start(near, 0)
    total.start(z, 0)
    normed.relay_one(mid, 0)
    for i in range(2):
        weight_grad(i)
    for pair in (far, mid, near):
        total.relay_one(pair, 0)
        weight_grad(len(copies))
    for i in range(len(copies), len(tiles)):
        weight_grad(i)
    normed.last(0)
    total.last(0)
    for copy in copies[-2:]:
        copy.wait()
    rows.finish()
    normed.finish()
    total.finish()


def feed(rows, grads, weight, down):
    part, width = down.shape
    low = rows.dtype
    tokens = rows.shape[0]
    summed = jax.ShapeDtypeStruct(rows.shape, jnp.float32)
    return pl.pallas_call(
        feed_kernel,
        out_shape=(
            summed,
            summed,
            jax.ShapeDtypeStruct(weight.shape, low),
            jax.ShapeDtypeStruct(down.shape, low),
        ),
        in_specs=[ANY] + [VMEM] * 3,
        out_specs=(VMEM,) * 2 + (ANY,) * 2,
        scratch_shapes=[
            pltpu.VMEM((PLANE, tokens, width), low),
            pltpu.VMEM((PLANE, tokens, part), jnp.float32),
            pltpu.VMEM((PLANE, tokens, part), jnp.float32),
            pltpu.VMEM((PLANE, tokens, part), low),
            pltpu.VMEM((PLANE, tokens, 2 * part), low),
            pltpu.VMEM((PLANE, tokens, width), low),
            pltpu.VMEM((PLANE, tokens, width), low),
            pltpu.VMEM((256, PLANE * tokens), low),
            pltpu.VMEM((2, 256, width), low),
            pltpu.SemaphoreType.DMA((2,)),
            *SequenceGather.scratch(2),
            *SequenceScatter.scratch(tokens, width, 1),
            *SequenceScatter.scratch(tokens, width, 1),
        ],
        compiler_params=params(5, 60),
        name="feed",
    )(rows, grads, weight, down)


def attention_back_kernel(
    query_ref,
    key_ref,
    value_ref,
    spot_ref,
    start_ref,
    key_spot_ref,
    mixed_ref,
    parts_ref,
    down_ref,
    query_out,
    key_out,
    value_out,
    out_ref,
    down_out,
    *scratch,
):
    mixed_all = scratch[0]
    exchange = PlaneExchange(mixed_ref, mixed_all, scratch[1:4])
    weights = WeightScatter(parts_ref, out_ref, scratch[4:8], scratch[8:14])
    down = ChipScatter(down_ref, *scratch[14:17], scratch[17:], DOWN_PARTS)
    d, c, x, core, z, y = place()
    greet(plane_peers(d, c) + chip_peers(d, c, x, core))
    for off in range(1, PLANE + 1):
        exchange.send(off)
    weights.first()
    for j in range(DOWN_PARTS):
        down.start(j)
    key_out[...] = jnp.zeros_like(key_out)
    value_out[...] = jnp.zeros_like(value_out)
    for step in range(PLANE):
        block = lax.rem(c + PLANE - step, PLANE)
        exchange.arrive(step)

        @pl.loop(0, PAIRS)
        def _(pair):
            keys = key_ref[...].reshape(key_out.shape)
            values = value_ref[...].reshape(value_out.shape)
            for half in range(2):
                query = query_ref[block, pair, half]
                grad = mixed_all[block, pair][:, half * HEAD_SIZE : (half + 1) * HEAD_SIZE]
                probs = probabilities(
                    query, keys, spot_ref[block], start_ref[block], key_spot_ref[:1]
                )
                grad_probs = times_rows(grad, values)
                delta = jnp.sum(probs * grad_probs, axis=-1, keepdims=True)
                grad_scores = (probs * (grad_probs - delta) * SCORE_SCALE).astype(jnp.bfloat16)
                query_out[block, pair, half] = jnp.dot(
                    grad_scores, keys, preferred_element_type=jnp.float32
                )
                key_out[...] += transposed_times(grad_scores, query)
                value_out[...] += transposed_times(probs.astype(jnp.bfloat16), grad)

        weights.relay(step + 1)
        if step >= 2:
            weights.send(step - 1)
    for off in (PLANE - 1, PLANE):
        weights.send(off)
    for j in range(DOWN_PARTS):
        down.relay(j)
    for j in range(DOWN_PARTS):
        down.total(j, down_out.at[j])
    weights.last()
    down.finish()
    exchange.finish()


def attention_back(query, keys, values, spots, starts, key_spots, mixed, parts, down):
    return pl.pallas_call(
        attention_back_kernel,
        out_shape=(
            jax.ShapeDtypeStruct(query.shape, jnp.float32),
            jax.ShapeDtypeStruct((PLANE * keys.shape[1], HEAD_SIZE), jnp.float32),
            jax.ShapeDtypeStruct((PLANE * values.shape[1], HEAD_SIZE), jnp.float32),
            jax.ShapeDtypeStruct((PLANE, *parts.shape[1:]), parts.dtype),
            jax.ShapeDtypeStruct((DOWN_PARTS, *down.shape[1:]), jnp.float32),
        ),
        in_specs=[VMEM] * 9,
        out_specs=(VMEM,) * 5,
        scratch_shapes=[
            pltpu.VMEM(mixed.shape, jnp.bfloat16),
            *PlaneExchange.scratch(),
            *WeightScatter.scratch(*parts.shape[1:]),
            *ChipScatter.scratch(DOWN_PARTS, *down.shape[1:]),
        ],
        compiler_params=params(3),
        name="attention_back",
    )(query, keys, values, spots, starts, key_spots, mixed, parts, down)


def closing_kernel(rows_ref, parts_ref, outs_ref, rows_out, out_ref, outs_out, *scratch):
    scatter = SequenceScatter(rows_ref, rows_out, *scratch[:2], scratch[2:6], CHUNKS)
    weights = WeightScatter(parts_ref, out_ref, scratch[6:10], scratch[10:16])
    outs_sum = scratch[16]
    chip = ChipScatter(outs_ref, *scratch[17:20], scratch[20:24], PLANE)
    outs = SequenceScatter(outs_sum, outs_out, *scratch[24:26], scratch[26:], 1)
    d, c, x, core, z, y = place()
    greet(plane_peers(d, c) + chip_peers(d, c, x, core))
    places = (*near_first(z)[::-1], z)
    slots = [place * YS + 1 - y for place in places] + [place * YS + y for place in places]
    for j in slots:
        chip.start(j)
    weights.first()
    scatter.first()
    for j in slots:
        chip.relay(j)
    for off in range(1, PLANE + 1):
        weights.relay(off)
    for k in range(CHUNKS):
        scatter.relay(k)
    for off in range(1, PLANE + 1):
        weights.send(off)
    for i, j in enumerate(slots):
        chip.total(j, outs_sum.at[j])
        if i < ZS:
            outs.start(places[i], 0)
    outs.relay(0)
    for k in range(CHUNKS):
        scatter.last(k)
    weights.last()
    outs.last(0)
    scatter.finish()
    chip.finish()
    outs.finish()


def closing(rows, parts, outs):
    return pl.pallas_call(
        closing_kernel,
        out_shape=(
            jax.ShapeDtypeStruct(rows.shape[1:], jnp.float32),
            jax.ShapeDtypeStruct((PLANE, *parts.shape[1:]), parts.dtype),
            jax.ShapeDtypeStruct(outs.shape[1:], jnp.float32),
        ),
        in_specs=[VMEM] * 3,
        out_specs=(VMEM,) * 3,
        scratch_shapes=[
            *SequenceScatter.scratch(*rows.shape[1:], CHUNKS),
            *WeightScatter.scratch(*parts.shape[1:]),
            pltpu.VMEM((PLANE, *outs.shape[1:]), jnp.bfloat16),
            *ChipScatter.scratch(PLANE, *outs.shape[1:]),
            *SequenceScatter.scratch(*outs.shape[1:], 1),
        ],
        compiler_params=params(4),
        name="closing",
    )(rows, parts, outs)


def body(
    layer_in,
    positions,
    doc_starts,
    out_grad,
    norm_gains,
    norm_gains_m,
    norm_gains_v,
    w_query,
    w_query_m,
    w_query_v,
    key_value_weight,
    key_value_first_moment,
    key_value_second_moment,
    w_out,
    w_out_m,
    w_out_v,
    w_gate_up,
    w_gate_up_m,
    w_gate_up_v,
    w_down,
    w_down_m,
    w_down_v,
):
    number_of_tokens = layer_in.shape[0]
    ctx_count = lax.axis_size("ctx")
    seq_len = number_of_tokens * ctx_count
    key_value_width = KEY_VALUE_HEADS * HEAD_SIZE
    query_group_size = QUERY_HEADS // KEY_VALUE_HEADS
    score_scale = 1.0 / math.sqrt(HEAD_SIZE)
    needed = -(-512 // number_of_tokens)
    shard_span = min(ctx_count, 1 << max(0, (needed - 1).bit_length()))
    width_of_block = shard_span * number_of_tokens
    count_of_blocks = ctx_count // shard_span
    key_places = lax.all_gather(positions, "ctx", axis=0, tiled=True)
    starts = doc_starts[0]
    own_docs = doc_lookup(positions, starts)
    key_docs = doc_lookup(key_places, starts)
    query_full, keyval_full, out_full, gains_full = (
        lax.all_gather(w_query.astype(jnp.bfloat16), ("dp", "ctx"), axis=0, tiled=True),
        lax.all_gather(key_value_weight.astype(jnp.bfloat16), ("dp", "ctx"), axis=0, tiled=True),
        lax.all_gather(w_out.astype(jnp.bfloat16), ("dp", "ctx"), axis=0, tiled=True),
        lax.all_gather(norm_gains.astype(jnp.bfloat16), ("dp", "ctx"), axis=1, tiled=True),
    )
    gain_one = gains_full[0].astype(jnp.float32)
    gain_two = gains_full[1].astype(jnp.float32)
    layer_rows = layer_in.astype(jnp.float32)
    normed_one, inverse_one = norm_forward(layer_rows)
    input_one = (normed_one * gain_one).astype(jnp.bfloat16)
    query_pre = jnp.dot(input_one, query_full, preferred_element_type=jnp.float32)
    key_value_projected = jnp.dot(input_one, keyval_full, preferred_element_type=jnp.float32)
    cosine_table, sine_table = rope_tables(positions, HEAD_SIZE)
    query_rows = (
        apply_rotation(
            query_pre.reshape(number_of_tokens, QUERY_HEADS, HEAD_SIZE), cosine_table, sine_table
        )
        .astype(jnp.bfloat16)
        .reshape(number_of_tokens, KEY_VALUE_HEADS, query_group_size, HEAD_SIZE)
    )
    keys_own = (
        apply_rotation(
            key_value_projected[:, :key_value_width].reshape(
                number_of_tokens, KEY_VALUE_HEADS, HEAD_SIZE
            ),
            cosine_table,
            sine_table,
        )
        .astype(jnp.bfloat16)
        .reshape(number_of_tokens, key_value_width)
    )
    values_own = key_value_projected[:, key_value_width:].astype(jnp.bfloat16)
    every_key, every_value = (
        lax.all_gather(keys_own, "ctx", axis=0, tiled=True),
        lax.all_gather(values_own, "ctx", axis=0, tiled=True),
    )
    blocked_keys = every_key.reshape(count_of_blocks, width_of_block, KEY_VALUE_HEADS, HEAD_SIZE)
    blocked_values = every_value.reshape(
        count_of_blocks, width_of_block, KEY_VALUE_HEADS, HEAD_SIZE
    )
    place_blocks = key_places.reshape(count_of_blocks, width_of_block)
    doc_blocks = key_docs.reshape(count_of_blocks, width_of_block)

    def visible(place_blk, doc_blk):
        allowed = (place_blk[None, :] <= positions[:, None]) & (
            doc_blk[None, :] == own_docs[:, None]
        )
        return allowed[:, None, None, :]

    def scores_of(key_blk):
        return (
            jnp.einsum("tkgd,nkd->tkgn", query_rows, key_blk, preferred_element_type=jnp.float32)
            * score_scale
        )

    def stats_step(carry, block):
        row_top, row_total = carry
        key_blk, place_blk, doc_blk = block
        allowed = visible(place_blk, doc_blk)
        masked = jnp.where(allowed, scores_of(key_blk), masked_score)
        new_top = jnp.maximum(row_top, jnp.max(masked, axis=-1, keepdims=True))
        row_total = row_total * jnp.exp(row_top - new_top) + jnp.sum(
            jnp.where(allowed, jnp.exp(masked - new_top), 0.0), axis=-1, keepdims=True
        )
        return ((new_top, row_total), None)

    statistic_shape = (number_of_tokens, KEY_VALUE_HEADS, query_group_size, 1)
    (row_top, row_total), unused = lax.scan(
        stats_step,
        (
            jnp.full(statistic_shape, masked_score, jnp.float32),
            jnp.zeros(statistic_shape, jnp.float32),
        ),
        (blocked_keys, place_blocks, doc_blocks),
    )
    log_total = row_top + jnp.log(row_total)

    def probs_of(key_blk, place_blk, doc_blk):
        allowed = visible(place_blk, doc_blk)
        masked = jnp.where(allowed, scores_of(key_blk), masked_score)
        return jnp.where(allowed, jnp.exp(masked - log_total), 0.0)

    def output_step(carry, block):
        key_blk, value_blk, place_blk, doc_blk = block
        probs_low = probs_of(key_blk, place_blk, doc_blk).astype(jnp.bfloat16)
        added = jnp.einsum(
            "tkgn,nkd->tkgd", probs_low, value_blk, preferred_element_type=jnp.float32
        )
        return (carry + added, None)

    attention_output, unused = lax.scan(
        output_step,
        jnp.zeros((number_of_tokens, KEY_VALUE_HEADS, query_group_size, HEAD_SIZE), jnp.float32),
        (blocked_keys, blocked_values, place_blocks, doc_blocks),
    )
    mixed = attention_output.reshape(number_of_tokens, QUERY_HEADS * HEAD_SIZE).astype(jnp.bfloat16)
    middle = layer_rows + jnp.dot(mixed, out_full, preferred_element_type=jnp.float32)
    normed_two, inverse_two = norm_forward(middle)
    input_two = (normed_two * gain_two).astype(jnp.bfloat16)
    gate_up_low = w_gate_up.astype(jnp.bfloat16)
    down_low = w_down.astype(jnp.bfloat16)
    columns = input_two
    gate_up = jnp.dot(
        columns,
        lax.all_gather(gate_up_low, ("dp", "ctx"), axis=0, tiled=True),
        preferred_element_type=jnp.float32,
    )
    gate_part = gate_up[:, :FF]
    up_part = gate_up[:, FF:]
    sigmoid_gate = jax.nn.sigmoid(gate_part)
    silu_gate = gate_part * sigmoid_gate
    hidden = (silu_gate * up_part).astype(jnp.bfloat16)
    columns = hidden
    down_sum = jnp.dot(
        columns,
        lax.all_gather(down_low, ("dp", "ctx"), axis=0, tiled=True),
        preferred_element_type=jnp.float32,
    )
    layer_out = (middle + down_sum).astype(jnp.bfloat16)
    grad_rows = out_grad.astype(jnp.float32)
    grad_hidden = times_transposed(
        out_grad, lax.all_gather(down_low, ("dp", "ctx"), axis=0, tiled=True)
    )
    grad_gate = grad_hidden * up_part * sigmoid_gate * (1.0 + gate_part * (1.0 - sigmoid_gate))
    grad_up = grad_hidden * silu_gate
    grad_gate_up = jnp.concatenate([grad_gate, grad_up], axis=1).astype(jnp.bfloat16)
    down_grad = lax.psum_scatter(
        transposed_times(hidden, out_grad), ("dp", "ctx"), scatter_dimension=0, tiled=True
    )
    grad_normed_two = times_transposed(
        grad_gate_up, lax.all_gather(gate_up_low, ("dp", "ctx"), axis=0, tiled=True)
    )
    gate_up_grad = lax.psum_scatter(
        transposed_times(input_two, grad_gate_up), ("dp", "ctx"), scatter_dimension=0, tiled=True
    )
    grad_norm_two, gain_two_grad = norm_backward(grad_normed_two, normed_two, inverse_two, gain_two)
    grad_middle = grad_rows + grad_norm_two
    grad_middle_low = grad_middle.astype(jnp.bfloat16)
    out_term = transposed_times(mixed, grad_middle_low)
    grad_mixed = (
        times_transposed(grad_middle_low, out_full)
        .astype(jnp.bfloat16)
        .reshape(number_of_tokens, KEY_VALUE_HEADS, query_group_size, HEAD_SIZE)
    )
    delta = jnp.sum(grad_mixed.astype(jnp.float32) * attention_output, axis=-1, keepdims=True)

    def back_step(grad_query, block):
        key_blk, value_blk, place_blk, doc_blk = block
        probs = probs_of(key_blk, place_blk, doc_blk)
        probs_low = probs.astype(jnp.bfloat16)
        grad_probs = jnp.einsum(
            "tkgd,nkd->tkgn", grad_mixed, value_blk, preferred_element_type=jnp.float32
        )
        grad_scores = (probs * (grad_probs - delta) * score_scale).astype(jnp.bfloat16)
        grad_query = grad_query + jnp.einsum(
            "tkgn,nkd->tkgd", grad_scores, key_blk, preferred_element_type=jnp.float32
        )
        key_grad = jnp.einsum(
            "tkgn,tkgd->nkd", grad_scores, query_rows, preferred_element_type=jnp.float32
        )
        value_grad = jnp.einsum(
            "tkgn,tkgd->nkd", probs_low, grad_mixed, preferred_element_type=jnp.float32
        )
        return (grad_query, (key_grad, value_grad))

    grad_query, (key_grads, value_grads) = lax.scan(
        back_step,
        jnp.zeros((number_of_tokens, KEY_VALUE_HEADS, query_group_size, HEAD_SIZE), jnp.float32),
        (blocked_keys, blocked_values, place_blocks, doc_blocks),
    )
    summed_key_gradient, value_sum = (
        lax.psum_scatter(
            key_grads.reshape(seq_len, key_value_width).astype(jnp.bfloat16),
            "ctx",
            scatter_dimension=0,
            tiled=True,
        ).astype(jnp.float32),
        lax.psum_scatter(
            value_grads.reshape(seq_len, key_value_width).astype(jnp.bfloat16),
            "ctx",
            scatter_dimension=0,
            tiled=True,
        ).astype(jnp.float32),
    )
    key_gradient_unrotated = reverse_rotation(
        summed_key_gradient.reshape(number_of_tokens, KEY_VALUE_HEADS, HEAD_SIZE),
        cosine_table,
        sine_table,
    ).reshape(number_of_tokens, key_value_width)
    grad_keyval = jnp.concatenate([key_gradient_unrotated, value_sum], axis=1).astype(jnp.bfloat16)
    grad_query_low = (
        reverse_rotation(
            grad_query.reshape(number_of_tokens, QUERY_HEADS, HEAD_SIZE), cosine_table, sine_table
        )
        .reshape(number_of_tokens, QUERY_HEADS * HEAD_SIZE)
        .astype(jnp.bfloat16)
    )
    grad_normed_one = times_transposed(grad_query_low, query_full) + times_transposed(
        grad_keyval, keyval_full
    )
    query_term = transposed_times(input_one, grad_query_low)
    keyval_term = transposed_times(input_one, grad_keyval)
    grad_norm_one, gain_one_grad = norm_backward(grad_normed_one, normed_one, inverse_one, gain_one)
    in_grad = grad_middle + grad_norm_one
    gain_term = jnp.stack([gain_one_grad, gain_two_grad])
    query_grad, keyval_grad, out_weight_grad, gains_grad = (
        lax.psum_scatter(query_term, ("dp", "ctx"), scatter_dimension=0, tiled=True),
        lax.psum_scatter(keyval_term, ("dp", "ctx"), scatter_dimension=0, tiled=True),
        lax.psum_scatter(out_term, ("dp", "ctx"), scatter_dimension=0, tiled=True),
        lax.psum_scatter(gain_term, ("dp", "ctx"), scatter_dimension=1, tiled=True),
    )
    rates = rates_for(seq_len)
    gains_m_new, gains_v_new, gains_new = adamw(
        norm_gains, gains_grad, norm_gains_m, norm_gains_v, rates[0], 0.0
    )
    query_m_new, query_v_new, query_new = adamw(
        w_query, query_grad, w_query_m, w_query_v, rates[1], weight_decay
    )
    keyval_m_new, keyval_v_new, keyval_new = adamw(
        key_value_weight,
        keyval_grad,
        key_value_first_moment,
        key_value_second_moment,
        rates[2],
        weight_decay,
    )
    out_m_new, out_v_new, out_new = adamw(
        w_out, out_weight_grad, w_out_m, w_out_v, rates[3], weight_decay
    )
    gate_up_m_new, gate_up_v_new, gate_up_new = adamw(
        w_gate_up, gate_up_grad, w_gate_up_m, w_gate_up_v, rates[4], weight_decay
    )
    down_m_new, down_v_new, down_new = adamw(
        w_down, down_grad, w_down_m, w_down_v, rates[5], weight_decay
    )
    return (
        layer_out,
        in_grad,
        gains_grad,
        gains_m_new,
        gains_v_new,
        gains_new,
        query_grad,
        query_m_new,
        query_v_new,
        query_new,
        keyval_grad,
        keyval_m_new,
        keyval_v_new,
        keyval_new,
        out_weight_grad,
        out_m_new,
        out_v_new,
        out_new,
        gate_up_grad,
        gate_up_m_new,
        gate_up_v_new,
        gate_up_new,
        down_grad,
        down_m_new,
        down_v_new,
        down_new,
    )


def tensor_parallel(
    layer_in,
    positions,
    doc_starts,
    out_grad,
    norm_gains,
    norm_gains_m,
    norm_gains_v,
    w_query,
    w_query_m,
    w_query_v,
    key_value_weight,
    key_value_first_moment,
    key_value_second_moment,
    w_out,
    w_out_m,
    w_out_v,
    w_gate_up,
    w_gate_up_m,
    w_gate_up_v,
    w_down,
    w_down_m,
    w_down_v,
):
    low = jnp.bfloat16
    own_tokens, width = layer_in.shape
    seq_len = own_tokens * PLANE
    group = GROUP
    group_width = group * HEAD_SIZE
    ff_part = FF // PLANE
    ff_own = FF // RANKS
    rows = w_query.shape[0]

    gains_low = norm_gains.astype(low)
    small = jnp.broadcast_to(
        jnp.pad(gains_low.T, ((0, 0), (0, 126)))[None], (PLANE, rows, 128)
    )
    attention_blocks = jnp.concatenate(
        [
            w_query.astype(low).reshape(rows, PLANE, group_width).transpose(1, 0, 2),
            key_value_weight.astype(low)
            .reshape(rows, 2, PLANE, HEAD_SIZE)
            .transpose(2, 0, 1, 3)
            .reshape(PLANE, rows, 2 * HEAD_SIZE),
            small,
        ],
        axis=2,
    )
    feed_blocks = (
        w_gate_up.astype(low)
        .reshape(rows, 2, 4, PLANE, ff_own)
        .transpose(3, 0, 1, 2, 4)
        .reshape(PLANE, rows, 2 * ff_part)
    )
    spots = jnp.broadcast_to(positions[None, :].astype(jnp.float32), (8, own_tokens))
    cosine_own, sine_own = rope_tables(positions, HEAD_SIZE)
    cosine_own, sine_own = cosine_own[:, 0], sine_own[:, 0]
    table = jnp.concatenate([cosine_own, cosine_own, -sine_own, sine_own], axis=1)
    qkv_width = QKV_WIDTH
    (
        input_one_all,
        table_all,
        attention_all,
        gain_rows,
        query_rows,
        key_rows,
        value_rows,
        token_spots,
        token_starts,
        key_spots,
        mixed_parts,
        feed_all,
        out_all,
        down_all,
        grads_all,
    ) = attention(
        doc_starts,
        layer_in,
        table,
        spots,
        attention_blocks,
        feed_blocks,
        w_out.astype(low),
        w_down.astype(low).reshape(DOWN_PARTS, -1, width),
        out_grad,
    )
    gain_one, gain_two = gain_rows[0], gain_rows[1]
    input_one = input_one_all.reshape(seq_len, width)
    qkv_weight = attention_all.reshape(width, -1)[:, :qkv_width]
    cosine_table = table_all[:, :, : HEAD_SIZE // 2].reshape(seq_len, 1, -1)
    sine_table = table_all[:, :, 3 * HEAD_SIZE // 2 :].reshape(seq_len, 1, -1)
    mixed = mixed_parts.transpose(2, 0, 1, 3).reshape(own_tokens, width)
    out_weight = out_all.reshape(width, width)
    branch = jnp.dot(mixed, out_weight, preferred_element_type=jnp.float32)

    layer_rows = layer_in.astype(jnp.float32)
    middle = layer_rows + branch
    normed_two, inverse_two = norm_forward(middle)
    grad_normed_two, down_sum, feed_term, down_term = feed(
        (normed_two * gain_two).astype(low),
        grads_all,
        feed_all.reshape(width, 2 * ff_part),
        down_all.reshape(ff_part, width),
    )
    layer_out = (middle + down_sum).astype(low)

    grad_norm_two, unused = norm_backward(grad_normed_two, normed_two, inverse_two, gain_two)
    grad_middle = out_grad.astype(jnp.float32) + grad_norm_two
    grad_middle_low = grad_middle.astype(low)
    out_term = transposed_times(mixed, grad_middle_low).astype(low)
    grad_mixed = (
        times_transposed(grad_middle_low, out_weight)
        .astype(low)
        .reshape(own_tokens, PLANE, PAIRS, 2 * HEAD_SIZE)
        .transpose(1, 2, 0, 3)
    )
    grad_query, grad_key, grad_value, feed_grad, down_grad = attention_back(
        query_rows,
        key_rows,
        value_rows,
        token_spots,
        token_starts,
        key_spots,
        grad_mixed,
        feed_term.reshape(RANKS, rows, 2 * ff_part),
        down_term.reshape(4 * DOWN_PARTS, -1, width),
    )
    gate_up_grad = (
        feed_grad.reshape(PLANE, rows, 2, 4, ff_own)
        .transpose(1, 2, 3, 0, 4)
        .reshape(rows, 2 * FF)
        .astype(jnp.float32)
    )
    down_grad = down_grad.reshape(w_down.shape)
    grad_query = grad_query.transpose(0, 3, 1, 2, 4).reshape(seq_len, group, HEAD_SIZE)
    grad_qkv = jnp.concatenate(
        [
            reverse_rotation(grad_query, cosine_table, sine_table).reshape(seq_len, group_width),
            reverse_rotation(grad_key[:, None], cosine_table, sine_table)[:, 0],
            grad_value,
        ],
        axis=1,
    ).astype(low)
    one_parts = times_transposed(grad_qkv, qkv_weight).astype(low)
    qkv_term = transposed_times(input_one, grad_qkv).astype(low)
    grad_normed_one, qkv_grad, out_weight_grad = closing(
        one_parts.reshape(PLANE, own_tokens, width),
        qkv_term.reshape(RANKS, rows, qkv_width),
        out_term.reshape(RANKS, rows, width),
    )
    normed_one, inverse_one = norm_forward(layer_rows)
    grad_norm_one, unused = norm_backward(grad_normed_one, normed_one, inverse_one, gain_one)
    in_grad = grad_middle + grad_norm_one
    qkv_grad = qkv_grad.astype(jnp.float32)
    query_grad = qkv_grad[:, :, :group_width].transpose(1, 0, 2).reshape(w_query.shape)
    keyval_grad = (
        qkv_grad[:, :, group_width:]
        .reshape(PLANE, rows, 2, HEAD_SIZE)
        .transpose(1, 2, 0, 3)
        .reshape(key_value_weight.shape)
    )
    def low_times(weight, grad):
        return jnp.sum(weight.astype(low).astype(jnp.float32) * grad, axis=1)

    gains_grad = jnp.stack(
        [
            low_times(w_query, query_grad) + low_times(key_value_weight, keyval_grad),
            low_times(w_gate_up, gate_up_grad),
        ]
    ) / gains_low.astype(jnp.float32)

    rates = rates_for(seq_len)
    return (
        layer_out,
        in_grad,
        gains_grad,
        *adamw(norm_gains, gains_grad, norm_gains_m, norm_gains_v, rates[0], 0.0),
        query_grad,
        *adamw(w_query, query_grad, w_query_m, w_query_v, rates[1], weight_decay),
        keyval_grad,
        *adamw(
            key_value_weight,
            keyval_grad,
            key_value_first_moment,
            key_value_second_moment,
            rates[2],
            weight_decay,
        ),
        out_weight_grad,
        *adamw(w_out, out_weight_grad, w_out_m, w_out_v, rates[3], weight_decay),
        gate_up_grad,
        *adamw(w_gate_up, gate_up_grad, w_gate_up_m, w_gate_up_v, rates[4], weight_decay),
        down_grad,
        *adamw(w_down, down_grad, w_down_m, w_down_v, rates[5], weight_decay),
    )


def solution(mesh):
    planned = tensor_parallel if dict(mesh.shape) == {"dp": 2 * XS, "ctx": ZS * YS} else body
    return jax.shard_map(
        planned,
        mesh=mesh,
        in_specs=(
            P(("dp", "ctx"), None),
            P(("dp", "ctx")),
            P("dp", None),
            P(("dp", "ctx"), None),
            P(None, ("dp", "ctx")),
            P(None, ("dp", "ctx")),
            P(None, ("dp", "ctx")),
            P(("dp", "ctx"), None),
            P(("dp", "ctx"), None),
            P(("dp", "ctx"), None),
            P(("dp", "ctx"), None),
            P(("dp", "ctx"), None),
            P(("dp", "ctx"), None),
            P(("dp", "ctx"), None),
            P(("dp", "ctx"), None),
            P(("dp", "ctx"), None),
            P(("dp", "ctx"), None),
            P(("dp", "ctx"), None),
            P(("dp", "ctx"), None),
            P(("dp", "ctx"), None),
            P(("dp", "ctx"), None),
            P(("dp", "ctx"), None),
        ),
        out_specs=(
            P(("dp", "ctx"), None),
            P(("dp", "ctx"), None),
            P(None, ("dp", "ctx")),
            P(None, ("dp", "ctx")),
            P(None, ("dp", "ctx")),
            P(None, ("dp", "ctx")),
            P(("dp", "ctx"), None),
            P(("dp", "ctx"), None),
            P(("dp", "ctx"), None),
            P(("dp", "ctx"), None),
            P(("dp", "ctx"), None),
            P(("dp", "ctx"), None),
            P(("dp", "ctx"), None),
            P(("dp", "ctx"), None),
            P(("dp", "ctx"), None),
            P(("dp", "ctx"), None),
            P(("dp", "ctx"), None),
            P(("dp", "ctx"), None),
            P(("dp", "ctx"), None),
            P(("dp", "ctx"), None),
            P(("dp", "ctx"), None),
            P(("dp", "ctx"), None),
            P(("dp", "ctx"), None),
            P(("dp", "ctx"), None),
            P(("dp", "ctx"), None),
            P(("dp", "ctx"), None),
        ),
        check_vma=False,
    )
```

```python
import functools
import math

import jax
import jax.numpy as jnp
from jax import lax
from jax.experimental import pallas as pl
from jax.experimental.pallas import tpu as pltpu
from jax.sharding import PartitionSpec as P

MODEL_WIDTH = 2048
QUERY_HEADS = 32
KEY_VALUE_HEADS = 8
HEAD_SIZE = 64
FF = 8192
STEP = 10


eps_norm = 1e-05
rope_base = 500000.0
beta_one = 0.9
beta_two = 0.95
eps_adam = 1e-08
weight_decay = 0.1
masked_score = -1e30


def rates_for(seq_len):
    return (
        0.6,
        0.8 / math.sqrt(MODEL_WIDTH // 4),
        0.8 / math.sqrt(MODEL_WIDTH),
        0.8 / math.sqrt(max(220 * MODEL_WIDTH // seq_len, 1)),
        0.8 / math.sqrt(MODEL_WIDTH),
        0.8 / math.sqrt(FF // 2),
    )


def adamw(weight, grad_sum, first, second, rate, decay):
    first_new = beta_one * first + (1.0 - beta_one) * grad_sum
    second_new = beta_two * second + (1.0 - beta_two) * grad_sum * grad_sum
    first_hat = first_new / (1.0 - beta_one**STEP)
    second_hat = second_new / (1.0 - beta_two**STEP)
    weight_new = weight - rate * (first_hat / (jnp.sqrt(second_hat) + eps_adam) + decay * weight)
    return (first_new, second_new, weight_new)


def norm_forward(layer_rows):
    inverse = lax.rsqrt(jnp.mean(layer_rows * layer_rows, axis=-1, keepdims=True) + eps_norm)
    return (layer_rows * inverse, inverse)


def norm_backward(grad_out, normed, inverse, gain_row):
    scaled = grad_out * gain_row
    grad_in = inverse * (scaled - normed * jnp.mean(scaled * normed, axis=-1, keepdims=True))
    return (grad_in, jnp.sum(grad_out * normed, axis=0))


def rope_tables(token_placement, head_dim):
    half_dim = head_dim // 2
    frequencies = jnp.exp(
        jnp.arange(half_dim, dtype=jnp.float32) * (-2.0 * math.log(rope_base) / head_dim)
    )
    angles = token_placement.astype(jnp.float32)[:, None] * frequencies[None, :]
    return (jnp.cos(angles)[:, None, :], jnp.sin(angles)[:, None, :])


def apply_rotation(value_rows, cosine_table, sine_table):
    half_dim = value_rows.shape[-1] // 2
    first_half = value_rows[..., :half_dim]
    second_half = value_rows[..., half_dim:]
    return jnp.concatenate(
        [
            first_half * cosine_table - second_half * sine_table,
            second_half * cosine_table + first_half * sine_table,
        ],
        axis=-1,
    )


def reverse_rotation(grad_rows, cosine_table, sine_table):
    half_dim = grad_rows.shape[-1] // 2
    first_half = grad_rows[..., :half_dim]
    second_half = grad_rows[..., half_dim:]
    return jnp.concatenate(
        [
            first_half * cosine_table + second_half * sine_table,
            second_half * cosine_table - first_half * sine_table,
        ],
        axis=-1,
    )


def doc_lookup(token_placement, starts):
    return jnp.sum((token_placement[:, None] >= starts[None, :]).astype(jnp.int32), axis=1) - 1


def times_transposed(left, right):
    return lax.dot_general(
        left, right, (((1,), (1,)), ((), ())), preferred_element_type=jnp.float32
    )


def transposed_times(left, right):
    return lax.dot_general(
        left, right, (((0,), (0,)), ((), ())), preferred_element_type=jnp.float32
    )


XS = 2
YS = 2
ZS = 4
PLANE = ZS * YS
RANKS = 2 * XS * PLANE
MESH = pl.DeviceIdType.MESH


def place():
    d = lax.axis_index("dp")
    c = lax.axis_index("ctx")
    return d, c, lax.div(d, 2), lax.rem(d, 2), lax.div(c, YS), lax.rem(c, YS)


def remote(src, dst, send_sem, recv_sem, d, c):
    return pltpu.make_async_remote_copy(
        src_ref=src,
        dst_ref=dst,
        send_sem=send_sem,
        recv_sem=recv_sem,
        device_id=(d, c),
        device_id_type=MESH,
    )


def greet(peers):
    barrier = pltpu.get_barrier_semaphore()
    for d, c in peers:
        pl.semaphore_signal(barrier, inc=1, device_id=(d, c), device_id_type=MESH)
    pl.semaphore_wait(barrier, len(peers))


def plane_peers(d, c):
    return [(d, lax.rem(c + k, PLANE)) for k in range(1, PLANE)]


def chip_peers(d, c, x, core):
    return [(x * 2 + 1 - core, c), ((1 - x) * 2 + core, c)]


def add_into(target, sources, rows, step=16):
    @pl.loop(0, rows, step=step)
    def _(r):
        at = pl.ds(pl.multiple_of(r, step), step)
        total = sources[0][at].astype(jnp.float32)
        for source in sources[1:]:
            total = total + source[at].astype(jnp.float32)
        target[at] = total.astype(target.dtype)


def near_first(z):
    half = lax.div(z, 2)
    return [half * 4 + 1 - z, 2 - half, 3 - 3 * half]


class SequenceGather:
    def __init__(self, own, out, sems, chunks):
        self.own, self.out, self.chunks = own, out, chunks
        self.zs, self.zr, self.ys, self.yr, self.local_sem = sems
        self.d, self.c, _, _, self.z, self.y = place()
        self.rows = own.shape[0] // chunks
        self.sent = []

    @staticmethod
    def scratch(chunks):
        return [
            pltpu.SemaphoreType.DMA((ZS, chunks)),
            pltpu.SemaphoreType.DMA((ZS, chunks)),
            pltpu.SemaphoreType.DMA((ZS, chunks)),
            pltpu.SemaphoreType.DMA((ZS, chunks)),
            pltpu.SemaphoreType.DMA(()),
        ]

    def part(self, ref, k):
        return ref.at[pl.ds(k * self.rows, self.rows)]

    def across(self, z, k, src):
        slot = z * YS + self.y
        return remote(
            src,
            self.part(self.out.at[slot], k),
            self.ys.at[z, k],
            self.yr.at[z, k],
            self.d,
            self.z * YS + 1 - self.y,
        )

    def along(self, to, k):
        return remote(
            self.part(self.own, k),
            self.part(self.out.at[self.c], k),
            self.zs.at[to, k],
            self.zr.at[self.z, k],
            self.d,
            to * YS + self.y,
        )

    def start(self, copy):
        copy.start()
        self.sent.append(copy)

    def first(self, by_block=False):
        self.local = pltpu.make_async_copy(self.own, self.out.at[self.c], self.local_sem)
        self.local.start()
        near = near_first(self.z)
        if by_block:
            for k in range(self.chunks):
                self.start(self.across(self.z, k, self.part(self.own, k)))
            for to in near:
                for k in range(self.chunks):
                    self.start(self.along(to, k))
            return
        for k in range(self.chunks):
            for to in near[::-1]:
                self.start(self.along(to, k))
            self.start(self.across(self.z, k, self.part(self.own, k)))

    def relay_one(self, source, k):
        slot = source * YS + self.y
        block = self.part(self.out.at[slot], k)
        remote(
            block, block, self.zs.at[source, k], self.zr.at[source, k], self.d, slot
        ).wait_recv()
        self.start(self.across(source, k, block))

    def relay(self, k):
        for source in near_first(self.z):
            self.relay_one(source, k)

    def relay_block(self, source):
        for k in range(self.chunks):
            self.relay_one(source, k)

    def arrive_across(self, z):
        for k in range(self.chunks):
            block = self.part(self.out.at[z * YS + 1 - self.y], k)
            remote(
                block,
                block,
                self.ys.at[z, k],
                self.yr.at[z, k],
                self.d,
                self.z * YS + 1 - self.y,
            ).wait_recv()

    def finish(self):
        for copy in self.sent:
            copy.wait_send()

    def last(self):
        for z in range(ZS):
            self.arrive_across(z)
        self.finish()
        self.local.wait()


class SequenceScatter:
    def __init__(self, parts, out, ybuf, zbuf, sems, chunks):
        self.parts, self.out, self.chunks = parts, out, chunks
        self.ybuf, self.zbuf = ybuf, zbuf
        self.ys, self.yr, self.zs, self.zr = sems
        self.d, self.c, _, _, self.z, self.y = place()
        self.rows = parts.shape[1] // chunks
        self.sent = []

    @staticmethod
    def scratch(rows, width, chunks):
        return [
            pltpu.VMEM((ZS, rows, width), jnp.bfloat16),
            pltpu.VMEM((ZS, rows, width), jnp.bfloat16),
            pltpu.SemaphoreType.DMA((ZS, chunks)),
            pltpu.SemaphoreType.DMA((ZS, chunks)),
            pltpu.SemaphoreType.DMA((ZS, chunks)),
            pltpu.SemaphoreType.DMA((ZS, chunks)),
        ]

    def span(self, k):
        return pl.ds(k * self.rows, self.rows)

    def across(self, z, k):
        return remote(
            self.parts.at[z * YS + 1 - self.y, self.span(k)],
            self.ybuf.at[z, self.span(k)],
            self.ys.at[z, k],
            self.yr.at[z, k],
            self.d,
            self.z * YS + 1 - self.y,
        )

    def along(self, to, k):
        return remote(
            self.ybuf.at[to, self.span(k)],
            self.zbuf.at[self.z, self.span(k)],
            self.zs.at[to, k],
            self.zr.at[self.z, k],
            self.d,
            to * YS + self.y,
        )

    def start(self, z, k):
        copy = self.across(z, k)
        copy.start()
        self.sent.append(copy)

    def first(self):
        for k in range(self.chunks):
            for z in (*near_first(self.z)[::-1], self.z):
                self.start(z, k)

    def relay_one(self, z, k):
        self.across(z, k).wait_recv()
        block = self.ybuf.at[z, self.span(k)]
        add_into(block, [self.parts.at[z * YS + self.y, self.span(k)], block], self.rows)
        copy = self.along(z, k)
        copy.start()
        self.sent.append(copy)

    def relay(self, k):
        for z in near_first(self.z)[::-1]:
            self.relay_one(z, k)

    def last(self, k):
        self.across(self.z, k).wait_recv()
        blocks = [self.parts.at[self.c, self.span(k)], self.ybuf.at[self.z, self.span(k)]]
        for source in near_first(self.z):
            block = self.zbuf.at[source, self.span(k)]
            remote(
                block,
                block,
                self.zs.at[source, k],
                self.zr.at[source, k],
                self.d,
                source * YS + self.y,
            ).wait_recv()
            blocks.append(block)
        add_into(self.out.at[self.span(k)], blocks, self.rows)

    def finish(self):
        for copy in self.sent:
            copy.wait_send()


class ChipGather:
    def __init__(self, out, sems, count, rows=None):
        self.out, self.count, self.rows = out, count, rows
        self.cs, self.cr, self.xs, self.xr = sems
        self.d, self.c, self.x, self.core, _, _ = place()
        self.sent = []

    @staticmethod
    def scratch(count):
        return [
            pltpu.SemaphoreType.DMA((2, count)),
            pltpu.SemaphoreType.DMA((2, count)),
            pltpu.SemaphoreType.DMA((count,)),
            pltpu.SemaphoreType.DMA((count,)),
        ]

    def block(self, slot):
        if self.rows is None:
            return self.out.at[slot]
        return self.out.at[pl.ds(slot * self.rows, self.rows)]

    def to_core(self, far, j, src=None):
        x = 1 - self.x if far else self.x
        block = self.block((x * 2 + self.core) * self.count + j)
        return remote(
            block if src is None else src,
            block,
            self.cs.at[far, j],
            self.cr.at[far, j],
            self.x * 2 + 1 - self.core,
            self.c,
        )

    def to_x(self, j, src=None):
        block = self.block(self.d * self.count + j)
        return remote(
            block if src is None else src,
            block,
            self.xs.at[j],
            self.xr.at[j],
            (1 - self.x) * 2 + self.core,
            self.c,
        )

    def start(self, j, src=None):
        for copy in (self.to_x(j, src), self.to_core(0, j, src)):
            copy.start()
            self.sent.append(copy)

    def relay(self, j):
        self.to_x(j).wait_recv()
        copy = self.to_core(1, j)
        copy.start()
        self.sent.append(copy)

    def last(self):
        for far in (0, 1):
            for j in range(self.count):
                self.to_core(far, j).wait_recv()
        for copy in self.sent:
            copy.wait_send()


class WeightGather:
    def __init__(self, blocks, out, sems):
        self.blocks, self.out = blocks, out
        self.ps, self.pr, self.local_sem = sems[:3]
        self.chip = ChipGather(out, sems[3:], PLANE)
        self.d, self.c = self.chip.d, self.chip.c
        self.sent = []

    @staticmethod
    def scratch():
        return [
            pltpu.SemaphoreType.DMA((PLANE,)),
            pltpu.SemaphoreType.DMA((PLANE,)),
            pltpu.SemaphoreType.DMA(()),
        ] + ChipGather.scratch(PLANE)

    def send(self, off):
        to = lax.rem(self.c + off, PLANE)
        copy = remote(
            self.blocks.at[to],
            self.out.at[self.d * PLANE + self.c],
            self.ps.at[off],
            self.pr.at[self.c],
            self.d,
            to,
        )
        copy.start()
        self.sent.append(copy)

    def first(self, ahead=PLANE - 1):
        self.ahead = ahead
        self.local = pltpu.make_async_copy(
            self.blocks.at[self.c], self.out.at[self.d * PLANE + self.c], self.local_sem
        )
        self.local.start()
        for off in range(1, 1 + ahead):
            self.send(off)
        self.chip.start(self.c, self.blocks.at[self.c])

    def relay(self, off):
        if off + self.ahead < PLANE:
            self.send(off + self.ahead)
        source = lax.rem(self.c + PLANE - off, PLANE)
        block = self.out.at[self.d * PLANE + source]
        remote(
            block, block, self.ps.at[off], self.pr.at[source], self.d, source
        ).wait_recv()
        self.chip.start(source)

    def relay_chip(self):
        for off in range(PLANE):
            self.chip.relay(lax.rem(self.c + off, PLANE))

    def last(self):
        self.chip.last()
        for copy in self.sent:
            copy.wait_send()
        self.local.wait()


class ChipScatter:
    def __init__(self, parts, cbuf, stage, xbuf, sems, count):
        self.parts, self.count = parts, count
        self.cbuf, self.stage, self.xbuf = cbuf, stage, xbuf
        self.cs, self.cr, self.xs, self.xr = sems
        self.d, self.c, self.x, self.core, _, _ = place()
        self.sent = []

    @staticmethod
    def scratch(count, rows, width):
        return [
            pltpu.VMEM((2, count, rows, width), jnp.bfloat16),
            pltpu.VMEM((count, rows, width), jnp.bfloat16),
            pltpu.VMEM((count, rows, width), jnp.bfloat16),
            pltpu.SemaphoreType.DMA((2, count)),
            pltpu.SemaphoreType.DMA((2, count)),
            pltpu.SemaphoreType.DMA((count,)),
            pltpu.SemaphoreType.DMA((count,)),
        ]

    def to_core(self, far, j):
        x = 1 - self.x if far else self.x
        return remote(
            self.parts.at[(x * 2 + 1 - self.core) * self.count + j],
            self.cbuf.at[far, j],
            self.cs.at[far, j],
            self.cr.at[far, j],
            self.x * 2 + 1 - self.core,
            self.c,
        )

    def to_x(self, j):
        return remote(
            self.stage.at[j],
            self.xbuf.at[j],
            self.xs.at[j],
            self.xr.at[j],
            (1 - self.x) * 2 + self.core,
            self.c,
        )

    def start(self, j):
        for far in (1, 0):
            copy = self.to_core(far, j)
            copy.start()
            self.sent.append(copy)

    def relay(self, j):
        self.to_core(1, j).wait_recv()
        own = self.parts.at[((1 - self.x) * 2 + self.core) * self.count + j]
        add_into(self.stage.at[j], [own, self.cbuf.at[1, j]], own.shape[0])
        copy = self.to_x(j)
        copy.start()
        self.sent.append(copy)

    def total(self, j, target):
        self.to_core(0, j).wait_recv()
        self.to_x(j).wait_recv()
        own = self.parts.at[self.d * self.count + j]
        add_into(target, [own, self.cbuf.at[0, j], self.xbuf.at[j]], own.shape[0])

    def finish(self):
        for copy in self.sent:
            copy.wait_send()


class WeightScatter:
    def __init__(self, parts, out, bufs, sems):
        self.stage = bufs[0]
        self.ps, self.pr = sems[:2]
        self.chip = ChipScatter(parts, *bufs[1:], sems[2:], PLANE)
        self.out = out
        self.d, self.c = self.chip.d, self.chip.c
        self.sent = []

    @staticmethod
    def scratch(rows, width):
        chip = ChipScatter.scratch(PLANE, rows, width)
        return [
            pltpu.VMEM((PLANE, rows, width), jnp.bfloat16),
            *chip[:3],
            pltpu.SemaphoreType.DMA((PLANE,)),
            pltpu.SemaphoreType.DMA((PLANE,)),
            *chip[3:],
        ]

    def first(self):
        for off in range(1, PLANE + 1):
            self.chip.start(lax.rem(self.c + off, PLANE))

    def relay(self, off):
        self.chip.relay(lax.rem(self.c + off, PLANE))

    def send(self, off):
        to = lax.rem(self.c + off, PLANE)
        if off == PLANE:
            self.chip.total(to, self.out.at[self.c])
            return
        self.chip.total(to, self.stage.at[to])
        copy = remote(
            self.stage.at[to],
            self.out.at[self.c],
            self.ps.at[off],
            self.pr.at[self.c],
            self.d,
            to,
        )
        copy.start()
        self.sent.append(copy)

    def last(self):
        for off in range(1, PLANE):
            source = lax.rem(self.c + off, PLANE)
            block = self.out.at[source]
            remote(
                block, block, self.ps.at[off], self.pr.at[source], self.d, source
            ).wait_recv()
        for copy in self.sent:
            copy.wait_send()
        self.chip.finish()


def params(collective_id, mebibytes=56):
    return pltpu.CompilerParams(
        collective_id=collective_id, has_side_effects=True, vmem_limit_bytes=mebibytes * 2**20
    )


ANY = pl.BlockSpec(memory_space=pl.ANY)
VMEM = pl.BlockSpec(memory_space=pltpu.VMEM)
CHUNKS = 4


DOWN_PARTS = 4
SCORE_SCALE = 1.0 / math.sqrt(HEAD_SIZE)
GROUP = QUERY_HEADS // KEY_VALUE_HEADS
PAIRS = GROUP // 2


def times_rows(left, right):
    return lax.dot_general(
        left, right, (((1,), (1,)), ((), ())), preferred_element_type=jnp.float32
    )


class PlaneExchange:
    def __init__(self, blocks, out, sems):
        self.blocks, self.out = blocks, out
        self.ps, self.pr, self.local_sem = sems
        self.d, self.c = lax.axis_index("dp"), lax.axis_index("ctx")
        self.sent = []

    @staticmethod
    def scratch():
        return [
            pltpu.SemaphoreType.DMA((PLANE,)),
            pltpu.SemaphoreType.DMA((PLANE,)),
            pltpu.SemaphoreType.DMA(()),
        ]

    def send(self, off):
        to = lax.rem(self.c + off, PLANE)
        if off % PLANE == 0:
            self.local = pltpu.make_async_copy(
                self.blocks.at[to], self.out.at[self.c], self.local_sem
            )
            self.local.start()
            return
        copy = remote(
            self.blocks.at[to],
            self.out.at[self.c],
            self.ps.at[off],
            self.pr.at[self.c],
            self.d,
            to,
        )
        copy.start()
        self.sent.append(copy)

    def arrive(self, off):
        if off % PLANE == 0:
            self.local.wait()
            return
        source = lax.rem(self.c + PLANE - off, PLANE)
        block = self.out.at[source]
        remote(
            block, block, self.ps.at[off], self.pr.at[source], self.d, source
        ).wait_recv()

    def finish(self):
        for copy in self.sent:
            copy.wait_send()


def probabilities(query, keys, spot, start, key_spots):
    scores = times_rows(query, keys) * SCORE_SCALE
    masked = jnp.where((key_spots <= spot) & (key_spots >= start), scores, masked_score)
    exponent = jnp.exp(masked - jnp.max(masked, axis=-1, keepdims=True))
    return exponent * (1.0 / jnp.sum(exponent, axis=-1, keepdims=True))


def rotate(value, table, back=False):
    lane = lax.broadcasted_iota(jnp.int32, value.shape, 1)
    turned = pltpu.roll(table, HEAD_SIZE, 1)
    cosine = jnp.where(lane < HEAD_SIZE, table, turned)
    sine = jnp.where(lane < HEAD_SIZE, turned, table)
    half = HEAD_SIZE // 2
    other = jnp.where(
        lax.rem(lane, HEAD_SIZE) < half,
        pltpu.roll(value, 2 * HEAD_SIZE - half, 1),
        pltpu.roll(value, half, 1),
    )
    if back:
        return value * cosine - other * sine
    return value * cosine + other * sine


QKV_WIDTH = (GROUP + 2) * HEAD_SIZE


def wide_columns(width):
    run = width // (8 * PLANE)
    for to in range(PLANE):
        for part in range(8):
            yield to, part * run, (part * PLANE + to) * run


def attention_kernel(
    starts_ref,
    rows_ref,
    table_ref,
    spots_ref,
    qkv_ref,
    blocks_ref,
    out_rows_ref,
    down_ref,
    grads_ref,
    input_out,
    table_out,
    qkv_out,
    gains_out,
    query_out,
    key_out,
    value_out,
    spot_out,
    start_out,
    key_spot_out,
    mixed_out,
    blocks_out,
    out_rows_out,
    down_out,
    grads_out,
    *scratch,
):
    mixed_stage, spots_all, rows_all, wide_full, wide_blocks = scratch[:5]
    down_full, down_blocks, out_full, out_block, load_sem = scratch[5:10]
    scratch = list(scratch[10:])

    def take(count):
        taken, scratch[:count] = scratch[:count], []
        return taken

    d, c, x, core, z, y = place()
    exchange = PlaneExchange(mixed_stage, mixed_out, take(3))
    qkv = WeightGather(qkv_ref, qkv_out, take(7))
    weights = WeightGather(wide_blocks, blocks_out, take(7))
    outs = SequenceGather(out_block, out_rows_out.at[pl.ds(d * PLANE, PLANE)], take(5), 1)
    outs_chip = ChipGather(out_rows_out, take(4), PLANE)
    rows = SequenceGather(rows_ref, rows_all, take(5), 2)
    table = SequenceGather(table_ref, table_out, take(5), 1)
    grads = SequenceGather(grads_ref, grads_out, take(5), CHUNKS)
    down_rows = down_ref.shape[0] // DOWN_PARTS
    down = ChipGather(down_out, take(4), DOWN_PARTS, down_rows)
    spot_send, spot_recv, spot_local, down_local = take(4)
    greet(plane_peers(d, c) + chip_peers(d, c, x, core))
    order = near_first(z)

    loads = [
        pltpu.make_async_copy(source, target, load_sem.at[i])
        for i, (source, target) in enumerate(
            [(out_rows_ref, out_full), (down_ref, down_full), (blocks_ref, wide_full)]
        )
    ]
    for load in loads:
        load.start()
    qkv.first()
    spots_own = pltpu.make_async_copy(spots_ref, spots_all.at[c], spot_local)
    spots_own.start()
    spots_sent = []
    for off in range(1, PLANE):
        to = lax.rem(c + off, PLANE)
        copy = remote(
            spots_ref, spots_all.at[c], spot_send.at[off], spot_recv.at[c], d, to
        )
        copy.start()
        spots_sent.append(copy)
    table.first()
    rows.first(by_block=True)
    loads[1].wait()

    @pl.loop(0, down_full.shape[0], step=16)
    def _(r):
        at = pl.ds(pl.multiple_of(r, 16), 16)
        down_blocks[at] = down_full[at].astype(jnp.bfloat16)

    down_own = pltpu.make_async_copy(
        down_blocks, down_out.at[pl.ds(d * down_full.shape[0], down_full.shape[0])], down_local
    )
    down_own.start()
    for j in range(DOWN_PARTS):
        down.start(j, down_blocks.at[pl.ds(j * down_rows, down_rows)])
    loads[0].wait()
    out_block[...] = out_full[...].astype(jnp.bfloat16)
    outs.first()
    outs_chip.start(c, out_block)
    loads[2].wait()

    @pl.loop(0, wide_full.shape[0], step=16)
    def _(r):
        at = pl.ds(pl.multiple_of(r, 16), 16)
        for to, start, after in wide_columns(wide_full.shape[1]):
            size = wide_full.shape[1] // (8 * PLANE)
            wide_blocks[to, at, start : start + size] = wide_full[
                at, after : after + size
            ].astype(jnp.bfloat16)

    for off in range(1, PLANE):
        qkv.relay(off)
    table.relay(0)
    rows.relay_block(order[0])
    qkv.relay_chip()
    rows.relay_block(order[1])
    rows.relay_block(order[2])
    weights.first()
    for off in range(1, PLANE):
        source = lax.rem(c + off, PLANE)
        block = spots_all.at[source]
        remote(block, block, spot_send.at[off], spot_recv.at[source], d, source).wait_recv()
    spots_own.wait()
    table.last()
    for slot in range(PLANE):
        key_spot_out[:, slot * 128 : (slot + 1) * 128] = spots_all[slot]
        spot = jnp.broadcast_to(spots_all[slot][:1], (128, 128)).T[:, :1]
        start = jnp.zeros_like(spot)
        for doc in range(starts_ref.shape[1]):
            first = starts_ref[0, doc].astype(jnp.float32)
            start = jnp.maximum(start, jnp.where(spot >= first, first, 0.0))
        spot_out[slot] = spot
        start_out[slot] = start
    qkv.last()
    for pair in range(RANKS // 2):
        columns = qkv_out[2 * pair : 2 * pair + 2, :, QKV_WIDTH:]
        turned = columns.reshape(128, 128).astype(jnp.float32).T
        gains_out[:, pair * 128 : (pair + 1) * 128] = turned[:8]

    tokens, width = rows_ref.shape
    wide = 2 * HEAD_SIZE

    def project(pair):
        for slot in range(YS):

            @pl.loop(0, tokens, step=32)
            def _(r):
                at = pl.ds(pl.multiple_of(r, 32), 32)
                value = rows_all[pair * YS + slot, at].astype(jnp.float32)
                inverse = lax.rsqrt(
                    jnp.mean(value * value, axis=-1, keepdims=True) + eps_norm
                )
                input_out[pair * YS + slot, at] = (value * inverse * gains_out[:1]).astype(
                    jnp.bfloat16
                )

        both = pl.ds(pair * YS, YS)
        weight = qkv_out[:, :, :QKV_WIDTH].reshape(width, QKV_WIDTH)
        projected = jnp.dot(
            input_out[both].reshape(YS * tokens, width),
            weight,
            preferred_element_type=jnp.float32,
        )
        turns = table_out[both].reshape(YS * tokens, wide)
        for slot in range(YS):
            span = slice(slot * tokens, (slot + 1) * tokens)
            block = pair * YS + slot
            for heads in range(PAIRS):
                query = rotate(
                    projected[span, heads * wide : (heads + 1) * wide], turns[span]
                ).astype(jnp.bfloat16)
                query_out[block, heads, 0] = query[:, :HEAD_SIZE]
                query_out[block, heads, 1] = query[:, HEAD_SIZE:]
            key = rotate(projected[span, PAIRS * wide :], turns[span])
            key_out[block] = key[:, :HEAD_SIZE].astype(jnp.bfloat16)
            value_out[block] = projected[span, PAIRS * wide + HEAD_SIZE :].astype(
                jnp.bfloat16
            )

    rows.local.wait()
    rows.arrive_across(z)
    project(z)
    outs.relay(0)
    for source in order:
        outs_chip.start(source * YS + y)
    for pair in order:
        rows.arrive_across(pair)
        project(pair)
    rows.finish()
    for other in range(ZS):
        outs.arrive_across(other)
        outs_chip.start(other * YS + 1 - y)
    grads.first()

    for step in range(1, PLANE + 1):
        block = lax.rem(c + step, PLANE)

        @pl.loop(0, PAIRS)
        def _(pair):
            halves = []
            keys = key_out[...].reshape(PLANE * tokens, HEAD_SIZE)
            values = value_out[...].reshape(PLANE * tokens, HEAD_SIZE)
            for half in range(2):
                probs = probabilities(
                    query_out[block, pair, half],
                    keys,
                    spot_out[block],
                    start_out[block],
                    key_spot_out[:1],
                )
                halves.append(
                    jnp.dot(
                        probs.astype(jnp.bfloat16), values, preferred_element_type=jnp.float32
                    ).astype(jnp.bfloat16)
                )
            mixed_stage[block, pair] = jnp.concatenate(halves, axis=1)

        exchange.send(step)
        if step < PLANE:
            weights.relay(step)
    for k in range(CHUNKS):
        grads.relay(k)
    for j in range(DOWN_PARTS):
        down.relay(j)
    for off in range(PLANE):
        outs_chip.relay(lax.rem(c + off, PLANE))
    weights.relay_chip()
    for off in range(1, PLANE + 1):
        exchange.arrive(off)
    grads.last()
    down.last()
    outs_chip.last()
    weights.last()
    outs.finish()
    outs.local.wait()
    exchange.finish()
    for copy in spots_sent:
        copy.wait_send()
    down_own.wait()


def attention(starts, rows, table, spots, qkv, blocks, out_rows, down, grads):
    low, full = jnp.bfloat16, jnp.float32
    tokens, width = rows.shape
    mixed = jax.ShapeDtypeStruct((PLANE, PAIRS, tokens, 2 * HEAD_SIZE), low)
    seq_len = PLANE * tokens
    wide_block = (blocks.shape[0], blocks.shape[1] // PLANE)
    return pl.pallas_call(
        attention_kernel,
        out_shape=(
            jax.ShapeDtypeStruct((PLANE, tokens, width), low),
            jax.ShapeDtypeStruct((PLANE, *table.shape), full),
            jax.ShapeDtypeStruct((RANKS, *qkv.shape[1:]), low),
            jax.ShapeDtypeStruct((8, width), full),
            jax.ShapeDtypeStruct((PLANE, PAIRS, 2, tokens, HEAD_SIZE), low),
            jax.ShapeDtypeStruct((PLANE, tokens, HEAD_SIZE), low),
            jax.ShapeDtypeStruct((PLANE, tokens, HEAD_SIZE), low),
            jax.ShapeDtypeStruct((PLANE, tokens, 1), full),
            jax.ShapeDtypeStruct((PLANE, tokens, 1), full),
            jax.ShapeDtypeStruct((8, seq_len), full),
            mixed,
            jax.ShapeDtypeStruct((RANKS, *wide_block), low),
            jax.ShapeDtypeStruct((RANKS, *out_rows.shape), low),
            jax.ShapeDtypeStruct((4 * down.shape[0], down.shape[1]), low),
            jax.ShapeDtypeStruct((PLANE, *grads.shape), low),
        ),
        in_specs=[pl.BlockSpec(memory_space=pltpu.SMEM)] + [ANY] * 8,
        out_specs=(VMEM,) * 11 + (ANY,) * 4,
        scratch_shapes=[
            pltpu.VMEM(mixed.shape, low),
            pltpu.VMEM((PLANE, *spots.shape), full),
            pltpu.VMEM((PLANE, tokens, width), low),
            pltpu.VMEM(blocks.shape, full),
            pltpu.VMEM((PLANE, *wide_block), low),
            pltpu.VMEM(down.shape, full),
            pltpu.VMEM(down.shape, low),
            pltpu.VMEM(out_rows.shape, full),
            pltpu.VMEM(out_rows.shape, low),
            pltpu.SemaphoreType.DMA((3,)),
            *PlaneExchange.scratch(),
            *WeightGather.scratch(),
            *WeightGather.scratch(),
            *SequenceGather.scratch(1),
            *ChipGather.scratch(PLANE),
            *SequenceGather.scratch(2),
            *SequenceGather.scratch(1),
            *SequenceGather.scratch(CHUNKS),
            *ChipGather.scratch(DOWN_PARTS),
            pltpu.SemaphoreType.DMA((PLANE,)),
            pltpu.SemaphoreType.DMA((PLANE,)),
            pltpu.SemaphoreType.DMA(()),
            pltpu.SemaphoreType.DMA(()),
        ],
        compiler_params=params(2),
        name="attention",
    )(starts, rows, table, spots, qkv, blocks, out_rows, down, grads)


def feed_kernel(
    rows_ref,
    grads_all,
    weight_ref,
    down_ref,
    normed_out,
    total_out,
    weight_grad_out,
    down_grad_out,
    *scratch,
):
    rows_all, slope_gate, slope_up, hidden_all, gate_grads = scratch[:5]
    normed_parts, down_parts, turned, stage, stage_sem = scratch[5:10]
    scratch = list(scratch[10:])

    def take(count):
        taken, scratch[:count] = scratch[:count], []
        return taken

    rows = SequenceGather(rows_ref, rows_all, take(5), 2)
    normed = SequenceScatter(normed_parts, normed_out, *take(2), take(4), 1)
    total = SequenceScatter(down_parts, total_out, *take(2), take(4), 1)
    d, c, x, core, z, y = place()
    greet(
        [(d, lax.rem(z + off, ZS) * YS + y) for off in range(1, ZS)] + [(d, z * YS + 1 - y)]
    )
    tokens, width = rows_ref.shape
    part = down_ref.shape[0]
    tile = 256
    blocks = PLANE // 2
    half = lax.div(z, 2)
    near, mid, far = near_first(z)

    def slots(side):
        return pl.ds(side * blocks, blocks)

    def columns(n, start=0, size=tile):
        return pl.ds(pl.multiple_of(n + start, size), size)

    def flat(ref, side):
        value = ref[slots(side)]
        return value.reshape(blocks * tokens, value.shape[2])

    def held(value, dtype=jnp.bfloat16):
        return value.astype(dtype).reshape(blocks, tokens, value.shape[1])

    def forward(side):
        @pl.loop(0, part, step=tile)
        def _(n):
            at, after = columns(n), columns(n, part)
            value = flat(rows_all, side)
            gate = jnp.dot(value, weight_ref[:, at], preferred_element_type=jnp.float32)
            up = jnp.dot(value, weight_ref[:, after], preferred_element_type=jnp.float32)
            sigmoid = jax.nn.sigmoid(gate)
            silu = gate * sigmoid
            hidden_all[slots(side), :, at] = held(silu * up)
            slope_up[slots(side), :, at] = held(silu, jnp.float32)
            slope_gate[slots(side), :, at] = held(
                up * sigmoid * (1.0 + gate * (1.0 - sigmoid)), jnp.float32
            )

    def downward(side):
        @pl.loop(0, width, step=2 * tile)
        def _(n):
            at = columns(n, 0, 2 * tile)
            down_parts[slots(side), :, at] = held(
                jnp.dot(
                    flat(hidden_all, side), down_ref[:, at], preferred_element_type=jnp.float32
                )
            )

    def backward(side):
        @pl.loop(0, part, step=tile)
        def _(n):
            at, after = columns(n), columns(n, part)
            grad = held(times_rows(flat(grads_all, side), down_ref[at, :]), jnp.float32)
            gate_grads[slots(side), :, at] = (grad * slope_gate[slots(side), :, at]).astype(
                jnp.bfloat16
            )
            gate_grads[slots(side), :, after] = (grad * slope_up[slots(side), :, at]).astype(
                jnp.bfloat16
            )

    def inward(side):
        @pl.loop(0, width, step=2 * tile)
        def _(n):
            at = columns(n, 0, 2 * tile)
            normed_parts[slots(side), :, at] = held(
                times_rows(flat(gate_grads, side), weight_ref[at, :])
            )

    tiles = [(hidden_all, grads_all, down_grad_out, n) for n in range(part // tile)]
    tiles += [(rows_all, gate_grads, weight_grad_out, n) for n in range(width // tile)]
    copies = []

    def weight_grad(i):
        left, right, out, n = tiles[i]
        if i >= 2:
            copies[i - 2].wait()
        value = left[:, :, n * tile : (n + 1) * tile].reshape(PLANE * tokens, tile)
        turned[...] = value.T

        @pl.loop(0, width, step=2 * tile)
        def _(m):
            at = columns(m, 0, 2 * tile)
            stage[i % 2, :, at] = jnp.dot(
                turned[...],
                right[:, :, at].reshape(PLANE * tokens, 2 * tile),
                preferred_element_type=jnp.float32,
            ).astype(jnp.bfloat16)

        copy = pltpu.make_async_copy(
            stage.at[i % 2], out.at[pl.ds(n * tile, tile)], stage_sem.at[i % 2]
        )
        copy.start()
        copies.append(copy)

    rows.first(by_block=True)
    rows.local.wait()
    rows.relay_block(near)
    rows.arrive_across(z)
    rows.arrive_across(near)
    forward(half)
    rows.relay_block(mid)
    rows.relay_block(far)
    backward(half)
    inward(half)
    normed.start(near, 0)
    normed.start(z, 0)
    rows.arrive_across(mid)
    rows.arrive_across(far)
    forward(1 - half)
    backward(1 - half)
    inward(1 - half)
    normed.start(far, 0)
    normed.start(mid, 0)
    normed.relay_one(near, 0)
    downward(1 - half)
    total.start(far, 0)
    total.start(mid, 0)
    normed.relay_one(far, 0)
    downward(half)
    total.start(near, 0)
    total.start(z, 0)
    normed.relay_one(mid, 0)
    for i in range(2):
        weight_grad(i)
    for pair in (far, mid, near):
        total.relay_one(pair, 0)
        weight_grad(len(copies))
    for i in range(len(copies), len(tiles)):
        weight_grad(i)
    normed.last(0)
    total.last(0)
    for copy in copies[-2:]:
        copy.wait()
    rows.finish()
    normed.finish()
    total.finish()


def feed(rows, grads, weight, down):
    part, width = down.shape
    low = rows.dtype
    tokens = rows.shape[0]
    summed = jax.ShapeDtypeStruct(rows.shape, jnp.float32)
    return pl.pallas_call(
        feed_kernel,
        out_shape=(
            summed,
            summed,
            jax.ShapeDtypeStruct(weight.shape, low),
            jax.ShapeDtypeStruct(down.shape, low),
        ),
        in_specs=[ANY] + [VMEM] * 3,
        out_specs=(VMEM,) * 2 + (ANY,) * 2,
        scratch_shapes=[
            pltpu.VMEM((PLANE, tokens, width), low),
            pltpu.VMEM((PLANE, tokens, part), jnp.float32),
            pltpu.VMEM((PLANE, tokens, part), jnp.float32),
            pltpu.VMEM((PLANE, tokens, part), low),
            pltpu.VMEM((PLANE, tokens, 2 * part), low),
            pltpu.VMEM((PLANE, tokens, width), low),
            pltpu.VMEM((PLANE, tokens, width), low),
            pltpu.VMEM((256, PLANE * tokens), low),
            pltpu.VMEM((2, 256, width), low),
            pltpu.SemaphoreType.DMA((2,)),
            *SequenceGather.scratch(2),
            *SequenceScatter.scratch(tokens, width, 1),
            *SequenceScatter.scratch(tokens, width, 1),
        ],
        compiler_params=params(5, 60),
        name="feed",
    )(rows, grads, weight, down)


def attention_back_kernel(
    query_ref,
    key_ref,
    value_ref,
    spot_ref,
    start_ref,
    key_spot_ref,
    mixed_ref,
    parts_ref,
    down_ref,
    query_out,
    key_out,
    value_out,
    wide_out,
    down_out,
    *scratch,
):
    mixed_all, out_ref = scratch[:2]
    scratch = scratch[2:]
    exchange = PlaneExchange(mixed_ref, mixed_all, scratch[:3])
    weights = WeightScatter(parts_ref, out_ref, scratch[3:7], scratch[7:13])
    down = ChipScatter(down_ref, *scratch[13:16], scratch[16:], DOWN_PARTS)
    d, c, x, core, z, y = place()
    greet(plane_peers(d, c) + chip_peers(d, c, x, core))
    for off in range(1, PLANE + 1):
        exchange.send(off)
    weights.first()
    for j in range(DOWN_PARTS):
        down.start(j)
    key_out[...] = jnp.zeros_like(key_out)
    value_out[...] = jnp.zeros_like(value_out)
    for step in range(PLANE):
        block = lax.rem(c + PLANE - step, PLANE)
        exchange.arrive(step)

        @pl.loop(0, PAIRS)
        def _(pair):
            keys = key_ref[...].reshape(key_out.shape)
            values = value_ref[...].reshape(value_out.shape)
            for half in range(2):
                query = query_ref[block, pair, half]
                grad = mixed_all[block, pair][:, half * HEAD_SIZE : (half + 1) * HEAD_SIZE]
                probs = probabilities(
                    query, keys, spot_ref[block], start_ref[block], key_spot_ref[:1]
                )
                grad_probs = times_rows(grad, values)
                delta = jnp.sum(probs * grad_probs, axis=-1, keepdims=True)
                grad_scores = (probs * (grad_probs - delta) * SCORE_SCALE).astype(jnp.bfloat16)
                query_out[block, pair, half] = jnp.dot(
                    grad_scores, keys, preferred_element_type=jnp.float32
                )
                key_out[...] += transposed_times(grad_scores, query)
                value_out[...] += transposed_times(probs.astype(jnp.bfloat16), grad)

        weights.relay(step + 1)
        if step >= 2:
            weights.send(step - 1)
    for off in (PLANE - 1, PLANE):
        weights.send(off)
    for j in range(DOWN_PARTS):
        down.relay(j)
    for j in range(DOWN_PARTS):
        down.total(j, down_out.at[j])
    weights.last()
    for source, start, after in wide_columns(wide_out.shape[1]):
        size = wide_out.shape[1] // (8 * PLANE)
        wide_out[:, after : after + size] = out_ref[source, :, start : start + size]
    down.finish()
    exchange.finish()


def attention_back(query, keys, values, spots, starts, key_spots, mixed, parts, down):
    return pl.pallas_call(
        attention_back_kernel,
        out_shape=(
            jax.ShapeDtypeStruct(query.shape, jnp.float32),
            jax.ShapeDtypeStruct((PLANE * keys.shape[1], HEAD_SIZE), jnp.float32),
            jax.ShapeDtypeStruct((PLANE * values.shape[1], HEAD_SIZE), jnp.float32),
            jax.ShapeDtypeStruct((parts.shape[1], PLANE * parts.shape[2]), parts.dtype),
            jax.ShapeDtypeStruct((DOWN_PARTS, *down.shape[1:]), jnp.float32),
        ),
        in_specs=[VMEM] * 9,
        out_specs=(VMEM,) * 5,
        scratch_shapes=[
            pltpu.VMEM(mixed.shape, jnp.bfloat16),
            pltpu.VMEM((PLANE, *parts.shape[1:]), parts.dtype),
            *PlaneExchange.scratch(),
            *WeightScatter.scratch(*parts.shape[1:]),
            *ChipScatter.scratch(DOWN_PARTS, *down.shape[1:]),
        ],
        compiler_params=params(3),
        name="attention_back",
    )(query, keys, values, spots, starts, key_spots, mixed, parts, down)


def closing_kernel(
    rows_ref, parts_ref, outs_ref, rows_out, query_out, keyval_out, outs_out, out_ref, *scratch
):
    scatter = SequenceScatter(rows_ref, rows_out, *scratch[:2], scratch[2:6], CHUNKS)
    weights = WeightScatter(parts_ref, out_ref, scratch[6:10], scratch[10:16])
    outs_sum = scratch[16]
    chip = ChipScatter(outs_ref, *scratch[17:20], scratch[20:24], PLANE)
    outs = SequenceScatter(outs_sum, outs_out, *scratch[24:26], scratch[26:], 1)
    d, c, x, core, z, y = place()
    greet(plane_peers(d, c) + chip_peers(d, c, x, core))
    places = (*near_first(z)[::-1], z)
    slots = [place * YS + 1 - y for place in places] + [place * YS + y for place in places]
    for j in slots:
        chip.start(j)
    weights.first()
    scatter.first()
    for j in slots:
        chip.relay(j)
    for off in range(1, PLANE + 1):
        weights.relay(off)
    for k in range(CHUNKS):
        scatter.relay(k)
    for off in range(1, PLANE + 1):
        weights.send(off)
    for i, j in enumerate(slots):
        chip.total(j, outs_sum.at[j])
        if i < ZS:
            outs.start(places[i], 0)
    outs.relay(0)
    for k in range(CHUNKS):
        scatter.last(k)
    weights.last()
    group_width = GROUP * HEAD_SIZE
    for source in range(PLANE):
        query_out[:, source * group_width : (source + 1) * group_width] = out_ref[
            source, :, :group_width
        ]
    for kind in range(2):
        start = group_width + kind * HEAD_SIZE
        for source in range(0, PLANE, 2):
            after = (kind * PLANE + source) * HEAD_SIZE
            keyval_out[:, after : after + 2 * HEAD_SIZE] = jnp.concatenate(
                [out_ref[source + i, :, start : start + HEAD_SIZE] for i in range(2)], axis=1
            )
    outs.last(0)
    scatter.finish()
    chip.finish()
    outs.finish()


def closing(rows, parts, outs):
    return pl.pallas_call(
        closing_kernel,
        out_shape=(
            jax.ShapeDtypeStruct(rows.shape[1:], jnp.float32),
            jax.ShapeDtypeStruct((parts.shape[1], QUERY_HEADS * HEAD_SIZE), parts.dtype),
            jax.ShapeDtypeStruct((parts.shape[1], 2 * PLANE * HEAD_SIZE), parts.dtype),
            jax.ShapeDtypeStruct(outs.shape[1:], jnp.float32),
        ),
        in_specs=[VMEM] * 3,
        out_specs=(VMEM,) * 4,
        scratch_shapes=[
            pltpu.VMEM((PLANE, *parts.shape[1:]), parts.dtype),
            *SequenceScatter.scratch(*rows.shape[1:], CHUNKS),
            *WeightScatter.scratch(*parts.shape[1:]),
            pltpu.VMEM((PLANE, *outs.shape[1:]), jnp.bfloat16),
            *ChipScatter.scratch(PLANE, *outs.shape[1:]),
            *SequenceScatter.scratch(*outs.shape[1:], 1),
        ],
        compiler_params=params(4),
        name="closing",
    )(rows, parts, outs)


def body(
    layer_in,
    positions,
    doc_starts,
    out_grad,
    norm_gains,
    norm_gains_m,
    norm_gains_v,
    w_query,
    w_query_m,
    w_query_v,
    key_value_weight,
    key_value_first_moment,
    key_value_second_moment,
    w_out,
    w_out_m,
    w_out_v,
    w_gate_up,
    w_gate_up_m,
    w_gate_up_v,
    w_down,
    w_down_m,
    w_down_v,
):
    number_of_tokens = layer_in.shape[0]
    ctx_count = lax.axis_size("ctx")
    seq_len = number_of_tokens * ctx_count
    key_value_width = KEY_VALUE_HEADS * HEAD_SIZE
    query_group_size = QUERY_HEADS // KEY_VALUE_HEADS
    score_scale = 1.0 / math.sqrt(HEAD_SIZE)
    needed = -(-512 // number_of_tokens)
    shard_span = min(ctx_count, 1 << max(0, (needed - 1).bit_length()))
    width_of_block = shard_span * number_of_tokens
    count_of_blocks = ctx_count // shard_span
    key_places = lax.all_gather(positions, "ctx", axis=0, tiled=True)
    starts = doc_starts[0]
    own_docs = doc_lookup(positions, starts)
    key_docs = doc_lookup(key_places, starts)
    query_full, keyval_full, out_full, gains_full = (
        lax.all_gather(w_query.astype(jnp.bfloat16), ("dp", "ctx"), axis=0, tiled=True),
        lax.all_gather(key_value_weight.astype(jnp.bfloat16), ("dp", "ctx"), axis=0, tiled=True),
        lax.all_gather(w_out.astype(jnp.bfloat16), ("dp", "ctx"), axis=0, tiled=True),
        lax.all_gather(norm_gains.astype(jnp.bfloat16), ("dp", "ctx"), axis=1, tiled=True),
    )
    gain_one = gains_full[0].astype(jnp.float32)
    gain_two = gains_full[1].astype(jnp.float32)
    layer_rows = layer_in.astype(jnp.float32)
    normed_one, inverse_one = norm_forward(layer_rows)
    input_one = (normed_one * gain_one).astype(jnp.bfloat16)
    query_pre = jnp.dot(input_one, query_full, preferred_element_type=jnp.float32)
    key_value_projected = jnp.dot(input_one, keyval_full, preferred_element_type=jnp.float32)
    cosine_table, sine_table = rope_tables(positions, HEAD_SIZE)
    query_rows = (
        apply_rotation(
            query_pre.reshape(number_of_tokens, QUERY_HEADS, HEAD_SIZE), cosine_table, sine_table
        )
        .astype(jnp.bfloat16)
        .reshape(number_of_tokens, KEY_VALUE_HEADS, query_group_size, HEAD_SIZE)
    )
    keys_own = (
        apply_rotation(
            key_value_projected[:, :key_value_width].reshape(
                number_of_tokens, KEY_VALUE_HEADS, HEAD_SIZE
            ),
            cosine_table,
            sine_table,
        )
        .astype(jnp.bfloat16)
        .reshape(number_of_tokens, key_value_width)
    )
    values_own = key_value_projected[:, key_value_width:].astype(jnp.bfloat16)
    every_key, every_value = (
        lax.all_gather(keys_own, "ctx", axis=0, tiled=True),
        lax.all_gather(values_own, "ctx", axis=0, tiled=True),
    )
    blocked_keys = every_key.reshape(count_of_blocks, width_of_block, KEY_VALUE_HEADS, HEAD_SIZE)
    blocked_values = every_value.reshape(
        count_of_blocks, width_of_block, KEY_VALUE_HEADS, HEAD_SIZE
    )
    place_blocks = key_places.reshape(count_of_blocks, width_of_block)
    doc_blocks = key_docs.reshape(count_of_blocks, width_of_block)

    def visible(place_blk, doc_blk):
        allowed = (place_blk[None, :] <= positions[:, None]) & (
            doc_blk[None, :] == own_docs[:, None]
        )
        return allowed[:, None, None, :]

    def scores_of(key_blk):
        return (
            jnp.einsum("tkgd,nkd->tkgn", query_rows, key_blk, preferred_element_type=jnp.float32)
            * score_scale
        )

    def stats_step(carry, block):
        row_top, row_total = carry
        key_blk, place_blk, doc_blk = block
        allowed = visible(place_blk, doc_blk)
        masked = jnp.where(allowed, scores_of(key_blk), masked_score)
        new_top = jnp.maximum(row_top, jnp.max(masked, axis=-1, keepdims=True))
        row_total = row_total * jnp.exp(row_top - new_top) + jnp.sum(
            jnp.where(allowed, jnp.exp(masked - new_top), 0.0), axis=-1, keepdims=True
        )
        return ((new_top, row_total), None)

    statistic_shape = (number_of_tokens, KEY_VALUE_HEADS, query_group_size, 1)
    (row_top, row_total), unused = lax.scan(
        stats_step,
        (
            jnp.full(statistic_shape, masked_score, jnp.float32),
            jnp.zeros(statistic_shape, jnp.float32),
        ),
        (blocked_keys, place_blocks, doc_blocks),
    )
    log_total = row_top + jnp.log(row_total)

    def probs_of(key_blk, place_blk, doc_blk):
        allowed = visible(place_blk, doc_blk)
        masked = jnp.where(allowed, scores_of(key_blk), masked_score)
        return jnp.where(allowed, jnp.exp(masked - log_total), 0.0)

    def output_step(carry, block):
        key_blk, value_blk, place_blk, doc_blk = block
        probs_low = probs_of(key_blk, place_blk, doc_blk).astype(jnp.bfloat16)
        added = jnp.einsum(
            "tkgn,nkd->tkgd", probs_low, value_blk, preferred_element_type=jnp.float32
        )
        return (carry + added, None)

    attention_output, unused = lax.scan(
        output_step,
        jnp.zeros((number_of_tokens, KEY_VALUE_HEADS, query_group_size, HEAD_SIZE), jnp.float32),
        (blocked_keys, blocked_values, place_blocks, doc_blocks),
    )
    mixed = attention_output.reshape(number_of_tokens, QUERY_HEADS * HEAD_SIZE).astype(jnp.bfloat16)
    middle = layer_rows + jnp.dot(mixed, out_full, preferred_element_type=jnp.float32)
    normed_two, inverse_two = norm_forward(middle)
    input_two = (normed_two * gain_two).astype(jnp.bfloat16)
    gate_up_low = w_gate_up.astype(jnp.bfloat16)
    down_low = w_down.astype(jnp.bfloat16)
    columns = input_two
    gate_up = jnp.dot(
        columns,
        lax.all_gather(gate_up_low, ("dp", "ctx"), axis=0, tiled=True),
        preferred_element_type=jnp.float32,
    )
    gate_part = gate_up[:, :FF]
    up_part = gate_up[:, FF:]
    sigmoid_gate = jax.nn.sigmoid(gate_part)
    silu_gate = gate_part * sigmoid_gate
    hidden = (silu_gate * up_part).astype(jnp.bfloat16)
    columns = hidden
    down_sum = jnp.dot(
        columns,
        lax.all_gather(down_low, ("dp", "ctx"), axis=0, tiled=True),
        preferred_element_type=jnp.float32,
    )
    layer_out = (middle + down_sum).astype(jnp.bfloat16)
    grad_rows = out_grad.astype(jnp.float32)
    grad_hidden = times_transposed(
        out_grad, lax.all_gather(down_low, ("dp", "ctx"), axis=0, tiled=True)
    )
    grad_gate = grad_hidden * up_part * sigmoid_gate * (1.0 + gate_part * (1.0 - sigmoid_gate))
    grad_up = grad_hidden * silu_gate
    grad_gate_up = jnp.concatenate([grad_gate, grad_up], axis=1).astype(jnp.bfloat16)
    down_grad = lax.psum_scatter(
        transposed_times(hidden, out_grad), ("dp", "ctx"), scatter_dimension=0, tiled=True
    )
    grad_normed_two = times_transposed(
        grad_gate_up, lax.all_gather(gate_up_low, ("dp", "ctx"), axis=0, tiled=True)
    )
    gate_up_grad = lax.psum_scatter(
        transposed_times(input_two, grad_gate_up), ("dp", "ctx"), scatter_dimension=0, tiled=True
    )
    grad_norm_two, gain_two_grad = norm_backward(grad_normed_two, normed_two, inverse_two, gain_two)
    grad_middle = grad_rows + grad_norm_two
    grad_middle_low = grad_middle.astype(jnp.bfloat16)
    out_term = transposed_times(mixed, grad_middle_low)
    grad_mixed = (
        times_transposed(grad_middle_low, out_full)
        .astype(jnp.bfloat16)
        .reshape(number_of_tokens, KEY_VALUE_HEADS, query_group_size, HEAD_SIZE)
    )
    delta = jnp.sum(grad_mixed.astype(jnp.float32) * attention_output, axis=-1, keepdims=True)

    def back_step(grad_query, block):
        key_blk, value_blk, place_blk, doc_blk = block
        probs = probs_of(key_blk, place_blk, doc_blk)
        probs_low = probs.astype(jnp.bfloat16)
        grad_probs = jnp.einsum(
            "tkgd,nkd->tkgn", grad_mixed, value_blk, preferred_element_type=jnp.float32
        )
        grad_scores = (probs * (grad_probs - delta) * score_scale).astype(jnp.bfloat16)
        grad_query = grad_query + jnp.einsum(
            "tkgn,nkd->tkgd", grad_scores, key_blk, preferred_element_type=jnp.float32
        )
        key_grad = jnp.einsum(
            "tkgn,tkgd->nkd", grad_scores, query_rows, preferred_element_type=jnp.float32
        )
        value_grad = jnp.einsum(
            "tkgn,tkgd->nkd", probs_low, grad_mixed, preferred_element_type=jnp.float32
        )
        return (grad_query, (key_grad, value_grad))

    grad_query, (key_grads, value_grads) = lax.scan(
        back_step,
        jnp.zeros((number_of_tokens, KEY_VALUE_HEADS, query_group_size, HEAD_SIZE), jnp.float32),
        (blocked_keys, blocked_values, place_blocks, doc_blocks),
    )
    summed_key_gradient, value_sum = (
        lax.psum_scatter(
            key_grads.reshape(seq_len, key_value_width).astype(jnp.bfloat16),
            "ctx",
            scatter_dimension=0,
            tiled=True,
        ).astype(jnp.float32),
        lax.psum_scatter(
            value_grads.reshape(seq_len, key_value_width).astype(jnp.bfloat16),
            "ctx",
            scatter_dimension=0,
            tiled=True,
        ).astype(jnp.float32),
    )
    key_gradient_unrotated = reverse_rotation(
        summed_key_gradient.reshape(number_of_tokens, KEY_VALUE_HEADS, HEAD_SIZE),
        cosine_table,
        sine_table,
    ).reshape(number_of_tokens, key_value_width)
    grad_keyval = jnp.concatenate([key_gradient_unrotated, value_sum], axis=1).astype(jnp.bfloat16)
    grad_query_low = (
        reverse_rotation(
            grad_query.reshape(number_of_tokens, QUERY_HEADS, HEAD_SIZE), cosine_table, sine_table
        )
        .reshape(number_of_tokens, QUERY_HEADS * HEAD_SIZE)
        .astype(jnp.bfloat16)
    )
    grad_normed_one = times_transposed(grad_query_low, query_full) + times_transposed(
        grad_keyval, keyval_full
    )
    query_term = transposed_times(input_one, grad_query_low)
    keyval_term = transposed_times(input_one, grad_keyval)
    grad_norm_one, gain_one_grad = norm_backward(grad_normed_one, normed_one, inverse_one, gain_one)
    in_grad = grad_middle + grad_norm_one
    gain_term = jnp.stack([gain_one_grad, gain_two_grad])
    query_grad, keyval_grad, out_weight_grad, gains_grad = (
        lax.psum_scatter(query_term, ("dp", "ctx"), scatter_dimension=0, tiled=True),
        lax.psum_scatter(keyval_term, ("dp", "ctx"), scatter_dimension=0, tiled=True),
        lax.psum_scatter(out_term, ("dp", "ctx"), scatter_dimension=0, tiled=True),
        lax.psum_scatter(gain_term, ("dp", "ctx"), scatter_dimension=1, tiled=True),
    )
    rates = rates_for(seq_len)
    gains_m_new, gains_v_new, gains_new = adamw(
        norm_gains, gains_grad, norm_gains_m, norm_gains_v, rates[0], 0.0
    )
    query_m_new, query_v_new, query_new = adamw(
        w_query, query_grad, w_query_m, w_query_v, rates[1], weight_decay
    )
    keyval_m_new, keyval_v_new, keyval_new = adamw(
        key_value_weight,
        keyval_grad,
        key_value_first_moment,
        key_value_second_moment,
        rates[2],
        weight_decay,
    )
    out_m_new, out_v_new, out_new = adamw(
        w_out, out_weight_grad, w_out_m, w_out_v, rates[3], weight_decay
    )
    gate_up_m_new, gate_up_v_new, gate_up_new = adamw(
        w_gate_up, gate_up_grad, w_gate_up_m, w_gate_up_v, rates[4], weight_decay
    )
    down_m_new, down_v_new, down_new = adamw(
        w_down, down_grad, w_down_m, w_down_v, rates[5], weight_decay
    )
    return (
        layer_out,
        in_grad,
        gains_grad,
        gains_m_new,
        gains_v_new,
        gains_new,
        query_grad,
        query_m_new,
        query_v_new,
        query_new,
        keyval_grad,
        keyval_m_new,
        keyval_v_new,
        keyval_new,
        out_weight_grad,
        out_m_new,
        out_v_new,
        out_new,
        gate_up_grad,
        gate_up_m_new,
        gate_up_v_new,
        gate_up_new,
        down_grad,
        down_m_new,
        down_v_new,
        down_new,
    )


def tensor_parallel(
    layer_in,
    positions,
    doc_starts,
    out_grad,
    norm_gains,
    norm_gains_m,
    norm_gains_v,
    w_query,
    w_query_m,
    w_query_v,
    key_value_weight,
    key_value_first_moment,
    key_value_second_moment,
    w_out,
    w_out_m,
    w_out_v,
    w_gate_up,
    w_gate_up_m,
    w_gate_up_v,
    w_down,
    w_down_m,
    w_down_v,
):
    low = jnp.bfloat16
    own_tokens, width = layer_in.shape
    seq_len = own_tokens * PLANE
    group = GROUP
    group_width = group * HEAD_SIZE
    ff_part = FF // PLANE
    rows = w_query.shape[0]

    gains_low = norm_gains.astype(low)
    small = jnp.broadcast_to(
        jnp.pad(gains_low.T, ((0, 0), (0, 126)))[None], (PLANE, rows, 128)
    )
    attention_blocks = jnp.concatenate(
        [
            w_query.astype(low).reshape(rows, PLANE, group_width).transpose(1, 0, 2),
            key_value_weight.astype(low)
            .reshape(rows, 2, PLANE, HEAD_SIZE)
            .transpose(2, 0, 1, 3)
            .reshape(PLANE, rows, 2 * HEAD_SIZE),
            small,
        ],
        axis=2,
    )
    spots = jnp.broadcast_to(positions[None, :].astype(jnp.float32), (8, own_tokens))
    cosine_own, sine_own = rope_tables(positions, HEAD_SIZE)
    cosine_own, sine_own = cosine_own[:, 0], sine_own[:, 0]
    table = jnp.concatenate([cosine_own, cosine_own, -sine_own, sine_own], axis=1)
    qkv_width = QKV_WIDTH
    (
        input_one_all,
        table_all,
        attention_all,
        gain_rows,
        query_rows,
        key_rows,
        value_rows,
        token_spots,
        token_starts,
        key_spots,
        mixed_parts,
        feed_all,
        out_all,
        down_all,
        grads_all,
    ) = attention(
        doc_starts,
        layer_in,
        table,
        spots,
        attention_blocks,
        w_gate_up,
        w_out,
        w_down,
        out_grad,
    )
    gain_one, gain_two = gain_rows[0], gain_rows[1]
    input_one = input_one_all.reshape(seq_len, width)
    qkv_weight = attention_all.reshape(width, -1)[:, :qkv_width]
    cosine_table = table_all[:, :, : HEAD_SIZE // 2].reshape(seq_len, 1, -1)
    sine_table = table_all[:, :, 3 * HEAD_SIZE // 2 :].reshape(seq_len, 1, -1)
    mixed = mixed_parts.transpose(2, 0, 1, 3).reshape(own_tokens, width)
    out_weight = out_all.reshape(width, width)
    branch = jnp.dot(mixed, out_weight, preferred_element_type=jnp.float32)

    layer_rows = layer_in.astype(jnp.float32)
    middle = layer_rows + branch
    normed_two, inverse_two = norm_forward(middle)
    grad_normed_two, down_sum, feed_term, down_term = feed(
        (normed_two * gain_two).astype(low),
        grads_all,
        feed_all.reshape(width, 2 * ff_part),
        down_all,
    )
    layer_out = (middle + down_sum).astype(low)

    grad_norm_two, unused = norm_backward(grad_normed_two, normed_two, inverse_two, gain_two)
    grad_middle = out_grad.astype(jnp.float32) + grad_norm_two
    grad_middle_low = grad_middle.astype(low)
    out_term = transposed_times(mixed, grad_middle_low).astype(low)
    grad_mixed = (
        times_transposed(grad_middle_low, out_weight)
        .astype(low)
        .reshape(own_tokens, PLANE, PAIRS, 2 * HEAD_SIZE)
        .transpose(1, 2, 0, 3)
    )
    grad_query, grad_key, grad_value, feed_grad, down_grad = attention_back(
        query_rows,
        key_rows,
        value_rows,
        token_spots,
        token_starts,
        key_spots,
        grad_mixed,
        feed_term.reshape(RANKS, rows, 2 * ff_part),
        down_term.reshape(4 * DOWN_PARTS, -1, width),
    )
    gate_up_grad = feed_grad.astype(jnp.float32)
    down_grad = down_grad.reshape(w_down.shape)
    grad_query = grad_query.transpose(0, 3, 1, 2, 4).reshape(seq_len, group, HEAD_SIZE)
    grad_qkv = jnp.concatenate(
        [
            reverse_rotation(grad_query, cosine_table, sine_table).reshape(seq_len, group_width),
            reverse_rotation(grad_key[:, None], cosine_table, sine_table)[:, 0],
            grad_value,
        ],
        axis=1,
    ).astype(low)
    one_parts = times_transposed(grad_qkv, qkv_weight).astype(low)
    qkv_term = transposed_times(input_one, grad_qkv).astype(low)
    grad_normed_one, query_grad, keyval_grad, out_weight_grad = closing(
        one_parts.reshape(PLANE, own_tokens, width),
        qkv_term.reshape(RANKS, rows, qkv_width),
        out_term.reshape(RANKS, rows, width),
    )
    normed_one, inverse_one = norm_forward(layer_rows)
    grad_norm_one, unused = norm_backward(grad_normed_one, normed_one, inverse_one, gain_one)
    in_grad = grad_middle + grad_norm_one
    query_grad = query_grad.astype(jnp.float32)
    keyval_grad = keyval_grad.astype(jnp.float32)

    def low_times(weight, grad):
        return jnp.sum(weight.astype(low).astype(jnp.float32) * grad, axis=1)

    gains_grad = jnp.stack(
        [
            low_times(w_query, query_grad) + low_times(key_value_weight, keyval_grad),
            low_times(w_gate_up, gate_up_grad),
        ]
    ) / gains_low.astype(jnp.float32)

    rates = rates_for(seq_len)
    return (
        layer_out,
        in_grad,
        gains_grad,
        *adamw(norm_gains, gains_grad, norm_gains_m, norm_gains_v, rates[0], 0.0),
        query_grad,
        *adamw(w_query, query_grad, w_query_m, w_query_v, rates[1], weight_decay),
        keyval_grad,
        *adamw(
            key_value_weight,
            keyval_grad,
            key_value_first_moment,
            key_value_second_moment,
            rates[2],
            weight_decay,
        ),
        out_weight_grad,
        *adamw(w_out, out_weight_grad, w_out_m, w_out_v, rates[3], weight_decay),
        gate_up_grad,
        *adamw(w_gate_up, gate_up_grad, w_gate_up_m, w_gate_up_v, rates[4], weight_decay),
        down_grad,
        *adamw(w_down, down_grad, w_down_m, w_down_v, rates[5], weight_decay),
    )


def solution(mesh):
    planned = tensor_parallel if dict(mesh.shape) == {"dp": 2 * XS, "ctx": ZS * YS} else body
    return jax.shard_map(
        planned,
        mesh=mesh,
        in_specs=(
            P(("dp", "ctx"), None),
            P(("dp", "ctx")),
            P("dp", None),
            P(("dp", "ctx"), None),
            P(None, ("dp", "ctx")),
            P(None, ("dp", "ctx")),
            P(None, ("dp", "ctx")),
            P(("dp", "ctx"), None),
            P(("dp", "ctx"), None),
            P(("dp", "ctx"), None),
            P(("dp", "ctx"), None),
            P(("dp", "ctx"), None),
            P(("dp", "ctx"), None),
            P(("dp", "ctx"), None),
            P(("dp", "ctx"), None),
            P(("dp", "ctx"), None),
            P(("dp", "ctx"), None),
            P(("dp", "ctx"), None),
            P(("dp", "ctx"), None),
            P(("dp", "ctx"), None),
            P(("dp", "ctx"), None),
            P(("dp", "ctx"), None),
        ),
        out_specs=(
            P(("dp", "ctx"), None),
            P(("dp", "ctx"), None),
            P(None, ("dp", "ctx")),
            P(None, ("dp", "ctx")),
            P(None, ("dp", "ctx")),
            P(None, ("dp", "ctx")),
            P(("dp", "ctx"), None),
            P(("dp", "ctx"), None),
            P(("dp", "ctx"), None),
            P(("dp", "ctx"), None),
            P(("dp", "ctx"), None),
            P(("dp", "ctx"), None),
            P(("dp", "ctx"), None),
            P(("dp", "ctx"), None),
            P(("dp", "ctx"), None),
            P(("dp", "ctx"), None),
            P(("dp", "ctx"), None),
            P(("dp", "ctx"), None),
            P(("dp", "ctx"), None),
            P(("dp", "ctx"), None),
            P(("dp", "ctx"), None),
            P(("dp", "ctx"), None),
            P(("dp", "ctx"), None),
            P(("dp", "ctx"), None),
            P(("dp", "ctx"), None),
            P(("dp", "ctx"), None),
        ),
        check_vma=False,
    )
```

```python
import functools
import math

import jax
import jax.numpy as jnp
from jax import lax
from jax.experimental import pallas as pl
from jax.experimental.pallas import tpu as pltpu
from jax.sharding import PartitionSpec as P

MODEL_WIDTH = 2048
QUERY_HEADS = 32
KEY_VALUE_HEADS = 8
HEAD_SIZE = 64
FF = 8192
STEP = 10


eps_norm = 1e-05
rope_base = 500000.0
beta_one = 0.9
beta_two = 0.95
eps_adam = 1e-08
weight_decay = 0.1
masked_score = -1e30


def rates_for(seq_len):
    return (
        0.6,
        0.8 / math.sqrt(MODEL_WIDTH // 4),
        0.8 / math.sqrt(MODEL_WIDTH),
        0.8 / math.sqrt(max(220 * MODEL_WIDTH // seq_len, 1)),
        0.8 / math.sqrt(MODEL_WIDTH),
        0.8 / math.sqrt(FF // 2),
    )


def adamw(weight, grad_sum, first, second, rate, decay):
    first_new = beta_one * first + (1.0 - beta_one) * grad_sum
    second_new = beta_two * second + (1.0 - beta_two) * grad_sum * grad_sum
    first_hat = first_new / (1.0 - beta_one**STEP)
    second_hat = second_new / (1.0 - beta_two**STEP)
    weight_new = weight - rate * (first_hat / (jnp.sqrt(second_hat) + eps_adam) + decay * weight)
    return (first_new, second_new, weight_new)


def norm_forward(layer_rows):
    inverse = lax.rsqrt(jnp.mean(layer_rows * layer_rows, axis=-1, keepdims=True) + eps_norm)
    return (layer_rows * inverse, inverse)


def norm_backward(grad_out, normed, inverse, gain_row):
    scaled = grad_out * gain_row
    grad_in = inverse * (scaled - normed * jnp.mean(scaled * normed, axis=-1, keepdims=True))
    return (grad_in, jnp.sum(grad_out * normed, axis=0))


def rope_tables(token_placement, head_dim):
    half_dim = head_dim // 2
    frequencies = jnp.exp(
        jnp.arange(half_dim, dtype=jnp.float32) * (-2.0 * math.log(rope_base) / head_dim)
    )
    angles = token_placement.astype(jnp.float32)[:, None] * frequencies[None, :]
    return (jnp.cos(angles)[:, None, :], jnp.sin(angles)[:, None, :])


def apply_rotation(value_rows, cosine_table, sine_table):
    half_dim = value_rows.shape[-1] // 2
    first_half = value_rows[..., :half_dim]
    second_half = value_rows[..., half_dim:]
    return jnp.concatenate(
        [
            first_half * cosine_table - second_half * sine_table,
            second_half * cosine_table + first_half * sine_table,
        ],
        axis=-1,
    )


def reverse_rotation(grad_rows, cosine_table, sine_table):
    half_dim = grad_rows.shape[-1] // 2
    first_half = grad_rows[..., :half_dim]
    second_half = grad_rows[..., half_dim:]
    return jnp.concatenate(
        [
            first_half * cosine_table + second_half * sine_table,
            second_half * cosine_table - first_half * sine_table,
        ],
        axis=-1,
    )


def doc_lookup(token_placement, starts):
    return jnp.sum((token_placement[:, None] >= starts[None, :]).astype(jnp.int32), axis=1) - 1


def times_transposed(left, right):
    return lax.dot_general(
        left, right, (((1,), (1,)), ((), ())), preferred_element_type=jnp.float32
    )


def transposed_times(left, right):
    return lax.dot_general(
        left, right, (((0,), (0,)), ((), ())), preferred_element_type=jnp.float32
    )


XS = 2
YS = 2
ZS = 4
PLANE = ZS * YS
RANKS = 2 * XS * PLANE
MESH = pl.DeviceIdType.MESH


def place():
    d = lax.axis_index("dp")
    c = lax.axis_index("ctx")
    return d, c, lax.div(d, 2), lax.rem(d, 2), lax.div(c, YS), lax.rem(c, YS)


def remote(src, dst, send_sem, recv_sem, d, c):
    return pltpu.make_async_remote_copy(
        src_ref=src,
        dst_ref=dst,
        send_sem=send_sem,
        recv_sem=recv_sem,
        device_id=(d, c),
        device_id_type=MESH,
    )


def greet(peers):
    barrier = pltpu.get_barrier_semaphore()
    for d, c in peers:
        pl.semaphore_signal(barrier, inc=1, device_id=(d, c), device_id_type=MESH)
    pl.semaphore_wait(barrier, len(peers))


def plane_peers(d, c):
    return [(d, lax.rem(c + k, PLANE)) for k in range(1, PLANE)]


def chip_peers(d, c, x, core):
    return [(x * 2 + 1 - core, c), ((1 - x) * 2 + core, c)]


def add_into(target, sources, rows, step=16):
    @pl.loop(0, rows, step=step)
    def _(r):
        at = pl.ds(pl.multiple_of(r, step), step)
        total = sources[0][at].astype(jnp.float32)
        for source in sources[1:]:
            total = total + source[at].astype(jnp.float32)
        target[at] = total.astype(target.dtype)


def near_first(z):
    half = lax.div(z, 2)
    return [half * 4 + 1 - z, 2 - half, 3 - 3 * half]


class SequenceGather:
    def __init__(self, own, out, sems, chunks):
        self.own, self.out, self.chunks = own, out, chunks
        self.zs, self.zr, self.ys, self.yr, self.local_sem = sems
        self.d, self.c, _, _, self.z, self.y = place()
        self.rows = own.shape[0] // chunks
        self.sent = []

    @staticmethod
    def scratch(chunks):
        return [
            pltpu.SemaphoreType.DMA((ZS, chunks)),
            pltpu.SemaphoreType.DMA((ZS, chunks)),
            pltpu.SemaphoreType.DMA((ZS, chunks)),
            pltpu.SemaphoreType.DMA((ZS, chunks)),
            pltpu.SemaphoreType.DMA(()),
        ]

    def part(self, ref, k):
        return ref.at[pl.ds(k * self.rows, self.rows)]

    def across(self, z, k, src):
        slot = z * YS + self.y
        return remote(
            src,
            self.part(self.out.at[slot], k),
            self.ys.at[z, k],
            self.yr.at[z, k],
            self.d,
            self.z * YS + 1 - self.y,
        )

    def along(self, to, k):
        return remote(
            self.part(self.own, k),
            self.part(self.out.at[self.c], k),
            self.zs.at[to, k],
            self.zr.at[self.z, k],
            self.d,
            to * YS + self.y,
        )

    def start(self, copy):
        copy.start()
        self.sent.append(copy)

    def first(self, by_block=False):
        self.local = pltpu.make_async_copy(self.own, self.out.at[self.c], self.local_sem)
        self.local.start()
        near = near_first(self.z)
        if by_block:
            for k in range(self.chunks):
                self.start(self.across(self.z, k, self.part(self.own, k)))
            for to in near:
                for k in range(self.chunks):
                    self.start(self.along(to, k))
            return
        for k in range(self.chunks):
            for to in near[::-1]:
                self.start(self.along(to, k))
            self.start(self.across(self.z, k, self.part(self.own, k)))

    def relay_one(self, source, k):
        slot = source * YS + self.y
        block = self.part(self.out.at[slot], k)
        remote(
            block, block, self.zs.at[source, k], self.zr.at[source, k], self.d, slot
        ).wait_recv()
        self.start(self.across(source, k, block))

    def relay(self, k):
        for source in near_first(self.z):
            self.relay_one(source, k)

    def relay_block(self, source):
        for k in range(self.chunks):
            self.relay_one(source, k)

    def arrive_across(self, z):
        for k in range(self.chunks):
            block = self.part(self.out.at[z * YS + 1 - self.y], k)
            remote(
                block,
                block,
                self.ys.at[z, k],
                self.yr.at[z, k],
                self.d,
                self.z * YS + 1 - self.y,
            ).wait_recv()

    def finish(self):
        for copy in self.sent:
            copy.wait_send()

    def last(self):
        for z in range(ZS):
            self.arrive_across(z)
        self.finish()
        self.local.wait()


class SequenceScatter:
    def __init__(self, parts, out, ybuf, zbuf, sems, chunks):
        self.parts, self.out, self.chunks = parts, out, chunks
        self.ybuf, self.zbuf = ybuf, zbuf
        self.ys, self.yr, self.zs, self.zr = sems
        self.d, self.c, _, _, self.z, self.y = place()
        self.rows = parts.shape[1] // chunks
        self.sent = []

    @staticmethod
    def scratch(rows, width, chunks):
        return [
            pltpu.VMEM((ZS, rows, width), jnp.bfloat16),
            pltpu.VMEM((ZS, rows, width), jnp.bfloat16),
            pltpu.SemaphoreType.DMA((ZS, chunks)),
            pltpu.SemaphoreType.DMA((ZS, chunks)),
            pltpu.SemaphoreType.DMA((ZS, chunks)),
            pltpu.SemaphoreType.DMA((ZS, chunks)),
        ]

    def span(self, k):
        return pl.ds(k * self.rows, self.rows)

    def across(self, z, k):
        return remote(
            self.parts.at[z * YS + 1 - self.y, self.span(k)],
            self.ybuf.at[z, self.span(k)],
            self.ys.at[z, k],
            self.yr.at[z, k],
            self.d,
            self.z * YS + 1 - self.y,
        )

    def along(self, to, k):
        return remote(
            self.ybuf.at[to, self.span(k)],
            self.zbuf.at[self.z, self.span(k)],
            self.zs.at[to, k],
            self.zr.at[self.z, k],
            self.d,
            to * YS + self.y,
        )

    def start(self, z, k):
        copy = self.across(z, k)
        copy.start()
        self.sent.append(copy)

    def first(self):
        for k in range(self.chunks):
            for z in (*near_first(self.z)[::-1], self.z):
                self.start(z, k)

    def relay_one(self, z, k):
        self.across(z, k).wait_recv()
        block = self.ybuf.at[z, self.span(k)]
        add_into(block, [self.parts.at[z * YS + self.y, self.span(k)], block], self.rows)
        copy = self.along(z, k)
        copy.start()
        self.sent.append(copy)

    def relay(self, k):
        for z in near_first(self.z)[::-1]:
            self.relay_one(z, k)

    def last(self, k):
        self.across(self.z, k).wait_recv()
        blocks = [self.parts.at[self.c, self.span(k)], self.ybuf.at[self.z, self.span(k)]]
        for source in near_first(self.z):
            block = self.zbuf.at[source, self.span(k)]
            remote(
                block,
                block,
                self.zs.at[source, k],
                self.zr.at[source, k],
                self.d,
                source * YS + self.y,
            ).wait_recv()
            blocks.append(block)
        add_into(self.out.at[self.span(k)], blocks, self.rows)

    def finish(self):
        for copy in self.sent:
            copy.wait_send()


class ChipGather:
    def __init__(self, out, sems, count, rows=None):
        self.out, self.count, self.rows = out, count, rows
        self.cs, self.cr, self.xs, self.xr = sems
        self.d, self.c, self.x, self.core, _, _ = place()
        self.sent = []

    @staticmethod
    def scratch(count):
        return [
            pltpu.SemaphoreType.DMA((2, count)),
            pltpu.SemaphoreType.DMA((2, count)),
            pltpu.SemaphoreType.DMA((count,)),
            pltpu.SemaphoreType.DMA((count,)),
        ]

    def block(self, slot):
        if self.rows is None:
            return self.out.at[slot]
        return self.out.at[pl.ds(slot * self.rows, self.rows)]

    def to_core(self, far, j, src=None):
        x = 1 - self.x if far else self.x
        block = self.block((x * 2 + self.core) * self.count + j)
        return remote(
            block if src is None else src,
            block,
            self.cs.at[far, j],
            self.cr.at[far, j],
            self.x * 2 + 1 - self.core,
            self.c,
        )

    def to_x(self, j, src=None):
        block = self.block(self.d * self.count + j)
        return remote(
            block if src is None else src,
            block,
            self.xs.at[j],
            self.xr.at[j],
            (1 - self.x) * 2 + self.core,
            self.c,
        )

    def start(self, j, src=None):
        for copy in (self.to_x(j, src), self.to_core(0, j, src)):
            copy.start()
            self.sent.append(copy)

    def relay(self, j):
        self.to_x(j).wait_recv()
        copy = self.to_core(1, j)
        copy.start()
        self.sent.append(copy)

    def last(self):
        for far in (0, 1):
            for j in range(self.count):
                self.to_core(far, j).wait_recv()
        for copy in self.sent:
            copy.wait_send()


class WeightGather:
    def __init__(self, blocks, out, sems):
        self.blocks, self.out = blocks, out
        self.ps, self.pr, self.local_sem = sems[:3]
        self.chip = ChipGather(out, sems[3:], PLANE)
        self.d, self.c = self.chip.d, self.chip.c
        self.sent = []

    @staticmethod
    def scratch():
        return [
            pltpu.SemaphoreType.DMA((PLANE,)),
            pltpu.SemaphoreType.DMA((PLANE,)),
            pltpu.SemaphoreType.DMA(()),
        ] + ChipGather.scratch(PLANE)

    def send(self, off):
        to = lax.rem(self.c + off, PLANE)
        copy = remote(
            self.blocks.at[to],
            self.out.at[self.d * PLANE + self.c],
            self.ps.at[off],
            self.pr.at[self.c],
            self.d,
            to,
        )
        copy.start()
        self.sent.append(copy)

    def first(self, ahead=PLANE - 1):
        self.ahead = ahead
        self.local = pltpu.make_async_copy(
            self.blocks.at[self.c], self.out.at[self.d * PLANE + self.c], self.local_sem
        )
        self.local.start()
        for off in range(1, 1 + ahead):
            self.send(off)
        self.chip.start(self.c, self.blocks.at[self.c])

    def relay(self, off):
        if off + self.ahead < PLANE:
            self.send(off + self.ahead)
        source = lax.rem(self.c + PLANE - off, PLANE)
        block = self.out.at[self.d * PLANE + source]
        remote(
            block, block, self.ps.at[off], self.pr.at[source], self.d, source
        ).wait_recv()
        self.chip.start(source)

    def relay_chip(self):
        for off in range(PLANE):
            self.chip.relay(lax.rem(self.c + off, PLANE))

    def last(self):
        self.chip.last()
        for copy in self.sent:
            copy.wait_send()
        self.local.wait()


class ChipScatter:
    def __init__(self, parts, cbuf, stage, xbuf, sems, count):
        self.parts, self.count = parts, count
        self.cbuf, self.stage, self.xbuf = cbuf, stage, xbuf
        self.cs, self.cr, self.xs, self.xr = sems
        self.d, self.c, self.x, self.core, _, _ = place()
        self.sent = []

    @staticmethod
    def scratch(count, rows, width):
        return [
            pltpu.VMEM((2, count, rows, width), jnp.bfloat16),
            pltpu.VMEM((count, rows, width), jnp.bfloat16),
            pltpu.VMEM((count, rows, width), jnp.bfloat16),
            pltpu.SemaphoreType.DMA((2, count)),
            pltpu.SemaphoreType.DMA((2, count)),
            pltpu.SemaphoreType.DMA((count,)),
            pltpu.SemaphoreType.DMA((count,)),
        ]

    def to_core(self, far, j):
        x = 1 - self.x if far else self.x
        return remote(
            self.parts.at[(x * 2 + 1 - self.core) * self.count + j],
            self.cbuf.at[far, j],
            self.cs.at[far, j],
            self.cr.at[far, j],
            self.x * 2 + 1 - self.core,
            self.c,
        )

    def to_x(self, j):
        return remote(
            self.stage.at[j],
            self.xbuf.at[j],
            self.xs.at[j],
            self.xr.at[j],
            (1 - self.x) * 2 + self.core,
            self.c,
        )

    def start(self, j):
        for far in (1, 0):
            copy = self.to_core(far, j)
            copy.start()
            self.sent.append(copy)

    def relay(self, j):
        self.to_core(1, j).wait_recv()
        own = self.parts.at[((1 - self.x) * 2 + self.core) * self.count + j]
        add_into(self.stage.at[j], [own, self.cbuf.at[1, j]], own.shape[0])
        copy = self.to_x(j)
        copy.start()
        self.sent.append(copy)

    def total(self, j, target):
        self.to_core(0, j).wait_recv()
        self.to_x(j).wait_recv()
        own = self.parts.at[self.d * self.count + j]
        add_into(target, [own, self.cbuf.at[0, j], self.xbuf.at[j]], own.shape[0])

    def finish(self):
        for copy in self.sent:
            copy.wait_send()


class WeightScatter:
    def __init__(self, parts, out, bufs, sems):
        self.stage = bufs[0]
        self.ps, self.pr = sems[:2]
        self.chip = ChipScatter(parts, *bufs[1:], sems[2:], PLANE)
        self.out = out
        self.d, self.c = self.chip.d, self.chip.c
        self.sent = []

    @staticmethod
    def scratch(rows, width):
        chip = ChipScatter.scratch(PLANE, rows, width)
        return [
            pltpu.VMEM((PLANE, rows, width), jnp.bfloat16),
            *chip[:3],
            pltpu.SemaphoreType.DMA((PLANE,)),
            pltpu.SemaphoreType.DMA((PLANE,)),
            *chip[3:],
        ]

    def first(self):
        for off in range(1, PLANE + 1):
            self.chip.start(lax.rem(self.c + off, PLANE))

    def relay(self, off):
        self.chip.relay(lax.rem(self.c + off, PLANE))

    def send(self, off):
        to = lax.rem(self.c + off, PLANE)
        if off == PLANE:
            self.chip.total(to, self.out.at[self.c])
            return
        self.chip.total(to, self.stage.at[to])
        copy = remote(
            self.stage.at[to],
            self.out.at[self.c],
            self.ps.at[off],
            self.pr.at[self.c],
            self.d,
            to,
        )
        copy.start()
        self.sent.append(copy)

    def last(self):
        for off in range(1, PLANE):
            source = lax.rem(self.c + off, PLANE)
            block = self.out.at[source]
            remote(
                block, block, self.ps.at[off], self.pr.at[source], self.d, source
            ).wait_recv()
        for copy in self.sent:
            copy.wait_send()
        self.chip.finish()


def params(collective_id, mebibytes=56):
    return pltpu.CompilerParams(
        collective_id=collective_id, has_side_effects=True, vmem_limit_bytes=mebibytes * 2**20
    )


ANY = pl.BlockSpec(memory_space=pl.ANY)
VMEM = pl.BlockSpec(memory_space=pltpu.VMEM)
CHUNKS = 4


DOWN_PARTS = 4
SCORE_SCALE = 1.0 / math.sqrt(HEAD_SIZE)
GROUP = QUERY_HEADS // KEY_VALUE_HEADS
PAIRS = GROUP // 2


def times_rows(left, right):
    return lax.dot_general(
        left, right, (((1,), (1,)), ((), ())), preferred_element_type=jnp.float32
    )


class PlaneExchange:
    def __init__(self, blocks, out, sems):
        self.blocks, self.out = blocks, out
        self.ps, self.pr, self.local_sem = sems
        self.d, self.c = lax.axis_index("dp"), lax.axis_index("ctx")
        self.sent = []

    @staticmethod
    def scratch():
        return [
            pltpu.SemaphoreType.DMA((PLANE,)),
            pltpu.SemaphoreType.DMA((PLANE,)),
            pltpu.SemaphoreType.DMA(()),
        ]

    def send(self, off):
        to = lax.rem(self.c + off, PLANE)
        if off % PLANE == 0:
            self.local = pltpu.make_async_copy(
                self.blocks.at[to], self.out.at[self.c], self.local_sem
            )
            self.local.start()
            return
        copy = remote(
            self.blocks.at[to],
            self.out.at[self.c],
            self.ps.at[off],
            self.pr.at[self.c],
            self.d,
            to,
        )
        copy.start()
        self.sent.append(copy)

    def arrive(self, off):
        if off % PLANE == 0:
            self.local.wait()
            return
        source = lax.rem(self.c + PLANE - off, PLANE)
        block = self.out.at[source]
        remote(
            block, block, self.ps.at[off], self.pr.at[source], self.d, source
        ).wait_recv()

    def finish(self):
        for copy in self.sent:
            copy.wait_send()


def probabilities(query, keys, spot, start, key_spots):
    scores = times_rows(query, keys) * SCORE_SCALE
    masked = jnp.where((key_spots <= spot) & (key_spots >= start), scores, masked_score)
    exponent = jnp.exp(masked - jnp.max(masked, axis=-1, keepdims=True))
    return exponent * (1.0 / jnp.sum(exponent, axis=-1, keepdims=True))


def rotate(value, table, back=False):
    lane = lax.broadcasted_iota(jnp.int32, value.shape, 1)
    turned = pltpu.roll(table, HEAD_SIZE, 1)
    cosine = jnp.where(lane < HEAD_SIZE, table, turned)
    sine = jnp.where(lane < HEAD_SIZE, turned, table)
    half = HEAD_SIZE // 2
    other = jnp.where(
        lax.rem(lane, HEAD_SIZE) < half,
        pltpu.roll(value, 2 * HEAD_SIZE - half, 1),
        pltpu.roll(value, half, 1),
    )
    if back:
        return value * cosine - other * sine
    return value * cosine + other * sine


QKV_WIDTH = (GROUP + 2) * HEAD_SIZE


def wide_columns(width):
    run = width // (8 * PLANE)
    for to in range(PLANE):
        for part in range(8):
            yield to, part * run, (part * PLANE + to) * run


def attention_kernel(
    starts_ref,
    rows_ref,
    table_ref,
    spots_ref,
    qkv_ref,
    blocks_ref,
    out_rows_ref,
    down_ref,
    grads_ref,
    input_out,
    table_out,
    qkv_out,
    gains_out,
    query_out,
    key_out,
    value_out,
    spot_out,
    start_out,
    key_spot_out,
    mixed_out,
    blocks_out,
    out_rows_out,
    down_out,
    grads_out,
    *scratch,
):
    mixed_stage, spots_all, rows_all, wide_full, wide_blocks = scratch[:5]
    down_full, down_blocks, out_full, out_block, load_sem = scratch[5:10]
    scratch = list(scratch[10:])

    def take(count):
        taken, scratch[:count] = scratch[:count], []
        return taken

    d, c, x, core, z, y = place()
    exchange = PlaneExchange(mixed_stage, mixed_out, take(3))
    qkv = WeightGather(qkv_ref, qkv_out, take(7))
    weights = WeightGather(wide_blocks, blocks_out, take(7))
    outs = SequenceGather(out_block, out_rows_out.at[pl.ds(d * PLANE, PLANE)], take(5), 1)
    outs_chip = ChipGather(out_rows_out, take(4), PLANE)
    rows = SequenceGather(rows_ref, rows_all, take(5), 2)
    table = SequenceGather(table_ref, table_out, take(5), 1)
    grads = SequenceGather(grads_ref, grads_out, take(5), CHUNKS)
    down_rows = down_ref.shape[0] // DOWN_PARTS
    down = ChipGather(down_out, take(4), DOWN_PARTS, down_rows)
    spot_send, spot_recv, spot_local, down_local = take(4)
    greet(plane_peers(d, c) + chip_peers(d, c, x, core))
    order = near_first(z)

    loads = [
        pltpu.make_async_copy(source, target, load_sem.at[i])
        for i, (source, target) in enumerate(
            [(out_rows_ref, out_full), (down_ref, down_full), (blocks_ref, wide_full)]
        )
    ]
    for load in loads:
        load.start()
    qkv.first()
    spots_own = pltpu.make_async_copy(spots_ref, spots_all.at[c], spot_local)
    spots_own.start()
    spots_sent = []
    for off in range(1, PLANE):
        to = lax.rem(c + off, PLANE)
        copy = remote(
            spots_ref, spots_all.at[c], spot_send.at[off], spot_recv.at[c], d, to
        )
        copy.start()
        spots_sent.append(copy)
    table.first()
    rows.first(by_block=True)
    loads[1].wait()

    @pl.loop(0, down_full.shape[0], step=16)
    def _(r):
        at = pl.ds(pl.multiple_of(r, 16), 16)
        down_blocks[at] = down_full[at].astype(jnp.bfloat16)

    down_own = pltpu.make_async_copy(
        down_blocks, down_out.at[pl.ds(d * down_full.shape[0], down_full.shape[0])], down_local
    )
    down_own.start()
    for j in range(DOWN_PARTS):
        down.start(j, down_blocks.at[pl.ds(j * down_rows, down_rows)])
    loads[0].wait()
    out_block[...] = out_full[...].astype(jnp.bfloat16)
    outs.first()
    outs_chip.start(c, out_block)
    loads[2].wait()

    @pl.loop(0, wide_full.shape[0], step=16)
    def _(r):
        at = pl.ds(pl.multiple_of(r, 16), 16)
        for to, start, after in wide_columns(wide_full.shape[1]):
            size = wide_full.shape[1] // (8 * PLANE)
            wide_blocks[to, at, start : start + size] = wide_full[
                at, after : after + size
            ].astype(jnp.bfloat16)

    for off in range(1, PLANE):
        qkv.relay(off)
    table.relay(0)
    rows.relay_block(order[0])
    qkv.relay_chip()
    rows.relay_block(order[1])
    rows.relay_block(order[2])
    weights.first()
    for off in range(1, PLANE):
        source = lax.rem(c + off, PLANE)
        block = spots_all.at[source]
        remote(block, block, spot_send.at[off], spot_recv.at[source], d, source).wait_recv()
    spots_own.wait()
    table.last()
    for slot in range(PLANE):
        key_spot_out[:, slot * 128 : (slot + 1) * 128] = spots_all[slot]
        spot = jnp.broadcast_to(spots_all[slot][:1], (128, 128)).T[:, :1]
        start = jnp.zeros_like(spot)
        for doc in range(starts_ref.shape[1]):
            first = starts_ref[0, doc].astype(jnp.float32)
            start = jnp.maximum(start, jnp.where(spot >= first, first, 0.0))
        spot_out[slot] = spot
        start_out[slot] = start
    qkv.last()
    for pair in range(RANKS // 2):
        columns = qkv_out[2 * pair : 2 * pair + 2, :, QKV_WIDTH:]
        turned = columns.reshape(128, 128).astype(jnp.float32).T
        gains_out[:, pair * 128 : (pair + 1) * 128] = turned[:8]

    tokens, width = rows_ref.shape
    wide = 2 * HEAD_SIZE

    def project(pair):
        for slot in range(YS):

            @pl.loop(0, tokens, step=32)
            def _(r):
                at = pl.ds(pl.multiple_of(r, 32), 32)
                value = rows_all[pair * YS + slot, at].astype(jnp.float32)
                inverse = lax.rsqrt(
                    jnp.mean(value * value, axis=-1, keepdims=True) + eps_norm
                )
                input_out[pair * YS + slot, at] = (value * inverse * gains_out[:1]).astype(
                    jnp.bfloat16
                )

        both = pl.ds(pair * YS, YS)
        weight = qkv_out[:, :, :QKV_WIDTH].reshape(width, QKV_WIDTH)
        projected = jnp.dot(
            input_out[both].reshape(YS * tokens, width),
            weight,
            preferred_element_type=jnp.float32,
        )
        turns = table_out[both].reshape(YS * tokens, wide)
        for slot in range(YS):
            span = slice(slot * tokens, (slot + 1) * tokens)
            block = pair * YS + slot
            for heads in range(PAIRS):
                query = rotate(
                    projected[span, heads * wide : (heads + 1) * wide], turns[span]
                ).astype(jnp.bfloat16)
                query_out[block, heads, 0] = query[:, :HEAD_SIZE]
                query_out[block, heads, 1] = query[:, HEAD_SIZE:]
            key = rotate(projected[span, PAIRS * wide :], turns[span])
            key_out[block] = key[:, :HEAD_SIZE].astype(jnp.bfloat16)
            value_out[block] = projected[span, PAIRS * wide + HEAD_SIZE :].astype(
                jnp.bfloat16
            )

    rows.local.wait()
    rows.arrive_across(z)
    project(z)
    outs.relay(0)
    for source in order:
        outs_chip.start(source * YS + y)
    for pair in order:
        rows.arrive_across(pair)
        project(pair)
    rows.finish()
    for other in range(ZS):
        outs.arrive_across(other)
        outs_chip.start(other * YS + 1 - y)
    grads.first()

    for step in range(1, PLANE + 1):
        block = lax.rem(c + step, PLANE)

        @pl.loop(0, PAIRS)
        def _(pair):
            halves = []
            keys = key_out[...].reshape(PLANE * tokens, HEAD_SIZE)
            values = value_out[...].reshape(PLANE * tokens, HEAD_SIZE)
            for half in range(2):
                probs = probabilities(
                    query_out[block, pair, half],
                    keys,
                    spot_out[block],
                    start_out[block],
                    key_spot_out[:1],
                )
                halves.append(
                    jnp.dot(
                        probs.astype(jnp.bfloat16), values, preferred_element_type=jnp.float32
                    ).astype(jnp.bfloat16)
                )
            mixed_stage[block, pair] = jnp.concatenate(halves, axis=1)

        exchange.send(step)
        if step < PLANE:
            weights.relay(step)
    for k in range(CHUNKS):
        grads.relay(k)
    for j in range(DOWN_PARTS):
        down.relay(j)
    for off in range(PLANE):
        outs_chip.relay(lax.rem(c + off, PLANE))
    weights.relay_chip()
    for off in range(1, PLANE + 1):
        exchange.arrive(off)
    grads.last()
    down.last()
    outs_chip.last()
    weights.last()
    outs.finish()
    outs.local.wait()
    exchange.finish()
    for copy in spots_sent:
        copy.wait_send()
    down_own.wait()


def attention(starts, rows, table, spots, qkv, blocks, out_rows, down, grads):
    low, full = jnp.bfloat16, jnp.float32
    tokens, width = rows.shape
    mixed = jax.ShapeDtypeStruct((PLANE, PAIRS, tokens, 2 * HEAD_SIZE), low)
    seq_len = PLANE * tokens
    wide_block = (blocks.shape[0], blocks.shape[1] // PLANE)
    return pl.pallas_call(
        attention_kernel,
        out_shape=(
            jax.ShapeDtypeStruct((PLANE, tokens, width), low),
            jax.ShapeDtypeStruct((PLANE, *table.shape), full),
            jax.ShapeDtypeStruct((RANKS, *qkv.shape[1:]), low),
            jax.ShapeDtypeStruct((8, width), full),
            jax.ShapeDtypeStruct((PLANE, PAIRS, 2, tokens, HEAD_SIZE), low),
            jax.ShapeDtypeStruct((PLANE, tokens, HEAD_SIZE), low),
            jax.ShapeDtypeStruct((PLANE, tokens, HEAD_SIZE), low),
            jax.ShapeDtypeStruct((PLANE, tokens, 1), full),
            jax.ShapeDtypeStruct((PLANE, tokens, 1), full),
            jax.ShapeDtypeStruct((8, seq_len), full),
            mixed,
            jax.ShapeDtypeStruct((RANKS, *wide_block), low),
            jax.ShapeDtypeStruct((RANKS, *out_rows.shape), low),
            jax.ShapeDtypeStruct((4 * down.shape[0], down.shape[1]), low),
            jax.ShapeDtypeStruct((PLANE, *grads.shape), low),
        ),
        in_specs=[pl.BlockSpec(memory_space=pltpu.SMEM)] + [ANY] * 8,
        out_specs=(VMEM,) * 11 + (ANY,) * 4,
        scratch_shapes=[
            pltpu.VMEM(mixed.shape, low),
            pltpu.VMEM((PLANE, *spots.shape), full),
            pltpu.VMEM((PLANE, tokens, width), low),
            pltpu.VMEM(blocks.shape, full),
            pltpu.VMEM((PLANE, *wide_block), low),
            pltpu.VMEM(down.shape, full),
            pltpu.VMEM(down.shape, low),
            pltpu.VMEM(out_rows.shape, full),
            pltpu.VMEM(out_rows.shape, low),
            pltpu.SemaphoreType.DMA((3,)),
            *PlaneExchange.scratch(),
            *WeightGather.scratch(),
            *WeightGather.scratch(),
            *SequenceGather.scratch(1),
            *ChipGather.scratch(PLANE),
            *SequenceGather.scratch(2),
            *SequenceGather.scratch(1),
            *SequenceGather.scratch(CHUNKS),
            *ChipGather.scratch(DOWN_PARTS),
            pltpu.SemaphoreType.DMA((PLANE,)),
            pltpu.SemaphoreType.DMA((PLANE,)),
            pltpu.SemaphoreType.DMA(()),
            pltpu.SemaphoreType.DMA(()),
        ],
        compiler_params=params(2),
        name="attention",
    )(starts, rows, table, spots, qkv, blocks, out_rows, down, grads)


def feed_kernel(
    rows_ref,
    grads_all,
    weight_ref,
    down_ref,
    normed_out,
    total_out,
    weight_grad_out,
    down_grad_out,
    *scratch,
):
    rows_all, slope_gate, slope_up, hidden_all, gate_grads = scratch[:5]
    normed_parts, down_parts, turned, stage, stage_sem = scratch[5:10]
    scratch = list(scratch[10:])

    def take(count):
        taken, scratch[:count] = scratch[:count], []
        return taken

    rows = SequenceGather(rows_ref, rows_all, take(5), 2)
    normed = SequenceScatter(normed_parts, normed_out, *take(2), take(4), 1)
    total = SequenceScatter(down_parts, total_out, *take(2), take(4), 1)
    d, c, x, core, z, y = place()
    greet(
        [(d, lax.rem(z + off, ZS) * YS + y) for off in range(1, ZS)] + [(d, z * YS + 1 - y)]
    )
    tokens, width = rows_ref.shape
    part = down_ref.shape[0]
    tile = 256
    blocks = PLANE // 2
    half = lax.div(z, 2)
    near, mid, far = near_first(z)

    def slots(side):
        return pl.ds(side * blocks, blocks)

    def columns(n, start=0, size=tile):
        return pl.ds(pl.multiple_of(n + start, size), size)

    def flat(ref, side):
        value = ref[slots(side)]
        return value.reshape(blocks * tokens, value.shape[2])

    def held(value, dtype=jnp.bfloat16):
        return value.astype(dtype).reshape(blocks, tokens, value.shape[1])

    def forward(side):
        @pl.loop(0, part, step=tile)
        def _(n):
            at, after = columns(n), columns(n, part)
            value = flat(rows_all, side)
            gate = jnp.dot(value, weight_ref[:, at], preferred_element_type=jnp.float32)
            up = jnp.dot(value, weight_ref[:, after], preferred_element_type=jnp.float32)
            sigmoid = jax.nn.sigmoid(gate)
            silu = gate * sigmoid
            hidden_all[slots(side), :, at] = held(silu * up)
            slope_up[slots(side), :, at] = held(silu, jnp.float32)
            slope_gate[slots(side), :, at] = held(
                up * sigmoid * (1.0 + gate * (1.0 - sigmoid)), jnp.float32
            )

    def downward(side):
        @pl.loop(0, width, step=2 * tile)
        def _(n):
            at = columns(n, 0, 2 * tile)
            down_parts[slots(side), :, at] = held(
                jnp.dot(
                    flat(hidden_all, side), down_ref[:, at], preferred_element_type=jnp.float32
                )
            )

    def backward(side):
        @pl.loop(0, part, step=tile)
        def _(n):
            at, after = columns(n), columns(n, part)
            grad = held(times_rows(flat(grads_all, side), down_ref[at, :]), jnp.float32)
            gate_grads[slots(side), :, at] = (grad * slope_gate[slots(side), :, at]).astype(
                jnp.bfloat16
            )
            gate_grads[slots(side), :, after] = (grad * slope_up[slots(side), :, at]).astype(
                jnp.bfloat16
            )

    def inward(side):
        @pl.loop(0, width, step=2 * tile)
        def _(n):
            at = columns(n, 0, 2 * tile)
            normed_parts[slots(side), :, at] = held(
                times_rows(flat(gate_grads, side), weight_ref[at, :])
            )

    tiles = [(hidden_all, grads_all, down_grad_out, n) for n in range(part // tile)]
    tiles += [(rows_all, gate_grads, weight_grad_out, n) for n in range(width // tile)]
    copies = []

    def weight_grad(i):
        left, right, out, n = tiles[i]
        if i >= 2:
            copies[i - 2].wait()
        value = left[:, :, n * tile : (n + 1) * tile].reshape(PLANE * tokens, tile)
        turned[...] = value.T

        @pl.loop(0, width, step=2 * tile)
        def _(m):
            at = columns(m, 0, 2 * tile)
            stage[i % 2, :, at] = jnp.dot(
                turned[...],
                right[:, :, at].reshape(PLANE * tokens, 2 * tile),
                preferred_element_type=jnp.float32,
            ).astype(jnp.bfloat16)

        copy = pltpu.make_async_copy(
            stage.at[i % 2], out.at[pl.ds(n * tile, tile)], stage_sem.at[i % 2]
        )
        copy.start()
        copies.append(copy)

    rows.first(by_block=True)
    rows.local.wait()
    rows.relay_block(near)
    rows.arrive_across(z)
    rows.arrive_across(near)
    forward(half)
    rows.relay_block(mid)
    rows.relay_block(far)
    backward(half)
    inward(half)
    normed.start(near, 0)
    normed.start(z, 0)
    rows.arrive_across(mid)
    rows.arrive_across(far)
    forward(1 - half)
    backward(1 - half)
    inward(1 - half)
    normed.start(far, 0)
    normed.start(mid, 0)
    normed.relay_one(near, 0)
    downward(1 - half)
    total.start(far, 0)
    total.start(mid, 0)
    normed.relay_one(far, 0)
    downward(half)
    total.start(near, 0)
    total.start(z, 0)
    normed.relay_one(mid, 0)
    for i in range(2):
        weight_grad(i)
    for pair in (far, mid, near):
        total.relay_one(pair, 0)
        weight_grad(len(copies))
    for i in range(len(copies), len(tiles)):
        weight_grad(i)
    normed.last(0)
    total.last(0)
    for copy in copies[-2:]:
        copy.wait()
    rows.finish()
    normed.finish()
    total.finish()


def feed(rows, grads, weight, down):
    part, width = down.shape
    low = rows.dtype
    tokens = rows.shape[0]
    summed = jax.ShapeDtypeStruct(rows.shape, jnp.float32)
    return pl.pallas_call(
        feed_kernel,
        out_shape=(
            summed,
            summed,
            jax.ShapeDtypeStruct(weight.shape, low),
            jax.ShapeDtypeStruct(down.shape, low),
        ),
        in_specs=[ANY] + [VMEM] * 3,
        out_specs=(VMEM,) * 2 + (ANY,) * 2,
        scratch_shapes=[
            pltpu.VMEM((PLANE, tokens, width), low),
            pltpu.VMEM((PLANE, tokens, part), jnp.float32),
            pltpu.VMEM((PLANE, tokens, part), jnp.float32),
            pltpu.VMEM((PLANE, tokens, part), low),
            pltpu.VMEM((PLANE, tokens, 2 * part), low),
            pltpu.VMEM((PLANE, tokens, width), low),
            pltpu.VMEM((PLANE, tokens, width), low),
            pltpu.VMEM((256, PLANE * tokens), low),
            pltpu.VMEM((2, 256, width), low),
            pltpu.SemaphoreType.DMA((2,)),
            *SequenceGather.scratch(2),
            *SequenceScatter.scratch(tokens, width, 1),
            *SequenceScatter.scratch(tokens, width, 1),
        ],
        compiler_params=params(5, 60),
        name="feed",
    )(rows, grads, weight, down)


def attention_back_kernel(
    query_ref,
    key_ref,
    value_ref,
    spot_ref,
    start_ref,
    key_spot_ref,
    table_ref,
    input_ref,
    qkv_ref,
    mixed_ref,
    parts_ref,
    rows_out,
    qkv_out,
    wide_out,
    *scratch,
):
    mixed_all, out_ref, grads, key_grad, value_grad, turned = scratch[:6]
    scratch = scratch[6:]
    exchange = PlaneExchange(mixed_ref, mixed_all, scratch[:3])
    weights = WeightScatter(parts_ref, out_ref, scratch[3:7], scratch[7:13])
    d, c, x, core, z, y = place()
    greet(plane_peers(d, c) + chip_peers(d, c, x, core))
    for off in range(1, PLANE + 1):
        exchange.send(off)
    weights.first()
    key_grad[...] = jnp.zeros_like(key_grad)
    value_grad[...] = jnp.zeros_like(value_grad)
    wide = 2 * HEAD_SIZE
    for step in range(PLANE):
        block = lax.rem(c + PLANE - step, PLANE)
        exchange.arrive(step)

        @pl.loop(0, PAIRS)
        def _(pair):
            keys = key_ref[...].reshape(key_grad.shape)
            values = value_ref[...].reshape(value_grad.shape)
            halves = []
            for half in range(2):
                query = query_ref[block, pair, half]
                grad = mixed_all[block, pair][:, half * HEAD_SIZE : (half + 1) * HEAD_SIZE]
                probs = probabilities(
                    query, keys, spot_ref[block], start_ref[block], key_spot_ref[:1]
                )
                grad_probs = times_rows(grad, values)
                delta = jnp.sum(probs * grad_probs, axis=-1, keepdims=True)
                grad_scores = (probs * (grad_probs - delta) * SCORE_SCALE).astype(jnp.bfloat16)
                halves.append(
                    jnp.dot(grad_scores, keys, preferred_element_type=jnp.float32)
                )
                key_grad[...] += transposed_times(grad_scores, query)
                value_grad[...] += transposed_times(probs.astype(jnp.bfloat16), grad)
            at = pl.ds(pl.multiple_of(pair * wide, wide), wide)
            grads[block, :, at] = rotate(
                jnp.concatenate(halves, axis=1), table_ref[block], back=True
            ).astype(jnp.bfloat16)

        weights.relay(step + 1)
        if step >= 2:
            weights.send(step - 1)
    tokens = grads.shape[1]
    for block in range(PLANE):
        span = slice(block * tokens, (block + 1) * tokens)
        both = jnp.concatenate([key_grad[span], value_grad[span]], axis=1)
        lane = lax.broadcasted_iota(jnp.int32, both.shape, 1)
        grads[block, :, PAIRS * wide :] = jnp.where(
            lane < HEAD_SIZE, rotate(both, table_ref[block], back=True), both
        ).astype(jnp.bfloat16)
    weights.send(PLANE - 1)
    width = input_ref.shape[2]
    rows = qkv_ref.shape[1]
    tile = 512

    @pl.loop(0, width // tile)
    def _(n):
        weight = qkv_ref[pl.ds(n * (tile // rows), tile // rows), :, :QKV_WIDTH]
        product = times_rows(
            grads[...].reshape(PLANE * tokens, QKV_WIDTH), weight.reshape(tile, QKV_WIDTH)
        )
        rows_out[:, :, pl.ds(pl.multiple_of(n * tile, tile), tile)] = product.astype(
            jnp.bfloat16
        ).reshape(PLANE, tokens, tile)

    weights.send(PLANE)

    @pl.loop(0, width // tile)
    def _(n):
        turned[...] = (
            input_ref[:, :, pl.ds(pl.multiple_of(n * tile, tile), tile)]
            .reshape(PLANE * tokens, tile)
            .T
        )
        product = jnp.dot(
            turned[...],
            grads[...].reshape(PLANE * tokens, QKV_WIDTH),
            preferred_element_type=jnp.float32,
        )
        qkv_out[pl.ds(n * (tile // rows), tile // rows)] = product.astype(
            jnp.bfloat16
        ).reshape(tile // rows, rows, QKV_WIDTH)

    weights.last()
    for source, start, after in wide_columns(wide_out.shape[1]):
        size = wide_out.shape[1] // (8 * PLANE)
        wide_out[:, after : after + size] = out_ref[source, :, start : start + size]
    exchange.finish()


def attention_back(
    query, keys, values, spots, starts, key_spots, table, inputs, qkv, mixed, parts
):
    low = jnp.bfloat16
    tokens = inputs.shape[1]
    sums = pltpu.VMEM((PLANE * tokens, HEAD_SIZE), jnp.float32)
    return pl.pallas_call(
        attention_back_kernel,
        out_shape=(
            jax.ShapeDtypeStruct(inputs.shape, low),
            jax.ShapeDtypeStruct((*qkv.shape[:2], QKV_WIDTH), low),
            jax.ShapeDtypeStruct((parts.shape[1], PLANE * parts.shape[2]), low),
        ),
        in_specs=[VMEM] * 11,
        out_specs=(VMEM,) * 3,
        scratch_shapes=[
            pltpu.VMEM(mixed.shape, low),
            pltpu.VMEM((PLANE, *parts.shape[1:]), low),
            pltpu.VMEM((PLANE, tokens, QKV_WIDTH), low),
            sums,
            sums,
            pltpu.VMEM((512, PLANE * tokens), low),
            *PlaneExchange.scratch(),
            *WeightScatter.scratch(*parts.shape[1:]),
        ],
        compiler_params=params(3),
        name="attention_back",
    )(query, keys, values, spots, starts, key_spots, table, inputs, qkv, mixed, parts)


def closing_kernel(
    rows_ref,
    parts_ref,
    outs_ref,
    down_ref,
    rows_out,
    query_out,
    keyval_out,
    outs_out,
    down_out,
    *scratch,
):
    out_ref, outs_sum = scratch[:2]
    scratch = list(scratch[2:])

    def take(count):
        taken, scratch[:count] = scratch[:count], []
        return taken

    scatter = SequenceScatter(rows_ref, rows_out, *take(2), take(4), CHUNKS)
    weights = WeightScatter(parts_ref, out_ref, take(4), take(6))
    chip = ChipScatter(outs_ref, *take(3), take(4), PLANE)
    outs = SequenceScatter(outs_sum, outs_out, *take(2), take(4), 1)
    down = ChipScatter(down_ref, *take(3), take(4), DOWN_PARTS)
    d, c, x, core, z, y = place()
    greet(plane_peers(d, c) + chip_peers(d, c, x, core))
    places = (*near_first(z)[::-1], z)
    slots = [place * YS + 1 - y for place in places] + [place * YS + y for place in places]
    weights.first()
    scatter.first()
    for j in slots:
        chip.start(j)
    for j in range(DOWN_PARTS):
        down.start(j)
    for off in range(1, PLANE + 1):
        weights.relay(off)
    for k in range(CHUNKS):
        scatter.relay(k)
        chip.relay(slots[2 * k])
        chip.relay(slots[2 * k + 1])
    for j in range(DOWN_PARTS):
        down.relay(j)
    for off in range(1, PLANE + 1):
        weights.send(off)
    for i, j in enumerate(slots):
        chip.total(j, outs_sum.at[j])
        if i < ZS:
            outs.start(places[i], 0)
        if i >= ZS and i < 2 * ZS - 1:
            outs.relay_one(places[i - ZS], 0)
    for j in range(DOWN_PARTS):
        down.total(j, down_out.at[j])
    for k in range(CHUNKS):
        scatter.last(k)
    weights.last()
    group_width = GROUP * HEAD_SIZE
    for source in range(PLANE):
        query_out[:, source * group_width : (source + 1) * group_width] = out_ref[
            source, :, :group_width
        ]
    for kind in range(2):
        start = group_width + kind * HEAD_SIZE
        for source in range(0, PLANE, 2):
            after = (kind * PLANE + source) * HEAD_SIZE
            keyval_out[:, after : after + 2 * HEAD_SIZE] = jnp.concatenate(
                [out_ref[source + i, :, start : start + HEAD_SIZE] for i in range(2)], axis=1
            )
    outs.last(0)
    scatter.finish()
    chip.finish()
    outs.finish()
    down.finish()


def closing(rows, parts, outs, down):
    return pl.pallas_call(
        closing_kernel,
        out_shape=(
            jax.ShapeDtypeStruct(rows.shape[1:], jnp.float32),
            jax.ShapeDtypeStruct((parts.shape[1], QUERY_HEADS * HEAD_SIZE), parts.dtype),
            jax.ShapeDtypeStruct((parts.shape[1], 2 * PLANE * HEAD_SIZE), parts.dtype),
            jax.ShapeDtypeStruct(outs.shape[1:], jnp.float32),
            jax.ShapeDtypeStruct((DOWN_PARTS, *down.shape[1:]), jnp.float32),
        ),
        in_specs=[VMEM] * 4,
        out_specs=(VMEM,) * 5,
        scratch_shapes=[
            pltpu.VMEM((PLANE, *parts.shape[1:]), parts.dtype),
            pltpu.VMEM((PLANE, *outs.shape[1:]), jnp.bfloat16),
            *SequenceScatter.scratch(*rows.shape[1:], CHUNKS),
            *WeightScatter.scratch(*parts.shape[1:]),
            *ChipScatter.scratch(PLANE, *outs.shape[1:]),
            *SequenceScatter.scratch(*outs.shape[1:], 1),
            *ChipScatter.scratch(DOWN_PARTS, *down.shape[1:]),
        ],
        compiler_params=params(4),
        name="closing",
    )(rows, parts, outs, down)


def body(
    layer_in,
    positions,
    doc_starts,
    out_grad,
    norm_gains,
    norm_gains_m,
    norm_gains_v,
    w_query,
    w_query_m,
    w_query_v,
    key_value_weight,
    key_value_first_moment,
    key_value_second_moment,
    w_out,
    w_out_m,
    w_out_v,
    w_gate_up,
    w_gate_up_m,
    w_gate_up_v,
    w_down,
    w_down_m,
    w_down_v,
):
    number_of_tokens = layer_in.shape[0]
    ctx_count = lax.axis_size("ctx")
    seq_len = number_of_tokens * ctx_count
    key_value_width = KEY_VALUE_HEADS * HEAD_SIZE
    query_group_size = QUERY_HEADS // KEY_VALUE_HEADS
    score_scale = 1.0 / math.sqrt(HEAD_SIZE)
    needed = -(-512 // number_of_tokens)
    shard_span = min(ctx_count, 1 << max(0, (needed - 1).bit_length()))
    width_of_block = shard_span * number_of_tokens
    count_of_blocks = ctx_count // shard_span
    key_places = lax.all_gather(positions, "ctx", axis=0, tiled=True)
    starts = doc_starts[0]
    own_docs = doc_lookup(positions, starts)
    key_docs = doc_lookup(key_places, starts)
    query_full, keyval_full, out_full, gains_full = (
        lax.all_gather(w_query.astype(jnp.bfloat16), ("dp", "ctx"), axis=0, tiled=True),
        lax.all_gather(key_value_weight.astype(jnp.bfloat16), ("dp", "ctx"), axis=0, tiled=True),
        lax.all_gather(w_out.astype(jnp.bfloat16), ("dp", "ctx"), axis=0, tiled=True),
        lax.all_gather(norm_gains.astype(jnp.bfloat16), ("dp", "ctx"), axis=1, tiled=True),
    )
    gain_one = gains_full[0].astype(jnp.float32)
    gain_two = gains_full[1].astype(jnp.float32)
    layer_rows = layer_in.astype(jnp.float32)
    normed_one, inverse_one = norm_forward(layer_rows)
    input_one = (normed_one * gain_one).astype(jnp.bfloat16)
    query_pre = jnp.dot(input_one, query_full, preferred_element_type=jnp.float32)
    key_value_projected = jnp.dot(input_one, keyval_full, preferred_element_type=jnp.float32)
    cosine_table, sine_table = rope_tables(positions, HEAD_SIZE)
    query_rows = (
        apply_rotation(
            query_pre.reshape(number_of_tokens, QUERY_HEADS, HEAD_SIZE), cosine_table, sine_table
        )
        .astype(jnp.bfloat16)
        .reshape(number_of_tokens, KEY_VALUE_HEADS, query_group_size, HEAD_SIZE)
    )
    keys_own = (
        apply_rotation(
            key_value_projected[:, :key_value_width].reshape(
                number_of_tokens, KEY_VALUE_HEADS, HEAD_SIZE
            ),
            cosine_table,
            sine_table,
        )
        .astype(jnp.bfloat16)
        .reshape(number_of_tokens, key_value_width)
    )
    values_own = key_value_projected[:, key_value_width:].astype(jnp.bfloat16)
    every_key, every_value = (
        lax.all_gather(keys_own, "ctx", axis=0, tiled=True),
        lax.all_gather(values_own, "ctx", axis=0, tiled=True),
    )
    blocked_keys = every_key.reshape(count_of_blocks, width_of_block, KEY_VALUE_HEADS, HEAD_SIZE)
    blocked_values = every_value.reshape(
        count_of_blocks, width_of_block, KEY_VALUE_HEADS, HEAD_SIZE
    )
    place_blocks = key_places.reshape(count_of_blocks, width_of_block)
    doc_blocks = key_docs.reshape(count_of_blocks, width_of_block)

    def visible(place_blk, doc_blk):
        allowed = (place_blk[None, :] <= positions[:, None]) & (
            doc_blk[None, :] == own_docs[:, None]
        )
        return allowed[:, None, None, :]

    def scores_of(key_blk):
        return (
            jnp.einsum("tkgd,nkd->tkgn", query_rows, key_blk, preferred_element_type=jnp.float32)
            * score_scale
        )

    def stats_step(carry, block):
        row_top, row_total = carry
        key_blk, place_blk, doc_blk = block
        allowed = visible(place_blk, doc_blk)
        masked = jnp.where(allowed, scores_of(key_blk), masked_score)
        new_top = jnp.maximum(row_top, jnp.max(masked, axis=-1, keepdims=True))
        row_total = row_total * jnp.exp(row_top - new_top) + jnp.sum(
            jnp.where(allowed, jnp.exp(masked - new_top), 0.0), axis=-1, keepdims=True
        )
        return ((new_top, row_total), None)

    statistic_shape = (number_of_tokens, KEY_VALUE_HEADS, query_group_size, 1)
    (row_top, row_total), unused = lax.scan(
        stats_step,
        (
            jnp.full(statistic_shape, masked_score, jnp.float32),
            jnp.zeros(statistic_shape, jnp.float32),
        ),
        (blocked_keys, place_blocks, doc_blocks),
    )
    log_total = row_top + jnp.log(row_total)

    def probs_of(key_blk, place_blk, doc_blk):
        allowed = visible(place_blk, doc_blk)
        masked = jnp.where(allowed, scores_of(key_blk), masked_score)
        return jnp.where(allowed, jnp.exp(masked - log_total), 0.0)

    def output_step(carry, block):
        key_blk, value_blk, place_blk, doc_blk = block
        probs_low = probs_of(key_blk, place_blk, doc_blk).astype(jnp.bfloat16)
        added = jnp.einsum(
            "tkgn,nkd->tkgd", probs_low, value_blk, preferred_element_type=jnp.float32
        )
        return (carry + added, None)

    attention_output, unused = lax.scan(
        output_step,
        jnp.zeros((number_of_tokens, KEY_VALUE_HEADS, query_group_size, HEAD_SIZE), jnp.float32),
        (blocked_keys, blocked_values, place_blocks, doc_blocks),
    )
    mixed = attention_output.reshape(number_of_tokens, QUERY_HEADS * HEAD_SIZE).astype(jnp.bfloat16)
    middle = layer_rows + jnp.dot(mixed, out_full, preferred_element_type=jnp.float32)
    normed_two, inverse_two = norm_forward(middle)
    input_two = (normed_two * gain_two).astype(jnp.bfloat16)
    gate_up_low = w_gate_up.astype(jnp.bfloat16)
    down_low = w_down.astype(jnp.bfloat16)
    columns = input_two
    gate_up = jnp.dot(
        columns,
        lax.all_gather(gate_up_low, ("dp", "ctx"), axis=0, tiled=True),
        preferred_element_type=jnp.float32,
    )
    gate_part = gate_up[:, :FF]
    up_part = gate_up[:, FF:]
    sigmoid_gate = jax.nn.sigmoid(gate_part)
    silu_gate = gate_part * sigmoid_gate
    hidden = (silu_gate * up_part).astype(jnp.bfloat16)
    columns = hidden
    down_sum = jnp.dot(
        columns,
        lax.all_gather(down_low, ("dp", "ctx"), axis=0, tiled=True),
        preferred_element_type=jnp.float32,
    )
    layer_out = (middle + down_sum).astype(jnp.bfloat16)
    grad_rows = out_grad.astype(jnp.float32)
    grad_hidden = times_transposed(
        out_grad, lax.all_gather(down_low, ("dp", "ctx"), axis=0, tiled=True)
    )
    grad_gate = grad_hidden * up_part * sigmoid_gate * (1.0 + gate_part * (1.0 - sigmoid_gate))
    grad_up = grad_hidden * silu_gate
    grad_gate_up = jnp.concatenate([grad_gate, grad_up], axis=1).astype(jnp.bfloat16)
    down_grad = lax.psum_scatter(
        transposed_times(hidden, out_grad), ("dp", "ctx"), scatter_dimension=0, tiled=True
    )
    grad_normed_two = times_transposed(
        grad_gate_up, lax.all_gather(gate_up_low, ("dp", "ctx"), axis=0, tiled=True)
    )
    gate_up_grad = lax.psum_scatter(
        transposed_times(input_two, grad_gate_up), ("dp", "ctx"), scatter_dimension=0, tiled=True
    )
    grad_norm_two, gain_two_grad = norm_backward(grad_normed_two, normed_two, inverse_two, gain_two)
    grad_middle = grad_rows + grad_norm_two
    grad_middle_low = grad_middle.astype(jnp.bfloat16)
    out_term = transposed_times(mixed, grad_middle_low)
    grad_mixed = (
        times_transposed(grad_middle_low, out_full)
        .astype(jnp.bfloat16)
        .reshape(number_of_tokens, KEY_VALUE_HEADS, query_group_size, HEAD_SIZE)
    )
    delta = jnp.sum(grad_mixed.astype(jnp.float32) * attention_output, axis=-1, keepdims=True)

    def back_step(grad_query, block):
        key_blk, value_blk, place_blk, doc_blk = block
        probs = probs_of(key_blk, place_blk, doc_blk)
        probs_low = probs.astype(jnp.bfloat16)
        grad_probs = jnp.einsum(
            "tkgd,nkd->tkgn", grad_mixed, value_blk, preferred_element_type=jnp.float32
        )
        grad_scores = (probs * (grad_probs - delta) * score_scale).astype(jnp.bfloat16)
        grad_query = grad_query + jnp.einsum(
            "tkgn,nkd->tkgd", grad_scores, key_blk, preferred_element_type=jnp.float32
        )
        key_grad = jnp.einsum(
            "tkgn,tkgd->nkd", grad_scores, query_rows, preferred_element_type=jnp.float32
        )
        value_grad = jnp.einsum(
            "tkgn,tkgd->nkd", probs_low, grad_mixed, preferred_element_type=jnp.float32
        )
        return (grad_query, (key_grad, value_grad))

    grad_query, (key_grads, value_grads) = lax.scan(
        back_step,
        jnp.zeros((number_of_tokens, KEY_VALUE_HEADS, query_group_size, HEAD_SIZE), jnp.float32),
        (blocked_keys, blocked_values, place_blocks, doc_blocks),
    )
    summed_key_gradient, value_sum = (
        lax.psum_scatter(
            key_grads.reshape(seq_len, key_value_width).astype(jnp.bfloat16),
            "ctx",
            scatter_dimension=0,
            tiled=True,
        ).astype(jnp.float32),
        lax.psum_scatter(
            value_grads.reshape(seq_len, key_value_width).astype(jnp.bfloat16),
            "ctx",
            scatter_dimension=0,
            tiled=True,
        ).astype(jnp.float32),
    )
    key_gradient_unrotated = reverse_rotation(
        summed_key_gradient.reshape(number_of_tokens, KEY_VALUE_HEADS, HEAD_SIZE),
        cosine_table,
        sine_table,
    ).reshape(number_of_tokens, key_value_width)
    grad_keyval = jnp.concatenate([key_gradient_unrotated, value_sum], axis=1).astype(jnp.bfloat16)
    grad_query_low = (
        reverse_rotation(
            grad_query.reshape(number_of_tokens, QUERY_HEADS, HEAD_SIZE), cosine_table, sine_table
        )
        .reshape(number_of_tokens, QUERY_HEADS * HEAD_SIZE)
        .astype(jnp.bfloat16)
    )
    grad_normed_one = times_transposed(grad_query_low, query_full) + times_transposed(
        grad_keyval, keyval_full
    )
    query_term = transposed_times(input_one, grad_query_low)
    keyval_term = transposed_times(input_one, grad_keyval)
    grad_norm_one, gain_one_grad = norm_backward(grad_normed_one, normed_one, inverse_one, gain_one)
    in_grad = grad_middle + grad_norm_one
    gain_term = jnp.stack([gain_one_grad, gain_two_grad])
    query_grad, keyval_grad, out_weight_grad, gains_grad = (
        lax.psum_scatter(query_term, ("dp", "ctx"), scatter_dimension=0, tiled=True),
        lax.psum_scatter(keyval_term, ("dp", "ctx"), scatter_dimension=0, tiled=True),
        lax.psum_scatter(out_term, ("dp", "ctx"), scatter_dimension=0, tiled=True),
        lax.psum_scatter(gain_term, ("dp", "ctx"), scatter_dimension=1, tiled=True),
    )
    rates = rates_for(seq_len)
    gains_m_new, gains_v_new, gains_new = adamw(
        norm_gains, gains_grad, norm_gains_m, norm_gains_v, rates[0], 0.0
    )
    query_m_new, query_v_new, query_new = adamw(
        w_query, query_grad, w_query_m, w_query_v, rates[1], weight_decay
    )
    keyval_m_new, keyval_v_new, keyval_new = adamw(
        key_value_weight,
        keyval_grad,
        key_value_first_moment,
        key_value_second_moment,
        rates[2],
        weight_decay,
    )
    out_m_new, out_v_new, out_new = adamw(
        w_out, out_weight_grad, w_out_m, w_out_v, rates[3], weight_decay
    )
    gate_up_m_new, gate_up_v_new, gate_up_new = adamw(
        w_gate_up, gate_up_grad, w_gate_up_m, w_gate_up_v, rates[4], weight_decay
    )
    down_m_new, down_v_new, down_new = adamw(
        w_down, down_grad, w_down_m, w_down_v, rates[5], weight_decay
    )
    return (
        layer_out,
        in_grad,
        gains_grad,
        gains_m_new,
        gains_v_new,
        gains_new,
        query_grad,
        query_m_new,
        query_v_new,
        query_new,
        keyval_grad,
        keyval_m_new,
        keyval_v_new,
        keyval_new,
        out_weight_grad,
        out_m_new,
        out_v_new,
        out_new,
        gate_up_grad,
        gate_up_m_new,
        gate_up_v_new,
        gate_up_new,
        down_grad,
        down_m_new,
        down_v_new,
        down_new,
    )


def tensor_parallel(
    layer_in,
    positions,
    doc_starts,
    out_grad,
    norm_gains,
    norm_gains_m,
    norm_gains_v,
    w_query,
    w_query_m,
    w_query_v,
    key_value_weight,
    key_value_first_moment,
    key_value_second_moment,
    w_out,
    w_out_m,
    w_out_v,
    w_gate_up,
    w_gate_up_m,
    w_gate_up_v,
    w_down,
    w_down_m,
    w_down_v,
):
    low = jnp.bfloat16
    own_tokens, width = layer_in.shape
    seq_len = own_tokens * PLANE
    group = GROUP
    group_width = group * HEAD_SIZE
    ff_part = FF // PLANE
    rows = w_query.shape[0]

    gains_low = norm_gains.astype(low)
    small = jnp.broadcast_to(
        jnp.pad(gains_low.T, ((0, 0), (0, 126)))[None], (PLANE, rows, 128)
    )
    attention_blocks = jnp.concatenate(
        [
            w_query.astype(low).reshape(rows, PLANE, group_width).transpose(1, 0, 2),
            key_value_weight.astype(low)
            .reshape(rows, 2, PLANE, HEAD_SIZE)
            .transpose(2, 0, 1, 3)
            .reshape(PLANE, rows, 2 * HEAD_SIZE),
            small,
        ],
        axis=2,
    )
    spots = jnp.broadcast_to(positions[None, :].astype(jnp.float32), (8, own_tokens))
    cosine_own, sine_own = rope_tables(positions, HEAD_SIZE)
    cosine_own, sine_own = cosine_own[:, 0], sine_own[:, 0]
    table = jnp.concatenate([cosine_own, cosine_own, -sine_own, sine_own], axis=1)
    (
        input_one_all,
        table_all,
        attention_all,
        gain_rows,
        query_rows,
        key_rows,
        value_rows,
        token_spots,
        token_starts,
        key_spots,
        mixed_parts,
        feed_all,
        out_all,
        down_all,
        grads_all,
    ) = attention(
        doc_starts,
        layer_in,
        table,
        spots,
        attention_blocks,
        w_gate_up,
        w_out,
        w_down,
        out_grad,
    )
    gain_one, gain_two = gain_rows[0], gain_rows[1]
    mixed = mixed_parts.transpose(2, 0, 1, 3).reshape(own_tokens, width)
    out_weight = out_all.reshape(width, width)
    branch = jnp.dot(mixed, out_weight, preferred_element_type=jnp.float32)

    layer_rows = layer_in.astype(jnp.float32)
    middle = layer_rows + branch
    normed_two, inverse_two = norm_forward(middle)
    grad_normed_two, down_sum, feed_term, down_term = feed(
        (normed_two * gain_two).astype(low),
        grads_all,
        feed_all.reshape(width, 2 * ff_part),
        down_all,
    )
    layer_out = (middle + down_sum).astype(low)

    grad_norm_two, unused = norm_backward(grad_normed_two, normed_two, inverse_two, gain_two)
    grad_middle = out_grad.astype(jnp.float32) + grad_norm_two
    grad_middle_low = grad_middle.astype(low)
    out_term = transposed_times(mixed, grad_middle_low).astype(low)
    grad_mixed = (
        times_transposed(grad_middle_low, out_weight)
        .astype(low)
        .reshape(own_tokens, PLANE, PAIRS, 2 * HEAD_SIZE)
        .transpose(1, 2, 0, 3)
    )
    one_parts, qkv_term, feed_grad = attention_back(
        query_rows,
        key_rows,
        value_rows,
        token_spots,
        token_starts,
        key_spots,
        table_all,
        input_one_all,
        attention_all,
        grad_mixed,
        feed_term.reshape(RANKS, rows, 2 * ff_part),
    )
    gate_up_grad = feed_grad.astype(jnp.float32)
    grad_normed_one, query_grad, keyval_grad, out_weight_grad, down_grad = closing(
        one_parts,
        qkv_term,
        out_term.reshape(RANKS, rows, width),
        down_term.reshape(4 * DOWN_PARTS, -1, width),
    )
    down_grad = down_grad.reshape(w_down.shape)
    normed_one, inverse_one = norm_forward(layer_rows)
    grad_norm_one, unused = norm_backward(grad_normed_one, normed_one, inverse_one, gain_one)
    in_grad = grad_middle + grad_norm_one
    query_grad = query_grad.astype(jnp.float32)
    keyval_grad = keyval_grad.astype(jnp.float32)

    def low_times(weight, grad):
        return jnp.sum(weight.astype(low).astype(jnp.float32) * grad, axis=1)

    gains_grad = jnp.stack(
        [
            low_times(w_query, query_grad) + low_times(key_value_weight, keyval_grad),
            low_times(w_gate_up, gate_up_grad),
        ]
    ) / gains_low.astype(jnp.float32)

    rates = rates_for(seq_len)
    return (
        layer_out,
        in_grad,
        gains_grad,
        *adamw(norm_gains, gains_grad, norm_gains_m, norm_gains_v, rates[0], 0.0),
        query_grad,
        *adamw(w_query, query_grad, w_query_m, w_query_v, rates[1], weight_decay),
        keyval_grad,
        *adamw(
            key_value_weight,
            keyval_grad,
            key_value_first_moment,
            key_value_second_moment,
            rates[2],
            weight_decay,
        ),
        out_weight_grad,
        *adamw(w_out, out_weight_grad, w_out_m, w_out_v, rates[3], weight_decay),
        gate_up_grad,
        *adamw(w_gate_up, gate_up_grad, w_gate_up_m, w_gate_up_v, rates[4], weight_decay),
        down_grad,
        *adamw(w_down, down_grad, w_down_m, w_down_v, rates[5], weight_decay),
    )


def solution(mesh):
    planned = tensor_parallel if dict(mesh.shape) == {"dp": 2 * XS, "ctx": ZS * YS} else body
    return jax.shard_map(
        planned,
        mesh=mesh,
        in_specs=(
            P(("dp", "ctx"), None),
            P(("dp", "ctx")),
            P("dp", None),
            P(("dp", "ctx"), None),
            P(None, ("dp", "ctx")),
            P(None, ("dp", "ctx")),
            P(None, ("dp", "ctx")),
            P(("dp", "ctx"), None),
            P(("dp", "ctx"), None),
            P(("dp", "ctx"), None),
            P(("dp", "ctx"), None),
            P(("dp", "ctx"), None),
            P(("dp", "ctx"), None),
            P(("dp", "ctx"), None),
            P(("dp", "ctx"), None),
            P(("dp", "ctx"), None),
            P(("dp", "ctx"), None),
            P(("dp", "ctx"), None),
            P(("dp", "ctx"), None),
            P(("dp", "ctx"), None),
            P(("dp", "ctx"), None),
            P(("dp", "ctx"), None),
        ),
        out_specs=(
            P(("dp", "ctx"), None),
            P(("dp", "ctx"), None),
            P(None, ("dp", "ctx")),
            P(None, ("dp", "ctx")),
            P(None, ("dp", "ctx")),
            P(None, ("dp", "ctx")),
            P(("dp", "ctx"), None),
            P(("dp", "ctx"), None),
            P(("dp", "ctx"), None),
            P(("dp", "ctx"), None),
            P(("dp", "ctx"), None),
            P(("dp", "ctx"), None),
            P(("dp", "ctx"), None),
            P(("dp", "ctx"), None),
            P(("dp", "ctx"), None),
            P(("dp", "ctx"), None),
            P(("dp", "ctx"), None),
            P(("dp", "ctx"), None),
            P(("dp", "ctx"), None),
            P(("dp", "ctx"), None),
            P(("dp", "ctx"), None),
            P(("dp", "ctx"), None),
            P(("dp", "ctx"), None),
            P(("dp", "ctx"), None),
            P(("dp", "ctx"), None),
            P(("dp", "ctx"), None),
        ),
        check_vma=False,
    )
```

```python
import functools
import math

import jax
import jax.numpy as jnp
from jax import lax
from jax.experimental import pallas as pl
from jax.experimental.pallas import tpu as pltpu
from jax.sharding import PartitionSpec as P

MODEL_WIDTH = 2048
QUERY_HEADS = 32
KEY_VALUE_HEADS = 8
HEAD_SIZE = 64
FF = 8192
STEP = 10


eps_norm = 1e-05
rope_base = 500000.0
beta_one = 0.9
beta_two = 0.95
eps_adam = 1e-08
weight_decay = 0.1
masked_score = -1e30


def rates_for(seq_len):
    return (
        0.6,
        0.8 / math.sqrt(MODEL_WIDTH // 4),
        0.8 / math.sqrt(MODEL_WIDTH),
        0.8 / math.sqrt(max(220 * MODEL_WIDTH // seq_len, 1)),
        0.8 / math.sqrt(MODEL_WIDTH),
        0.8 / math.sqrt(FF // 2),
    )


def adamw(weight, grad_sum, first, second, rate, decay):
    first_new = beta_one * first + (1.0 - beta_one) * grad_sum
    second_new = beta_two * second + (1.0 - beta_two) * grad_sum * grad_sum
    first_hat = first_new / (1.0 - beta_one**STEP)
    second_hat = second_new / (1.0 - beta_two**STEP)
    weight_new = weight - rate * (first_hat / (jnp.sqrt(second_hat) + eps_adam) + decay * weight)
    return (first_new, second_new, weight_new)


def norm_forward(layer_rows):
    inverse = lax.rsqrt(jnp.mean(layer_rows * layer_rows, axis=-1, keepdims=True) + eps_norm)
    return (layer_rows * inverse, inverse)


def norm_backward(grad_out, normed, inverse, gain_row):
    scaled = grad_out * gain_row
    grad_in = inverse * (scaled - normed * jnp.mean(scaled * normed, axis=-1, keepdims=True))
    return (grad_in, jnp.sum(grad_out * normed, axis=0))


def rope_tables(token_placement, head_dim):
    half_dim = head_dim // 2
    frequencies = jnp.exp(
        jnp.arange(half_dim, dtype=jnp.float32) * (-2.0 * math.log(rope_base) / head_dim)
    )
    angles = token_placement.astype(jnp.float32)[:, None] * frequencies[None, :]
    return (jnp.cos(angles)[:, None, :], jnp.sin(angles)[:, None, :])


def apply_rotation(value_rows, cosine_table, sine_table):
    half_dim = value_rows.shape[-1] // 2
    first_half = value_rows[..., :half_dim]
    second_half = value_rows[..., half_dim:]
    return jnp.concatenate(
        [
            first_half * cosine_table - second_half * sine_table,
            second_half * cosine_table + first_half * sine_table,
        ],
        axis=-1,
    )


def reverse_rotation(grad_rows, cosine_table, sine_table):
    half_dim = grad_rows.shape[-1] // 2
    first_half = grad_rows[..., :half_dim]
    second_half = grad_rows[..., half_dim:]
    return jnp.concatenate(
        [
            first_half * cosine_table + second_half * sine_table,
            second_half * cosine_table - first_half * sine_table,
        ],
        axis=-1,
    )


def doc_lookup(token_placement, starts):
    return jnp.sum((token_placement[:, None] >= starts[None, :]).astype(jnp.int32), axis=1) - 1


def times_transposed(left, right):
    return lax.dot_general(
        left, right, (((1,), (1,)), ((), ())), preferred_element_type=jnp.float32
    )


def transposed_times(left, right):
    return lax.dot_general(
        left, right, (((0,), (0,)), ((), ())), preferred_element_type=jnp.float32
    )


XS = 2
YS = 2
ZS = 4
PLANE = ZS * YS
RANKS = 2 * XS * PLANE
MESH = pl.DeviceIdType.MESH


def place():
    d = lax.axis_index("dp")
    c = lax.axis_index("ctx")
    return d, c, lax.div(d, 2), lax.rem(d, 2), lax.div(c, YS), lax.rem(c, YS)


def remote(src, dst, send_sem, recv_sem, d, c):
    return pltpu.make_async_remote_copy(
        src_ref=src,
        dst_ref=dst,
        send_sem=send_sem,
        recv_sem=recv_sem,
        device_id=(d, c),
        device_id_type=MESH,
    )


def greet(peers):
    barrier = pltpu.get_barrier_semaphore()
    for d, c in peers:
        pl.semaphore_signal(barrier, inc=1, device_id=(d, c), device_id_type=MESH)
    pl.semaphore_wait(barrier, len(peers))


def plane_peers(d, c):
    return [(d, lax.rem(c + k, PLANE)) for k in range(1, PLANE)]


def chip_peers(d, c, x, core):
    return [(x * 2 + 1 - core, c), ((1 - x) * 2 + core, c)]


def add_into(target, sources, rows, step=16):
    @pl.loop(0, rows, step=step)
    def _(r):
        at = pl.ds(pl.multiple_of(r, step), step)
        total = sources[0][at].astype(jnp.float32)
        for source in sources[1:]:
            total = total + source[at].astype(jnp.float32)
        target[at] = total.astype(target.dtype)


def near_first(z):
    half = lax.div(z, 2)
    return [half * 4 + 1 - z, 2 - half, 3 - 3 * half]


def is_inner(z):
    return (z == 1) | (z == 2)


class SequenceGather:
    def __init__(self, own, out, sems, chunks):
        self.own, self.out, self.chunks = own, out, chunks
        self.zs, self.zr, self.ys, self.yr, self.local_sem = sems
        self.d, self.c, _, _, self.z, self.y = place()
        self.rows = own.shape[0] // chunks
        self.sent = []

    @staticmethod
    def scratch(chunks):
        return [
            pltpu.SemaphoreType.DMA((ZS, chunks)),
            pltpu.SemaphoreType.DMA((ZS, chunks)),
            pltpu.SemaphoreType.DMA((ZS, chunks)),
            pltpu.SemaphoreType.DMA((ZS, chunks)),
            pltpu.SemaphoreType.DMA(()),
        ]

    def part(self, ref, k):
        return ref.at[pl.ds(k * self.rows, self.rows)]

    def across(self, z, k, src):
        slot = z * YS + self.y
        return remote(
            src,
            self.part(self.out.at[slot], k),
            self.ys.at[z, k],
            self.yr.at[z, k],
            self.d,
            self.z * YS + 1 - self.y,
        )

    def along(self, to, k):
        return remote(
            self.part(self.own, k),
            self.part(self.out.at[self.c], k),
            self.zs.at[to, k],
            self.zr.at[self.z, k],
            self.d,
            to * YS + self.y,
        )

    def start(self, copy):
        copy.start()
        self.sent.append(copy)

    def first(self, by_block=False):
        self.local = pltpu.make_async_copy(self.own, self.out.at[self.c], self.local_sem)
        self.local.start()
        near, mid, _ = near_first(self.z)
        if by_block:
            for k in range(self.chunks):
                self.start(self.across(self.z, k, self.part(self.own, k)))
            for to in (mid, near):
                for k in range(self.chunks):
                    self.start(self.along(to, k))
            return
        for k in range(self.chunks):
            for to in (mid, near):
                self.start(self.along(to, k))
            self.start(self.across(self.z, k, self.part(self.own, k)))

    def inward(self, i, source, k):
        near, _, far = near_first(self.z)
        block = self.part(self.out.at[source * YS + self.y], k)
        return remote(
            block,
            block,
            self.zs.at[(far, self.z)[i], k],
            self.zr.at[source, k],
            self.d,
            near * YS + self.y,
        )

    def relay_one(self, source, k):
        slot = source * YS + self.y
        block = self.part(self.out.at[slot], k)
        remote(
            block, block, self.zs.at[source, k], self.zr.at[source, k], self.d, slot
        ).wait_recv()
        self.start(self.across(source, k, block))

    def relay_half(self):
        for k in range(self.chunks):
            self.relay_far(k)

    def relay_far(self, k):
        _, mid, far = near_first(self.z)
        for i, source in enumerate((mid, far)):
            self.relay_one(source, k)

            @pl.when(is_inner(self.z))
            def _(i=i, source=source):
                self.inward(i, source, k).start()

    def relay(self, k):
        self.relay_one(near_first(self.z)[0], k)
        self.relay_far(k)

    def relay_block(self, source):
        for k in range(self.chunks):
            self.relay_one(source, k)

    def arrive_across(self, z):
        for k in range(self.chunks):
            block = self.part(self.out.at[z * YS + 1 - self.y], k)
            remote(
                block,
                block,
                self.ys.at[z, k],
                self.yr.at[z, k],
                self.d,
                self.z * YS + 1 - self.y,
            ).wait_recv()

    def finish(self):
        for copy in self.sent:
            copy.wait_send()
        _, mid, far = near_first(self.z)

        @pl.when(is_inner(self.z))
        def _():
            for k in range(self.chunks):
                for i, source in enumerate((mid, far)):
                    self.inward(i, source, k).wait_send()

    def last(self):
        for z in range(ZS):
            self.arrive_across(z)
        self.finish()
        self.local.wait()


class SequenceScatter:
    def __init__(self, parts, out, ybuf, zbuf, sems, chunks):
        self.parts, self.out, self.chunks = parts, out, chunks
        self.ybuf, self.zbuf = ybuf, zbuf
        self.ys, self.yr, self.zs, self.zr = sems
        self.d, self.c, _, _, self.z, self.y = place()
        self.rows = parts.shape[1] // chunks
        self.sent = []

    @staticmethod
    def scratch(rows, width, chunks):
        return [
            pltpu.VMEM((ZS, rows, width), jnp.bfloat16),
            pltpu.VMEM((ZS, rows, width), jnp.bfloat16),
            pltpu.SemaphoreType.DMA((ZS, chunks)),
            pltpu.SemaphoreType.DMA((ZS, chunks)),
            pltpu.SemaphoreType.DMA((ZS, chunks)),
            pltpu.SemaphoreType.DMA((ZS, chunks)),
        ]

    def span(self, k):
        return pl.ds(k * self.rows, self.rows)

    def across(self, z, k):
        return remote(
            self.parts.at[z * YS + 1 - self.y, self.span(k)],
            self.ybuf.at[z, self.span(k)],
            self.ys.at[z, k],
            self.yr.at[z, k],
            self.d,
            self.z * YS + 1 - self.y,
        )

    def along(self, to, k, slot):
        return remote(
            self.ybuf.at[to, self.span(k)],
            self.zbuf.at[slot, self.span(k)],
            self.zs.at[to, k],
            self.zr.at[slot, k],
            self.d,
            to * YS + self.y,
        )

    def inward(self, i, to, k):
        return remote(
            self.ybuf.at[to, self.span(k)],
            self.zbuf.at[2 + i, self.span(k)],
            self.zs.at[to, k],
            self.zr.at[2 + i, k],
            self.d,
            near_first(self.z)[0] * YS + self.y,
        )

    def start(self, z, k):
        copy = self.across(z, k)
        copy.start()
        self.sent.append(copy)

    def first(self):
        for k in range(self.chunks):
            for z in (*near_first(self.z)[::-1], self.z):
                self.start(z, k)

    def added(self, z, k):
        self.across(z, k).wait_recv()
        block = self.ybuf.at[z, self.span(k)]
        add_into(block, [self.parts.at[z * YS + self.y, self.span(k)], block], self.rows)

    def relay_near(self, k):
        near = near_first(self.z)[0]
        self.added(near, k)
        copy = self.along(near, k, 0)
        copy.start()
        self.sent.append(copy)

    def relay_far(self, k):
        _, mid, far = near_first(self.z)
        for to in (far, mid):
            self.added(to, k)

            @pl.when(jnp.logical_not(is_inner(self.z)))
            def _(to=to, i=0 if to is mid else 1):
                self.inward(i, to, k).start()

        @pl.when(is_inner(self.z))
        def _():
            for i, to in ((1, far), (0, mid)):
                self.inward(i, to, k).wait_recv()
                block = self.ybuf.at[to, self.span(k)]
                add_into(block, [block, self.zbuf.at[2 + i, self.span(k)]], self.rows)
                self.along(to, k, 1).start()

    def relay(self, k):
        self.relay_far(k)
        self.relay_near(k)

    def last(self, k):
        self.across(self.z, k).wait_recv()
        blocks = [self.parts.at[self.c, self.span(k)], self.ybuf.at[self.z, self.span(k)]]
        near, mid, _ = near_first(self.z)
        for slot, source in enumerate((near, mid)):
            block = self.zbuf.at[slot, self.span(k)]
            self.along(source, k, slot).wait_recv()
            blocks.append(block)
        add_into(self.out.at[self.span(k)], blocks, self.rows)

    def finish(self):
        for copy in self.sent:
            copy.wait_send()
        _, mid, far = near_first(self.z)
        for k in range(self.chunks):
            for to in (mid, far):
                self.along(to, k, 1).wait_send()


class ChipGather:
    def __init__(self, out, sems, count, rows=None):
        self.out, self.count, self.rows = out, count, rows
        self.cs, self.cr, self.xs, self.xr = sems
        self.d, self.c, self.x, self.core, _, _ = place()
        self.sent = []

    @staticmethod
    def scratch(count):
        return [
            pltpu.SemaphoreType.DMA((2, count)),
            pltpu.SemaphoreType.DMA((2, count)),
            pltpu.SemaphoreType.DMA((count,)),
            pltpu.SemaphoreType.DMA((count,)),
        ]

    def block(self, slot):
        if self.rows is None:
            return self.out.at[slot]
        return self.out.at[pl.ds(slot * self.rows, self.rows)]

    def to_core(self, far, j, src=None):
        x = 1 - self.x if far else self.x
        block = self.block((x * 2 + self.core) * self.count + j)
        return remote(
            block if src is None else src,
            block,
            self.cs.at[far, j],
            self.cr.at[far, j],
            self.x * 2 + 1 - self.core,
            self.c,
        )

    def to_x(self, j, src=None):
        block = self.block(self.d * self.count + j)
        return remote(
            block if src is None else src,
            block,
            self.xs.at[j],
            self.xr.at[j],
            (1 - self.x) * 2 + self.core,
            self.c,
        )

    def start(self, j, src=None):
        for copy in (self.to_x(j, src), self.to_core(0, j, src)):
            copy.start()
            self.sent.append(copy)

    def relay(self, j):
        self.to_x(j).wait_recv()
        copy = self.to_core(1, j)
        copy.start()
        self.sent.append(copy)

    def last(self):
        for far in (0, 1):
            for j in range(self.count):
                self.to_core(far, j).wait_recv()
        for copy in self.sent:
            copy.wait_send()


class WeightGather:
    def __init__(self, blocks, out, sems):
        self.blocks, self.out = blocks, out
        self.ps, self.pr, self.local_sem = sems[:3]
        self.chip = ChipGather(out, sems[3:], PLANE)
        self.d, self.c = self.chip.d, self.chip.c
        self.sent = []

    @staticmethod
    def scratch():
        return [
            pltpu.SemaphoreType.DMA((PLANE,)),
            pltpu.SemaphoreType.DMA((PLANE,)),
            pltpu.SemaphoreType.DMA(()),
        ] + ChipGather.scratch(PLANE)

    def send(self, off):
        to = lax.rem(self.c + off, PLANE)
        copy = remote(
            self.blocks.at[to],
            self.out.at[self.d * PLANE + self.c],
            self.ps.at[off],
            self.pr.at[self.c],
            self.d,
            to,
        )
        copy.start()
        self.sent.append(copy)

    def first(self, ahead=PLANE - 1):
        self.ahead = ahead
        self.local = pltpu.make_async_copy(
            self.blocks.at[self.c], self.out.at[self.d * PLANE + self.c], self.local_sem
        )
        self.local.start()
        for off in range(1, 1 + ahead):
            self.send(off)
        self.chip.start(self.c, self.blocks.at[self.c])

    def relay(self, off):
        if off + self.ahead < PLANE:
            self.send(off + self.ahead)
        source = lax.rem(self.c + PLANE - off, PLANE)
        block = self.out.at[self.d * PLANE + source]
        remote(
            block, block, self.ps.at[off], self.pr.at[source], self.d, source
        ).wait_recv()
        self.chip.start(source)

    def relay_chip(self):
        for off in range(PLANE):
            self.chip.relay(lax.rem(self.c + off, PLANE))

    def last(self):
        self.chip.last()
        for copy in self.sent:
            copy.wait_send()
        self.local.wait()


class ChipScatter:
    def __init__(self, parts, cbuf, stage, xbuf, sems, count):
        self.parts, self.count = parts, count
        self.cbuf, self.stage, self.xbuf = cbuf, stage, xbuf
        self.cs, self.cr, self.xs, self.xr = sems
        self.d, self.c, self.x, self.core, _, _ = place()
        self.sent = []

    @staticmethod
    def scratch(count, rows, width):
        return [
            pltpu.VMEM((2, count, rows, width), jnp.bfloat16),
            pltpu.VMEM((count, rows, width), jnp.bfloat16),
            pltpu.VMEM((count, rows, width), jnp.bfloat16),
            pltpu.SemaphoreType.DMA((2, count)),
            pltpu.SemaphoreType.DMA((2, count)),
            pltpu.SemaphoreType.DMA((count,)),
            pltpu.SemaphoreType.DMA((count,)),
        ]

    def to_core(self, far, j):
        x = 1 - self.x if far else self.x
        return remote(
            self.parts.at[(x * 2 + 1 - self.core) * self.count + j],
            self.cbuf.at[far, j],
            self.cs.at[far, j],
            self.cr.at[far, j],
            self.x * 2 + 1 - self.core,
            self.c,
        )

    def to_x(self, j):
        return remote(
            self.stage.at[j],
            self.xbuf.at[j],
            self.xs.at[j],
            self.xr.at[j],
            (1 - self.x) * 2 + self.core,
            self.c,
        )

    def start(self, j):
        for far in (1, 0):
            copy = self.to_core(far, j)
            copy.start()
            self.sent.append(copy)

    def relay(self, j):
        self.to_core(1, j).wait_recv()
        own = self.parts.at[((1 - self.x) * 2 + self.core) * self.count + j]
        add_into(self.stage.at[j], [own, self.cbuf.at[1, j]], own.shape[0])
        copy = self.to_x(j)
        copy.start()
        self.sent.append(copy)

    def total(self, j, target):
        self.to_core(0, j).wait_recv()
        self.to_x(j).wait_recv()
        own = self.parts.at[self.d * self.count + j]
        add_into(target, [own, self.cbuf.at[0, j], self.xbuf.at[j]], own.shape[0])

    def finish(self):
        for copy in self.sent:
            copy.wait_send()


class WeightScatter:
    def __init__(self, parts, out, bufs, sems):
        self.stage = bufs[0]
        self.ps, self.pr = sems[:2]
        self.chip = ChipScatter(parts, *bufs[1:], sems[2:], PLANE)
        self.out = out
        self.d, self.c = self.chip.d, self.chip.c
        self.sent = []

    @staticmethod
    def scratch(rows, width):
        chip = ChipScatter.scratch(PLANE, rows, width)
        return [
            pltpu.VMEM((PLANE, rows, width), jnp.bfloat16),
            *chip[:3],
            pltpu.SemaphoreType.DMA((PLANE,)),
            pltpu.SemaphoreType.DMA((PLANE,)),
            *chip[3:],
        ]

    def first(self):
        for off in range(1, PLANE + 1):
            self.chip.start(lax.rem(self.c + off, PLANE))

    def relay(self, off):
        self.chip.relay(lax.rem(self.c + off, PLANE))

    def send(self, off):
        to = lax.rem(self.c + off, PLANE)
        if off == PLANE:
            self.chip.total(to, self.out.at[self.c])
            return
        self.chip.total(to, self.stage.at[to])
        copy = remote(
            self.stage.at[to],
            self.out.at[self.c],
            self.ps.at[off],
            self.pr.at[self.c],
            self.d,
            to,
        )
        copy.start()
        self.sent.append(copy)

    def last(self):
        for off in range(1, PLANE):
            source = lax.rem(self.c + off, PLANE)
            block = self.out.at[source]
            remote(
                block, block, self.ps.at[off], self.pr.at[source], self.d, source
            ).wait_recv()
        for copy in self.sent:
            copy.wait_send()
        self.chip.finish()


def params(collective_id, mebibytes=56):
    return pltpu.CompilerParams(
        collective_id=collective_id, has_side_effects=True, vmem_limit_bytes=mebibytes * 2**20
    )


ANY = pl.BlockSpec(memory_space=pl.ANY)
VMEM = pl.BlockSpec(memory_space=pltpu.VMEM)
CHUNKS = 4


DOWN_PARTS = 4
SCORE_SCALE = 1.0 / math.sqrt(HEAD_SIZE)
GROUP = QUERY_HEADS // KEY_VALUE_HEADS
PAIRS = GROUP // 2


def times_rows(left, right):
    return lax.dot_general(
        left, right, (((1,), (1,)), ((), ())), preferred_element_type=jnp.float32
    )


class PlaneExchange:
    def __init__(self, blocks, out, sems):
        self.blocks, self.out = blocks, out
        self.ps, self.pr, self.local_sem = sems
        self.d, self.c = lax.axis_index("dp"), lax.axis_index("ctx")
        self.sent = []

    @staticmethod
    def scratch():
        return [
            pltpu.SemaphoreType.DMA((PLANE,)),
            pltpu.SemaphoreType.DMA((PLANE,)),
            pltpu.SemaphoreType.DMA(()),
        ]

    def send(self, off):
        to = lax.rem(self.c + off, PLANE)
        if off % PLANE == 0:
            self.local = pltpu.make_async_copy(
                self.blocks.at[to], self.out.at[self.c], self.local_sem
            )
            self.local.start()
            return
        copy = remote(
            self.blocks.at[to],
            self.out.at[self.c],
            self.ps.at[off],
            self.pr.at[self.c],
            self.d,
            to,
        )
        copy.start()
        self.sent.append(copy)

    def arrive(self, off):
        if off % PLANE == 0:
            self.local.wait()
            return
        source = lax.rem(self.c + PLANE - off, PLANE)
        block = self.out.at[source]
        remote(
            block, block, self.ps.at[off], self.pr.at[source], self.d, source
        ).wait_recv()

    def finish(self):
        for copy in self.sent:
            copy.wait_send()


def probabilities(query, keys, spot, start, key_spots):
    scores = times_rows(query, keys) * SCORE_SCALE
    masked = jnp.where((key_spots <= spot) & (key_spots >= start), scores, masked_score)
    exponent = jnp.exp(masked - jnp.max(masked, axis=-1, keepdims=True))
    return exponent * (1.0 / jnp.sum(exponent, axis=-1, keepdims=True))


def rotate(value, table, back=False):
    lane = lax.broadcasted_iota(jnp.int32, value.shape, 1)
    turned = pltpu.roll(table, HEAD_SIZE, 1)
    cosine = jnp.where(lane < HEAD_SIZE, table, turned)
    sine = jnp.where(lane < HEAD_SIZE, turned, table)
    half = HEAD_SIZE // 2
    other = jnp.where(
        lax.rem(lane, HEAD_SIZE) < half,
        pltpu.roll(value, 2 * HEAD_SIZE - half, 1),
        pltpu.roll(value, half, 1),
    )
    if back:
        return value * cosine - other * sine
    return value * cosine + other * sine


QKV_WIDTH = (GROUP + 2) * HEAD_SIZE


def wide_columns(width):
    run = width // (8 * PLANE)
    for to in range(PLANE):
        for part in range(8):
            yield to, part * run, (part * PLANE + to) * run


def attention_kernel(
    starts_ref,
    rows_ref,
    table_ref,
    spots_ref,
    qkv_ref,
    blocks_ref,
    out_rows_ref,
    down_ref,
    grads_ref,
    input_out,
    table_out,
    qkv_out,
    gains_out,
    query_out,
    key_out,
    value_out,
    spot_out,
    start_out,
    key_spot_out,
    mixed_out,
    blocks_out,
    out_rows_out,
    down_out,
    grads_out,
    *scratch,
):
    mixed_stage, spots_all, rows_all, wide_full, wide_blocks = scratch[:5]
    down_full, down_blocks, out_full, out_block, load_sem = scratch[5:10]
    scratch = list(scratch[10:])

    def take(count):
        taken, scratch[:count] = scratch[:count], []
        return taken

    d, c, x, core, z, y = place()
    exchange = PlaneExchange(mixed_stage, mixed_out, take(3))
    qkv = WeightGather(qkv_ref, qkv_out, take(7))
    weights = WeightGather(wide_blocks, blocks_out, take(7))
    outs = SequenceGather(out_block, out_rows_out.at[pl.ds(d * PLANE, PLANE)], take(5), 1)
    outs_chip = ChipGather(out_rows_out, take(4), PLANE)
    rows = SequenceGather(rows_ref, rows_all, take(5), 2)
    table = SequenceGather(table_ref, table_out, take(5), 1)
    grads = SequenceGather(grads_ref, grads_out, take(5), CHUNKS)
    down_rows = down_ref.shape[0] // DOWN_PARTS
    down = ChipGather(down_out, take(4), DOWN_PARTS, down_rows)
    spot_send, spot_recv, spot_local, down_local = take(4)
    greet(plane_peers(d, c) + chip_peers(d, c, x, core))
    order = near_first(z)

    loads = [
        pltpu.make_async_copy(source, target, load_sem.at[i])
        for i, (source, target) in enumerate(
            [(out_rows_ref, out_full), (down_ref, down_full), (blocks_ref, wide_full)]
        )
    ]
    for load in loads:
        load.start()
    qkv.first()
    spots_own = pltpu.make_async_copy(spots_ref, spots_all.at[c], spot_local)
    spots_own.start()
    spots_sent = []
    for off in range(1, PLANE):
        to = lax.rem(c + off, PLANE)
        copy = remote(
            spots_ref, spots_all.at[c], spot_send.at[off], spot_recv.at[c], d, to
        )
        copy.start()
        spots_sent.append(copy)
    table.first()
    rows.first(by_block=True)
    loads[1].wait()

    @pl.loop(0, down_full.shape[0], step=16)
    def _(r):
        at = pl.ds(pl.multiple_of(r, 16), 16)
        down_blocks[at] = down_full[at].astype(jnp.bfloat16)

    down_own = pltpu.make_async_copy(
        down_blocks, down_out.at[pl.ds(d * down_full.shape[0], down_full.shape[0])], down_local
    )
    down_own.start()
    for j in range(DOWN_PARTS):
        down.start(j, down_blocks.at[pl.ds(j * down_rows, down_rows)])
    loads[0].wait()
    out_block[...] = out_full[...].astype(jnp.bfloat16)
    outs.first()
    outs_chip.start(c, out_block)
    loads[2].wait()

    @pl.loop(0, wide_full.shape[0], step=16)
    def _(r):
        at = pl.ds(pl.multiple_of(r, 16), 16)
        for to, start, after in wide_columns(wide_full.shape[1]):
            size = wide_full.shape[1] // (8 * PLANE)
            wide_blocks[to, at, start : start + size] = wide_full[
                at, after : after + size
            ].astype(jnp.bfloat16)

    for off in range(1, PLANE):
        qkv.relay(off)
    table.relay(0)
    rows.relay_block(order[0])
    qkv.relay_chip()
    rows.relay_half()
    weights.first()
    for off in range(1, PLANE):
        source = lax.rem(c + off, PLANE)
        block = spots_all.at[source]
        remote(block, block, spot_send.at[off], spot_recv.at[source], d, source).wait_recv()
    spots_own.wait()
    table.last()
    for slot in range(PLANE):
        key_spot_out[:, slot * 128 : (slot + 1) * 128] = spots_all[slot]
        spot = jnp.broadcast_to(spots_all[slot][:1], (128, 128)).T[:, :1]
        start = jnp.zeros_like(spot)
        for doc in range(starts_ref.shape[1]):
            first = starts_ref[0, doc].astype(jnp.float32)
            start = jnp.maximum(start, jnp.where(spot >= first, first, 0.0))
        spot_out[slot] = spot
        start_out[slot] = start
    qkv.last()
    for pair in range(RANKS // 2):
        columns = qkv_out[2 * pair : 2 * pair + 2, :, QKV_WIDTH:]
        turned = columns.reshape(128, 128).astype(jnp.float32).T
        gains_out[:, pair * 128 : (pair + 1) * 128] = turned[:8]

    tokens, width = rows_ref.shape
    wide = 2 * HEAD_SIZE

    def project(pair):
        for slot in range(YS):

            @pl.loop(0, tokens, step=32)
            def _(r):
                at = pl.ds(pl.multiple_of(r, 32), 32)
                value = rows_all[pair * YS + slot, at].astype(jnp.float32)
                inverse = lax.rsqrt(
                    jnp.mean(value * value, axis=-1, keepdims=True) + eps_norm
                )
                input_out[pair * YS + slot, at] = (value * inverse * gains_out[:1]).astype(
                    jnp.bfloat16
                )

        both = pl.ds(pair * YS, YS)
        weight = qkv_out[:, :, :QKV_WIDTH].reshape(width, QKV_WIDTH)
        projected = jnp.dot(
            input_out[both].reshape(YS * tokens, width),
            weight,
            preferred_element_type=jnp.float32,
        )
        turns = table_out[both].reshape(YS * tokens, wide)
        for slot in range(YS):
            span = slice(slot * tokens, (slot + 1) * tokens)
            block = pair * YS + slot
            for heads in range(PAIRS):
                query = rotate(
                    projected[span, heads * wide : (heads + 1) * wide], turns[span]
                ).astype(jnp.bfloat16)
                query_out[block, heads, 0] = query[:, :HEAD_SIZE]
                query_out[block, heads, 1] = query[:, HEAD_SIZE:]
            key = rotate(projected[span, PAIRS * wide :], turns[span])
            key_out[block] = key[:, :HEAD_SIZE].astype(jnp.bfloat16)
            value_out[block] = projected[span, PAIRS * wide + HEAD_SIZE :].astype(
                jnp.bfloat16
            )

    rows.local.wait()
    rows.arrive_across(z)
    project(z)
    outs.relay(0)
    for source in order:
        outs_chip.start(source * YS + y)
    for pair in order:
        rows.arrive_across(pair)
        project(pair)
    rows.finish()
    for other in range(ZS):
        outs.arrive_across(other)
        outs_chip.start(other * YS + 1 - y)
    grads.first()

    for step in range(1, PLANE + 1):
        block = lax.rem(c + step, PLANE)

        @pl.loop(0, PAIRS)
        def _(pair):
            halves = []
            keys = key_out[...].reshape(PLANE * tokens, HEAD_SIZE)
            values = value_out[...].reshape(PLANE * tokens, HEAD_SIZE)
            for half in range(2):
                probs = probabilities(
                    query_out[block, pair, half],
                    keys,
                    spot_out[block],
                    start_out[block],
                    key_spot_out[:1],
                )
                halves.append(
                    jnp.dot(
                        probs.astype(jnp.bfloat16), values, preferred_element_type=jnp.float32
                    ).astype(jnp.bfloat16)
                )
            mixed_stage[block, pair] = jnp.concatenate(halves, axis=1)

        exchange.send(step)
        if step < PLANE:
            weights.relay(step)
    for k in range(CHUNKS):
        grads.relay(k)
    for j in range(DOWN_PARTS):
        down.relay(j)
    for off in range(PLANE):
        outs_chip.relay(lax.rem(c + off, PLANE))
    weights.relay_chip()
    for off in range(1, PLANE + 1):
        exchange.arrive(off)
    grads.last()
    down.last()
    outs_chip.last()
    weights.last()
    outs.finish()
    outs.local.wait()
    exchange.finish()
    for copy in spots_sent:
        copy.wait_send()
    down_own.wait()


def attention(starts, rows, table, spots, qkv, blocks, out_rows, down, grads):
    low, full = jnp.bfloat16, jnp.float32
    tokens, width = rows.shape
    mixed = jax.ShapeDtypeStruct((PLANE, PAIRS, tokens, 2 * HEAD_SIZE), low)
    seq_len = PLANE * tokens
    wide_block = (blocks.shape[0], blocks.shape[1] // PLANE)
    return pl.pallas_call(
        attention_kernel,
        out_shape=(
            jax.ShapeDtypeStruct((PLANE, tokens, width), low),
            jax.ShapeDtypeStruct((PLANE, *table.shape), full),
            jax.ShapeDtypeStruct((RANKS, *qkv.shape[1:]), low),
            jax.ShapeDtypeStruct((8, width), full),
            jax.ShapeDtypeStruct((PLANE, PAIRS, 2, tokens, HEAD_SIZE), low),
            jax.ShapeDtypeStruct((PLANE, tokens, HEAD_SIZE), low),
            jax.ShapeDtypeStruct((PLANE, tokens, HEAD_SIZE), low),
            jax.ShapeDtypeStruct((PLANE, tokens, 1), full),
            jax.ShapeDtypeStruct((PLANE, tokens, 1), full),
            jax.ShapeDtypeStruct((8, seq_len), full),
            mixed,
            jax.ShapeDtypeStruct((RANKS, *wide_block), low),
            jax.ShapeDtypeStruct((RANKS, *out_rows.shape), low),
            jax.ShapeDtypeStruct((4 * down.shape[0], down.shape[1]), low),
            jax.ShapeDtypeStruct((PLANE, *grads.shape), low),
        ),
        in_specs=[pl.BlockSpec(memory_space=pltpu.SMEM)] + [ANY] * 8,
        out_specs=(VMEM,) * 11 + (ANY,) * 4,
        scratch_shapes=[
            pltpu.VMEM(mixed.shape, low),
            pltpu.VMEM((PLANE, *spots.shape), full),
            pltpu.VMEM((PLANE, tokens, width), low),
            pltpu.VMEM(blocks.shape, full),
            pltpu.VMEM((PLANE, *wide_block), low),
            pltpu.VMEM(down.shape, full),
            pltpu.VMEM(down.shape, low),
            pltpu.VMEM(out_rows.shape, full),
            pltpu.VMEM(out_rows.shape, low),
            pltpu.SemaphoreType.DMA((3,)),
            *PlaneExchange.scratch(),
            *WeightGather.scratch(),
            *WeightGather.scratch(),
            *SequenceGather.scratch(1),
            *ChipGather.scratch(PLANE),
            *SequenceGather.scratch(2),
            *SequenceGather.scratch(1),
            *SequenceGather.scratch(CHUNKS),
            *ChipGather.scratch(DOWN_PARTS),
            pltpu.SemaphoreType.DMA((PLANE,)),
            pltpu.SemaphoreType.DMA((PLANE,)),
            pltpu.SemaphoreType.DMA(()),
            pltpu.SemaphoreType.DMA(()),
        ],
        compiler_params=params(2),
        name="attention",
    )(starts, rows, table, spots, qkv, blocks, out_rows, down, grads)


def feed_kernel(
    rows_ref,
    grads_all,
    weight_ref,
    down_ref,
    normed_out,
    total_out,
    weight_grad_out,
    down_grad_out,
    *scratch,
):
    rows_all, slope_gate, slope_up, hidden_all, gate_grads = scratch[:5]
    normed_parts, down_parts, turned, stage, stage_sem = scratch[5:10]
    scratch = list(scratch[10:])

    def take(count):
        taken, scratch[:count] = scratch[:count], []
        return taken

    rows = SequenceGather(rows_ref, rows_all, take(5), 2)
    normed = SequenceScatter(normed_parts, normed_out, *take(2), take(4), 1)
    total = SequenceScatter(down_parts, total_out, *take(2), take(4), 1)
    d, c, x, core, z, y = place()
    greet(
        [(d, lax.rem(z + off, ZS) * YS + y) for off in range(1, ZS)] + [(d, z * YS + 1 - y)]
    )
    tokens, width = rows_ref.shape
    part = down_ref.shape[0]
    tile = 256
    blocks = PLANE // 2
    half = lax.div(z, 2)
    near, mid, far = near_first(z)

    def slots(side):
        return pl.ds(side * blocks, blocks)

    def columns(n, start=0, size=tile):
        return pl.ds(pl.multiple_of(n + start, size), size)

    def flat(ref, side):
        value = ref[slots(side)]
        return value.reshape(blocks * tokens, value.shape[2])

    def held(value, dtype=jnp.bfloat16):
        return value.astype(dtype).reshape(blocks, tokens, value.shape[1])

    def forward(side):
        @pl.loop(0, part, step=tile)
        def _(n):
            at, after = columns(n), columns(n, part)
            value = flat(rows_all, side)
            gate = jnp.dot(value, weight_ref[:, at], preferred_element_type=jnp.float32)
            up = jnp.dot(value, weight_ref[:, after], preferred_element_type=jnp.float32)
            sigmoid = jax.nn.sigmoid(gate)
            silu = gate * sigmoid
            hidden_all[slots(side), :, at] = held(silu * up)
            slope_up[slots(side), :, at] = held(silu, jnp.float32)
            slope_gate[slots(side), :, at] = held(
                up * sigmoid * (1.0 + gate * (1.0 - sigmoid)), jnp.float32
            )

    def downward(side):
        @pl.loop(0, width, step=2 * tile)
        def _(n):
            at = columns(n, 0, 2 * tile)
            down_parts[slots(side), :, at] = held(
                jnp.dot(
                    flat(hidden_all, side), down_ref[:, at], preferred_element_type=jnp.float32
                )
            )

    def backward(side):
        @pl.loop(0, part, step=tile)
        def _(n):
            at, after = columns(n), columns(n, part)
            grad = held(times_rows(flat(grads_all, side), down_ref[at, :]), jnp.float32)
            gate_grads[slots(side), :, at] = (grad * slope_gate[slots(side), :, at]).astype(
                jnp.bfloat16
            )
            gate_grads[slots(side), :, after] = (grad * slope_up[slots(side), :, at]).astype(
                jnp.bfloat16
            )

    def inward(side):
        @pl.loop(0, width, step=2 * tile)
        def _(n):
            at = columns(n, 0, 2 * tile)
            normed_parts[slots(side), :, at] = held(
                times_rows(flat(gate_grads, side), weight_ref[at, :])
            )

    tiles = [(hidden_all, grads_all, down_grad_out, n) for n in range(part // tile)]
    tiles += [(rows_all, gate_grads, weight_grad_out, n) for n in range(width // tile)]
    copies = []

    def weight_grad(i):
        left, right, out, n = tiles[i]
        if i >= 2:
            copies[i - 2].wait()
        value = left[:, :, n * tile : (n + 1) * tile].reshape(PLANE * tokens, tile)
        turned[...] = value.T

        @pl.loop(0, width, step=2 * tile)
        def _(m):
            at = columns(m, 0, 2 * tile)
            stage[i % 2, :, at] = jnp.dot(
                turned[...],
                right[:, :, at].reshape(PLANE * tokens, 2 * tile),
                preferred_element_type=jnp.float32,
            ).astype(jnp.bfloat16)

        copy = pltpu.make_async_copy(
            stage.at[i % 2], out.at[pl.ds(n * tile, tile)], stage_sem.at[i % 2]
        )
        copy.start()
        copies.append(copy)

    rows.first(by_block=True)
    rows.local.wait()
    rows.relay_block(near)
    rows.arrive_across(z)
    rows.arrive_across(near)
    forward(half)
    rows.relay_half()
    backward(half)
    inward(half)
    normed.start(near, 0)
    normed.start(z, 0)
    rows.arrive_across(mid)
    rows.arrive_across(far)
    forward(1 - half)
    backward(1 - half)
    inward(1 - half)
    normed.start(far, 0)
    normed.start(mid, 0)
    normed.relay_near(0)
    downward(1 - half)
    total.start(far, 0)
    total.start(mid, 0)
    normed.relay_far(0)
    downward(half)
    total.start(near, 0)
    total.start(z, 0)
    for i in range(2):
        weight_grad(i)
    total.relay_far(0)
    weight_grad(len(copies))
    total.relay_near(0)
    for i in range(len(copies), len(tiles)):
        weight_grad(i)
    normed.last(0)
    total.last(0)
    for copy in copies[-2:]:
        copy.wait()
    rows.finish()
    normed.finish()
    total.finish()


def feed(rows, grads, weight, down):
    part, width = down.shape
    low = rows.dtype
    tokens = rows.shape[0]
    summed = jax.ShapeDtypeStruct(rows.shape, jnp.float32)
    return pl.pallas_call(
        feed_kernel,
        out_shape=(
            summed,
            summed,
            jax.ShapeDtypeStruct(weight.shape, low),
            jax.ShapeDtypeStruct(down.shape, low),
        ),
        in_specs=[ANY] + [VMEM] * 3,
        out_specs=(VMEM,) * 2 + (ANY,) * 2,
        scratch_shapes=[
            pltpu.VMEM((PLANE, tokens, width), low),
            pltpu.VMEM((PLANE, tokens, part), jnp.float32),
            pltpu.VMEM((PLANE, tokens, part), jnp.float32),
            pltpu.VMEM((PLANE, tokens, part), low),
            pltpu.VMEM((PLANE, tokens, 2 * part), low),
            pltpu.VMEM((PLANE, tokens, width), low),
            pltpu.VMEM((PLANE, tokens, width), low),
            pltpu.VMEM((256, PLANE * tokens), low),
            pltpu.VMEM((2, 256, width), low),
            pltpu.SemaphoreType.DMA((2,)),
            *SequenceGather.scratch(2),
            *SequenceScatter.scratch(tokens, width, 1),
            *SequenceScatter.scratch(tokens, width, 1),
        ],
        compiler_params=params(5, 60),
        name="feed",
    )(rows, grads, weight, down)


def attention_back_kernel(
    query_ref,
    key_ref,
    value_ref,
    spot_ref,
    start_ref,
    key_spot_ref,
    table_ref,
    input_ref,
    qkv_ref,
    mixed_ref,
    parts_ref,
    rows_out,
    qkv_out,
    wide_out,
    *scratch,
):
    mixed_all, out_ref, grads, key_grad, value_grad, turned = scratch[:6]
    scratch = scratch[6:]
    exchange = PlaneExchange(mixed_ref, mixed_all, scratch[:3])
    weights = WeightScatter(parts_ref, out_ref, scratch[3:7], scratch[7:13])
    d, c, x, core, z, y = place()
    greet(plane_peers(d, c) + chip_peers(d, c, x, core))
    for off in range(1, PLANE + 1):
        exchange.send(off)
    weights.first()
    key_grad[...] = jnp.zeros_like(key_grad)
    value_grad[...] = jnp.zeros_like(value_grad)
    wide = 2 * HEAD_SIZE
    for step in range(PLANE):
        block = lax.rem(c + PLANE - step, PLANE)
        exchange.arrive(step)

        @pl.loop(0, PAIRS)
        def _(pair):
            keys = key_ref[...].reshape(key_grad.shape)
            values = value_ref[...].reshape(value_grad.shape)
            halves = []
            for half in range(2):
                query = query_ref[block, pair, half]
                grad = mixed_all[block, pair][:, half * HEAD_SIZE : (half + 1) * HEAD_SIZE]
                probs = probabilities(
                    query, keys, spot_ref[block], start_ref[block], key_spot_ref[:1]
                )
                grad_probs = times_rows(grad, values)
                delta = jnp.sum(probs * grad_probs, axis=-1, keepdims=True)
                grad_scores = (probs * (grad_probs - delta) * SCORE_SCALE).astype(jnp.bfloat16)
                halves.append(
                    jnp.dot(grad_scores, keys, preferred_element_type=jnp.float32)
                )
                key_grad[...] += transposed_times(grad_scores, query)
                value_grad[...] += transposed_times(probs.astype(jnp.bfloat16), grad)
            at = pl.ds(pl.multiple_of(pair * wide, wide), wide)
            grads[block, :, at] = rotate(
                jnp.concatenate(halves, axis=1), table_ref[block], back=True
            ).astype(jnp.bfloat16)

        weights.relay(step + 1)
        if step >= 2:
            weights.send(step - 1)
    tokens = grads.shape[1]
    for block in range(PLANE):
        span = slice(block * tokens, (block + 1) * tokens)
        both = jnp.concatenate([key_grad[span], value_grad[span]], axis=1)
        lane = lax.broadcasted_iota(jnp.int32, both.shape, 1)
        grads[block, :, PAIRS * wide :] = jnp.where(
            lane < HEAD_SIZE, rotate(both, table_ref[block], back=True), both
        ).astype(jnp.bfloat16)
    weights.send(PLANE - 1)
    width = input_ref.shape[2]
    rows = qkv_ref.shape[1]
    tile = 512

    @pl.loop(0, width // tile)
    def _(n):
        weight = qkv_ref[pl.ds(n * (tile // rows), tile // rows), :, :QKV_WIDTH]
        product = times_rows(
            grads[...].reshape(PLANE * tokens, QKV_WIDTH), weight.reshape(tile, QKV_WIDTH)
        )
        rows_out[:, :, pl.ds(pl.multiple_of(n * tile, tile), tile)] = product.astype(
            jnp.bfloat16
        ).reshape(PLANE, tokens, tile)

    weights.send(PLANE)

    @pl.loop(0, width // tile)
    def _(n):
        turned[...] = (
            input_ref[:, :, pl.ds(pl.multiple_of(n * tile, tile), tile)]
            .reshape(PLANE * tokens, tile)
            .T
        )
        product = jnp.dot(
            turned[...],
            grads[...].reshape(PLANE * tokens, QKV_WIDTH),
            preferred_element_type=jnp.float32,
        )
        qkv_out[pl.ds(n * (tile // rows), tile // rows)] = product.astype(
            jnp.bfloat16
        ).reshape(tile // rows, rows, QKV_WIDTH)

    weights.last()
    for source, start, after in wide_columns(wide_out.shape[1]):
        size = wide_out.shape[1] // (8 * PLANE)
        wide_out[:, after : after + size] = out_ref[source, :, start : start + size]
    exchange.finish()


def attention_back(
    query, keys, values, spots, starts, key_spots, table, inputs, qkv, mixed, parts
):
    low = jnp.bfloat16
    tokens = inputs.shape[1]
    sums = pltpu.VMEM((PLANE * tokens, HEAD_SIZE), jnp.float32)
    return pl.pallas_call(
        attention_back_kernel,
        out_shape=(
            jax.ShapeDtypeStruct(inputs.shape, low),
            jax.ShapeDtypeStruct((*qkv.shape[:2], QKV_WIDTH), low),
            jax.ShapeDtypeStruct((parts.shape[1], PLANE * parts.shape[2]), low),
        ),
        in_specs=[VMEM] * 11,
        out_specs=(VMEM,) * 3,
        scratch_shapes=[
            pltpu.VMEM(mixed.shape, low),
            pltpu.VMEM((PLANE, *parts.shape[1:]), low),
            pltpu.VMEM((PLANE, tokens, QKV_WIDTH), low),
            sums,
            sums,
            pltpu.VMEM((512, PLANE * tokens), low),
            *PlaneExchange.scratch(),
            *WeightScatter.scratch(*parts.shape[1:]),
        ],
        compiler_params=params(3),
        name="attention_back",
    )(query, keys, values, spots, starts, key_spots, table, inputs, qkv, mixed, parts)


def closing_kernel(
    rows_ref,
    parts_ref,
    outs_ref,
    down_ref,
    rows_out,
    query_out,
    keyval_out,
    outs_out,
    down_out,
    *scratch,
):
    out_ref, outs_sum = scratch[:2]
    scratch = list(scratch[2:])

    def take(count):
        taken, scratch[:count] = scratch[:count], []
        return taken

    scatter = SequenceScatter(rows_ref, rows_out, *take(2), take(4), CHUNKS)
    weights = WeightScatter(parts_ref, out_ref, take(4), take(6))
    chip = ChipScatter(outs_ref, *take(3), take(4), PLANE)
    outs = SequenceScatter(outs_sum, outs_out, *take(2), take(4), 1)
    down = ChipScatter(down_ref, *take(3), take(4), DOWN_PARTS)
    d, c, x, core, z, y = place()
    greet(plane_peers(d, c) + chip_peers(d, c, x, core))
    places = (*near_first(z)[::-1], z)
    slots = [place * YS + 1 - y for place in places] + [place * YS + y for place in places]
    weights.first()
    scatter.first()
    for j in slots:
        chip.start(j)
    for j in range(DOWN_PARTS):
        down.start(j)
    for off in range(1, PLANE + 1):
        weights.relay(off)
    for k in range(CHUNKS):
        scatter.relay(k)
        chip.relay(slots[2 * k])
        chip.relay(slots[2 * k + 1])
    for j in range(DOWN_PARTS):
        down.relay(j)
    for off in range(1, PLANE + 1):
        weights.send(off)
    for i, j in enumerate(slots):
        chip.total(j, outs_sum.at[j])
        if i < ZS:
            outs.start(places[i], 0)
        if i == ZS + 1:
            outs.relay_far(0)
        if i == ZS + 2:
            outs.relay_near(0)
    for j in range(DOWN_PARTS):
        down.total(j, down_out.at[j])
    for k in range(CHUNKS):
        scatter.last(k)
    weights.last()
    group_width = GROUP * HEAD_SIZE
    for source in range(PLANE):
        query_out[:, source * group_width : (source + 1) * group_width] = out_ref[
            source, :, :group_width
        ]
    for kind in range(2):
        start = group_width + kind * HEAD_SIZE
        for source in range(0, PLANE, 2):
            after = (kind * PLANE + source) * HEAD_SIZE
            keyval_out[:, after : after + 2 * HEAD_SIZE] = jnp.concatenate(
                [out_ref[source + i, :, start : start + HEAD_SIZE] for i in range(2)], axis=1
            )
    outs.last(0)
    scatter.finish()
    chip.finish()
    outs.finish()
    down.finish()


def closing(rows, parts, outs, down):
    return pl.pallas_call(
        closing_kernel,
        out_shape=(
            jax.ShapeDtypeStruct(rows.shape[1:], jnp.float32),
            jax.ShapeDtypeStruct((parts.shape[1], QUERY_HEADS * HEAD_SIZE), parts.dtype),
            jax.ShapeDtypeStruct((parts.shape[1], 2 * PLANE * HEAD_SIZE), parts.dtype),
            jax.ShapeDtypeStruct(outs.shape[1:], jnp.float32),
            jax.ShapeDtypeStruct((DOWN_PARTS, *down.shape[1:]), jnp.float32),
        ),
        in_specs=[VMEM] * 4,
        out_specs=(VMEM,) * 5,
        scratch_shapes=[
            pltpu.VMEM((PLANE, *parts.shape[1:]), parts.dtype),
            pltpu.VMEM((PLANE, *outs.shape[1:]), jnp.bfloat16),
            *SequenceScatter.scratch(*rows.shape[1:], CHUNKS),
            *WeightScatter.scratch(*parts.shape[1:]),
            *ChipScatter.scratch(PLANE, *outs.shape[1:]),
            *SequenceScatter.scratch(*outs.shape[1:], 1),
            *ChipScatter.scratch(DOWN_PARTS, *down.shape[1:]),
        ],
        compiler_params=params(4),
        name="closing",
    )(rows, parts, outs, down)


def body(
    layer_in,
    positions,
    doc_starts,
    out_grad,
    norm_gains,
    norm_gains_m,
    norm_gains_v,
    w_query,
    w_query_m,
    w_query_v,
    key_value_weight,
    key_value_first_moment,
    key_value_second_moment,
    w_out,
    w_out_m,
    w_out_v,
    w_gate_up,
    w_gate_up_m,
    w_gate_up_v,
    w_down,
    w_down_m,
    w_down_v,
):
    number_of_tokens = layer_in.shape[0]
    ctx_count = lax.axis_size("ctx")
    seq_len = number_of_tokens * ctx_count
    key_value_width = KEY_VALUE_HEADS * HEAD_SIZE
    query_group_size = QUERY_HEADS // KEY_VALUE_HEADS
    score_scale = 1.0 / math.sqrt(HEAD_SIZE)
    needed = -(-512 // number_of_tokens)
    shard_span = min(ctx_count, 1 << max(0, (needed - 1).bit_length()))
    width_of_block = shard_span * number_of_tokens
    count_of_blocks = ctx_count // shard_span
    key_places = lax.all_gather(positions, "ctx", axis=0, tiled=True)
    starts = doc_starts[0]
    own_docs = doc_lookup(positions, starts)
    key_docs = doc_lookup(key_places, starts)
    query_full, keyval_full, out_full, gains_full = (
        lax.all_gather(w_query.astype(jnp.bfloat16), ("dp", "ctx"), axis=0, tiled=True),
        lax.all_gather(key_value_weight.astype(jnp.bfloat16), ("dp", "ctx"), axis=0, tiled=True),
        lax.all_gather(w_out.astype(jnp.bfloat16), ("dp", "ctx"), axis=0, tiled=True),
        lax.all_gather(norm_gains.astype(jnp.bfloat16), ("dp", "ctx"), axis=1, tiled=True),
    )
    gain_one = gains_full[0].astype(jnp.float32)
    gain_two = gains_full[1].astype(jnp.float32)
    layer_rows = layer_in.astype(jnp.float32)
    normed_one, inverse_one = norm_forward(layer_rows)
    input_one = (normed_one * gain_one).astype(jnp.bfloat16)
    query_pre = jnp.dot(input_one, query_full, preferred_element_type=jnp.float32)
    key_value_projected = jnp.dot(input_one, keyval_full, preferred_element_type=jnp.float32)
    cosine_table, sine_table = rope_tables(positions, HEAD_SIZE)
    query_rows = (
        apply_rotation(
            query_pre.reshape(number_of_tokens, QUERY_HEADS, HEAD_SIZE), cosine_table, sine_table
        )
        .astype(jnp.bfloat16)
        .reshape(number_of_tokens, KEY_VALUE_HEADS, query_group_size, HEAD_SIZE)
    )
    keys_own = (
        apply_rotation(
            key_value_projected[:, :key_value_width].reshape(
                number_of_tokens, KEY_VALUE_HEADS, HEAD_SIZE
            ),
            cosine_table,
            sine_table,
        )
        .astype(jnp.bfloat16)
        .reshape(number_of_tokens, key_value_width)
    )
    values_own = key_value_projected[:, key_value_width:].astype(jnp.bfloat16)
    every_key, every_value = (
        lax.all_gather(keys_own, "ctx", axis=0, tiled=True),
        lax.all_gather(values_own, "ctx", axis=0, tiled=True),
    )
    blocked_keys = every_key.reshape(count_of_blocks, width_of_block, KEY_VALUE_HEADS, HEAD_SIZE)
    blocked_values = every_value.reshape(
        count_of_blocks, width_of_block, KEY_VALUE_HEADS, HEAD_SIZE
    )
    place_blocks = key_places.reshape(count_of_blocks, width_of_block)
    doc_blocks = key_docs.reshape(count_of_blocks, width_of_block)

    def visible(place_blk, doc_blk):
        allowed = (place_blk[None, :] <= positions[:, None]) & (
            doc_blk[None, :] == own_docs[:, None]
        )
        return allowed[:, None, None, :]

    def scores_of(key_blk):
        return (
            jnp.einsum("tkgd,nkd->tkgn", query_rows, key_blk, preferred_element_type=jnp.float32)
            * score_scale
        )

    def stats_step(carry, block):
        row_top, row_total = carry
        key_blk, place_blk, doc_blk = block
        allowed = visible(place_blk, doc_blk)
        masked = jnp.where(allowed, scores_of(key_blk), masked_score)
        new_top = jnp.maximum(row_top, jnp.max(masked, axis=-1, keepdims=True))
        row_total = row_total * jnp.exp(row_top - new_top) + jnp.sum(
            jnp.where(allowed, jnp.exp(masked - new_top), 0.0), axis=-1, keepdims=True
        )
        return ((new_top, row_total), None)

    statistic_shape = (number_of_tokens, KEY_VALUE_HEADS, query_group_size, 1)
    (row_top, row_total), unused = lax.scan(
        stats_step,
        (
            jnp.full(statistic_shape, masked_score, jnp.float32),
            jnp.zeros(statistic_shape, jnp.float32),
        ),
        (blocked_keys, place_blocks, doc_blocks),
    )
    log_total = row_top + jnp.log(row_total)

    def probs_of(key_blk, place_blk, doc_blk):
        allowed = visible(place_blk, doc_blk)
        masked = jnp.where(allowed, scores_of(key_blk), masked_score)
        return jnp.where(allowed, jnp.exp(masked - log_total), 0.0)

    def output_step(carry, block):
        key_blk, value_blk, place_blk, doc_blk = block
        probs_low = probs_of(key_blk, place_blk, doc_blk).astype(jnp.bfloat16)
        added = jnp.einsum(
            "tkgn,nkd->tkgd", probs_low, value_blk, preferred_element_type=jnp.float32
        )
        return (carry + added, None)

    attention_output, unused = lax.scan(
        output_step,
        jnp.zeros((number_of_tokens, KEY_VALUE_HEADS, query_group_size, HEAD_SIZE), jnp.float32),
        (blocked_keys, blocked_values, place_blocks, doc_blocks),
    )
    mixed = attention_output.reshape(number_of_tokens, QUERY_HEADS * HEAD_SIZE).astype(jnp.bfloat16)
    middle = layer_rows + jnp.dot(mixed, out_full, preferred_element_type=jnp.float32)
    normed_two, inverse_two = norm_forward(middle)
    input_two = (normed_two * gain_two).astype(jnp.bfloat16)
    gate_up_low = w_gate_up.astype(jnp.bfloat16)
    down_low = w_down.astype(jnp.bfloat16)
    columns = input_two
    gate_up = jnp.dot(
        columns,
        lax.all_gather(gate_up_low, ("dp", "ctx"), axis=0, tiled=True),
        preferred_element_type=jnp.float32,
    )
    gate_part = gate_up[:, :FF]
    up_part = gate_up[:, FF:]
    sigmoid_gate = jax.nn.sigmoid(gate_part)
    silu_gate = gate_part * sigmoid_gate
    hidden = (silu_gate * up_part).astype(jnp.bfloat16)
    columns = hidden
    down_sum = jnp.dot(
        columns,
        lax.all_gather(down_low, ("dp", "ctx"), axis=0, tiled=True),
        preferred_element_type=jnp.float32,
    )
    layer_out = (middle + down_sum).astype(jnp.bfloat16)
    grad_rows = out_grad.astype(jnp.float32)
    grad_hidden = times_transposed(
        out_grad, lax.all_gather(down_low, ("dp", "ctx"), axis=0, tiled=True)
    )
    grad_gate = grad_hidden * up_part * sigmoid_gate * (1.0 + gate_part * (1.0 - sigmoid_gate))
    grad_up = grad_hidden * silu_gate
    grad_gate_up = jnp.concatenate([grad_gate, grad_up], axis=1).astype(jnp.bfloat16)
    down_grad = lax.psum_scatter(
        transposed_times(hidden, out_grad), ("dp", "ctx"), scatter_dimension=0, tiled=True
    )
    grad_normed_two = times_transposed(
        grad_gate_up, lax.all_gather(gate_up_low, ("dp", "ctx"), axis=0, tiled=True)
    )
    gate_up_grad = lax.psum_scatter(
        transposed_times(input_two, grad_gate_up), ("dp", "ctx"), scatter_dimension=0, tiled=True
    )
    grad_norm_two, gain_two_grad = norm_backward(grad_normed_two, normed_two, inverse_two, gain_two)
    grad_middle = grad_rows + grad_norm_two
    grad_middle_low = grad_middle.astype(jnp.bfloat16)
    out_term = transposed_times(mixed, grad_middle_low)
    grad_mixed = (
        times_transposed(grad_middle_low, out_full)
        .astype(jnp.bfloat16)
        .reshape(number_of_tokens, KEY_VALUE_HEADS, query_group_size, HEAD_SIZE)
    )
    delta = jnp.sum(grad_mixed.astype(jnp.float32) * attention_output, axis=-1, keepdims=True)

    def back_step(grad_query, block):
        key_blk, value_blk, place_blk, doc_blk = block
        probs = probs_of(key_blk, place_blk, doc_blk)
        probs_low = probs.astype(jnp.bfloat16)
        grad_probs = jnp.einsum(
            "tkgd,nkd->tkgn", grad_mixed, value_blk, preferred_element_type=jnp.float32
        )
        grad_scores = (probs * (grad_probs - delta) * score_scale).astype(jnp.bfloat16)
        grad_query = grad_query + jnp.einsum(
            "tkgn,nkd->tkgd", grad_scores, key_blk, preferred_element_type=jnp.float32
        )
        key_grad = jnp.einsum(
            "tkgn,tkgd->nkd", grad_scores, query_rows, preferred_element_type=jnp.float32
        )
        value_grad = jnp.einsum(
            "tkgn,tkgd->nkd", probs_low, grad_mixed, preferred_element_type=jnp.float32
        )
        return (grad_query, (key_grad, value_grad))

    grad_query, (key_grads, value_grads) = lax.scan(
        back_step,
        jnp.zeros((number_of_tokens, KEY_VALUE_HEADS, query_group_size, HEAD_SIZE), jnp.float32),
        (blocked_keys, blocked_values, place_blocks, doc_blocks),
    )
    summed_key_gradient, value_sum = (
        lax.psum_scatter(
            key_grads.reshape(seq_len, key_value_width).astype(jnp.bfloat16),
            "ctx",
            scatter_dimension=0,
            tiled=True,
        ).astype(jnp.float32),
        lax.psum_scatter(
            value_grads.reshape(seq_len, key_value_width).astype(jnp.bfloat16),
            "ctx",
            scatter_dimension=0,
            tiled=True,
        ).astype(jnp.float32),
    )
    key_gradient_unrotated = reverse_rotation(
        summed_key_gradient.reshape(number_of_tokens, KEY_VALUE_HEADS, HEAD_SIZE),
        cosine_table,
        sine_table,
    ).reshape(number_of_tokens, key_value_width)
    grad_keyval = jnp.concatenate([key_gradient_unrotated, value_sum], axis=1).astype(jnp.bfloat16)
    grad_query_low = (
        reverse_rotation(
            grad_query.reshape(number_of_tokens, QUERY_HEADS, HEAD_SIZE), cosine_table, sine_table
        )
        .reshape(number_of_tokens, QUERY_HEADS * HEAD_SIZE)
        .astype(jnp.bfloat16)
    )
    grad_normed_one = times_transposed(grad_query_low, query_full) + times_transposed(
        grad_keyval, keyval_full
    )
    query_term = transposed_times(input_one, grad_query_low)
    keyval_term = transposed_times(input_one, grad_keyval)
    grad_norm_one, gain_one_grad = norm_backward(grad_normed_one, normed_one, inverse_one, gain_one)
    in_grad = grad_middle + grad_norm_one
    gain_term = jnp.stack([gain_one_grad, gain_two_grad])
    query_grad, keyval_grad, out_weight_grad, gains_grad = (
        lax.psum_scatter(query_term, ("dp", "ctx"), scatter_dimension=0, tiled=True),
        lax.psum_scatter(keyval_term, ("dp", "ctx"), scatter_dimension=0, tiled=True),
        lax.psum_scatter(out_term, ("dp", "ctx"), scatter_dimension=0, tiled=True),
        lax.psum_scatter(gain_term, ("dp", "ctx"), scatter_dimension=1, tiled=True),
    )
    rates = rates_for(seq_len)
    gains_m_new, gains_v_new, gains_new = adamw(
        norm_gains, gains_grad, norm_gains_m, norm_gains_v, rates[0], 0.0
    )
    query_m_new, query_v_new, query_new = adamw(
        w_query, query_grad, w_query_m, w_query_v, rates[1], weight_decay
    )
    keyval_m_new, keyval_v_new, keyval_new = adamw(
        key_value_weight,
        keyval_grad,
        key_value_first_moment,
        key_value_second_moment,
        rates[2],
        weight_decay,
    )
    out_m_new, out_v_new, out_new = adamw(
        w_out, out_weight_grad, w_out_m, w_out_v, rates[3], weight_decay
    )
    gate_up_m_new, gate_up_v_new, gate_up_new = adamw(
        w_gate_up, gate_up_grad, w_gate_up_m, w_gate_up_v, rates[4], weight_decay
    )
    down_m_new, down_v_new, down_new = adamw(
        w_down, down_grad, w_down_m, w_down_v, rates[5], weight_decay
    )
    return (
        layer_out,
        in_grad,
        gains_grad,
        gains_m_new,
        gains_v_new,
        gains_new,
        query_grad,
        query_m_new,
        query_v_new,
        query_new,
        keyval_grad,
        keyval_m_new,
        keyval_v_new,
        keyval_new,
        out_weight_grad,
        out_m_new,
        out_v_new,
        out_new,
        gate_up_grad,
        gate_up_m_new,
        gate_up_v_new,
        gate_up_new,
        down_grad,
        down_m_new,
        down_v_new,
        down_new,
    )


def tensor_parallel(
    layer_in,
    positions,
    doc_starts,
    out_grad,
    norm_gains,
    norm_gains_m,
    norm_gains_v,
    w_query,
    w_query_m,
    w_query_v,
    key_value_weight,
    key_value_first_moment,
    key_value_second_moment,
    w_out,
    w_out_m,
    w_out_v,
    w_gate_up,
    w_gate_up_m,
    w_gate_up_v,
    w_down,
    w_down_m,
    w_down_v,
):
    low = jnp.bfloat16
    own_tokens, width = layer_in.shape
    seq_len = own_tokens * PLANE
    group = GROUP
    group_width = group * HEAD_SIZE
    ff_part = FF // PLANE
    rows = w_query.shape[0]

    gains_low = norm_gains.astype(low)
    small = jnp.broadcast_to(
        jnp.pad(gains_low.T, ((0, 0), (0, 126)))[None], (PLANE, rows, 128)
    )
    attention_blocks = jnp.concatenate(
        [
            w_query.astype(low).reshape(rows, PLANE, group_width).transpose(1, 0, 2),
            key_value_weight.astype(low)
            .reshape(rows, 2, PLANE, HEAD_SIZE)
            .transpose(2, 0, 1, 3)
            .reshape(PLANE, rows, 2 * HEAD_SIZE),
            small,
        ],
        axis=2,
    )
    spots = jnp.broadcast_to(positions[None, :].astype(jnp.float32), (8, own_tokens))
    cosine_own, sine_own = rope_tables(positions, HEAD_SIZE)
    cosine_own, sine_own = cosine_own[:, 0], sine_own[:, 0]
    table = jnp.concatenate([cosine_own, cosine_own, -sine_own, sine_own], axis=1)
    (
        input_one_all,
        table_all,
        attention_all,
        gain_rows,
        query_rows,
        key_rows,
        value_rows,
        token_spots,
        token_starts,
        key_spots,
        mixed_parts,
        feed_all,
        out_all,
        down_all,
        grads_all,
    ) = attention(
        doc_starts,
        layer_in,
        table,
        spots,
        attention_blocks,
        w_gate_up,
        w_out,
        w_down,
        out_grad,
    )
    gain_one, gain_two = gain_rows[0], gain_rows[1]
    mixed = mixed_parts.transpose(2, 0, 1, 3).reshape(own_tokens, width)
    out_weight = out_all.reshape(width, width)
    branch = jnp.dot(mixed, out_weight, preferred_element_type=jnp.float32)

    layer_rows = layer_in.astype(jnp.float32)
    middle = layer_rows + branch
    normed_two, inverse_two = norm_forward(middle)
    grad_normed_two, down_sum, feed_term, down_term = feed(
        (normed_two * gain_two).astype(low),
        grads_all,
        feed_all.reshape(width, 2 * ff_part),
        down_all,
    )
    layer_out = (middle + down_sum).astype(low)

    grad_norm_two, unused = norm_backward(grad_normed_two, normed_two, inverse_two, gain_two)
    grad_middle = out_grad.astype(jnp.float32) + grad_norm_two
    grad_middle_low = grad_middle.astype(low)
    out_term = transposed_times(mixed, grad_middle_low).astype(low)
    grad_mixed = (
        times_transposed(grad_middle_low, out_weight)
        .astype(low)
        .reshape(own_tokens, PLANE, PAIRS, 2 * HEAD_SIZE)
        .transpose(1, 2, 0, 3)
    )
    one_parts, qkv_term, feed_grad = attention_back(
        query_rows,
        key_rows,
        value_rows,
        token_spots,
        token_starts,
        key_spots,
        table_all,
        input_one_all,
        attention_all,
        grad_mixed,
        feed_term.reshape(RANKS, rows, 2 * ff_part),
    )
    gate_up_grad = feed_grad.astype(jnp.float32)
    grad_normed_one, query_grad, keyval_grad, out_weight_grad, down_grad = closing(
        one_parts,
        qkv_term,
        out_term.reshape(RANKS, rows, width),
        down_term.reshape(4 * DOWN_PARTS, -1, width),
    )
    down_grad = down_grad.reshape(w_down.shape)
    normed_one, inverse_one = norm_forward(layer_rows)
    grad_norm_one, unused = norm_backward(grad_normed_one, normed_one, inverse_one, gain_one)
    in_grad = grad_middle + grad_norm_one
    query_grad = query_grad.astype(jnp.float32)
    keyval_grad = keyval_grad.astype(jnp.float32)

    def low_times(weight, grad):
        return jnp.sum(weight.astype(low).astype(jnp.float32) * grad, axis=1)

    gains_grad = jnp.stack(
        [
            low_times(w_query, query_grad) + low_times(key_value_weight, keyval_grad),
            low_times(w_gate_up, gate_up_grad),
        ]
    ) / gains_low.astype(jnp.float32)

    rates = rates_for(seq_len)
    return (
        layer_out,
        in_grad,
        gains_grad,
        *adamw(norm_gains, gains_grad, norm_gains_m, norm_gains_v, rates[0], 0.0),
        query_grad,
        *adamw(w_query, query_grad, w_query_m, w_query_v, rates[1], weight_decay),
        keyval_grad,
        *adamw(
            key_value_weight,
            keyval_grad,
            key_value_first_moment,
            key_value_second_moment,
            rates[2],
            weight_decay,
        ),
        out_weight_grad,
        *adamw(w_out, out_weight_grad, w_out_m, w_out_v, rates[3], weight_decay),
        gate_up_grad,
        *adamw(w_gate_up, gate_up_grad, w_gate_up_m, w_gate_up_v, rates[4], weight_decay),
        down_grad,
        *adamw(w_down, down_grad, w_down_m, w_down_v, rates[5], weight_decay),
    )


def solution(mesh):
    planned = tensor_parallel if dict(mesh.shape) == {"dp": 2 * XS, "ctx": ZS * YS} else body
    return jax.shard_map(
        planned,
        mesh=mesh,
        in_specs=(
            P(("dp", "ctx"), None),
            P(("dp", "ctx")),
            P("dp", None),
            P(("dp", "ctx"), None),
            P(None, ("dp", "ctx")),
            P(None, ("dp", "ctx")),
            P(None, ("dp", "ctx")),
            P(("dp", "ctx"), None),
            P(("dp", "ctx"), None),
            P(("dp", "ctx"), None),
            P(("dp", "ctx"), None),
            P(("dp", "ctx"), None),
            P(("dp", "ctx"), None),
            P(("dp", "ctx"), None),
            P(("dp", "ctx"), None),
            P(("dp", "ctx"), None),
            P(("dp", "ctx"), None),
            P(("dp", "ctx"), None),
            P(("dp", "ctx"), None),
            P(("dp", "ctx"), None),
            P(("dp", "ctx"), None),
            P(("dp", "ctx"), None),
        ),
        out_specs=(
            P(("dp", "ctx"), None),
            P(("dp", "ctx"), None),
            P(None, ("dp", "ctx")),
            P(None, ("dp", "ctx")),
            P(None, ("dp", "ctx")),
            P(None, ("dp", "ctx")),
            P(("dp", "ctx"), None),
            P(("dp", "ctx"), None),
            P(("dp", "ctx"), None),
            P(("dp", "ctx"), None),
            P(("dp", "ctx"), None),
            P(("dp", "ctx"), None),
            P(("dp", "ctx"), None),
            P(("dp", "ctx"), None),
            P(("dp", "ctx"), None),
            P(("dp", "ctx"), None),
            P(("dp", "ctx"), None),
            P(("dp", "ctx"), None),
            P(("dp", "ctx"), None),
            P(("dp", "ctx"), None),
            P(("dp", "ctx"), None),
            P(("dp", "ctx"), None),
            P(("dp", "ctx"), None),
            P(("dp", "ctx"), None),
            P(("dp", "ctx"), None),
            P(("dp", "ctx"), None),
        ),
        check_vma=False,
    )
```

```python
import functools
import math

import jax
import jax.numpy as jnp
from jax import lax
from jax.experimental import pallas as pl
from jax.experimental.pallas import tpu as pltpu
from jax.sharding import PartitionSpec as P

MODEL_WIDTH = 2048
QUERY_HEADS = 32
KEY_VALUE_HEADS = 8
HEAD_SIZE = 64
FF = 8192
STEP = 10


eps_norm = 1e-05
rope_base = 500000.0
beta_one = 0.9
beta_two = 0.95
eps_adam = 1e-08
weight_decay = 0.1
masked_score = -1e30


def rates_for(seq_len):
    return (
        0.6,
        0.8 / math.sqrt(MODEL_WIDTH // 4),
        0.8 / math.sqrt(MODEL_WIDTH),
        0.8 / math.sqrt(max(220 * MODEL_WIDTH // seq_len, 1)),
        0.8 / math.sqrt(MODEL_WIDTH),
        0.8 / math.sqrt(FF // 2),
    )


def adamw(weight, grad_sum, first, second, rate, decay):
    first_new = beta_one * first + (1.0 - beta_one) * grad_sum
    second_new = beta_two * second + (1.0 - beta_two) * grad_sum * grad_sum
    first_hat = first_new / (1.0 - beta_one**STEP)
    second_hat = second_new / (1.0 - beta_two**STEP)
    weight_new = weight - rate * (first_hat / (jnp.sqrt(second_hat) + eps_adam) + decay * weight)
    return (first_new, second_new, weight_new)


def norm_forward(layer_rows):
    inverse = lax.rsqrt(jnp.mean(layer_rows * layer_rows, axis=-1, keepdims=True) + eps_norm)
    return (layer_rows * inverse, inverse)


def norm_backward(grad_out, normed, inverse, gain_row):
    scaled = grad_out * gain_row
    grad_in = inverse * (scaled - normed * jnp.mean(scaled * normed, axis=-1, keepdims=True))
    return (grad_in, jnp.sum(grad_out * normed, axis=0))


def rope_tables(token_placement, head_dim):
    half_dim = head_dim // 2
    frequencies = jnp.exp(
        jnp.arange(half_dim, dtype=jnp.float32) * (-2.0 * math.log(rope_base) / head_dim)
    )
    angles = token_placement.astype(jnp.float32)[:, None] * frequencies[None, :]
    return (jnp.cos(angles)[:, None, :], jnp.sin(angles)[:, None, :])


def apply_rotation(value_rows, cosine_table, sine_table):
    half_dim = value_rows.shape[-1] // 2
    first_half = value_rows[..., :half_dim]
    second_half = value_rows[..., half_dim:]
    return jnp.concatenate(
        [
            first_half * cosine_table - second_half * sine_table,
            second_half * cosine_table + first_half * sine_table,
        ],
        axis=-1,
    )


def reverse_rotation(grad_rows, cosine_table, sine_table):
    half_dim = grad_rows.shape[-1] // 2
    first_half = grad_rows[..., :half_dim]
    second_half = grad_rows[..., half_dim:]
    return jnp.concatenate(
        [
            first_half * cosine_table + second_half * sine_table,
            second_half * cosine_table - first_half * sine_table,
        ],
        axis=-1,
    )


def doc_lookup(token_placement, starts):
    return jnp.sum((token_placement[:, None] >= starts[None, :]).astype(jnp.int32), axis=1) - 1


def times_transposed(left, right):
    return lax.dot_general(
        left, right, (((1,), (1,)), ((), ())), preferred_element_type=jnp.float32
    )


def transposed_times(left, right):
    return lax.dot_general(
        left, right, (((0,), (0,)), ((), ())), preferred_element_type=jnp.float32
    )


XS = 2
YS = 2
ZS = 4
PLANE = ZS * YS
RANKS = 2 * XS * PLANE
MESH = pl.DeviceIdType.MESH


def place():
    d = lax.axis_index("dp")
    c = lax.axis_index("ctx")
    return d, c, lax.div(d, 2), lax.rem(d, 2), lax.div(c, YS), lax.rem(c, YS)


def remote(src, dst, send_sem, recv_sem, d, c):
    return pltpu.make_async_remote_copy(
        src_ref=src,
        dst_ref=dst,
        send_sem=send_sem,
        recv_sem=recv_sem,
        device_id=(d, c),
        device_id_type=MESH,
    )


def greet(peers):
    barrier = pltpu.get_barrier_semaphore()
    for d, c in peers:
        pl.semaphore_signal(barrier, inc=1, device_id=(d, c), device_id_type=MESH)
    pl.semaphore_wait(barrier, len(peers))


def plane_peers(d, c):
    return [(d, lax.rem(c + k, PLANE)) for k in range(1, PLANE)]


def chip_peers(d, c, x, core):
    return [(x * 2 + 1 - core, c), ((1 - x) * 2 + core, c)]


def add_into(target, sources, rows, step=16):
    @pl.loop(0, rows, step=step)
    def _(r):
        at = pl.ds(pl.multiple_of(r, step), step)
        total = sources[0][at].astype(jnp.float32)
        for source in sources[1:]:
            total = total + source[at].astype(jnp.float32)
        target[at] = total.astype(target.dtype)


def near_first(z):
    half = lax.div(z, 2)
    return [half * 4 + 1 - z, 2 - half, 3 - 3 * half]


def is_inner(z):
    return (z == 1) | (z == 2)


class SequenceGather:
    def __init__(self, own, out, sems, chunks):
        self.own, self.out, self.chunks = own, out, chunks
        self.zs, self.zr, self.ys, self.yr, self.local_sem = sems
        self.d, self.c, _, _, self.z, self.y = place()
        self.rows = own.shape[0] // chunks
        self.sent = []

    @staticmethod
    def scratch(chunks):
        return [
            pltpu.SemaphoreType.DMA((ZS, chunks)),
            pltpu.SemaphoreType.DMA((ZS, chunks)),
            pltpu.SemaphoreType.DMA((ZS, chunks)),
            pltpu.SemaphoreType.DMA((ZS, chunks)),
            pltpu.SemaphoreType.DMA(()),
        ]

    def part(self, ref, k):
        return ref.at[pl.ds(k * self.rows, self.rows)]

    def across(self, z, k, src):
        slot = z * YS + self.y
        return remote(
            src,
            self.part(self.out.at[slot], k),
            self.ys.at[z, k],
            self.yr.at[z, k],
            self.d,
            self.z * YS + 1 - self.y,
        )

    def along(self, to, k):
        return remote(
            self.part(self.own, k),
            self.part(self.out.at[self.c], k),
            self.zs.at[to, k],
            self.zr.at[self.z, k],
            self.d,
            to * YS + self.y,
        )

    def start(self, copy):
        copy.start()
        self.sent.append(copy)

    def first(self, by_block=False):
        self.local = pltpu.make_async_copy(self.own, self.out.at[self.c], self.local_sem)
        self.local.start()
        near, mid, _ = near_first(self.z)
        if by_block:
            for k in range(self.chunks):
                self.start(self.across(self.z, k, self.part(self.own, k)))
            for to in (mid, near):
                for k in range(self.chunks):
                    self.start(self.along(to, k))
            return
        for k in range(self.chunks):
            for to in (mid, near):
                self.start(self.along(to, k))
            self.start(self.across(self.z, k, self.part(self.own, k)))

    def inward(self, i, source, k):
        near, _, far = near_first(self.z)
        block = self.part(self.out.at[source * YS + self.y], k)
        return remote(
            block,
            block,
            self.zs.at[(far, self.z)[i], k],
            self.zr.at[source, k],
            self.d,
            near * YS + self.y,
        )

    def relay_one(self, source, k):
        slot = source * YS + self.y
        block = self.part(self.out.at[slot], k)
        remote(
            block, block, self.zs.at[source, k], self.zr.at[source, k], self.d, slot
        ).wait_recv()
        self.start(self.across(source, k, block))

    def relay_half(self):
        for k in range(self.chunks):
            self.relay_far(k)

    def relay_far(self, k):
        _, mid, far = near_first(self.z)
        for i, source in enumerate((mid, far)):
            self.relay_one(source, k)

            @pl.when(is_inner(self.z))
            def _(i=i, source=source):
                self.inward(i, source, k).start()

    def relay(self, k):
        self.relay_one(near_first(self.z)[0], k)
        self.relay_far(k)

    def relay_block(self, source):
        for k in range(self.chunks):
            self.relay_one(source, k)

    def arrive_across(self, z):
        for k in range(self.chunks):
            block = self.part(self.out.at[z * YS + 1 - self.y], k)
            remote(
                block,
                block,
                self.ys.at[z, k],
                self.yr.at[z, k],
                self.d,
                self.z * YS + 1 - self.y,
            ).wait_recv()

    def finish(self):
        for copy in self.sent:
            copy.wait_send()
        _, mid, far = near_first(self.z)

        @pl.when(is_inner(self.z))
        def _():
            for k in range(self.chunks):
                for i, source in enumerate((mid, far)):
                    self.inward(i, source, k).wait_send()

    def last(self):
        for z in range(ZS):
            self.arrive_across(z)
        self.finish()
        self.local.wait()


class SequenceScatter:
    def __init__(self, parts, out, ybuf, zbuf, sems, chunks):
        self.parts, self.out, self.chunks = parts, out, chunks
        self.ybuf, self.zbuf = ybuf, zbuf
        self.ys, self.yr, self.zs, self.zr = sems
        self.d, self.c, _, _, self.z, self.y = place()
        self.rows = parts.shape[1] // chunks
        self.sent = []

    @staticmethod
    def scratch(rows, width, chunks):
        return [
            pltpu.VMEM((ZS, rows, width), jnp.bfloat16),
            pltpu.VMEM((ZS, rows, width), jnp.bfloat16),
            pltpu.SemaphoreType.DMA((ZS, chunks)),
            pltpu.SemaphoreType.DMA((ZS, chunks)),
            pltpu.SemaphoreType.DMA((ZS, chunks)),
            pltpu.SemaphoreType.DMA((ZS, chunks)),
        ]

    def span(self, k):
        return pl.ds(k * self.rows, self.rows)

    def across(self, z, k):
        return remote(
            self.parts.at[z * YS + 1 - self.y, self.span(k)],
            self.ybuf.at[z, self.span(k)],
            self.ys.at[z, k],
            self.yr.at[z, k],
            self.d,
            self.z * YS + 1 - self.y,
        )

    def along(self, to, k, slot):
        return remote(
            self.ybuf.at[to, self.span(k)],
            self.zbuf.at[slot, self.span(k)],
            self.zs.at[to, k],
            self.zr.at[slot, k],
            self.d,
            to * YS + self.y,
        )

    def inward(self, i, to, k):
        return remote(
            self.ybuf.at[to, self.span(k)],
            self.zbuf.at[2 + i, self.span(k)],
            self.zs.at[to, k],
            self.zr.at[2 + i, k],
            self.d,
            near_first(self.z)[0] * YS + self.y,
        )

    def start(self, z, k):
        copy = self.across(z, k)
        copy.start()
        self.sent.append(copy)

    def first(self):
        for k in range(self.chunks):
            for z in (*near_first(self.z)[::-1], self.z):
                self.start(z, k)

    def added(self, z, k):
        self.across(z, k).wait_recv()
        block = self.ybuf.at[z, self.span(k)]
        add_into(block, [self.parts.at[z * YS + self.y, self.span(k)], block], self.rows)

    def relay_near(self, k):
        near = near_first(self.z)[0]
        self.added(near, k)
        copy = self.along(near, k, 0)
        copy.start()
        self.sent.append(copy)

    def relay_far(self, k):
        _, mid, far = near_first(self.z)
        for to in (far, mid):
            self.added(to, k)

            @pl.when(jnp.logical_not(is_inner(self.z)))
            def _(to=to, i=0 if to is mid else 1):
                self.inward(i, to, k).start()

        @pl.when(is_inner(self.z))
        def _():
            for i, to in ((1, far), (0, mid)):
                self.inward(i, to, k).wait_recv()
                block = self.ybuf.at[to, self.span(k)]
                add_into(block, [block, self.zbuf.at[2 + i, self.span(k)]], self.rows)
                self.along(to, k, 1).start()

    def relay(self, k):
        self.relay_far(k)
        self.relay_near(k)

    def last(self, k):
        self.across(self.z, k).wait_recv()
        blocks = [self.parts.at[self.c, self.span(k)], self.ybuf.at[self.z, self.span(k)]]
        near, mid, _ = near_first(self.z)
        for slot, source in enumerate((near, mid)):
            block = self.zbuf.at[slot, self.span(k)]
            self.along(source, k, slot).wait_recv()
            blocks.append(block)
        add_into(self.out.at[self.span(k)], blocks, self.rows)

    def finish(self):
        for copy in self.sent:
            copy.wait_send()
        _, mid, far = near_first(self.z)
        for k in range(self.chunks):
            for to in (mid, far):
                self.along(to, k, 1).wait_send()


class ChipGather:
    def __init__(self, out, sems, count, rows=None):
        self.out, self.count, self.rows = out, count, rows
        self.cs, self.cr, self.xs, self.xr = sems
        self.d, self.c, self.x, self.core, _, _ = place()
        self.sent = []

    @staticmethod
    def scratch(count):
        return [
            pltpu.SemaphoreType.DMA((2, count)),
            pltpu.SemaphoreType.DMA((2, count)),
            pltpu.SemaphoreType.DMA((count,)),
            pltpu.SemaphoreType.DMA((count,)),
        ]

    def block(self, slot):
        if self.rows is None:
            return self.out.at[slot]
        return self.out.at[pl.ds(slot * self.rows, self.rows)]

    def to_core(self, far, j, src=None):
        x = 1 - self.x if far else self.x
        block = self.block((x * 2 + self.core) * self.count + j)
        return remote(
            block if src is None else src,
            block,
            self.cs.at[far, j],
            self.cr.at[far, j],
            self.x * 2 + 1 - self.core,
            self.c,
        )

    def to_x(self, j, src=None):
        block = self.block(self.d * self.count + j)
        return remote(
            block if src is None else src,
            block,
            self.xs.at[j],
            self.xr.at[j],
            (1 - self.x) * 2 + self.core,
            self.c,
        )

    def start(self, j, src=None):
        for copy in (self.to_x(j, src), self.to_core(0, j, src)):
            copy.start()
            self.sent.append(copy)

    def relay(self, j):
        self.to_x(j).wait_recv()
        copy = self.to_core(1, j)
        copy.start()
        self.sent.append(copy)

    def last(self):
        for far in (0, 1):
            for j in range(self.count):
                self.to_core(far, j).wait_recv()
        for copy in self.sent:
            copy.wait_send()


class WeightGather:
    def __init__(self, blocks, out, sems):
        self.blocks, self.out = blocks, out
        self.ps, self.pr, self.local_sem = sems[:3]
        self.chip = ChipGather(out, sems[3:], PLANE)
        self.d, self.c = self.chip.d, self.chip.c
        self.sent = []

    @staticmethod
    def scratch():
        return [
            pltpu.SemaphoreType.DMA((PLANE,)),
            pltpu.SemaphoreType.DMA((PLANE,)),
            pltpu.SemaphoreType.DMA(()),
        ] + ChipGather.scratch(PLANE)

    def send(self, off):
        to = lax.rem(self.c + off, PLANE)
        copy = remote(
            self.blocks.at[to],
            self.out.at[self.d * PLANE + self.c],
            self.ps.at[off],
            self.pr.at[self.c],
            self.d,
            to,
        )
        copy.start()
        self.sent.append(copy)

    def first(self, ahead=PLANE - 1):
        self.ahead = ahead
        self.local = pltpu.make_async_copy(
            self.blocks.at[self.c], self.out.at[self.d * PLANE + self.c], self.local_sem
        )
        self.local.start()
        for off in range(1, 1 + ahead):
            self.send(off)
        self.chip.start(self.c, self.blocks.at[self.c])

    def relay(self, off):
        if off + self.ahead < PLANE:
            self.send(off + self.ahead)
        source = lax.rem(self.c + PLANE - off, PLANE)
        block = self.out.at[self.d * PLANE + source]
        remote(
            block, block, self.ps.at[off], self.pr.at[source], self.d, source
        ).wait_recv()
        self.chip.start(source)

    def relay_chip(self):
        for off in range(PLANE):
            self.chip.relay(lax.rem(self.c + off, PLANE))

    def last(self):
        self.chip.last()
        for copy in self.sent:
            copy.wait_send()
        self.local.wait()


class ChipScatter:
    def __init__(self, parts, cbuf, stage, xbuf, sems, count):
        self.parts, self.count = parts, count
        self.cbuf, self.stage, self.xbuf = cbuf, stage, xbuf
        self.cs, self.cr, self.xs, self.xr = sems
        self.d, self.c, self.x, self.core, _, _ = place()
        self.sent = []

    @staticmethod
    def scratch(count, rows, width):
        return [
            pltpu.VMEM((2, count, rows, width), jnp.bfloat16),
            pltpu.VMEM((count, rows, width), jnp.bfloat16),
            pltpu.VMEM((count, rows, width), jnp.bfloat16),
            pltpu.SemaphoreType.DMA((2, count)),
            pltpu.SemaphoreType.DMA((2, count)),
            pltpu.SemaphoreType.DMA((count,)),
            pltpu.SemaphoreType.DMA((count,)),
        ]

    def to_core(self, far, j):
        x = 1 - self.x if far else self.x
        return remote(
            self.parts.at[(x * 2 + 1 - self.core) * self.count + j],
            self.cbuf.at[far, j],
            self.cs.at[far, j],
            self.cr.at[far, j],
            self.x * 2 + 1 - self.core,
            self.c,
        )

    def to_x(self, j):
        return remote(
            self.stage.at[j],
            self.xbuf.at[j],
            self.xs.at[j],
            self.xr.at[j],
            (1 - self.x) * 2 + self.core,
            self.c,
        )

    def start(self, j):
        for far in (1, 0):
            copy = self.to_core(far, j)
            copy.start()
            self.sent.append(copy)

    def relay(self, j):
        self.to_core(1, j).wait_recv()
        own = self.parts.at[((1 - self.x) * 2 + self.core) * self.count + j]
        add_into(self.stage.at[j], [own, self.cbuf.at[1, j]], own.shape[0])
        copy = self.to_x(j)
        copy.start()
        self.sent.append(copy)

    def total(self, j, target):
        self.to_core(0, j).wait_recv()
        self.to_x(j).wait_recv()
        own = self.parts.at[self.d * self.count + j]
        add_into(target, [own, self.cbuf.at[0, j], self.xbuf.at[j]], own.shape[0])

    def finish(self):
        for copy in self.sent:
            copy.wait_send()


class WeightScatter:
    def __init__(self, parts, out, bufs, sems):
        self.stage = bufs[0]
        self.ps, self.pr = sems[:2]
        self.chip = ChipScatter(parts, *bufs[1:], sems[2:], PLANE)
        self.out = out
        self.d, self.c = self.chip.d, self.chip.c
        self.sent = []

    @staticmethod
    def scratch(rows, width):
        chip = ChipScatter.scratch(PLANE, rows, width)
        return [
            pltpu.VMEM((PLANE, rows, width), jnp.bfloat16),
            *chip[:3],
            pltpu.SemaphoreType.DMA((PLANE,)),
            pltpu.SemaphoreType.DMA((PLANE,)),
            *chip[3:],
        ]

    def first(self):
        for off in range(1, PLANE + 1):
            self.chip.start(lax.rem(self.c + off, PLANE))

    def relay(self, off):
        self.chip.relay(lax.rem(self.c + off, PLANE))

    def send(self, off):
        to = lax.rem(self.c + off, PLANE)
        if off == PLANE:
            self.chip.total(to, self.out.at[self.c])
            return
        self.chip.total(to, self.stage.at[to])
        copy = remote(
            self.stage.at[to],
            self.out.at[self.c],
            self.ps.at[off],
            self.pr.at[self.c],
            self.d,
            to,
        )
        copy.start()
        self.sent.append(copy)

    def last(self):
        for off in range(1, PLANE):
            source = lax.rem(self.c + off, PLANE)
            block = self.out.at[source]
            remote(
                block, block, self.ps.at[off], self.pr.at[source], self.d, source
            ).wait_recv()
        for copy in self.sent:
            copy.wait_send()
        self.chip.finish()


def params(collective_id, mebibytes=56):
    return pltpu.CompilerParams(
        collective_id=collective_id, has_side_effects=True, vmem_limit_bytes=mebibytes * 2**20
    )


ANY = pl.BlockSpec(memory_space=pl.ANY)
VMEM = pl.BlockSpec(memory_space=pltpu.VMEM)
CHUNKS = 4


DOWN_PARTS = 4
SCORE_SCALE = 1.0 / math.sqrt(HEAD_SIZE)
GROUP = QUERY_HEADS // KEY_VALUE_HEADS
PAIRS = GROUP // 2


def times_rows(left, right):
    return lax.dot_general(
        left, right, (((1,), (1,)), ((), ())), preferred_element_type=jnp.float32
    )


class PlaneExchange:
    def __init__(self, blocks, out, sems):
        self.blocks, self.out = blocks, out
        self.ps, self.pr, self.local_sem = sems
        self.d, self.c = lax.axis_index("dp"), lax.axis_index("ctx")
        self.sent = []

    @staticmethod
    def scratch():
        return [
            pltpu.SemaphoreType.DMA((PLANE,)),
            pltpu.SemaphoreType.DMA((PLANE,)),
            pltpu.SemaphoreType.DMA(()),
        ]

    def send(self, off):
        to = lax.rem(self.c + off, PLANE)
        if off % PLANE == 0:
            self.local = pltpu.make_async_copy(
                self.blocks.at[to], self.out.at[self.c], self.local_sem
            )
            self.local.start()
            return
        copy = remote(
            self.blocks.at[to],
            self.out.at[self.c],
            self.ps.at[off],
            self.pr.at[self.c],
            self.d,
            to,
        )
        copy.start()
        self.sent.append(copy)

    def arrive(self, off):
        if off % PLANE == 0:
            self.local.wait()
            return
        source = lax.rem(self.c + PLANE - off, PLANE)
        block = self.out.at[source]
        remote(
            block, block, self.ps.at[off], self.pr.at[source], self.d, source
        ).wait_recv()

    def finish(self):
        for copy in self.sent:
            copy.wait_send()


def probabilities(query, keys, spot, start, key_spots):
    scores = times_rows(query, keys) * SCORE_SCALE
    masked = jnp.where((key_spots <= spot) & (key_spots >= start), scores, masked_score)
    exponent = jnp.exp(masked - jnp.max(masked, axis=-1, keepdims=True))
    return exponent * (1.0 / jnp.sum(exponent, axis=-1, keepdims=True))


def rotate(value, table, back=False):
    lane = lax.broadcasted_iota(jnp.int32, value.shape, 1)
    turned = pltpu.roll(table, HEAD_SIZE, 1)
    cosine = jnp.where(lane < HEAD_SIZE, table, turned)
    sine = jnp.where(lane < HEAD_SIZE, turned, table)
    half = HEAD_SIZE // 2
    other = jnp.where(
        lax.rem(lane, HEAD_SIZE) < half,
        pltpu.roll(value, 2 * HEAD_SIZE - half, 1),
        pltpu.roll(value, half, 1),
    )
    if back:
        return value * cosine - other * sine
    return value * cosine + other * sine


QKV_WIDTH = (GROUP + 2) * HEAD_SIZE


def wide_columns(width):
    run = width // (8 * PLANE)
    for to in range(PLANE):
        for part in range(8):
            yield to, part * run, (part * PLANE + to) * run


def attention_kernel(
    starts_ref,
    rows_ref,
    table_ref,
    spots_ref,
    qkv_ref,
    blocks_ref,
    out_rows_ref,
    down_ref,
    grads_ref,
    input_out,
    table_out,
    qkv_out,
    gains_out,
    query_out,
    key_out,
    value_out,
    spot_out,
    start_out,
    key_spot_out,
    mixed_out,
    blocks_out,
    out_rows_out,
    down_out,
    grads_out,
    *scratch,
):
    mixed_stage, spots_all, rows_all, wide_full, wide_blocks = scratch[:5]
    down_full, down_blocks, out_full, out_block, load_sem = scratch[5:10]
    scratch = list(scratch[10:])

    def take(count):
        taken, scratch[:count] = scratch[:count], []
        return taken

    d, c, x, core, z, y = place()
    exchange = PlaneExchange(mixed_stage, mixed_out, take(3))
    qkv = WeightGather(qkv_ref, qkv_out, take(7))
    weights = WeightGather(wide_blocks, blocks_out, take(7))
    outs = SequenceGather(out_block, out_rows_out.at[pl.ds(d * PLANE, PLANE)], take(5), 1)
    outs_chip = ChipGather(out_rows_out, take(4), PLANE)
    rows = SequenceGather(rows_ref, rows_all, take(5), 2)
    table = SequenceGather(table_ref, table_out, take(5), 1)
    grads = SequenceGather(grads_ref, grads_out, take(5), CHUNKS)
    down_rows = down_ref.shape[0] // DOWN_PARTS
    down = ChipGather(down_out, take(4), DOWN_PARTS, down_rows)
    spot_send, spot_recv, spot_local, down_local = take(4)
    greet(plane_peers(d, c) + chip_peers(d, c, x, core))
    order = near_first(z)

    loads = [
        pltpu.make_async_copy(source, target, load_sem.at[i])
        for i, (source, target) in enumerate(
            [(out_rows_ref, out_full), (down_ref, down_full), (blocks_ref, wide_full)]
        )
    ]
    for load in loads:
        load.start()
    qkv.first()
    spots_own = pltpu.make_async_copy(spots_ref, spots_all.at[c], spot_local)
    spots_own.start()
    spots_sent = []
    for off in range(1, PLANE):
        to = lax.rem(c + off, PLANE)
        copy = remote(
            spots_ref, spots_all.at[c], spot_send.at[off], spot_recv.at[c], d, to
        )
        copy.start()
        spots_sent.append(copy)
    table.first()
    rows.first(by_block=True)
    loads[1].wait()

    @pl.loop(0, down_full.shape[0], step=16)
    def _(r):
        at = pl.ds(pl.multiple_of(r, 16), 16)
        down_blocks[at] = down_full[at].astype(jnp.bfloat16)

    down_own = pltpu.make_async_copy(
        down_blocks, down_out.at[pl.ds(d * down_full.shape[0], down_full.shape[0])], down_local
    )
    down_own.start()
    for j in range(DOWN_PARTS):
        down.start(j, down_blocks.at[pl.ds(j * down_rows, down_rows)])
    loads[0].wait()
    out_block[...] = out_full[...].astype(jnp.bfloat16)
    outs.first()
    outs_chip.start(c, out_block)
    loads[2].wait()

    @pl.loop(0, wide_full.shape[0], step=16)
    def _(r):
        at = pl.ds(pl.multiple_of(r, 16), 16)
        for to, start, after in wide_columns(wide_full.shape[1]):
            size = wide_full.shape[1] // (8 * PLANE)
            wide_blocks[to, at, start : start + size] = wide_full[
                at, after : after + size
            ].astype(jnp.bfloat16)

    for off in range(1, PLANE):
        qkv.relay(off)
    table.relay(0)
    rows.relay_block(order[0])
    qkv.relay_chip()
    rows.relay_half()
    weights.first()
    for off in range(1, PLANE):
        source = lax.rem(c + off, PLANE)
        block = spots_all.at[source]
        remote(block, block, spot_send.at[off], spot_recv.at[source], d, source).wait_recv()
    spots_own.wait()
    table.last()
    for slot in range(PLANE):
        key_spot_out[:, slot * 128 : (slot + 1) * 128] = spots_all[slot]
        spot = jnp.broadcast_to(spots_all[slot][:1], (128, 128)).T[:, :1]
        start = jnp.zeros_like(spot)
        for doc in range(starts_ref.shape[1]):
            first = starts_ref[0, doc].astype(jnp.float32)
            start = jnp.maximum(start, jnp.where(spot >= first, first, 0.0))
        spot_out[slot] = spot
        start_out[slot] = start
    qkv.last()
    for pair in range(RANKS // 2):
        columns = qkv_out[2 * pair : 2 * pair + 2, :, QKV_WIDTH:]
        turned = columns.reshape(128, 128).astype(jnp.float32).T
        gains_out[:, pair * 128 : (pair + 1) * 128] = turned[:8]

    tokens, width = rows_ref.shape
    wide = 2 * HEAD_SIZE

    def project(pair):
        for slot in range(YS):

            @pl.loop(0, tokens, step=32)
            def _(r):
                at = pl.ds(pl.multiple_of(r, 32), 32)
                value = rows_all[pair * YS + slot, at].astype(jnp.float32)
                inverse = lax.rsqrt(
                    jnp.mean(value * value, axis=-1, keepdims=True) + eps_norm
                )
                input_out[pair * YS + slot, at] = (value * inverse * gains_out[:1]).astype(
                    jnp.bfloat16
                )

        both = pl.ds(pair * YS, YS)
        weight = qkv_out[:, :, :QKV_WIDTH].reshape(width, QKV_WIDTH)
        projected = jnp.dot(
            input_out[both].reshape(YS * tokens, width),
            weight,
            preferred_element_type=jnp.float32,
        )
        turns = table_out[both].reshape(YS * tokens, wide)
        for slot in range(YS):
            span = slice(slot * tokens, (slot + 1) * tokens)
            block = pair * YS + slot
            for heads in range(PAIRS):
                query = rotate(
                    projected[span, heads * wide : (heads + 1) * wide], turns[span]
                ).astype(jnp.bfloat16)
                query_out[block, heads, 0] = query[:, :HEAD_SIZE]
                query_out[block, heads, 1] = query[:, HEAD_SIZE:]
            key = rotate(projected[span, PAIRS * wide :], turns[span])
            key_out[block] = key[:, :HEAD_SIZE].astype(jnp.bfloat16)
            value_out[block] = projected[span, PAIRS * wide + HEAD_SIZE :].astype(
                jnp.bfloat16
            )

    rows.local.wait()
    rows.arrive_across(z)
    project(z)
    outs.relay(0)
    for source in order:
        outs_chip.start(source * YS + y)
    for pair in order:
        rows.arrive_across(pair)
        project(pair)
    rows.finish()
    for other in range(ZS):
        outs.arrive_across(other)
        outs_chip.start(other * YS + 1 - y)
    grads.first()
    out_order = [c, *(source * YS + y for source in order)]
    out_order += [other * YS + 1 - y for other in range(ZS)]

    for step in range(1, PLANE + 1):
        block = lax.rem(c + step, PLANE)

        @pl.loop(0, PAIRS)
        def _(pair):
            halves = []
            keys = key_out[...].reshape(PLANE * tokens, HEAD_SIZE)
            values = value_out[...].reshape(PLANE * tokens, HEAD_SIZE)
            for half in range(2):
                probs = probabilities(
                    query_out[block, pair, half],
                    keys,
                    spot_out[block],
                    start_out[block],
                    key_spot_out[:1],
                )
                halves.append(
                    jnp.dot(
                        probs.astype(jnp.bfloat16), values, preferred_element_type=jnp.float32
                    ).astype(jnp.bfloat16)
                )
            mixed_stage[block, pair] = jnp.concatenate(halves, axis=1)

        exchange.send(step)
        if step < PLANE:
            weights.relay(step)
        if step == 2:
            for j in range(DOWN_PARTS):
                down.relay(j)
        if 3 <= step < 7:
            for j in out_order[2 * (step - 3) : 2 * (step - 2)]:
                outs_chip.relay(j)
    for k in range(CHUNKS):
        for off in (2 * k, 2 * k + 1):
            weights.chip.relay(lax.rem(c + PLANE - off, PLANE))
        grads.relay(k)
    for off in range(1, PLANE + 1):
        exchange.arrive(off)
    grads.last()
    down.last()
    outs_chip.last()
    weights.last()
    outs.finish()
    outs.local.wait()
    exchange.finish()
    for copy in spots_sent:
        copy.wait_send()
    down_own.wait()


def attention(starts, rows, table, spots, qkv, blocks, out_rows, down, grads):
    low, full = jnp.bfloat16, jnp.float32
    tokens, width = rows.shape
    mixed = jax.ShapeDtypeStruct((PLANE, PAIRS, tokens, 2 * HEAD_SIZE), low)
    seq_len = PLANE * tokens
    wide_block = (blocks.shape[0], blocks.shape[1] // PLANE)
    return pl.pallas_call(
        attention_kernel,
        out_shape=(
            jax.ShapeDtypeStruct((PLANE, tokens, width), low),
            jax.ShapeDtypeStruct((PLANE, *table.shape), full),
            jax.ShapeDtypeStruct((RANKS, *qkv.shape[1:]), low),
            jax.ShapeDtypeStruct((8, width), full),
            jax.ShapeDtypeStruct((PLANE, PAIRS, 2, tokens, HEAD_SIZE), low),
            jax.ShapeDtypeStruct((PLANE, tokens, HEAD_SIZE), low),
            jax.ShapeDtypeStruct((PLANE, tokens, HEAD_SIZE), low),
            jax.ShapeDtypeStruct((PLANE, tokens, 1), full),
            jax.ShapeDtypeStruct((PLANE, tokens, 1), full),
            jax.ShapeDtypeStruct((8, seq_len), full),
            mixed,
            jax.ShapeDtypeStruct((RANKS, *wide_block), low),
            jax.ShapeDtypeStruct((RANKS, *out_rows.shape), low),
            jax.ShapeDtypeStruct((4 * down.shape[0], down.shape[1]), low),
            jax.ShapeDtypeStruct((PLANE, *grads.shape), low),
        ),
        in_specs=[pl.BlockSpec(memory_space=pltpu.SMEM)] + [ANY] * 8,
        out_specs=(VMEM,) * 11 + (ANY,) * 4,
        scratch_shapes=[
            pltpu.VMEM(mixed.shape, low),
            pltpu.VMEM((PLANE, *spots.shape), full),
            pltpu.VMEM((PLANE, tokens, width), low),
            pltpu.VMEM(blocks.shape, full),
            pltpu.VMEM((PLANE, *wide_block), low),
            pltpu.VMEM(down.shape, full),
            pltpu.VMEM(down.shape, low),
            pltpu.VMEM(out_rows.shape, full),
            pltpu.VMEM(out_rows.shape, low),
            pltpu.SemaphoreType.DMA((3,)),
            *PlaneExchange.scratch(),
            *WeightGather.scratch(),
            *WeightGather.scratch(),
            *SequenceGather.scratch(1),
            *ChipGather.scratch(PLANE),
            *SequenceGather.scratch(2),
            *SequenceGather.scratch(1),
            *SequenceGather.scratch(CHUNKS),
            *ChipGather.scratch(DOWN_PARTS),
            pltpu.SemaphoreType.DMA((PLANE,)),
            pltpu.SemaphoreType.DMA((PLANE,)),
            pltpu.SemaphoreType.DMA(()),
            pltpu.SemaphoreType.DMA(()),
        ],
        compiler_params=params(2),
        name="attention",
    )(starts, rows, table, spots, qkv, blocks, out_rows, down, grads)


def feed_kernel(
    rows_ref,
    grads_all,
    weight_ref,
    down_ref,
    normed_out,
    total_out,
    weight_grad_out,
    down_grad_out,
    *scratch,
):
    rows_all, slope_gate, slope_up, hidden_all, gate_grads = scratch[:5]
    normed_parts, down_parts, turned, stage, stage_sem = scratch[5:10]
    scratch = list(scratch[10:])

    def take(count):
        taken, scratch[:count] = scratch[:count], []
        return taken

    rows = SequenceGather(rows_ref, rows_all, take(5), 2)
    normed = SequenceScatter(normed_parts, normed_out, *take(2), take(4), 1)
    total = SequenceScatter(down_parts, total_out, *take(2), take(4), 1)
    d, c, x, core, z, y = place()
    greet(
        [(d, lax.rem(z + off, ZS) * YS + y) for off in range(1, ZS)] + [(d, z * YS + 1 - y)]
    )
    tokens, width = rows_ref.shape
    part = down_ref.shape[0]
    tile = 256
    blocks = PLANE // 2
    half = lax.div(z, 2)
    near, mid, far = near_first(z)

    def slots(side):
        return pl.ds(side * blocks, blocks)

    def columns(n, start=0, size=tile):
        return pl.ds(pl.multiple_of(n + start, size), size)

    def flat(ref, side):
        value = ref[slots(side)]
        return value.reshape(blocks * tokens, value.shape[2])

    def held(value, dtype=jnp.bfloat16):
        return value.astype(dtype).reshape(blocks, tokens, value.shape[1])

    def forward(side):
        @pl.loop(0, part, step=tile)
        def _(n):
            at, after = columns(n), columns(n, part)
            value = flat(rows_all, side)
            gate = jnp.dot(value, weight_ref[:, at], preferred_element_type=jnp.float32)
            up = jnp.dot(value, weight_ref[:, after], preferred_element_type=jnp.float32)
            sigmoid = jax.nn.sigmoid(gate)
            silu = gate * sigmoid
            hidden_all[slots(side), :, at] = held(silu * up)
            slope_up[slots(side), :, at] = held(silu, jnp.float32)
            slope_gate[slots(side), :, at] = held(
                up * sigmoid * (1.0 + gate * (1.0 - sigmoid)), jnp.float32
            )

    def downward(side):
        @pl.loop(0, width, step=2 * tile)
        def _(n):
            at = columns(n, 0, 2 * tile)
            down_parts[slots(side), :, at] = held(
                jnp.dot(
                    flat(hidden_all, side), down_ref[:, at], preferred_element_type=jnp.float32
                )
            )

    def backward(side):
        @pl.loop(0, part, step=tile)
        def _(n):
            at, after = columns(n), columns(n, part)
            grad = held(times_rows(flat(grads_all, side), down_ref[at, :]), jnp.float32)
            gate_grads[slots(side), :, at] = (grad * slope_gate[slots(side), :, at]).astype(
                jnp.bfloat16
            )
            gate_grads[slots(side), :, after] = (grad * slope_up[slots(side), :, at]).astype(
                jnp.bfloat16
            )

    def inward(side):
        @pl.loop(0, width, step=2 * tile)
        def _(n):
            at = columns(n, 0, 2 * tile)
            normed_parts[slots(side), :, at] = held(
                times_rows(flat(gate_grads, side), weight_ref[at, :])
            )

    tiles = [(hidden_all, grads_all, down_grad_out, n) for n in range(part // tile)]
    tiles += [(rows_all, gate_grads, weight_grad_out, n) for n in range(width // tile)]
    copies = []

    def weight_grad(i):
        left, right, out, n = tiles[i]
        if i >= 2:
            copies[i - 2].wait()
        value = left[:, :, n * tile : (n + 1) * tile].reshape(PLANE * tokens, tile)
        turned[...] = value.T

        @pl.loop(0, width, step=2 * tile)
        def _(m):
            at = columns(m, 0, 2 * tile)
            stage[i % 2, :, at] = jnp.dot(
                turned[...],
                right[:, :, at].reshape(PLANE * tokens, 2 * tile),
                preferred_element_type=jnp.float32,
            ).astype(jnp.bfloat16)

        copy = pltpu.make_async_copy(
            stage.at[i % 2], out.at[pl.ds(n * tile, tile)], stage_sem.at[i % 2]
        )
        copy.start()
        copies.append(copy)

    rows.first(by_block=True)
    rows.local.wait()
    rows.relay_block(near)
    rows.arrive_across(z)
    rows.arrive_across(near)
    forward(half)
    rows.relay_half()
    backward(half)
    inward(half)
    normed.start(near, 0)
    normed.start(z, 0)
    rows.arrive_across(mid)
    rows.arrive_across(far)
    forward(1 - half)
    backward(1 - half)
    inward(1 - half)
    normed.start(far, 0)
    normed.start(mid, 0)
    normed.relay_near(0)
    downward(1 - half)
    total.start(far, 0)
    total.start(mid, 0)
    normed.relay_far(0)
    downward(half)
    total.start(near, 0)
    total.start(z, 0)
    for i in range(2):
        weight_grad(i)
    total.relay_far(0)
    weight_grad(len(copies))
    total.relay_near(0)
    for i in range(len(copies), len(tiles)):
        weight_grad(i)
    normed.last(0)
    total.last(0)
    for copy in copies[-2:]:
        copy.wait()
    rows.finish()
    normed.finish()
    total.finish()


def feed(rows, grads, weight, down):
    part, width = down.shape
    low = rows.dtype
    tokens = rows.shape[0]
    summed = jax.ShapeDtypeStruct(rows.shape, jnp.float32)
    return pl.pallas_call(
        feed_kernel,
        out_shape=(
            summed,
            summed,
            jax.ShapeDtypeStruct(weight.shape, low),
            jax.ShapeDtypeStruct(down.shape, low),
        ),
        in_specs=[ANY] + [VMEM] * 3,
        out_specs=(VMEM,) * 2 + (ANY,) * 2,
        scratch_shapes=[
            pltpu.VMEM((PLANE, tokens, width), low),
            pltpu.VMEM((PLANE, tokens, part), jnp.float32),
            pltpu.VMEM((PLANE, tokens, part), jnp.float32),
            pltpu.VMEM((PLANE, tokens, part), low),
            pltpu.VMEM((PLANE, tokens, 2 * part), low),
            pltpu.VMEM((PLANE, tokens, width), low),
            pltpu.VMEM((PLANE, tokens, width), low),
            pltpu.VMEM((256, PLANE * tokens), low),
            pltpu.VMEM((2, 256, width), low),
            pltpu.SemaphoreType.DMA((2,)),
            *SequenceGather.scratch(2),
            *SequenceScatter.scratch(tokens, width, 1),
            *SequenceScatter.scratch(tokens, width, 1),
        ],
        compiler_params=params(5, 60),
        name="feed",
    )(rows, grads, weight, down)


def attention_back_kernel(
    query_ref,
    key_ref,
    value_ref,
    spot_ref,
    start_ref,
    key_spot_ref,
    table_ref,
    input_ref,
    qkv_ref,
    mixed_ref,
    parts_ref,
    rows_out,
    qkv_out,
    wide_out,
    *scratch,
):
    mixed_all, out_ref, grads, key_grad, value_grad, turned = scratch[:6]
    scratch = scratch[6:]
    exchange = PlaneExchange(mixed_ref, mixed_all, scratch[:3])
    weights = WeightScatter(parts_ref, out_ref, scratch[3:7], scratch[7:13])
    d, c, x, core, z, y = place()
    greet(plane_peers(d, c) + chip_peers(d, c, x, core))
    for off in range(1, PLANE + 1):
        exchange.send(off)
    weights.first()
    key_grad[...] = jnp.zeros_like(key_grad)
    value_grad[...] = jnp.zeros_like(value_grad)
    wide = 2 * HEAD_SIZE
    for step in range(PLANE):
        block = lax.rem(c + PLANE - step, PLANE)
        exchange.arrive(step)

        @pl.loop(0, PAIRS)
        def _(pair):
            keys = key_ref[...].reshape(key_grad.shape)
            values = value_ref[...].reshape(value_grad.shape)
            halves = []
            for half in range(2):
                query = query_ref[block, pair, half]
                grad = mixed_all[block, pair][:, half * HEAD_SIZE : (half + 1) * HEAD_SIZE]
                probs = probabilities(
                    query, keys, spot_ref[block], start_ref[block], key_spot_ref[:1]
                )
                grad_probs = times_rows(grad, values)
                delta = jnp.sum(probs * grad_probs, axis=-1, keepdims=True)
                grad_scores = (probs * (grad_probs - delta) * SCORE_SCALE).astype(jnp.bfloat16)
                halves.append(
                    jnp.dot(grad_scores, keys, preferred_element_type=jnp.float32)
                )
                key_grad[...] += transposed_times(grad_scores, query)
                value_grad[...] += transposed_times(probs.astype(jnp.bfloat16), grad)
            at = pl.ds(pl.multiple_of(pair * wide, wide), wide)
            grads[block, :, at] = rotate(
                jnp.concatenate(halves, axis=1), table_ref[block], back=True
            ).astype(jnp.bfloat16)

        weights.relay(step + 1)
        if step >= 2:
            weights.send(step - 1)
    tokens = grads.shape[1]
    for block in range(PLANE):
        span = slice(block * tokens, (block + 1) * tokens)
        both = jnp.concatenate([key_grad[span], value_grad[span]], axis=1)
        lane = lax.broadcasted_iota(jnp.int32, both.shape, 1)
        grads[block, :, PAIRS * wide :] = jnp.where(
            lane < HEAD_SIZE, rotate(both, table_ref[block], back=True), both
        ).astype(jnp.bfloat16)
    weights.send(PLANE - 1)
    width = input_ref.shape[2]
    rows = qkv_ref.shape[1]
    tile = 512

    @pl.loop(0, width // tile)
    def _(n):
        weight = qkv_ref[pl.ds(n * (tile // rows), tile // rows), :, :QKV_WIDTH]
        product = times_rows(
            grads[...].reshape(PLANE * tokens, QKV_WIDTH), weight.reshape(tile, QKV_WIDTH)
        )
        rows_out[:, :, pl.ds(pl.multiple_of(n * tile, tile), tile)] = product.astype(
            jnp.bfloat16
        ).reshape(PLANE, tokens, tile)

    weights.send(PLANE)

    @pl.loop(0, width // tile)
    def _(n):
        turned[...] = (
            input_ref[:, :, pl.ds(pl.multiple_of(n * tile, tile), tile)]
            .reshape(PLANE * tokens, tile)
            .T
        )
        product = jnp.dot(
            turned[...],
            grads[...].reshape(PLANE * tokens, QKV_WIDTH),
            preferred_element_type=jnp.float32,
        )
        qkv_out[pl.ds(n * (tile // rows), tile // rows)] = product.astype(
            jnp.bfloat16
        ).reshape(tile // rows, rows, QKV_WIDTH)

    weights.last()
    for source, start, after in wide_columns(wide_out.shape[1]):
        size = wide_out.shape[1] // (8 * PLANE)
        wide_out[:, after : after + size] = out_ref[source, :, start : start + size]
    exchange.finish()


def attention_back(
    query, keys, values, spots, starts, key_spots, table, inputs, qkv, mixed, parts
):
    low = jnp.bfloat16
    tokens = inputs.shape[1]
    sums = pltpu.VMEM((PLANE * tokens, HEAD_SIZE), jnp.float32)
    return pl.pallas_call(
        attention_back_kernel,
        out_shape=(
            jax.ShapeDtypeStruct(inputs.shape, low),
            jax.ShapeDtypeStruct((*qkv.shape[:2], QKV_WIDTH), low),
            jax.ShapeDtypeStruct((parts.shape[1], PLANE * parts.shape[2]), low),
        ),
        in_specs=[VMEM] * 11,
        out_specs=(VMEM,) * 3,
        scratch_shapes=[
            pltpu.VMEM(mixed.shape, low),
            pltpu.VMEM((PLANE, *parts.shape[1:]), low),
            pltpu.VMEM((PLANE, tokens, QKV_WIDTH), low),
            sums,
            sums,
            pltpu.VMEM((512, PLANE * tokens), low),
            *PlaneExchange.scratch(),
            *WeightScatter.scratch(*parts.shape[1:]),
        ],
        compiler_params=params(3),
        name="attention_back",
    )(query, keys, values, spots, starts, key_spots, table, inputs, qkv, mixed, parts)


def closing_kernel(
    rows_ref,
    parts_ref,
    outs_ref,
    down_ref,
    rows_out,
    query_out,
    keyval_out,
    outs_out,
    down_out,
    *scratch,
):
    out_ref, outs_sum = scratch[:2]
    scratch = list(scratch[2:])

    def take(count):
        taken, scratch[:count] = scratch[:count], []
        return taken

    scatter = SequenceScatter(rows_ref, rows_out, *take(2), take(4), CHUNKS)
    weights = WeightScatter(parts_ref, out_ref, take(4), take(6))
    chip = ChipScatter(outs_ref, *take(3), take(4), PLANE)
    outs = SequenceScatter(outs_sum, outs_out, *take(2), take(4), 1)
    down = ChipScatter(down_ref, *take(3), take(4), DOWN_PARTS)
    d, c, x, core, z, y = place()
    greet(plane_peers(d, c) + chip_peers(d, c, x, core))
    places = (*near_first(z)[::-1], z)
    slots = [place * YS + 1 - y for place in places] + [place * YS + y for place in places]
    weights.first()
    scatter.first()
    for j in slots:
        chip.start(j)
    for j in range(DOWN_PARTS):
        down.start(j)
    for off in range(1, PLANE + 1):
        weights.relay(off)
    for k in range(CHUNKS):
        scatter.relay(k)
        chip.relay(slots[2 * k])
        chip.relay(slots[2 * k + 1])
    for j in range(DOWN_PARTS):
        down.relay(j)
    for off in range(1, PLANE + 1):
        weights.send(off)
    for i, j in enumerate(slots):
        chip.total(j, outs_sum.at[j])
        if i < ZS:
            outs.start(places[i], 0)
        if i == ZS + 1:
            outs.relay_far(0)
        if i == ZS + 2:
            outs.relay_near(0)
    for j in range(DOWN_PARTS):
        down.total(j, down_out.at[j])
    for k in range(CHUNKS):
        scatter.last(k)
    weights.last()
    group_width = GROUP * HEAD_SIZE
    for source in range(PLANE):
        query_out[:, source * group_width : (source + 1) * group_width] = out_ref[
            source, :, :group_width
        ]
    for kind in range(2):
        start = group_width + kind * HEAD_SIZE
        for source in range(0, PLANE, 2):
            after = (kind * PLANE + source) * HEAD_SIZE
            keyval_out[:, after : after + 2 * HEAD_SIZE] = jnp.concatenate(
                [out_ref[source + i, :, start : start + HEAD_SIZE] for i in range(2)], axis=1
            )
    outs.last(0)
    scatter.finish()
    chip.finish()
    outs.finish()
    down.finish()


def closing(rows, parts, outs, down):
    return pl.pallas_call(
        closing_kernel,
        out_shape=(
            jax.ShapeDtypeStruct(rows.shape[1:], jnp.float32),
            jax.ShapeDtypeStruct((parts.shape[1], QUERY_HEADS * HEAD_SIZE), parts.dtype),
            jax.ShapeDtypeStruct((parts.shape[1], 2 * PLANE * HEAD_SIZE), parts.dtype),
            jax.ShapeDtypeStruct(outs.shape[1:], jnp.float32),
            jax.ShapeDtypeStruct((DOWN_PARTS, *down.shape[1:]), jnp.float32),
        ),
        in_specs=[VMEM] * 4,
        out_specs=(VMEM,) * 5,
        scratch_shapes=[
            pltpu.VMEM((PLANE, *parts.shape[1:]), parts.dtype),
            pltpu.VMEM((PLANE, *outs.shape[1:]), jnp.bfloat16),
            *SequenceScatter.scratch(*rows.shape[1:], CHUNKS),
            *WeightScatter.scratch(*parts.shape[1:]),
            *ChipScatter.scratch(PLANE, *outs.shape[1:]),
            *SequenceScatter.scratch(*outs.shape[1:], 1),
            *ChipScatter.scratch(DOWN_PARTS, *down.shape[1:]),
        ],
        compiler_params=params(4),
        name="closing",
    )(rows, parts, outs, down)


def body(
    layer_in,
    positions,
    doc_starts,
    out_grad,
    norm_gains,
    norm_gains_m,
    norm_gains_v,
    w_query,
    w_query_m,
    w_query_v,
    key_value_weight,
    key_value_first_moment,
    key_value_second_moment,
    w_out,
    w_out_m,
    w_out_v,
    w_gate_up,
    w_gate_up_m,
    w_gate_up_v,
    w_down,
    w_down_m,
    w_down_v,
):
    number_of_tokens = layer_in.shape[0]
    ctx_count = lax.axis_size("ctx")
    seq_len = number_of_tokens * ctx_count
    key_value_width = KEY_VALUE_HEADS * HEAD_SIZE
    query_group_size = QUERY_HEADS // KEY_VALUE_HEADS
    score_scale = 1.0 / math.sqrt(HEAD_SIZE)
    needed = -(-512 // number_of_tokens)
    shard_span = min(ctx_count, 1 << max(0, (needed - 1).bit_length()))
    width_of_block = shard_span * number_of_tokens
    count_of_blocks = ctx_count // shard_span
    key_places = lax.all_gather(positions, "ctx", axis=0, tiled=True)
    starts = doc_starts[0]
    own_docs = doc_lookup(positions, starts)
    key_docs = doc_lookup(key_places, starts)
    query_full, keyval_full, out_full, gains_full = (
        lax.all_gather(w_query.astype(jnp.bfloat16), ("dp", "ctx"), axis=0, tiled=True),
        lax.all_gather(key_value_weight.astype(jnp.bfloat16), ("dp", "ctx"), axis=0, tiled=True),
        lax.all_gather(w_out.astype(jnp.bfloat16), ("dp", "ctx"), axis=0, tiled=True),
        lax.all_gather(norm_gains.astype(jnp.bfloat16), ("dp", "ctx"), axis=1, tiled=True),
    )
    gain_one = gains_full[0].astype(jnp.float32)
    gain_two = gains_full[1].astype(jnp.float32)
    layer_rows = layer_in.astype(jnp.float32)
    normed_one, inverse_one = norm_forward(layer_rows)
    input_one = (normed_one * gain_one).astype(jnp.bfloat16)
    query_pre = jnp.dot(input_one, query_full, preferred_element_type=jnp.float32)
    key_value_projected = jnp.dot(input_one, keyval_full, preferred_element_type=jnp.float32)
    cosine_table, sine_table = rope_tables(positions, HEAD_SIZE)
    query_rows = (
        apply_rotation(
            query_pre.reshape(number_of_tokens, QUERY_HEADS, HEAD_SIZE), cosine_table, sine_table
        )
        .astype(jnp.bfloat16)
        .reshape(number_of_tokens, KEY_VALUE_HEADS, query_group_size, HEAD_SIZE)
    )
    keys_own = (
        apply_rotation(
            key_value_projected[:, :key_value_width].reshape(
                number_of_tokens, KEY_VALUE_HEADS, HEAD_SIZE
            ),
            cosine_table,
            sine_table,
        )
        .astype(jnp.bfloat16)
        .reshape(number_of_tokens, key_value_width)
    )
    values_own = key_value_projected[:, key_value_width:].astype(jnp.bfloat16)
    every_key, every_value = (
        lax.all_gather(keys_own, "ctx", axis=0, tiled=True),
        lax.all_gather(values_own, "ctx", axis=0, tiled=True),
    )
    blocked_keys = every_key.reshape(count_of_blocks, width_of_block, KEY_VALUE_HEADS, HEAD_SIZE)
    blocked_values = every_value.reshape(
        count_of_blocks, width_of_block, KEY_VALUE_HEADS, HEAD_SIZE
    )
    place_blocks = key_places.reshape(count_of_blocks, width_of_block)
    doc_blocks = key_docs.reshape(count_of_blocks, width_of_block)

    def visible(place_blk, doc_blk):
        allowed = (place_blk[None, :] <= positions[:, None]) & (
            doc_blk[None, :] == own_docs[:, None]
        )
        return allowed[:, None, None, :]

    def scores_of(key_blk):
        return (
            jnp.einsum("tkgd,nkd->tkgn", query_rows, key_blk, preferred_element_type=jnp.float32)
            * score_scale
        )

    def stats_step(carry, block):
        row_top, row_total = carry
        key_blk, place_blk, doc_blk = block
        allowed = visible(place_blk, doc_blk)
        masked = jnp.where(allowed, scores_of(key_blk), masked_score)
        new_top = jnp.maximum(row_top, jnp.max(masked, axis=-1, keepdims=True))
        row_total = row_total * jnp.exp(row_top - new_top) + jnp.sum(
            jnp.where(allowed, jnp.exp(masked - new_top), 0.0), axis=-1, keepdims=True
        )
        return ((new_top, row_total), None)

    statistic_shape = (number_of_tokens, KEY_VALUE_HEADS, query_group_size, 1)
    (row_top, row_total), unused = lax.scan(
        stats_step,
        (
            jnp.full(statistic_shape, masked_score, jnp.float32),
            jnp.zeros(statistic_shape, jnp.float32),
        ),
        (blocked_keys, place_blocks, doc_blocks),
    )
    log_total = row_top + jnp.log(row_total)

    def probs_of(key_blk, place_blk, doc_blk):
        allowed = visible(place_blk, doc_blk)
        masked = jnp.where(allowed, scores_of(key_blk), masked_score)
        return jnp.where(allowed, jnp.exp(masked - log_total), 0.0)

    def output_step(carry, block):
        key_blk, value_blk, place_blk, doc_blk = block
        probs_low = probs_of(key_blk, place_blk, doc_blk).astype(jnp.bfloat16)
        added = jnp.einsum(
            "tkgn,nkd->tkgd", probs_low, value_blk, preferred_element_type=jnp.float32
        )
        return (carry + added, None)

    attention_output, unused = lax.scan(
        output_step,
        jnp.zeros((number_of_tokens, KEY_VALUE_HEADS, query_group_size, HEAD_SIZE), jnp.float32),
        (blocked_keys, blocked_values, place_blocks, doc_blocks),
    )
    mixed = attention_output.reshape(number_of_tokens, QUERY_HEADS * HEAD_SIZE).astype(jnp.bfloat16)
    middle = layer_rows + jnp.dot(mixed, out_full, preferred_element_type=jnp.float32)
    normed_two, inverse_two = norm_forward(middle)
    input_two = (normed_two * gain_two).astype(jnp.bfloat16)
    gate_up_low = w_gate_up.astype(jnp.bfloat16)
    down_low = w_down.astype(jnp.bfloat16)
    columns = input_two
    gate_up = jnp.dot(
        columns,
        lax.all_gather(gate_up_low, ("dp", "ctx"), axis=0, tiled=True),
        preferred_element_type=jnp.float32,
    )
    gate_part = gate_up[:, :FF]
    up_part = gate_up[:, FF:]
    sigmoid_gate = jax.nn.sigmoid(gate_part)
    silu_gate = gate_part * sigmoid_gate
    hidden = (silu_gate * up_part).astype(jnp.bfloat16)
    columns = hidden
    down_sum = jnp.dot(
        columns,
        lax.all_gather(down_low, ("dp", "ctx"), axis=0, tiled=True),
        preferred_element_type=jnp.float32,
    )
    layer_out = (middle + down_sum).astype(jnp.bfloat16)
    grad_rows = out_grad.astype(jnp.float32)
    grad_hidden = times_transposed(
        out_grad, lax.all_gather(down_low, ("dp", "ctx"), axis=0, tiled=True)
    )
    grad_gate = grad_hidden * up_part * sigmoid_gate * (1.0 + gate_part * (1.0 - sigmoid_gate))
    grad_up = grad_hidden * silu_gate
    grad_gate_up = jnp.concatenate([grad_gate, grad_up], axis=1).astype(jnp.bfloat16)
    down_grad = lax.psum_scatter(
        transposed_times(hidden, out_grad), ("dp", "ctx"), scatter_dimension=0, tiled=True
    )
    grad_normed_two = times_transposed(
        grad_gate_up, lax.all_gather(gate_up_low, ("dp", "ctx"), axis=0, tiled=True)
    )
    gate_up_grad = lax.psum_scatter(
        transposed_times(input_two, grad_gate_up), ("dp", "ctx"), scatter_dimension=0, tiled=True
    )
    grad_norm_two, gain_two_grad = norm_backward(grad_normed_two, normed_two, inverse_two, gain_two)
    grad_middle = grad_rows + grad_norm_two
    grad_middle_low = grad_middle.astype(jnp.bfloat16)
    out_term = transposed_times(mixed, grad_middle_low)
    grad_mixed = (
        times_transposed(grad_middle_low, out_full)
        .astype(jnp.bfloat16)
        .reshape(number_of_tokens, KEY_VALUE_HEADS, query_group_size, HEAD_SIZE)
    )
    delta = jnp.sum(grad_mixed.astype(jnp.float32) * attention_output, axis=-1, keepdims=True)

    def back_step(grad_query, block):
        key_blk, value_blk, place_blk, doc_blk = block
        probs = probs_of(key_blk, place_blk, doc_blk)
        probs_low = probs.astype(jnp.bfloat16)
        grad_probs = jnp.einsum(
            "tkgd,nkd->tkgn", grad_mixed, value_blk, preferred_element_type=jnp.float32
        )
        grad_scores = (probs * (grad_probs - delta) * score_scale).astype(jnp.bfloat16)
        grad_query = grad_query + jnp.einsum(
            "tkgn,nkd->tkgd", grad_scores, key_blk, preferred_element_type=jnp.float32
        )
        key_grad = jnp.einsum(
            "tkgn,tkgd->nkd", grad_scores, query_rows, preferred_element_type=jnp.float32
        )
        value_grad = jnp.einsum(
            "tkgn,tkgd->nkd", probs_low, grad_mixed, preferred_element_type=jnp.float32
        )
        return (grad_query, (key_grad, value_grad))

    grad_query, (key_grads, value_grads) = lax.scan(
        back_step,
        jnp.zeros((number_of_tokens, KEY_VALUE_HEADS, query_group_size, HEAD_SIZE), jnp.float32),
        (blocked_keys, blocked_values, place_blocks, doc_blocks),
    )
    summed_key_gradient, value_sum = (
        lax.psum_scatter(
            key_grads.reshape(seq_len, key_value_width).astype(jnp.bfloat16),
            "ctx",
            scatter_dimension=0,
            tiled=True,
        ).astype(jnp.float32),
        lax.psum_scatter(
            value_grads.reshape(seq_len, key_value_width).astype(jnp.bfloat16),
            "ctx",
            scatter_dimension=0,
            tiled=True,
        ).astype(jnp.float32),
    )
    key_gradient_unrotated = reverse_rotation(
        summed_key_gradient.reshape(number_of_tokens, KEY_VALUE_HEADS, HEAD_SIZE),
        cosine_table,
        sine_table,
    ).reshape(number_of_tokens, key_value_width)
    grad_keyval = jnp.concatenate([key_gradient_unrotated, value_sum], axis=1).astype(jnp.bfloat16)
    grad_query_low = (
        reverse_rotation(
            grad_query.reshape(number_of_tokens, QUERY_HEADS, HEAD_SIZE), cosine_table, sine_table
        )
        .reshape(number_of_tokens, QUERY_HEADS * HEAD_SIZE)
        .astype(jnp.bfloat16)
    )
    grad_normed_one = times_transposed(grad_query_low, query_full) + times_transposed(
        grad_keyval, keyval_full
    )
    query_term = transposed_times(input_one, grad_query_low)
    keyval_term = transposed_times(input_one, grad_keyval)
    grad_norm_one, gain_one_grad = norm_backward(grad_normed_one, normed_one, inverse_one, gain_one)
    in_grad = grad_middle + grad_norm_one
    gain_term = jnp.stack([gain_one_grad, gain_two_grad])
    query_grad, keyval_grad, out_weight_grad, gains_grad = (
        lax.psum_scatter(query_term, ("dp", "ctx"), scatter_dimension=0, tiled=True),
        lax.psum_scatter(keyval_term, ("dp", "ctx"), scatter_dimension=0, tiled=True),
        lax.psum_scatter(out_term, ("dp", "ctx"), scatter_dimension=0, tiled=True),
        lax.psum_scatter(gain_term, ("dp", "ctx"), scatter_dimension=1, tiled=True),
    )
    rates = rates_for(seq_len)
    gains_m_new, gains_v_new, gains_new = adamw(
        norm_gains, gains_grad, norm_gains_m, norm_gains_v, rates[0], 0.0
    )
    query_m_new, query_v_new, query_new = adamw(
        w_query, query_grad, w_query_m, w_query_v, rates[1], weight_decay
    )
    keyval_m_new, keyval_v_new, keyval_new = adamw(
        key_value_weight,
        keyval_grad,
        key_value_first_moment,
        key_value_second_moment,
        rates[2],
        weight_decay,
    )
    out_m_new, out_v_new, out_new = adamw(
        w_out, out_weight_grad, w_out_m, w_out_v, rates[3], weight_decay
    )
    gate_up_m_new, gate_up_v_new, gate_up_new = adamw(
        w_gate_up, gate_up_grad, w_gate_up_m, w_gate_up_v, rates[4], weight_decay
    )
    down_m_new, down_v_new, down_new = adamw(
        w_down, down_grad, w_down_m, w_down_v, rates[5], weight_decay
    )
    return (
        layer_out,
        in_grad,
        gains_grad,
        gains_m_new,
        gains_v_new,
        gains_new,
        query_grad,
        query_m_new,
        query_v_new,
        query_new,
        keyval_grad,
        keyval_m_new,
        keyval_v_new,
        keyval_new,
        out_weight_grad,
        out_m_new,
        out_v_new,
        out_new,
        gate_up_grad,
        gate_up_m_new,
        gate_up_v_new,
        gate_up_new,
        down_grad,
        down_m_new,
        down_v_new,
        down_new,
    )


def tensor_parallel(
    layer_in,
    positions,
    doc_starts,
    out_grad,
    norm_gains,
    norm_gains_m,
    norm_gains_v,
    w_query,
    w_query_m,
    w_query_v,
    key_value_weight,
    key_value_first_moment,
    key_value_second_moment,
    w_out,
    w_out_m,
    w_out_v,
    w_gate_up,
    w_gate_up_m,
    w_gate_up_v,
    w_down,
    w_down_m,
    w_down_v,
):
    low = jnp.bfloat16
    own_tokens, width = layer_in.shape
    seq_len = own_tokens * PLANE
    group = GROUP
    group_width = group * HEAD_SIZE
    ff_part = FF // PLANE
    rows = w_query.shape[0]

    gains_low = norm_gains.astype(low)
    small = jnp.broadcast_to(
        jnp.pad(gains_low.T, ((0, 0), (0, 126)))[None], (PLANE, rows, 128)
    )
    attention_blocks = jnp.concatenate(
        [
            w_query.astype(low).reshape(rows, PLANE, group_width).transpose(1, 0, 2),
            key_value_weight.astype(low)
            .reshape(rows, 2, PLANE, HEAD_SIZE)
            .transpose(2, 0, 1, 3)
            .reshape(PLANE, rows, 2 * HEAD_SIZE),
            small,
        ],
        axis=2,
    )
    spots = jnp.broadcast_to(positions[None, :].astype(jnp.float32), (8, own_tokens))
    cosine_own, sine_own = rope_tables(positions, HEAD_SIZE)
    cosine_own, sine_own = cosine_own[:, 0], sine_own[:, 0]
    table = jnp.concatenate([cosine_own, cosine_own, -sine_own, sine_own], axis=1)
    (
        input_one_all,
        table_all,
        attention_all,
        gain_rows,
        query_rows,
        key_rows,
        value_rows,
        token_spots,
        token_starts,
        key_spots,
        mixed_parts,
        feed_all,
        out_all,
        down_all,
        grads_all,
    ) = attention(
        doc_starts,
        layer_in,
        table,
        spots,
        attention_blocks,
        w_gate_up,
        w_out,
        w_down,
        out_grad,
    )
    gain_one, gain_two = gain_rows[0], gain_rows[1]
    mixed = mixed_parts.transpose(2, 0, 1, 3).reshape(own_tokens, width)
    out_weight = out_all.reshape(width, width)
    branch = jnp.dot(mixed, out_weight, preferred_element_type=jnp.float32)

    layer_rows = layer_in.astype(jnp.float32)
    middle = layer_rows + branch
    normed_two, inverse_two = norm_forward(middle)
    grad_normed_two, down_sum, feed_term, down_term = feed(
        (normed_two * gain_two).astype(low),
        grads_all,
        feed_all.reshape(width, 2 * ff_part),
        down_all,
    )
    layer_out = (middle + down_sum).astype(low)

    grad_norm_two, unused = norm_backward(grad_normed_two, normed_two, inverse_two, gain_two)
    grad_middle = out_grad.astype(jnp.float32) + grad_norm_two
    grad_middle_low = grad_middle.astype(low)
    out_term = transposed_times(mixed, grad_middle_low).astype(low)
    grad_mixed = (
        times_transposed(grad_middle_low, out_weight)
        .astype(low)
        .reshape(own_tokens, PLANE, PAIRS, 2 * HEAD_SIZE)
        .transpose(1, 2, 0, 3)
    )
    one_parts, qkv_term, feed_grad = attention_back(
        query_rows,
        key_rows,
        value_rows,
        token_spots,
        token_starts,
        key_spots,
        table_all,
        input_one_all,
        attention_all,
        grad_mixed,
        feed_term.reshape(RANKS, rows, 2 * ff_part),
    )
    gate_up_grad = feed_grad.astype(jnp.float32)
    grad_normed_one, query_grad, keyval_grad, out_weight_grad, down_grad = closing(
        one_parts,
        qkv_term,
        out_term.reshape(RANKS, rows, width),
        down_term.reshape(4 * DOWN_PARTS, -1, width),
    )
    down_grad = down_grad.reshape(w_down.shape)
    normed_one, inverse_one = norm_forward(layer_rows)
    grad_norm_one, unused = norm_backward(grad_normed_one, normed_one, inverse_one, gain_one)
    in_grad = grad_middle + grad_norm_one
    query_grad = query_grad.astype(jnp.float32)
    keyval_grad = keyval_grad.astype(jnp.float32)

    def low_times(weight, grad):
        return jnp.sum(weight.astype(low).astype(jnp.float32) * grad, axis=1)

    gains_grad = jnp.stack(
        [
            low_times(w_query, query_grad) + low_times(key_value_weight, keyval_grad),
            low_times(w_gate_up, gate_up_grad),
        ]
    ) / gains_low.astype(jnp.float32)

    rates = rates_for(seq_len)
    return (
        layer_out,
        in_grad,
        gains_grad,
        *adamw(norm_gains, gains_grad, norm_gains_m, norm_gains_v, rates[0], 0.0),
        query_grad,
        *adamw(w_query, query_grad, w_query_m, w_query_v, rates[1], weight_decay),
        keyval_grad,
        *adamw(
            key_value_weight,
            keyval_grad,
            key_value_first_moment,
            key_value_second_moment,
            rates[2],
            weight_decay,
        ),
        out_weight_grad,
        *adamw(w_out, out_weight_grad, w_out_m, w_out_v, rates[3], weight_decay),
        gate_up_grad,
        *adamw(w_gate_up, gate_up_grad, w_gate_up_m, w_gate_up_v, rates[4], weight_decay),
        down_grad,
        *adamw(w_down, down_grad, w_down_m, w_down_v, rates[5], weight_decay),
    )


def solution(mesh):
    planned = tensor_parallel if dict(mesh.shape) == {"dp": 2 * XS, "ctx": ZS * YS} else body
    return jax.shard_map(
        planned,
        mesh=mesh,
        in_specs=(
            P(("dp", "ctx"), None),
            P(("dp", "ctx")),
            P("dp", None),
            P(("dp", "ctx"), None),
            P(None, ("dp", "ctx")),
            P(None, ("dp", "ctx")),
            P(None, ("dp", "ctx")),
            P(("dp", "ctx"), None),
            P(("dp", "ctx"), None),
            P(("dp", "ctx"), None),
            P(("dp", "ctx"), None),
            P(("dp", "ctx"), None),
            P(("dp", "ctx"), None),
            P(("dp", "ctx"), None),
            P(("dp", "ctx"), None),
            P(("dp", "ctx"), None),
            P(("dp", "ctx"), None),
            P(("dp", "ctx"), None),
            P(("dp", "ctx"), None),
            P(("dp", "ctx"), None),
            P(("dp", "ctx"), None),
            P(("dp", "ctx"), None),
        ),
        out_specs=(
            P(("dp", "ctx"), None),
            P(("dp", "ctx"), None),
            P(None, ("dp", "ctx")),
            P(None, ("dp", "ctx")),
            P(None, ("dp", "ctx")),
            P(None, ("dp", "ctx")),
            P(("dp", "ctx"), None),
            P(("dp", "ctx"), None),
            P(("dp", "ctx"), None),
            P(("dp", "ctx"), None),
            P(("dp", "ctx"), None),
            P(("dp", "ctx"), None),
            P(("dp", "ctx"), None),
            P(("dp", "ctx"), None),
            P(("dp", "ctx"), None),
            P(("dp", "ctx"), None),
            P(("dp", "ctx"), None),
            P(("dp", "ctx"), None),
            P(("dp", "ctx"), None),
            P(("dp", "ctx"), None),
            P(("dp", "ctx"), None),
            P(("dp", "ctx"), None),
            P(("dp", "ctx"), None),
            P(("dp", "ctx"), None),
            P(("dp", "ctx"), None),
            P(("dp", "ctx"), None),
        ),
        check_vma=False,
    )
```

```python
import functools
import math

import jax
import jax.numpy as jnp
from jax import lax
from jax.experimental import pallas as pl
from jax.experimental.pallas import tpu as pltpu
from jax.sharding import PartitionSpec as P

MODEL_WIDTH = 2048
QUERY_HEADS = 32
KEY_VALUE_HEADS = 8
HEAD_SIZE = 64
FF = 8192
STEP = 10


eps_norm = 1e-05
rope_base = 500000.0
beta_one = 0.9
beta_two = 0.95
eps_adam = 1e-08
weight_decay = 0.1
masked_score = -1e30


def rates_for(seq_len):
    return (
        0.6,
        0.8 / math.sqrt(MODEL_WIDTH // 4),
        0.8 / math.sqrt(MODEL_WIDTH),
        0.8 / math.sqrt(max(220 * MODEL_WIDTH // seq_len, 1)),
        0.8 / math.sqrt(MODEL_WIDTH),
        0.8 / math.sqrt(FF // 2),
    )


def adamw(weight, grad_sum, first, second, rate, decay):
    first_new = beta_one * first + (1.0 - beta_one) * grad_sum
    second_new = beta_two * second + (1.0 - beta_two) * grad_sum * grad_sum
    first_hat = first_new / (1.0 - beta_one**STEP)
    second_hat = second_new / (1.0 - beta_two**STEP)
    weight_new = weight - rate * (first_hat / (jnp.sqrt(second_hat) + eps_adam) + decay * weight)
    return (first_new, second_new, weight_new)


def norm_forward(layer_rows):
    inverse = lax.rsqrt(jnp.mean(layer_rows * layer_rows, axis=-1, keepdims=True) + eps_norm)
    return (layer_rows * inverse, inverse)


def norm_backward(grad_out, normed, inverse, gain_row):
    scaled = grad_out * gain_row
    grad_in = inverse * (scaled - normed * jnp.mean(scaled * normed, axis=-1, keepdims=True))
    return (grad_in, jnp.sum(grad_out * normed, axis=0))


def rope_tables(token_placement, head_dim):
    half_dim = head_dim // 2
    frequencies = jnp.exp(
        jnp.arange(half_dim, dtype=jnp.float32) * (-2.0 * math.log(rope_base) / head_dim)
    )
    angles = token_placement.astype(jnp.float32)[:, None] * frequencies[None, :]
    return (jnp.cos(angles)[:, None, :], jnp.sin(angles)[:, None, :])


def apply_rotation(value_rows, cosine_table, sine_table):
    half_dim = value_rows.shape[-1] // 2
    first_half = value_rows[..., :half_dim]
    second_half = value_rows[..., half_dim:]
    return jnp.concatenate(
        [
            first_half * cosine_table - second_half * sine_table,
            second_half * cosine_table + first_half * sine_table,
        ],
        axis=-1,
    )


def reverse_rotation(grad_rows, cosine_table, sine_table):
    half_dim = grad_rows.shape[-1] // 2
    first_half = grad_rows[..., :half_dim]
    second_half = grad_rows[..., half_dim:]
    return jnp.concatenate(
        [
            first_half * cosine_table + second_half * sine_table,
            second_half * cosine_table - first_half * sine_table,
        ],
        axis=-1,
    )


def doc_lookup(token_placement, starts):
    return jnp.sum((token_placement[:, None] >= starts[None, :]).astype(jnp.int32), axis=1) - 1


def times_transposed(left, right):
    return lax.dot_general(
        left, right, (((1,), (1,)), ((), ())), preferred_element_type=jnp.float32
    )


def transposed_times(left, right):
    return lax.dot_general(
        left, right, (((0,), (0,)), ((), ())), preferred_element_type=jnp.float32
    )


XS = 2
YS = 2
ZS = 4
PLANE = ZS * YS
RANKS = 2 * XS * PLANE
MESH = pl.DeviceIdType.MESH


def place():
    d = lax.axis_index("dp")
    c = lax.axis_index("ctx")
    return d, c, lax.div(d, 2), lax.rem(d, 2), lax.div(c, YS), lax.rem(c, YS)


def remote(src, dst, send_sem, recv_sem, d, c):
    return pltpu.make_async_remote_copy(
        src_ref=src,
        dst_ref=dst,
        send_sem=send_sem,
        recv_sem=recv_sem,
        device_id=(d, c),
        device_id_type=MESH,
    )


def greet(peers):
    barrier = pltpu.get_barrier_semaphore()
    for d, c in peers:
        pl.semaphore_signal(barrier, inc=1, device_id=(d, c), device_id_type=MESH)
    pl.semaphore_wait(barrier, len(peers))


def plane_peers(d, c):
    return [(d, lax.rem(c + k, PLANE)) for k in range(1, PLANE)]


def chip_peers(d, c, x, core):
    return [(x * 2 + 1 - core, c), ((1 - x) * 2 + core, c)]


def add_into(target, sources, rows, step=16):
    @pl.loop(0, rows, step=step)
    def _(r):
        at = pl.ds(pl.multiple_of(r, step), step)
        total = sources[0][at].astype(jnp.float32)
        for source in sources[1:]:
            total = total + source[at].astype(jnp.float32)
        target[at] = total.astype(target.dtype)


def near_first(z):
    half = lax.div(z, 2)
    return [half * 4 + 1 - z, 2 - half, 3 - 3 * half]


def is_inner(z):
    return (z == 1) | (z == 2)


class SequenceGather:
    def __init__(self, own, out, sems, chunks, direct=False):
        self.own, self.out, self.chunks, self.direct = own, out, chunks, direct
        self.zs, self.zr, self.ys, self.yr, self.local_sem = sems
        self.d, self.c, _, _, self.z, self.y = place()
        self.rows = own.shape[0] // chunks
        self.sent = []

    @staticmethod
    def scratch(chunks):
        return [
            pltpu.SemaphoreType.DMA((ZS, chunks)),
            pltpu.SemaphoreType.DMA((ZS, chunks)),
            pltpu.SemaphoreType.DMA((ZS, chunks)),
            pltpu.SemaphoreType.DMA((ZS, chunks)),
            pltpu.SemaphoreType.DMA(()),
        ]

    def part(self, ref, k):
        return ref.at[pl.ds(k * self.rows, self.rows)]

    def across(self, z, k, src):
        slot = z * YS + self.y
        return remote(
            src,
            self.part(self.out.at[slot], k),
            self.ys.at[z, k],
            self.yr.at[z, k],
            self.d,
            self.z * YS + 1 - self.y,
        )

    def along(self, to, k):
        return remote(
            self.part(self.own, k),
            self.part(self.out.at[self.c], k),
            self.zs.at[to, k],
            self.zr.at[self.z, k],
            self.d,
            to * YS + self.y,
        )

    def start(self, copy):
        copy.start()
        self.sent.append(copy)

    def first(self, by_block=False):
        self.local = pltpu.make_async_copy(self.own, self.out.at[self.c], self.local_sem)
        self.local.start()
        near, mid, far = near_first(self.z)
        targets = (far, mid, near) if self.direct else (mid, near)
        if by_block:
            for k in range(self.chunks):
                self.start(self.across(self.z, k, self.part(self.own, k)))
            for to in targets:
                for k in range(self.chunks):
                    self.start(self.along(to, k))
            return
        for k in range(self.chunks):
            for to in targets:
                self.start(self.along(to, k))
            self.start(self.across(self.z, k, self.part(self.own, k)))

    def inward(self, i, source, k):
        near, _, far = near_first(self.z)
        block = self.part(self.out.at[source * YS + self.y], k)
        return remote(
            block,
            block,
            self.zs.at[(far, self.z)[i], k],
            self.zr.at[source, k],
            self.d,
            near * YS + self.y,
        )

    def relay_one(self, source, k):
        slot = source * YS + self.y
        block = self.part(self.out.at[slot], k)
        remote(
            block, block, self.zs.at[source, k], self.zr.at[source, k], self.d, slot
        ).wait_recv()
        self.start(self.across(source, k, block))

    def relay_half(self):
        for k in range(self.chunks):
            self.relay_far(k)

    def relay_far(self, k):
        _, mid, far = near_first(self.z)
        for i, source in enumerate((mid, far)):
            self.relay_one(source, k)
            if self.direct:
                continue

            @pl.when(is_inner(self.z))
            def _(i=i, source=source):
                self.inward(i, source, k).start()

    def relay(self, k):
        self.relay_one(near_first(self.z)[0], k)
        self.relay_far(k)

    def relay_block(self, source):
        for k in range(self.chunks):
            self.relay_one(source, k)

    def arrive_across(self, z):
        for k in range(self.chunks):
            block = self.part(self.out.at[z * YS + 1 - self.y], k)
            remote(
                block,
                block,
                self.ys.at[z, k],
                self.yr.at[z, k],
                self.d,
                self.z * YS + 1 - self.y,
            ).wait_recv()

    def finish(self):
        for copy in self.sent:
            copy.wait_send()
        if self.direct:
            return
        _, mid, far = near_first(self.z)

        @pl.when(is_inner(self.z))
        def _():
            for k in range(self.chunks):
                for i, source in enumerate((mid, far)):
                    self.inward(i, source, k).wait_send()

    def last(self):
        for z in range(ZS):
            self.arrive_across(z)
        self.finish()
        self.local.wait()


class SequenceScatter:
    def __init__(self, parts, out, ybuf, zbuf, sems, chunks):
        self.parts, self.out, self.chunks = parts, out, chunks
        self.ybuf, self.zbuf = ybuf, zbuf
        self.ys, self.yr, self.zs, self.zr = sems
        self.d, self.c, _, _, self.z, self.y = place()
        self.rows = parts.shape[1] // chunks
        self.sent = []

    @staticmethod
    def scratch(rows, width, chunks):
        return [
            pltpu.VMEM((ZS, rows, width), jnp.bfloat16),
            pltpu.VMEM((ZS, rows, width), jnp.bfloat16),
            pltpu.SemaphoreType.DMA((ZS, chunks)),
            pltpu.SemaphoreType.DMA((ZS, chunks)),
            pltpu.SemaphoreType.DMA((ZS, chunks)),
            pltpu.SemaphoreType.DMA((ZS, chunks)),
        ]

    def span(self, k):
        return pl.ds(k * self.rows, self.rows)

    def across(self, z, k):
        return remote(
            self.parts.at[z * YS + 1 - self.y, self.span(k)],
            self.ybuf.at[z, self.span(k)],
            self.ys.at[z, k],
            self.yr.at[z, k],
            self.d,
            self.z * YS + 1 - self.y,
        )

    def along(self, to, k, slot):
        return remote(
            self.ybuf.at[to, self.span(k)],
            self.zbuf.at[slot, self.span(k)],
            self.zs.at[to, k],
            self.zr.at[slot, k],
            self.d,
            to * YS + self.y,
        )

    def inward(self, i, to, k):
        return remote(
            self.ybuf.at[to, self.span(k)],
            self.zbuf.at[2 + i, self.span(k)],
            self.zs.at[to, k],
            self.zr.at[2 + i, k],
            self.d,
            near_first(self.z)[0] * YS + self.y,
        )

    def start(self, z, k):
        copy = self.across(z, k)
        copy.start()
        self.sent.append(copy)

    def first(self):
        for k in range(self.chunks):
            for z in (*near_first(self.z)[::-1], self.z):
                self.start(z, k)

    def added(self, z, k):
        self.across(z, k).wait_recv()
        block = self.ybuf.at[z, self.span(k)]
        add_into(block, [self.parts.at[z * YS + self.y, self.span(k)], block], self.rows)

    def relay_near(self, k):
        near = near_first(self.z)[0]
        self.added(near, k)
        copy = self.along(near, k, 0)
        copy.start()
        self.sent.append(copy)

    def relay_far(self, k):
        _, mid, far = near_first(self.z)
        for to in (far, mid):
            self.added(to, k)

            @pl.when(jnp.logical_not(is_inner(self.z)))
            def _(to=to, i=0 if to is mid else 1):
                self.inward(i, to, k).start()

        @pl.when(is_inner(self.z))
        def _():
            for i, to in ((1, far), (0, mid)):
                self.inward(i, to, k).wait_recv()
                block = self.ybuf.at[to, self.span(k)]
                add_into(block, [block, self.zbuf.at[2 + i, self.span(k)]], self.rows)
                self.along(to, k, 1).start()

    def relay(self, k):
        self.relay_far(k)
        self.relay_near(k)

    def last(self, k):
        self.across(self.z, k).wait_recv()
        blocks = [self.parts.at[self.c, self.span(k)], self.ybuf.at[self.z, self.span(k)]]
        near, mid, _ = near_first(self.z)
        for slot, source in enumerate((near, mid)):
            block = self.zbuf.at[slot, self.span(k)]
            self.along(source, k, slot).wait_recv()
            blocks.append(block)
        add_into(self.out.at[self.span(k)], blocks, self.rows)

    def finish(self):
        for copy in self.sent:
            copy.wait_send()
        _, mid, far = near_first(self.z)
        for k in range(self.chunks):
            for to in (mid, far):
                self.along(to, k, 1).wait_send()


class ChipGather:
    def __init__(self, out, sems, count, rows=None):
        self.out, self.count, self.rows = out, count, rows
        self.cs, self.cr, self.xs, self.xr = sems
        self.d, self.c, self.x, self.core, _, _ = place()
        self.sent = []

    @staticmethod
    def scratch(count):
        return [
            pltpu.SemaphoreType.DMA((2, count)),
            pltpu.SemaphoreType.DMA((2, count)),
            pltpu.SemaphoreType.DMA((count,)),
            pltpu.SemaphoreType.DMA((count,)),
        ]

    def block(self, slot):
        if self.rows is None:
            return self.out.at[slot]
        return self.out.at[pl.ds(slot * self.rows, self.rows)]

    def to_core(self, far, j, src=None):
        x = 1 - self.x if far else self.x
        block = self.block((x * 2 + self.core) * self.count + j)
        return remote(
            block if src is None else src,
            block,
            self.cs.at[far, j],
            self.cr.at[far, j],
            self.x * 2 + 1 - self.core,
            self.c,
        )

    def to_x(self, j, src=None):
        block = self.block(self.d * self.count + j)
        return remote(
            block if src is None else src,
            block,
            self.xs.at[j],
            self.xr.at[j],
            (1 - self.x) * 2 + self.core,
            self.c,
        )

    def start(self, j, src=None):
        for copy in (self.to_x(j, src), self.to_core(0, j, src)):
            copy.start()
            self.sent.append(copy)

    def relay(self, j):
        self.to_x(j).wait_recv()
        copy = self.to_core(1, j)
        copy.start()
        self.sent.append(copy)

    def last(self):
        for far in (0, 1):
            for j in range(self.count):
                self.to_core(far, j).wait_recv()
        for copy in self.sent:
            copy.wait_send()


class WeightGather:
    def __init__(self, blocks, out, sems):
        self.blocks, self.out = blocks, out
        self.ps, self.pr, self.local_sem = sems[:3]
        self.chip = ChipGather(out, sems[3:], PLANE)
        self.d, self.c = self.chip.d, self.chip.c
        self.sent = []

    @staticmethod
    def scratch():
        return [
            pltpu.SemaphoreType.DMA((PLANE,)),
            pltpu.SemaphoreType.DMA((PLANE,)),
            pltpu.SemaphoreType.DMA(()),
        ] + ChipGather.scratch(PLANE)

    def send(self, off):
        to = lax.rem(self.c + off, PLANE)
        copy = remote(
            self.blocks.at[to],
            self.out.at[self.d * PLANE + self.c],
            self.ps.at[off],
            self.pr.at[self.c],
            self.d,
            to,
        )
        copy.start()
        self.sent.append(copy)

    def first(self, ahead=PLANE - 1):
        self.ahead = ahead
        self.local = pltpu.make_async_copy(
            self.blocks.at[self.c], self.out.at[self.d * PLANE + self.c], self.local_sem
        )
        self.local.start()
        for off in range(1, 1 + ahead):
            self.send(off)
        self.chip.start(self.c, self.blocks.at[self.c])

    def relay(self, off):
        if off + self.ahead < PLANE:
            self.send(off + self.ahead)
        source = lax.rem(self.c + PLANE - off, PLANE)
        block = self.out.at[self.d * PLANE + source]
        remote(
            block, block, self.ps.at[off], self.pr.at[source], self.d, source
        ).wait_recv()
        self.chip.start(source)

    def relay_chip(self):
        for off in range(PLANE):
            self.chip.relay(lax.rem(self.c + off, PLANE))

    def last(self):
        self.chip.last()
        for copy in self.sent:
            copy.wait_send()
        self.local.wait()


class ChipScatter:
    def __init__(self, parts, cbuf, stage, xbuf, sems, count):
        self.parts, self.count = parts, count
        self.cbuf, self.stage, self.xbuf = cbuf, stage, xbuf
        self.cs, self.cr, self.xs, self.xr = sems
        self.d, self.c, self.x, self.core, _, _ = place()
        self.sent = []

    @staticmethod
    def scratch(count, rows, width):
        return [
            pltpu.VMEM((2, count, rows, width), jnp.bfloat16),
            pltpu.VMEM((count, rows, width), jnp.bfloat16),
            pltpu.VMEM((count, rows, width), jnp.bfloat16),
            pltpu.SemaphoreType.DMA((2, count)),
            pltpu.SemaphoreType.DMA((2, count)),
            pltpu.SemaphoreType.DMA((count,)),
            pltpu.SemaphoreType.DMA((count,)),
        ]

    def to_core(self, far, j):
        x = 1 - self.x if far else self.x
        return remote(
            self.parts.at[(x * 2 + 1 - self.core) * self.count + j],
            self.cbuf.at[far, j],
            self.cs.at[far, j],
            self.cr.at[far, j],
            self.x * 2 + 1 - self.core,
            self.c,
        )

    def to_x(self, j):
        return remote(
            self.stage.at[j],
            self.xbuf.at[j],
            self.xs.at[j],
            self.xr.at[j],
            (1 - self.x) * 2 + self.core,
            self.c,
        )

    def start(self, j):
        for far in (1, 0):
            copy = self.to_core(far, j)
            copy.start()
            self.sent.append(copy)

    def relay(self, j):
        self.to_core(1, j).wait_recv()
        own = self.parts.at[((1 - self.x) * 2 + self.core) * self.count + j]
        add_into(self.stage.at[j], [own, self.cbuf.at[1, j]], own.shape[0])
        copy = self.to_x(j)
        copy.start()
        self.sent.append(copy)

    def total(self, j, target):
        self.to_core(0, j).wait_recv()
        self.to_x(j).wait_recv()
        own = self.parts.at[self.d * self.count + j]
        add_into(target, [own, self.cbuf.at[0, j], self.xbuf.at[j]], own.shape[0])

    def finish(self):
        for copy in self.sent:
            copy.wait_send()


class WeightScatter:
    def __init__(self, parts, out, bufs, sems):
        self.stage = bufs[0]
        self.ps, self.pr = sems[:2]
        self.chip = ChipScatter(parts, *bufs[1:], sems[2:], PLANE)
        self.out = out
        self.d, self.c = self.chip.d, self.chip.c
        self.sent = []

    @staticmethod
    def scratch(rows, width):
        chip = ChipScatter.scratch(PLANE, rows, width)
        return [
            pltpu.VMEM((PLANE, rows, width), jnp.bfloat16),
            *chip[:3],
            pltpu.SemaphoreType.DMA((PLANE,)),
            pltpu.SemaphoreType.DMA((PLANE,)),
            *chip[3:],
        ]

    def first(self):
        for off in range(1, PLANE + 1):
            self.chip.start(lax.rem(self.c + off, PLANE))

    def relay(self, off):
        self.chip.relay(lax.rem(self.c + off, PLANE))

    def send(self, off):
        to = lax.rem(self.c + off, PLANE)
        if off == PLANE:
            self.chip.total(to, self.out.at[self.c])
            return
        self.chip.total(to, self.stage.at[to])
        copy = remote(
            self.stage.at[to],
            self.out.at[self.c],
            self.ps.at[off],
            self.pr.at[self.c],
            self.d,
            to,
        )
        copy.start()
        self.sent.append(copy)

    def last(self):
        for off in range(1, PLANE):
            source = lax.rem(self.c + off, PLANE)
            block = self.out.at[source]
            remote(
                block, block, self.ps.at[off], self.pr.at[source], self.d, source
            ).wait_recv()
        for copy in self.sent:
            copy.wait_send()
        self.chip.finish()


def params(collective_id, mebibytes=56):
    return pltpu.CompilerParams(
        collective_id=collective_id, has_side_effects=True, vmem_limit_bytes=mebibytes * 2**20
    )


ANY = pl.BlockSpec(memory_space=pl.ANY)
VMEM = pl.BlockSpec(memory_space=pltpu.VMEM)
CHUNKS = 4


DOWN_PARTS = 4
SCORE_SCALE = 1.0 / math.sqrt(HEAD_SIZE)
GROUP = QUERY_HEADS // KEY_VALUE_HEADS
PAIRS = GROUP // 2


def times_rows(left, right):
    return lax.dot_general(
        left, right, (((1,), (1,)), ((), ())), preferred_element_type=jnp.float32
    )


class PlaneExchange:
    def __init__(self, blocks, out, sems):
        self.blocks, self.out = blocks, out
        self.ps, self.pr, self.local_sem = sems
        self.d, self.c = lax.axis_index("dp"), lax.axis_index("ctx")
        self.sent = []

    @staticmethod
    def scratch():
        return [
            pltpu.SemaphoreType.DMA((PLANE,)),
            pltpu.SemaphoreType.DMA((PLANE,)),
            pltpu.SemaphoreType.DMA(()),
        ]

    def send(self, off):
        to = lax.rem(self.c + off, PLANE)
        if off % PLANE == 0:
            self.local = pltpu.make_async_copy(
                self.blocks.at[to], self.out.at[self.c], self.local_sem
            )
            self.local.start()
            return
        copy = remote(
            self.blocks.at[to],
            self.out.at[self.c],
            self.ps.at[off],
            self.pr.at[self.c],
            self.d,
            to,
        )
        copy.start()
        self.sent.append(copy)

    def arrive(self, off):
        if off % PLANE == 0:
            self.local.wait()
            return
        source = lax.rem(self.c + PLANE - off, PLANE)
        block = self.out.at[source]
        remote(
            block, block, self.ps.at[off], self.pr.at[source], self.d, source
        ).wait_recv()

    def finish(self):
        for copy in self.sent:
            copy.wait_send()


def probabilities(query, keys, spot, start, key_spots):
    scores = times_rows(query, keys) * SCORE_SCALE
    masked = jnp.where((key_spots <= spot) & (key_spots >= start), scores, masked_score)
    exponent = jnp.exp(masked - jnp.max(masked, axis=-1, keepdims=True))
    return exponent * (1.0 / jnp.sum(exponent, axis=-1, keepdims=True))


def rotate(value, table, back=False):
    lane = lax.broadcasted_iota(jnp.int32, value.shape, 1)
    turned = pltpu.roll(table, HEAD_SIZE, 1)
    cosine = jnp.where(lane < HEAD_SIZE, table, turned)
    sine = jnp.where(lane < HEAD_SIZE, turned, table)
    half = HEAD_SIZE // 2
    other = jnp.where(
        lax.rem(lane, HEAD_SIZE) < half,
        pltpu.roll(value, 2 * HEAD_SIZE - half, 1),
        pltpu.roll(value, half, 1),
    )
    if back:
        return value * cosine - other * sine
    return value * cosine + other * sine


QKV_WIDTH = (GROUP + 2) * HEAD_SIZE


def wide_columns(width):
    run = width // (8 * PLANE)
    for to in range(PLANE):
        for part in range(8):
            yield to, part * run, (part * PLANE + to) * run


def attention_kernel(
    starts_ref,
    rows_ref,
    table_ref,
    spots_ref,
    qkv_ref,
    blocks_ref,
    out_rows_ref,
    down_ref,
    grads_ref,
    input_out,
    table_out,
    qkv_out,
    gains_out,
    query_out,
    key_out,
    value_out,
    spot_out,
    start_out,
    key_spot_out,
    mixed_out,
    blocks_out,
    out_rows_out,
    down_out,
    grads_out,
    *scratch,
):
    mixed_stage, spots_all, rows_all, wide_full, wide_blocks = scratch[:5]
    down_full, down_blocks, out_full, out_block, load_sem = scratch[5:10]
    scratch = list(scratch[10:])

    def take(count):
        taken, scratch[:count] = scratch[:count], []
        return taken

    d, c, x, core, z, y = place()
    exchange = PlaneExchange(mixed_stage, mixed_out, take(3))
    qkv = WeightGather(qkv_ref, qkv_out, take(7))
    weights = WeightGather(wide_blocks, blocks_out, take(7))
    outs = SequenceGather(out_block, out_rows_out.at[pl.ds(d * PLANE, PLANE)], take(5), 1)
    outs_chip = ChipGather(out_rows_out, take(4), PLANE)
    rows = SequenceGather(rows_ref, rows_all, take(5), 2)
    table = SequenceGather(table_ref, table_out, take(5), 1)
    grads = SequenceGather(grads_ref, grads_out, take(5), CHUNKS, direct=True)
    down_rows = down_ref.shape[0] // DOWN_PARTS
    down = ChipGather(down_out, take(4), DOWN_PARTS, down_rows)
    spot_send, spot_recv, spot_local, down_local = take(4)
    greet(plane_peers(d, c) + chip_peers(d, c, x, core))
    order = near_first(z)

    loads = [
        pltpu.make_async_copy(source, target, load_sem.at[i])
        for i, (source, target) in enumerate(
            [(out_rows_ref, out_full), (down_ref, down_full), (blocks_ref, wide_full)]
        )
    ]
    for load in loads:
        load.start()
    qkv.first()
    spots_own = pltpu.make_async_copy(spots_ref, spots_all.at[c], spot_local)
    spots_own.start()
    spots_sent = []
    for off in range(1, PLANE):
        to = lax.rem(c + off, PLANE)
        copy = remote(
            spots_ref, spots_all.at[c], spot_send.at[off], spot_recv.at[c], d, to
        )
        copy.start()
        spots_sent.append(copy)
    table.first()
    rows.first(by_block=True)
    loads[1].wait()

    @pl.loop(0, down_full.shape[0], step=16)
    def _(r):
        at = pl.ds(pl.multiple_of(r, 16), 16)
        down_blocks[at] = down_full[at].astype(jnp.bfloat16)

    down_own = pltpu.make_async_copy(
        down_blocks, down_out.at[pl.ds(d * down_full.shape[0], down_full.shape[0])], down_local
    )
    down_own.start()
    for j in range(DOWN_PARTS):
        down.start(j, down_blocks.at[pl.ds(j * down_rows, down_rows)])
    loads[0].wait()
    out_block[...] = out_full[...].astype(jnp.bfloat16)
    outs.first()
    outs_chip.start(c, out_block)
    loads[2].wait()

    @pl.loop(0, wide_full.shape[0], step=16)
    def _(r):
        at = pl.ds(pl.multiple_of(r, 16), 16)
        for to, start, after in wide_columns(wide_full.shape[1]):
            size = wide_full.shape[1] // (8 * PLANE)
            wide_blocks[to, at, start : start + size] = wide_full[
                at, after : after + size
            ].astype(jnp.bfloat16)

    for off in range(1, PLANE):
        qkv.relay(off)
    table.relay(0)
    rows.relay_block(order[0])
    qkv.relay_chip()
    rows.relay_half()
    weights.first()
    for off in range(1, PLANE):
        source = lax.rem(c + off, PLANE)
        block = spots_all.at[source]
        remote(block, block, spot_send.at[off], spot_recv.at[source], d, source).wait_recv()
    spots_own.wait()
    table.last()
    for slot in range(PLANE):
        key_spot_out[:, slot * 128 : (slot + 1) * 128] = spots_all[slot]
        spot = jnp.broadcast_to(spots_all[slot][:1], (128, 128)).T[:, :1]
        start = jnp.zeros_like(spot)
        for doc in range(starts_ref.shape[1]):
            first = starts_ref[0, doc].astype(jnp.float32)
            start = jnp.maximum(start, jnp.where(spot >= first, first, 0.0))
        spot_out[slot] = spot
        start_out[slot] = start
    qkv.last()
    for pair in range(RANKS // 2):
        columns = qkv_out[2 * pair : 2 * pair + 2, :, QKV_WIDTH:]
        turned = columns.reshape(128, 128).astype(jnp.float32).T
        gains_out[:, pair * 128 : (pair + 1) * 128] = turned[:8]

    tokens, width = rows_ref.shape
    wide = 2 * HEAD_SIZE

    def project(pair):
        for slot in range(YS):

            @pl.loop(0, tokens, step=32)
            def _(r):
                at = pl.ds(pl.multiple_of(r, 32), 32)
                value = rows_all[pair * YS + slot, at].astype(jnp.float32)
                inverse = lax.rsqrt(
                    jnp.mean(value * value, axis=-1, keepdims=True) + eps_norm
                )
                input_out[pair * YS + slot, at] = (value * inverse * gains_out[:1]).astype(
                    jnp.bfloat16
                )

        both = pl.ds(pair * YS, YS)
        weight = qkv_out[:, :, :QKV_WIDTH].reshape(width, QKV_WIDTH)
        projected = jnp.dot(
            input_out[both].reshape(YS * tokens, width),
            weight,
            preferred_element_type=jnp.float32,
        )
        turns = table_out[both].reshape(YS * tokens, wide)
        for slot in range(YS):
            span = slice(slot * tokens, (slot + 1) * tokens)
            block = pair * YS + slot
            for heads in range(PAIRS):
                query = rotate(
                    projected[span, heads * wide : (heads + 1) * wide], turns[span]
                ).astype(jnp.bfloat16)
                query_out[block, heads, 0] = query[:, :HEAD_SIZE]
                query_out[block, heads, 1] = query[:, HEAD_SIZE:]
            key = rotate(projected[span, PAIRS * wide :], turns[span])
            key_out[block] = key[:, :HEAD_SIZE].astype(jnp.bfloat16)
            value_out[block] = projected[span, PAIRS * wide + HEAD_SIZE :].astype(
                jnp.bfloat16
            )

    rows.local.wait()
    rows.arrive_across(z)
    project(z)
    outs.relay(0)
    for source in order:
        outs_chip.start(source * YS + y)
    for pair in order:
        rows.arrive_across(pair)
        project(pair)
    rows.finish()
    for other in range(ZS):
        outs.arrive_across(other)
        outs_chip.start(other * YS + 1 - y)
    grads.first()
    out_order = [c, *(source * YS + y for source in order)]
    out_order += [other * YS + 1 - y for other in range(ZS)]

    for step in range(1, PLANE + 1):
        block = lax.rem(c + step, PLANE)

        @pl.loop(0, PAIRS)
        def _(pair):
            halves = []
            keys = key_out[...].reshape(PLANE * tokens, HEAD_SIZE)
            values = value_out[...].reshape(PLANE * tokens, HEAD_SIZE)
            for half in range(2):
                probs = probabilities(
                    query_out[block, pair, half],
                    keys,
                    spot_out[block],
                    start_out[block],
                    key_spot_out[:1],
                )
                halves.append(
                    jnp.dot(
                        probs.astype(jnp.bfloat16), values, preferred_element_type=jnp.float32
                    ).astype(jnp.bfloat16)
                )
            mixed_stage[block, pair] = jnp.concatenate(halves, axis=1)

        exchange.send(step)
        if step < PLANE:
            weights.relay(step)
        if step == 2:
            for j in range(DOWN_PARTS):
                down.relay(j)
        if 3 <= step < 7:
            for j in out_order[2 * (step - 3) : 2 * (step - 2)]:
                outs_chip.relay(j)
    for k in range(CHUNKS):
        for off in (2 * k, 2 * k + 1):
            weights.chip.relay(lax.rem(c + PLANE - off, PLANE))
        grads.relay(k)
    for off in range(1, PLANE + 1):
        exchange.arrive(off)
    grads.last()
    down.last()
    outs_chip.last()
    weights.last()
    outs.finish()
    outs.local.wait()
    exchange.finish()
    for copy in spots_sent:
        copy.wait_send()
    down_own.wait()


def attention(starts, rows, table, spots, qkv, blocks, out_rows, down, grads):
    low, full = jnp.bfloat16, jnp.float32
    tokens, width = rows.shape
    mixed = jax.ShapeDtypeStruct((PLANE, PAIRS, tokens, 2 * HEAD_SIZE), low)
    seq_len = PLANE * tokens
    wide_block = (blocks.shape[0], blocks.shape[1] // PLANE)
    return pl.pallas_call(
        attention_kernel,
        out_shape=(
            jax.ShapeDtypeStruct((PLANE, tokens, width), low),
            jax.ShapeDtypeStruct((PLANE, *table.shape), full),
            jax.ShapeDtypeStruct((RANKS, *qkv.shape[1:]), low),
            jax.ShapeDtypeStruct((8, width), full),
            jax.ShapeDtypeStruct((PLANE, PAIRS, 2, tokens, HEAD_SIZE), low),
            jax.ShapeDtypeStruct((PLANE, tokens, HEAD_SIZE), low),
            jax.ShapeDtypeStruct((PLANE, tokens, HEAD_SIZE), low),
            jax.ShapeDtypeStruct((PLANE, tokens, 1), full),
            jax.ShapeDtypeStruct((PLANE, tokens, 1), full),
            jax.ShapeDtypeStruct((8, seq_len), full),
            mixed,
            jax.ShapeDtypeStruct((RANKS, *wide_block), low),
            jax.ShapeDtypeStruct((RANKS, *out_rows.shape), low),
            jax.ShapeDtypeStruct((4 * down.shape[0], down.shape[1]), low),
            jax.ShapeDtypeStruct((PLANE, *grads.shape), low),
        ),
        in_specs=[pl.BlockSpec(memory_space=pltpu.SMEM)] + [ANY] * 8,
        out_specs=(VMEM,) * 11 + (ANY,) * 4,
        scratch_shapes=[
            pltpu.VMEM(mixed.shape, low),
            pltpu.VMEM((PLANE, *spots.shape), full),
            pltpu.VMEM((PLANE, tokens, width), low),
            pltpu.VMEM(blocks.shape, full),
            pltpu.VMEM((PLANE, *wide_block), low),
            pltpu.VMEM(down.shape, full),
            pltpu.VMEM(down.shape, low),
            pltpu.VMEM(out_rows.shape, full),
            pltpu.VMEM(out_rows.shape, low),
            pltpu.SemaphoreType.DMA((3,)),
            *PlaneExchange.scratch(),
            *WeightGather.scratch(),
            *WeightGather.scratch(),
            *SequenceGather.scratch(1),
            *ChipGather.scratch(PLANE),
            *SequenceGather.scratch(2),
            *SequenceGather.scratch(1),
            *SequenceGather.scratch(CHUNKS),
            *ChipGather.scratch(DOWN_PARTS),
            pltpu.SemaphoreType.DMA((PLANE,)),
            pltpu.SemaphoreType.DMA((PLANE,)),
            pltpu.SemaphoreType.DMA(()),
            pltpu.SemaphoreType.DMA(()),
        ],
        compiler_params=params(2),
        name="attention",
    )(starts, rows, table, spots, qkv, blocks, out_rows, down, grads)


def feed_kernel(
    rows_ref,
    grads_all,
    weight_ref,
    down_ref,
    normed_out,
    total_out,
    weight_grad_out,
    down_grad_out,
    *scratch,
):
    rows_all, slope_gate, slope_up, hidden_all, gate_grads = scratch[:5]
    normed_parts, down_parts, turned, stage, stage_sem = scratch[5:10]
    scratch = list(scratch[10:])

    def take(count):
        taken, scratch[:count] = scratch[:count], []
        return taken

    rows = SequenceGather(rows_ref, rows_all, take(5), 2)
    normed = SequenceScatter(normed_parts, normed_out, *take(2), take(4), 1)
    total = SequenceScatter(down_parts, total_out, *take(2), take(4), 1)
    d, c, x, core, z, y = place()
    greet(
        [(d, lax.rem(z + off, ZS) * YS + y) for off in range(1, ZS)] + [(d, z * YS + 1 - y)]
    )
    tokens, width = rows_ref.shape
    part = down_ref.shape[0]
    tile = 256
    blocks = PLANE // 2
    half = lax.div(z, 2)
    near, mid, far = near_first(z)

    def slots(side):
        return pl.ds(side * blocks, blocks)

    def columns(n, start=0, size=tile):
        return pl.ds(pl.multiple_of(n + start, size), size)

    def flat(ref, side):
        value = ref[slots(side)]
        return value.reshape(blocks * tokens, value.shape[2])

    def held(value, dtype=jnp.bfloat16):
        return value.astype(dtype).reshape(blocks, tokens, value.shape[1])

    def forward(side):
        @pl.loop(0, part, step=tile)
        def _(n):
            at, after = columns(n), columns(n, part)
            value = flat(rows_all, side)
            gate = jnp.dot(value, weight_ref[:, at], preferred_element_type=jnp.float32)
            up = jnp.dot(value, weight_ref[:, after], preferred_element_type=jnp.float32)
            sigmoid = jax.nn.sigmoid(gate)
            silu = gate * sigmoid
            hidden_all[slots(side), :, at] = held(silu * up)
            slope_up[slots(side), :, at] = held(silu, jnp.float32)
            slope_gate[slots(side), :, at] = held(
                up * sigmoid * (1.0 + gate * (1.0 - sigmoid)), jnp.float32
            )

    def downward(side):
        @pl.loop(0, width, step=2 * tile)
        def _(n):
            at = columns(n, 0, 2 * tile)
            down_parts[slots(side), :, at] = held(
                jnp.dot(
                    flat(hidden_all, side), down_ref[:, at], preferred_element_type=jnp.float32
                )
            )

    def backward(side):
        @pl.loop(0, part, step=tile)
        def _(n):
            at, after = columns(n), columns(n, part)
            grad = held(times_rows(flat(grads_all, side), down_ref[at, :]), jnp.float32)
            gate_grads[slots(side), :, at] = (grad * slope_gate[slots(side), :, at]).astype(
                jnp.bfloat16
            )
            gate_grads[slots(side), :, after] = (grad * slope_up[slots(side), :, at]).astype(
                jnp.bfloat16
            )

    def inward(side):
        @pl.loop(0, width, step=2 * tile)
        def _(n):
            at = columns(n, 0, 2 * tile)
            normed_parts[slots(side), :, at] = held(
                times_rows(flat(gate_grads, side), weight_ref[at, :])
            )

    tiles = [(hidden_all, grads_all, down_grad_out, n) for n in range(part // tile)]
    tiles += [(rows_all, gate_grads, weight_grad_out, n) for n in range(width // tile)]
    copies = []

    def weight_grad(i):
        left, right, out, n = tiles[i]
        if i >= 2:
            copies[i - 2].wait()
        value = left[:, :, n * tile : (n + 1) * tile].reshape(PLANE * tokens, tile)
        turned[...] = value.T

        @pl.loop(0, width, step=2 * tile)
        def _(m):
            at = columns(m, 0, 2 * tile)
            stage[i % 2, :, at] = jnp.dot(
                turned[...],
                right[:, :, at].reshape(PLANE * tokens, 2 * tile),
                preferred_element_type=jnp.float32,
            ).astype(jnp.bfloat16)

        copy = pltpu.make_async_copy(
            stage.at[i % 2], out.at[pl.ds(n * tile, tile)], stage_sem.at[i % 2]
        )
        copy.start()
        copies.append(copy)

    rows.first(by_block=True)
    rows.local.wait()
    rows.relay_block(near)
    rows.arrive_across(z)
    rows.arrive_across(near)
    forward(half)
    rows.relay_half()
    backward(half)
    inward(half)
    normed.start(near, 0)
    normed.start(z, 0)
    rows.arrive_across(mid)
    rows.arrive_across(far)
    forward(1 - half)
    backward(1 - half)
    inward(1 - half)
    normed.start(far, 0)
    normed.start(mid, 0)
    normed.relay_near(0)
    downward(1 - half)
    total.start(far, 0)
    total.start(mid, 0)
    normed.relay_far(0)
    downward(half)
    total.start(near, 0)
    total.start(z, 0)
    for i in range(2):
        weight_grad(i)
    total.relay_far(0)
    weight_grad(len(copies))
    total.relay_near(0)
    for i in range(len(copies), len(tiles)):
        weight_grad(i)
    normed.last(0)
    total.last(0)
    for copy in copies[-2:]:
        copy.wait()
    rows.finish()
    normed.finish()
    total.finish()


def feed(rows, grads, weight, down):
    part, width = down.shape
    low = rows.dtype
    tokens = rows.shape[0]
    summed = jax.ShapeDtypeStruct(rows.shape, jnp.float32)
    return pl.pallas_call(
        feed_kernel,
        out_shape=(
            summed,
            summed,
            jax.ShapeDtypeStruct(weight.shape, low),
            jax.ShapeDtypeStruct(down.shape, low),
        ),
        in_specs=[ANY] + [VMEM] * 3,
        out_specs=(VMEM,) * 2 + (ANY,) * 2,
        scratch_shapes=[
            pltpu.VMEM((PLANE, tokens, width), low),
            pltpu.VMEM((PLANE, tokens, part), jnp.float32),
            pltpu.VMEM((PLANE, tokens, part), jnp.float32),
            pltpu.VMEM((PLANE, tokens, part), low),
            pltpu.VMEM((PLANE, tokens, 2 * part), low),
            pltpu.VMEM((PLANE, tokens, width), low),
            pltpu.VMEM((PLANE, tokens, width), low),
            pltpu.VMEM((256, PLANE * tokens), low),
            pltpu.VMEM((2, 256, width), low),
            pltpu.SemaphoreType.DMA((2,)),
            *SequenceGather.scratch(2),
            *SequenceScatter.scratch(tokens, width, 1),
            *SequenceScatter.scratch(tokens, width, 1),
        ],
        compiler_params=params(5, 60),
        name="feed",
    )(rows, grads, weight, down)


def attention_back_kernel(
    query_ref,
    key_ref,
    value_ref,
    spot_ref,
    start_ref,
    key_spot_ref,
    table_ref,
    input_ref,
    qkv_ref,
    mixed_ref,
    parts_ref,
    rows_out,
    qkv_out,
    wide_out,
    *scratch,
):
    mixed_all, out_ref, grads, key_grad, value_grad, turned = scratch[:6]
    scratch = scratch[6:]
    exchange = PlaneExchange(mixed_ref, mixed_all, scratch[:3])
    weights = WeightScatter(parts_ref, out_ref, scratch[3:7], scratch[7:13])
    d, c, x, core, z, y = place()
    greet(plane_peers(d, c) + chip_peers(d, c, x, core))
    for off in range(1, PLANE + 1):
        exchange.send(off)
    weights.first()
    key_grad[...] = jnp.zeros_like(key_grad)
    value_grad[...] = jnp.zeros_like(value_grad)
    wide = 2 * HEAD_SIZE
    for step in range(PLANE):
        block = lax.rem(c + PLANE - step, PLANE)
        exchange.arrive(step)

        @pl.loop(0, PAIRS)
        def _(pair):
            keys = key_ref[...].reshape(key_grad.shape)
            values = value_ref[...].reshape(value_grad.shape)
            halves = []
            for half in range(2):
                query = query_ref[block, pair, half]
                grad = mixed_all[block, pair][:, half * HEAD_SIZE : (half + 1) * HEAD_SIZE]
                probs = probabilities(
                    query, keys, spot_ref[block], start_ref[block], key_spot_ref[:1]
                )
                grad_probs = times_rows(grad, values)
                delta = jnp.sum(probs * grad_probs, axis=-1, keepdims=True)
                grad_scores = (probs * (grad_probs - delta) * SCORE_SCALE).astype(jnp.bfloat16)
                halves.append(
                    jnp.dot(grad_scores, keys, preferred_element_type=jnp.float32)
                )
                key_grad[...] += transposed_times(grad_scores, query)
                value_grad[...] += transposed_times(probs.astype(jnp.bfloat16), grad)
            at = pl.ds(pl.multiple_of(pair * wide, wide), wide)
            grads[block, :, at] = rotate(
                jnp.concatenate(halves, axis=1), table_ref[block], back=True
            ).astype(jnp.bfloat16)

        weights.relay(step + 1)
        if step >= 2:
            weights.send(step - 1)
    tokens = grads.shape[1]
    for block in range(PLANE):
        span = slice(block * tokens, (block + 1) * tokens)
        both = jnp.concatenate([key_grad[span], value_grad[span]], axis=1)
        lane = lax.broadcasted_iota(jnp.int32, both.shape, 1)
        grads[block, :, PAIRS * wide :] = jnp.where(
            lane < HEAD_SIZE, rotate(both, table_ref[block], back=True), both
        ).astype(jnp.bfloat16)
    weights.send(PLANE - 1)
    width = input_ref.shape[2]
    rows = qkv_ref.shape[1]
    tile = 512

    @pl.loop(0, width // tile)
    def _(n):
        weight = qkv_ref[pl.ds(n * (tile // rows), tile // rows), :, :QKV_WIDTH]
        product = times_rows(
            grads[...].reshape(PLANE * tokens, QKV_WIDTH), weight.reshape(tile, QKV_WIDTH)
        )
        rows_out[:, :, pl.ds(pl.multiple_of(n * tile, tile), tile)] = product.astype(
            jnp.bfloat16
        ).reshape(PLANE, tokens, tile)

    weights.send(PLANE)

    @pl.loop(0, width // tile)
    def _(n):
        turned[...] = (
            input_ref[:, :, pl.ds(pl.multiple_of(n * tile, tile), tile)]
            .reshape(PLANE * tokens, tile)
            .T
        )
        product = jnp.dot(
            turned[...],
            grads[...].reshape(PLANE * tokens, QKV_WIDTH),
            preferred_element_type=jnp.float32,
        )
        qkv_out[pl.ds(n * (tile // rows), tile // rows)] = product.astype(
            jnp.bfloat16
        ).reshape(tile // rows, rows, QKV_WIDTH)

    weights.last()
    for source, start, after in wide_columns(wide_out.shape[1]):
        size = wide_out.shape[1] // (8 * PLANE)
        wide_out[:, after : after + size] = out_ref[source, :, start : start + size]
    exchange.finish()


def attention_back(
    query, keys, values, spots, starts, key_spots, table, inputs, qkv, mixed, parts
):
    low = jnp.bfloat16
    tokens = inputs.shape[1]
    sums = pltpu.VMEM((PLANE * tokens, HEAD_SIZE), jnp.float32)
    return pl.pallas_call(
        attention_back_kernel,
        out_shape=(
            jax.ShapeDtypeStruct(inputs.shape, low),
            jax.ShapeDtypeStruct((*qkv.shape[:2], QKV_WIDTH), low),
            jax.ShapeDtypeStruct((parts.shape[1], PLANE * parts.shape[2]), low),
        ),
        in_specs=[VMEM] * 11,
        out_specs=(VMEM,) * 3,
        scratch_shapes=[
            pltpu.VMEM(mixed.shape, low),
            pltpu.VMEM((PLANE, *parts.shape[1:]), low),
            pltpu.VMEM((PLANE, tokens, QKV_WIDTH), low),
            sums,
            sums,
            pltpu.VMEM((512, PLANE * tokens), low),
            *PlaneExchange.scratch(),
            *WeightScatter.scratch(*parts.shape[1:]),
        ],
        compiler_params=params(3),
        name="attention_back",
    )(query, keys, values, spots, starts, key_spots, table, inputs, qkv, mixed, parts)


def closing_kernel(
    rows_ref,
    parts_ref,
    outs_ref,
    down_ref,
    rows_out,
    query_out,
    keyval_out,
    outs_out,
    down_out,
    *scratch,
):
    out_ref, outs_sum = scratch[:2]
    scratch = list(scratch[2:])

    def take(count):
        taken, scratch[:count] = scratch[:count], []
        return taken

    scatter = SequenceScatter(rows_ref, rows_out, *take(2), take(4), CHUNKS)
    weights = WeightScatter(parts_ref, out_ref, take(4), take(6))
    chip = ChipScatter(outs_ref, *take(3), take(4), PLANE)
    outs = SequenceScatter(outs_sum, outs_out, *take(2), take(4), 1)
    down = ChipScatter(down_ref, *take(3), take(4), DOWN_PARTS)
    d, c, x, core, z, y = place()
    greet(plane_peers(d, c) + chip_peers(d, c, x, core))
    places = (*near_first(z)[::-1], z)
    slots = [place * YS + 1 - y for place in places] + [place * YS + y for place in places]
    weights.first()
    scatter.first()
    for j in slots:
        chip.start(j)
    for j in range(DOWN_PARTS):
        down.start(j)
    for off in range(1, PLANE + 1):
        weights.relay(off)
    for k in range(CHUNKS):
        scatter.relay(k)
        chip.relay(slots[2 * k])
        chip.relay(slots[2 * k + 1])
    for j in range(DOWN_PARTS):
        down.relay(j)
    for off in range(1, PLANE + 1):
        weights.send(off)
    for i, j in enumerate(slots):
        chip.total(j, outs_sum.at[j])
        if i < ZS:
            outs.start(places[i], 0)
        if i == ZS + 1:
            outs.relay_far(0)
        if i == ZS + 2:
            outs.relay_near(0)
    for j in range(DOWN_PARTS):
        down.total(j, down_out.at[j])
    for k in range(CHUNKS):
        scatter.last(k)
    weights.last()
    group_width = GROUP * HEAD_SIZE
    for source in range(PLANE):
        query_out[:, source * group_width : (source + 1) * group_width] = out_ref[
            source, :, :group_width
        ]
    for kind in range(2):
        start = group_width + kind * HEAD_SIZE
        for source in range(0, PLANE, 2):
            after = (kind * PLANE + source) * HEAD_SIZE
            keyval_out[:, after : after + 2 * HEAD_SIZE] = jnp.concatenate(
                [out_ref[source + i, :, start : start + HEAD_SIZE] for i in range(2)], axis=1
            )
    outs.last(0)
    scatter.finish()
    chip.finish()
    outs.finish()
    down.finish()


def closing(rows, parts, outs, down):
    return pl.pallas_call(
        closing_kernel,
        out_shape=(
            jax.ShapeDtypeStruct(rows.shape[1:], jnp.float32),
            jax.ShapeDtypeStruct((parts.shape[1], QUERY_HEADS * HEAD_SIZE), parts.dtype),
            jax.ShapeDtypeStruct((parts.shape[1], 2 * PLANE * HEAD_SIZE), parts.dtype),
            jax.ShapeDtypeStruct(outs.shape[1:], jnp.float32),
            jax.ShapeDtypeStruct((DOWN_PARTS, *down.shape[1:]), jnp.float32),
        ),
        in_specs=[VMEM] * 4,
        out_specs=(VMEM,) * 5,
        scratch_shapes=[
            pltpu.VMEM((PLANE, *parts.shape[1:]), parts.dtype),
            pltpu.VMEM((PLANE, *outs.shape[1:]), jnp.bfloat16),
            *SequenceScatter.scratch(*rows.shape[1:], CHUNKS),
            *WeightScatter.scratch(*parts.shape[1:]),
            *ChipScatter.scratch(PLANE, *outs.shape[1:]),
            *SequenceScatter.scratch(*outs.shape[1:], 1),
            *ChipScatter.scratch(DOWN_PARTS, *down.shape[1:]),
        ],
        compiler_params=params(4),
        name="closing",
    )(rows, parts, outs, down)


def body(
    layer_in,
    positions,
    doc_starts,
    out_grad,
    norm_gains,
    norm_gains_m,
    norm_gains_v,
    w_query,
    w_query_m,
    w_query_v,
    key_value_weight,
    key_value_first_moment,
    key_value_second_moment,
    w_out,
    w_out_m,
    w_out_v,
    w_gate_up,
    w_gate_up_m,
    w_gate_up_v,
    w_down,
    w_down_m,
    w_down_v,
):
    number_of_tokens = layer_in.shape[0]
    ctx_count = lax.axis_size("ctx")
    seq_len = number_of_tokens * ctx_count
    key_value_width = KEY_VALUE_HEADS * HEAD_SIZE
    query_group_size = QUERY_HEADS // KEY_VALUE_HEADS
    score_scale = 1.0 / math.sqrt(HEAD_SIZE)
    needed = -(-512 // number_of_tokens)
    shard_span = min(ctx_count, 1 << max(0, (needed - 1).bit_length()))
    width_of_block = shard_span * number_of_tokens
    count_of_blocks = ctx_count // shard_span
    key_places = lax.all_gather(positions, "ctx", axis=0, tiled=True)
    starts = doc_starts[0]
    own_docs = doc_lookup(positions, starts)
    key_docs = doc_lookup(key_places, starts)
    query_full, keyval_full, out_full, gains_full = (
        lax.all_gather(w_query.astype(jnp.bfloat16), ("dp", "ctx"), axis=0, tiled=True),
        lax.all_gather(key_value_weight.astype(jnp.bfloat16), ("dp", "ctx"), axis=0, tiled=True),
        lax.all_gather(w_out.astype(jnp.bfloat16), ("dp", "ctx"), axis=0, tiled=True),
        lax.all_gather(norm_gains.astype(jnp.bfloat16), ("dp", "ctx"), axis=1, tiled=True),
    )
    gain_one = gains_full[0].astype(jnp.float32)
    gain_two = gains_full[1].astype(jnp.float32)
    layer_rows = layer_in.astype(jnp.float32)
    normed_one, inverse_one = norm_forward(layer_rows)
    input_one = (normed_one * gain_one).astype(jnp.bfloat16)
    query_pre = jnp.dot(input_one, query_full, preferred_element_type=jnp.float32)
    key_value_projected = jnp.dot(input_one, keyval_full, preferred_element_type=jnp.float32)
    cosine_table, sine_table = rope_tables(positions, HEAD_SIZE)
    query_rows = (
        apply_rotation(
            query_pre.reshape(number_of_tokens, QUERY_HEADS, HEAD_SIZE), cosine_table, sine_table
        )
        .astype(jnp.bfloat16)
        .reshape(number_of_tokens, KEY_VALUE_HEADS, query_group_size, HEAD_SIZE)
    )
    keys_own = (
        apply_rotation(
            key_value_projected[:, :key_value_width].reshape(
                number_of_tokens, KEY_VALUE_HEADS, HEAD_SIZE
            ),
            cosine_table,
            sine_table,
        )
        .astype(jnp.bfloat16)
        .reshape(number_of_tokens, key_value_width)
    )
    values_own = key_value_projected[:, key_value_width:].astype(jnp.bfloat16)
    every_key, every_value = (
        lax.all_gather(keys_own, "ctx", axis=0, tiled=True),
        lax.all_gather(values_own, "ctx", axis=0, tiled=True),
    )
    blocked_keys = every_key.reshape(count_of_blocks, width_of_block, KEY_VALUE_HEADS, HEAD_SIZE)
    blocked_values = every_value.reshape(
        count_of_blocks, width_of_block, KEY_VALUE_HEADS, HEAD_SIZE
    )
    place_blocks = key_places.reshape(count_of_blocks, width_of_block)
    doc_blocks = key_docs.reshape(count_of_blocks, width_of_block)

    def visible(place_blk, doc_blk):
        allowed = (place_blk[None, :] <= positions[:, None]) & (
            doc_blk[None, :] == own_docs[:, None]
        )
        return allowed[:, None, None, :]

    def scores_of(key_blk):
        return (
            jnp.einsum("tkgd,nkd->tkgn", query_rows, key_blk, preferred_element_type=jnp.float32)
            * score_scale
        )

    def stats_step(carry, block):
        row_top, row_total = carry
        key_blk, place_blk, doc_blk = block
        allowed = visible(place_blk, doc_blk)
        masked = jnp.where(allowed, scores_of(key_blk), masked_score)
        new_top = jnp.maximum(row_top, jnp.max(masked, axis=-1, keepdims=True))
        row_total = row_total * jnp.exp(row_top - new_top) + jnp.sum(
            jnp.where(allowed, jnp.exp(masked - new_top), 0.0), axis=-1, keepdims=True
        )
        return ((new_top, row_total), None)

    statistic_shape = (number_of_tokens, KEY_VALUE_HEADS, query_group_size, 1)
    (row_top, row_total), unused = lax.scan(
        stats_step,
        (
            jnp.full(statistic_shape, masked_score, jnp.float32),
            jnp.zeros(statistic_shape, jnp.float32),
        ),
        (blocked_keys, place_blocks, doc_blocks),
    )
    log_total = row_top + jnp.log(row_total)

    def probs_of(key_blk, place_blk, doc_blk):
        allowed = visible(place_blk, doc_blk)
        masked = jnp.where(allowed, scores_of(key_blk), masked_score)
        return jnp.where(allowed, jnp.exp(masked - log_total), 0.0)

    def output_step(carry, block):
        key_blk, value_blk, place_blk, doc_blk = block
        probs_low = probs_of(key_blk, place_blk, doc_blk).astype(jnp.bfloat16)
        added = jnp.einsum(
            "tkgn,nkd->tkgd", probs_low, value_blk, preferred_element_type=jnp.float32
        )
        return (carry + added, None)

    attention_output, unused = lax.scan(
        output_step,
        jnp.zeros((number_of_tokens, KEY_VALUE_HEADS, query_group_size, HEAD_SIZE), jnp.float32),
        (blocked_keys, blocked_values, place_blocks, doc_blocks),
    )
    mixed = attention_output.reshape(number_of_tokens, QUERY_HEADS * HEAD_SIZE).astype(jnp.bfloat16)
    middle = layer_rows + jnp.dot(mixed, out_full, preferred_element_type=jnp.float32)
    normed_two, inverse_two = norm_forward(middle)
    input_two = (normed_two * gain_two).astype(jnp.bfloat16)
    gate_up_low = w_gate_up.astype(jnp.bfloat16)
    down_low = w_down.astype(jnp.bfloat16)
    columns = input_two
    gate_up = jnp.dot(
        columns,
        lax.all_gather(gate_up_low, ("dp", "ctx"), axis=0, tiled=True),
        preferred_element_type=jnp.float32,
    )
    gate_part = gate_up[:, :FF]
    up_part = gate_up[:, FF:]
    sigmoid_gate = jax.nn.sigmoid(gate_part)
    silu_gate = gate_part * sigmoid_gate
    hidden = (silu_gate * up_part).astype(jnp.bfloat16)
    columns = hidden
    down_sum = jnp.dot(
        columns,
        lax.all_gather(down_low, ("dp", "ctx"), axis=0, tiled=True),
        preferred_element_type=jnp.float32,
    )
    layer_out = (middle + down_sum).astype(jnp.bfloat16)
    grad_rows = out_grad.astype(jnp.float32)
    grad_hidden = times_transposed(
        out_grad, lax.all_gather(down_low, ("dp", "ctx"), axis=0, tiled=True)
    )
    grad_gate = grad_hidden * up_part * sigmoid_gate * (1.0 + gate_part * (1.0 - sigmoid_gate))
    grad_up = grad_hidden * silu_gate
    grad_gate_up = jnp.concatenate([grad_gate, grad_up], axis=1).astype(jnp.bfloat16)
    down_grad = lax.psum_scatter(
        transposed_times(hidden, out_grad), ("dp", "ctx"), scatter_dimension=0, tiled=True
    )
    grad_normed_two = times_transposed(
        grad_gate_up, lax.all_gather(gate_up_low, ("dp", "ctx"), axis=0, tiled=True)
    )
    gate_up_grad = lax.psum_scatter(
        transposed_times(input_two, grad_gate_up), ("dp", "ctx"), scatter_dimension=0, tiled=True
    )
    grad_norm_two, gain_two_grad = norm_backward(grad_normed_two, normed_two, inverse_two, gain_two)
    grad_middle = grad_rows + grad_norm_two
    grad_middle_low = grad_middle.astype(jnp.bfloat16)
    out_term = transposed_times(mixed, grad_middle_low)
    grad_mixed = (
        times_transposed(grad_middle_low, out_full)
        .astype(jnp.bfloat16)
        .reshape(number_of_tokens, KEY_VALUE_HEADS, query_group_size, HEAD_SIZE)
    )
    delta = jnp.sum(grad_mixed.astype(jnp.float32) * attention_output, axis=-1, keepdims=True)

    def back_step(grad_query, block):
        key_blk, value_blk, place_blk, doc_blk = block
        probs = probs_of(key_blk, place_blk, doc_blk)
        probs_low = probs.astype(jnp.bfloat16)
        grad_probs = jnp.einsum(
            "tkgd,nkd->tkgn", grad_mixed, value_blk, preferred_element_type=jnp.float32
        )
        grad_scores = (probs * (grad_probs - delta) * score_scale).astype(jnp.bfloat16)
        grad_query = grad_query + jnp.einsum(
            "tkgn,nkd->tkgd", grad_scores, key_blk, preferred_element_type=jnp.float32
        )
        key_grad = jnp.einsum(
            "tkgn,tkgd->nkd", grad_scores, query_rows, preferred_element_type=jnp.float32
        )
        value_grad = jnp.einsum(
            "tkgn,tkgd->nkd", probs_low, grad_mixed, preferred_element_type=jnp.float32
        )
        return (grad_query, (key_grad, value_grad))

    grad_query, (key_grads, value_grads) = lax.scan(
        back_step,
        jnp.zeros((number_of_tokens, KEY_VALUE_HEADS, query_group_size, HEAD_SIZE), jnp.float32),
        (blocked_keys, blocked_values, place_blocks, doc_blocks),
    )
    summed_key_gradient, value_sum = (
        lax.psum_scatter(
            key_grads.reshape(seq_len, key_value_width).astype(jnp.bfloat16),
            "ctx",
            scatter_dimension=0,
            tiled=True,
        ).astype(jnp.float32),
        lax.psum_scatter(
            value_grads.reshape(seq_len, key_value_width).astype(jnp.bfloat16),
            "ctx",
            scatter_dimension=0,
            tiled=True,
        ).astype(jnp.float32),
    )
    key_gradient_unrotated = reverse_rotation(
        summed_key_gradient.reshape(number_of_tokens, KEY_VALUE_HEADS, HEAD_SIZE),
        cosine_table,
        sine_table,
    ).reshape(number_of_tokens, key_value_width)
    grad_keyval = jnp.concatenate([key_gradient_unrotated, value_sum], axis=1).astype(jnp.bfloat16)
    grad_query_low = (
        reverse_rotation(
            grad_query.reshape(number_of_tokens, QUERY_HEADS, HEAD_SIZE), cosine_table, sine_table
        )
        .reshape(number_of_tokens, QUERY_HEADS * HEAD_SIZE)
        .astype(jnp.bfloat16)
    )
    grad_normed_one = times_transposed(grad_query_low, query_full) + times_transposed(
        grad_keyval, keyval_full
    )
    query_term = transposed_times(input_one, grad_query_low)
    keyval_term = transposed_times(input_one, grad_keyval)
    grad_norm_one, gain_one_grad = norm_backward(grad_normed_one, normed_one, inverse_one, gain_one)
    in_grad = grad_middle + grad_norm_one
    gain_term = jnp.stack([gain_one_grad, gain_two_grad])
    query_grad, keyval_grad, out_weight_grad, gains_grad = (
        lax.psum_scatter(query_term, ("dp", "ctx"), scatter_dimension=0, tiled=True),
        lax.psum_scatter(keyval_term, ("dp", "ctx"), scatter_dimension=0, tiled=True),
        lax.psum_scatter(out_term, ("dp", "ctx"), scatter_dimension=0, tiled=True),
        lax.psum_scatter(gain_term, ("dp", "ctx"), scatter_dimension=1, tiled=True),
    )
    rates = rates_for(seq_len)
    gains_m_new, gains_v_new, gains_new = adamw(
        norm_gains, gains_grad, norm_gains_m, norm_gains_v, rates[0], 0.0
    )
    query_m_new, query_v_new, query_new = adamw(
        w_query, query_grad, w_query_m, w_query_v, rates[1], weight_decay
    )
    keyval_m_new, keyval_v_new, keyval_new = adamw(
        key_value_weight,
        keyval_grad,
        key_value_first_moment,
        key_value_second_moment,
        rates[2],
        weight_decay,
    )
    out_m_new, out_v_new, out_new = adamw(
        w_out, out_weight_grad, w_out_m, w_out_v, rates[3], weight_decay
    )
    gate_up_m_new, gate_up_v_new, gate_up_new = adamw(
        w_gate_up, gate_up_grad, w_gate_up_m, w_gate_up_v, rates[4], weight_decay
    )
    down_m_new, down_v_new, down_new = adamw(
        w_down, down_grad, w_down_m, w_down_v, rates[5], weight_decay
    )
    return (
        layer_out,
        in_grad,
        gains_grad,
        gains_m_new,
        gains_v_new,
        gains_new,
        query_grad,
        query_m_new,
        query_v_new,
        query_new,
        keyval_grad,
        keyval_m_new,
        keyval_v_new,
        keyval_new,
        out_weight_grad,
        out_m_new,
        out_v_new,
        out_new,
        gate_up_grad,
        gate_up_m_new,
        gate_up_v_new,
        gate_up_new,
        down_grad,
        down_m_new,
        down_v_new,
        down_new,
    )


def tensor_parallel(
    layer_in,
    positions,
    doc_starts,
    out_grad,
    norm_gains,
    norm_gains_m,
    norm_gains_v,
    w_query,
    w_query_m,
    w_query_v,
    key_value_weight,
    key_value_first_moment,
    key_value_second_moment,
    w_out,
    w_out_m,
    w_out_v,
    w_gate_up,
    w_gate_up_m,
    w_gate_up_v,
    w_down,
    w_down_m,
    w_down_v,
):
    low = jnp.bfloat16
    own_tokens, width = layer_in.shape
    seq_len = own_tokens * PLANE
    group = GROUP
    group_width = group * HEAD_SIZE
    ff_part = FF // PLANE
    rows = w_query.shape[0]

    gains_low = norm_gains.astype(low)
    small = jnp.broadcast_to(
        jnp.pad(gains_low.T, ((0, 0), (0, 126)))[None], (PLANE, rows, 128)
    )
    attention_blocks = jnp.concatenate(
        [
            w_query.astype(low).reshape(rows, PLANE, group_width).transpose(1, 0, 2),
            key_value_weight.astype(low)
            .reshape(rows, 2, PLANE, HEAD_SIZE)
            .transpose(2, 0, 1, 3)
            .reshape(PLANE, rows, 2 * HEAD_SIZE),
            small,
        ],
        axis=2,
    )
    spots = jnp.broadcast_to(positions[None, :].astype(jnp.float32), (8, own_tokens))
    cosine_own, sine_own = rope_tables(positions, HEAD_SIZE)
    cosine_own, sine_own = cosine_own[:, 0], sine_own[:, 0]
    table = jnp.concatenate([cosine_own, cosine_own, -sine_own, sine_own], axis=1)
    (
        input_one_all,
        table_all,
        attention_all,
        gain_rows,
        query_rows,
        key_rows,
        value_rows,
        token_spots,
        token_starts,
        key_spots,
        mixed_parts,
        feed_all,
        out_all,
        down_all,
        grads_all,
    ) = attention(
        doc_starts,
        layer_in,
        table,
        spots,
        attention_blocks,
        w_gate_up,
        w_out,
        w_down,
        out_grad,
    )
    gain_one, gain_two = gain_rows[0], gain_rows[1]
    mixed = mixed_parts.transpose(2, 0, 1, 3).reshape(own_tokens, width)
    out_weight = out_all.reshape(width, width)
    branch = jnp.dot(mixed, out_weight, preferred_element_type=jnp.float32)

    layer_rows = layer_in.astype(jnp.float32)
    middle = layer_rows + branch
    normed_two, inverse_two = norm_forward(middle)
    grad_normed_two, down_sum, feed_term, down_term = feed(
        (normed_two * gain_two).astype(low),
        grads_all,
        feed_all.reshape(width, 2 * ff_part),
        down_all,
    )
    layer_out = (middle + down_sum).astype(low)

    grad_norm_two, unused = norm_backward(grad_normed_two, normed_two, inverse_two, gain_two)
    grad_middle = out_grad.astype(jnp.float32) + grad_norm_two
    grad_middle_low = grad_middle.astype(low)
    out_term = transposed_times(mixed, grad_middle_low).astype(low)
    grad_mixed = (
        times_transposed(grad_middle_low, out_weight)
        .astype(low)
        .reshape(own_tokens, PLANE, PAIRS, 2 * HEAD_SIZE)
        .transpose(1, 2, 0, 3)
    )
    one_parts, qkv_term, feed_grad = attention_back(
        query_rows,
        key_rows,
        value_rows,
        token_spots,
        token_starts,
        key_spots,
        table_all,
        input_one_all,
        attention_all,
        grad_mixed,
        feed_term.reshape(RANKS, rows, 2 * ff_part),
    )
    gate_up_grad = feed_grad.astype(jnp.float32)
    grad_normed_one, query_grad, keyval_grad, out_weight_grad, down_grad = closing(
        one_parts,
        qkv_term,
        out_term.reshape(RANKS, rows, width),
        down_term.reshape(4 * DOWN_PARTS, -1, width),
    )
    down_grad = down_grad.reshape(w_down.shape)
    normed_one, inverse_one = norm_forward(layer_rows)
    grad_norm_one, unused = norm_backward(grad_normed_one, normed_one, inverse_one, gain_one)
    in_grad = grad_middle + grad_norm_one
    query_grad = query_grad.astype(jnp.float32)
    keyval_grad = keyval_grad.astype(jnp.float32)

    def low_times(weight, grad):
        return jnp.sum(weight.astype(low).astype(jnp.float32) * grad, axis=1)

    gains_grad = jnp.stack(
        [
            low_times(w_query, query_grad) + low_times(key_value_weight, keyval_grad),
            low_times(w_gate_up, gate_up_grad),
        ]
    ) / gains_low.astype(jnp.float32)

    rates = rates_for(seq_len)
    return (
        layer_out,
        in_grad,
        gains_grad,
        *adamw(norm_gains, gains_grad, norm_gains_m, norm_gains_v, rates[0], 0.0),
        query_grad,
        *adamw(w_query, query_grad, w_query_m, w_query_v, rates[1], weight_decay),
        keyval_grad,
        *adamw(
            key_value_weight,
            keyval_grad,
            key_value_first_moment,
            key_value_second_moment,
            rates[2],
            weight_decay,
        ),
        out_weight_grad,
        *adamw(w_out, out_weight_grad, w_out_m, w_out_v, rates[3], weight_decay),
        gate_up_grad,
        *adamw(w_gate_up, gate_up_grad, w_gate_up_m, w_gate_up_v, rates[4], weight_decay),
        down_grad,
        *adamw(w_down, down_grad, w_down_m, w_down_v, rates[5], weight_decay),
    )


def solution(mesh):
    planned = tensor_parallel if dict(mesh.shape) == {"dp": 2 * XS, "ctx": ZS * YS} else body
    return jax.shard_map(
        planned,
        mesh=mesh,
        in_specs=(
            P(("dp", "ctx"), None),
            P(("dp", "ctx")),
            P("dp", None),
            P(("dp", "ctx"), None),
            P(None, ("dp", "ctx")),
            P(None, ("dp", "ctx")),
            P(None, ("dp", "ctx")),
            P(("dp", "ctx"), None),
            P(("dp", "ctx"), None),
            P(("dp", "ctx"), None),
            P(("dp", "ctx"), None),
            P(("dp", "ctx"), None),
            P(("dp", "ctx"), None),
            P(("dp", "ctx"), None),
            P(("dp", "ctx"), None),
            P(("dp", "ctx"), None),
            P(("dp", "ctx"), None),
            P(("dp", "ctx"), None),
            P(("dp", "ctx"), None),
            P(("dp", "ctx"), None),
            P(("dp", "ctx"), None),
            P(("dp", "ctx"), None),
        ),
        out_specs=(
            P(("dp", "ctx"), None),
            P(("dp", "ctx"), None),
            P(None, ("dp", "ctx")),
            P(None, ("dp", "ctx")),
            P(None, ("dp", "ctx")),
            P(None, ("dp", "ctx")),
            P(("dp", "ctx"), None),
            P(("dp", "ctx"), None),
            P(("dp", "ctx"), None),
            P(("dp", "ctx"), None),
            P(("dp", "ctx"), None),
            P(("dp", "ctx"), None),
            P(("dp", "ctx"), None),
            P(("dp", "ctx"), None),
            P(("dp", "ctx"), None),
            P(("dp", "ctx"), None),
            P(("dp", "ctx"), None),
            P(("dp", "ctx"), None),
            P(("dp", "ctx"), None),
            P(("dp", "ctx"), None),
            P(("dp", "ctx"), None),
            P(("dp", "ctx"), None),
            P(("dp", "ctx"), None),
            P(("dp", "ctx"), None),
            P(("dp", "ctx"), None),
            P(("dp", "ctx"), None),
        ),
        check_vma=False,
    )
```
